32 devices in a mesh: dp: 4 (over y, core), expert: 2 (over x), narrow: 4 (over z).
Axes of the slice: x: 2, y: 2, z: 4, core: 2. Of those that a mesh axis runs over, the one named last changes fastest.
Arguments:
- inputs: float32 [16384, 512], P('dp'), may hold values from -6 to 6
- seg_ids: int32 [16, 1024], P('dp'), may hold values from 0 to 7, never falling along the last dimension, each value on 1 to 256 neighbouring positions
- chosen: int32 [16384, 2], P('dp'), may hold values from 0 to 7, all different within a row
- gain_one: float32 [512], replicated, may hold values from 0.5 to 1.5
- shift_one: float32 [512], replicated, may hold values from -1.2 to 1.2
- query_w: bfloat16 [8, 512, 64], P('expert', None, 'narrow'), may hold values from -0.25 to 0.25
- query_b: float32 [8, 64], P('expert', 'narrow'), may hold values from -1.2 to 1.2
- key_w: bfloat16 [512, 64], P(None, 'narrow'), may hold values from -0.25 to 0.25
- value_w: bfloat16 [512, 64], P(None, 'narrow'), may hold values from -0.25 to 0.25
- value_b: float32 [64], P('narrow'), may hold values from -1.2 to 1.2
- out_w: bfloat16 [8, 64, 512], P('expert', 'narrow'), may hold values from -2 to 2
- out_b: float32 [512], replicated, may hold values from -1.2 to 1.2
- router_w: bfloat16 [512, 8], replicated, may hold values from -0.25 to 0.25
- router_b: float32 [8], replicated, may hold values from -0.6 to 0.6
- gain_two: float32 [512], replicated, may hold values from 0.5 to 1.5
- shift_two: float32 [512], replicated, may hold values from -1.2 to 1.2
- up_w: bfloat16 [512, 2048], P(None, 'narrow'), may hold values from -0.25 to 0.25
- up_b: float32 [2048], P('narrow'), may hold values from -1.2 to 1.2
- down_w: bfloat16 [2048, 512], P('narrow'), may hold values from -0.125 to 0.125
- down_b: float32 [512], replicated, may hold values from -1.2 to 1.2
- cotangent: bfloat16 [16384, 512], P(('dp', 'expert'), 'narrow'), may hold values from -6 to 6
Outputs:
- output: float32 [16384, 512], P(('dp', 'expert'), 'narrow')
- input_grad: float32 [16384, 512], P(('dp', 'expert', 'narrow'))
- gain_one_grad: float32 [512], replicated
- shift_one_grad: float32 [512], replicated
- query_w_grad: float32 [8, 512, 64], P('expert', None, 'narrow')
- query_b_grad: float32 [8, 64], P('expert', 'narrow')
- key_w_grad: float32 [512, 64], P(None, 'narrow')
- value_w_grad: float32 [512, 64], P(None, 'narrow')
- value_b_grad: float32 [64], P('narrow')
- out_w_grad: float32 [8, 64, 512], P('expert', 'narrow')
- out_b_grad: float32 [512], replicated
- router_w_grad: float32 [512, 8], replicated
- router_b_grad: float32 [8], replicated
- gain_two_grad: float32 [512], replicated
- shift_two_grad: float32 [512], replicated
- up_w_grad: float32 [512, 2048], P(None, 'narrow')
- up_b_grad: float32 [2048], P('narrow')
- down_w_grad: float32 [2048, 512], P('narrow')
- down_b_grad: float32 [512], replicated
The draws below stay inside these ranges and needn't reach their ends.
Inputs may be any that keep to these rules, and one draw needn't show every extreme that they name: `chosen`: each token names two different experts. `seg_ids`: sentence numbers never fall along a row; a sentence has 1 to 256 tokens.
All inputs are finite; a program needn't handle non-finite values.
Results may differ from the reference program's by a relative error of at most 0.02.
Values may be sent and summed in bfloat16 or wider, within the bound.
A program may use at most 320 MiB of HBM per device.

```python
import math
import jax
import jax.numpy as jnp
import numpy as np
from jax import lax

D = 512
HEAD = 64
EXPERTS = 8
FF = 2048
S = 1024
SENTS = 8
MOST = 256
ROWS_ALL = 16
TOKENS = 16384


def levels(key, extent, cuts, least, top_value):
    def one(axis_at, blocks):
        heights = jax.random.uniform(jax.random.fold_in(jax.random.fold_in(key, 6), axis_at), (blocks,), jnp.float32, least / len(cuts), top_value / len(cuts))
        return jnp.repeat(jnp.exp(heights), extent[axis_at] // blocks).reshape((-1,) + (1,) * (len(extent) - axis_at - 1))

    gain = one(*cuts[0])
    for cut in cuts[1:]:
        gain = gain * one(*cut)
    return gain


def choose_distinct(key, rows, count, top, lift):
    ranking = jax.random.permutation(jax.random.fold_in(key, 1), count)
    boost = ranking
    for power in range(3):
        boost = boost * boost // count
    boost = boost * lift // count
    tickets = jax.random.randint(jax.random.fold_in(key, 2), (rows, count), 0, 4096) + boost
    holders = jax.random.permutation(jax.random.fold_in(key, 3), rows)[jnp.arange(count) % rows]
    tickets = jnp.where(jnp.arange(rows)[:, None] == holders[None, :], 1 << 14, tickets)
    merit = tickets * count + jnp.arange(count)
    return lax.top_k(merit.astype(jnp.int32), top)[1].astype(jnp.int32)


def profile(number_of, total, reach, skew):
    portions = [(1 << 20) // math.isqrt(rank ** skew) + 1 for rank in range(2, number_of + 1)]
    rest, counts = total - reach - (number_of - 1), [1] * (number_of - 1)
    while rest > 0:
        free = [i for i in range(number_of - 1) if counts[i] < reach]
        pool, remaining = sum([portions[i] for i in free]), rest
        for i in free:
            extra = min(reach - counts[i], max(1, remaining * portions[i] // pool), rest)
            counts[i] = counts[i] + extra
            rest = rest - extra
    return np.array([reach] + counts)


def uneven_parts(rng, amount, total, limit, skew):
    if amount == 2:
        one = jax.random.randint(rng, (), max(1, total - limit), min(limit, total - 1) + 1)
        return jnp.stack([one, total - one])
    tallies = jnp.asarray(profile(amount, total, limit, skew), jnp.int32)
    pairs = (amount - 1) // 2
    donor, taker = tallies[1:1 + 2 * pairs:2], tallies[2:2 + 2 * pairs:2]
    room = jnp.minimum(donor - 1, limit - taker)
    moved = jax.random.randint(jax.random.fold_in(rng, 1), (pairs,), 0, 1 << 20) % (room + 1)
    tallies = tallies.at[1:1 + 2 * pairs:2].set(donor - moved).at[2:2 + 2 * pairs:2].set(taker + moved)
    return tallies[jax.random.permutation(jax.random.fold_in(rng, 2), amount)]


def gaussian(key, extent, deviation, bound, cuts=(), kind=jnp.bfloat16):
    factor_of = levels(key, extent, cuts, -0.22, 0.18) if cuts else 1.0
    result = jax.random.normal(key, extent, jnp.float32) * deviation * factor_of
    return jnp.minimum(jnp.maximum(result, -bound), bound).astype(kind)


def setup_inputs(seed: int = 0) -> dict:
    splits = jax.random.split(jax.random.key(seed), 22)
    return {
        "inputs": gaussian(splits[0], (TOKENS, D), 1.0, 6.0, ((0, 4),), jnp.float32),
        "seg_ids": jax.vmap(lambda own: jnp.searchsorted(jnp.cumsum(uneven_parts(own, SENTS, S, MOST, 2)), jnp.arange(S), side="right"))(jax.random.split(splits[1], ROWS_ALL)).reshape((ROWS_ALL, S)).astype(jnp.int32),
        "chosen": choose_distinct(splits[2], TOKENS, EXPERTS, 2, 2048),
        "gain_one": jnp.clip(1.0 + 0.1 * jax.random.normal(splits[3], (D,), jnp.float32), 0.5, 1.5),
        "shift_one": gaussian(splits[4], (D,), 0.2, 1.2, (), jnp.float32),
        "query_w": gaussian(splits[5], (EXPERTS, D, HEAD), D ** -0.5, 0.25, ((0, 2), (2, 4))),
        "query_b": gaussian(splits[6], (EXPERTS, HEAD), 0.2, 1.2, ((0, 2), (1, 4)), jnp.float32),
        "key_w": gaussian(splits[7], (D, HEAD), D ** -0.5, 0.25, ((1, 4),)),
        "value_w": gaussian(splits[8], (D, HEAD), D ** -0.5, 0.25, ((1, 4),)),
        "value_b": gaussian(splits[9], (HEAD,), 0.2, 1.2, ((0, 4),), jnp.float32),
        "out_w": gaussian(splits[10], (EXPERTS, HEAD, D), (HEAD // 8) ** -0.5, 2.0, ((0, 2), (1, 4))),
        "out_b": gaussian(splits[11], (D,), 0.2, 1.2, (), jnp.float32),
        "router_w": gaussian(splits[12], (D, EXPERTS), D ** -0.5, 0.25),
        "router_b": gaussian(splits[13], (EXPERTS,), 0.1, 0.6, (), jnp.float32),
        "gain_two": jnp.clip(1.0 + 0.1 * jax.random.normal(splits[14], (D,), jnp.float32), 0.5, 1.5),
        "shift_two": gaussian(splits[15], (D,), 0.2, 1.2, (), jnp.float32),
        "up_w": gaussian(splits[16], (D, FF), D ** -0.5, 0.25, ((1, 4),)),
        "up_b": gaussian(splits[17], (FF,), 0.2, 1.2, ((0, 4),), jnp.float32),
        "down_w": gaussian(splits[18], (FF, D), FF ** -0.5, 0.125, ((0, 4),)),
        "down_b": gaussian(splits[19], (D,), 0.2, 1.2, (), jnp.float32),
        "cotangent": gaussian(splits[20], (TOKENS, D), 1.0, 6.0, ((0, 8), (1, 4))),
    }


epsilon = 1e-05
masked_fill = -1000000000.0
precise = lax.Precision.HIGHEST

@jax.custom_vjp
def low(v):
    return lax.optimization_barrier(v.astype(jnp.bfloat16)).astype(jnp.float32)

@jax.custom_vjp
def low_back(v):
    return v

def low_keep(v):
    return (low(v), None)

def low_pass(kept, grad):
    return (grad,)

def back_keep(v):
    return (v, None)

def back_low(kept, grad):
    return (low(grad),)
low.defvjp(low_keep, low_pass)
low_back.defvjp(back_keep, back_low)

def normalize(values, scales, shifts):
    average = lax.optimization_barrier(jnp.mean(values, axis=1, keepdims=True))
    centred = values - average
    variance = lax.optimization_barrier(jnp.mean(centred * centred, axis=1, keepdims=True))
    return centred * lax.rsqrt(variance + epsilon) * scales + shifts

def attend_row(carried, pieces):
    query_row, key_row, value_row, seg_row = pieces
    raw_scores = jnp.einsum('esh,kh->esk', query_row, key_row, precision=precise) * (1.0 / math.sqrt(HEAD))
    scores = low_back(raw_scores)
    same_doc = (seg_row[:, None] == seg_row[None, :])[None]
    scores = jnp.where(same_doc, scores, masked_fill)
    row_top = lax.optimization_barrier(jnp.max(scores, axis=2, keepdims=True))
    exponent = jnp.exp(scores - row_top)
    probability = low(exponent / lax.optimization_barrier(jnp.sum(exponent, axis=2, keepdims=True)))
    mixed_row = low_back(low(jnp.einsum('esk,kh->esh', probability, value_row, precision=precise)))
    return (carried, mixed_row)

def layer(params, seg_ids, chosen):
    inputs, gain_one, shift_one, query_w, query_b, key_w, value_w, value_b, out_w, out_b, router_w, router_b, gain_two, shift_two, up_w, up_b, down_w, down_b = params
    rounded = low(normalize(inputs, gain_one, shift_one))
    queries = low_back(low(jnp.einsum('td,edh->eth', rounded, query_w, precision=precise) + query_b[:, None, :]))
    key_all = low(jnp.dot(rounded, key_w, precision=precise))
    value_all = low(jnp.dot(rounded, value_w, precision=precise) + value_b)
    logits = jnp.dot(rounded, router_w, precision=precise) + router_b
    onehot = (chosen[:, :, None] == jnp.arange(EXPERTS, dtype=jnp.int32)[None, None, :]).astype(logits.dtype)
    picked = lax.optimization_barrier(jnp.sum(logits[:, None, :] * onehot, axis=2))
    weights = jax.nn.softmax(picked, axis=1)
    gate_dense = lax.optimization_barrier(jnp.sum(weights[:, :, None] * onehot, axis=1))
    row_count = TOKENS // S
    query_rows = jnp.transpose(queries.reshape(EXPERTS, row_count, S, HEAD), (1, 0, 2, 3))
    key_rows = key_all.reshape(row_count, S, HEAD)
    value_rows = value_all.reshape(row_count, S, HEAD)
    start_carry = jnp.zeros((), logits.dtype)
    ignored, mixed_rows = lax.scan(jax.checkpoint(attend_row), start_carry, (query_rows, key_rows, value_rows, seg_ids))
    mixed = jnp.transpose(mixed_rows, (1, 0, 2, 3)).reshape(EXPERTS, TOKENS, HEAD)
    projected = low_back(jnp.einsum('eth,ehd->etd', mixed, out_w, precision=precise))
    attention = jnp.einsum('te,etd->td', gate_dense, projected, precision=precise) + out_b
    hidden = inputs + attention
    second = low(normalize(hidden, gain_two, shift_two))
    upper = low_back(jnp.dot(second, up_w, precision=precise) + up_b)
    active = low(jax.nn.gelu(upper))
    return hidden + jnp.dot(active, down_w, precision=precise) + down_b

def reference(inputs, seg_ids, chosen, gain_one, shift_one, query_w, query_b, key_w, value_w, value_b, out_w, out_b, router_w, router_b, gain_two, shift_two, up_w, up_b, down_w, down_b, cotangent):
    floats = tuple((item.astype(jnp.float32) for item in (inputs, gain_one, shift_one, query_w, query_b, key_w, value_w, value_b, out_w, out_b, router_w, router_b, gain_two, shift_two, up_w, up_b, down_w, down_b)))

    def forward(*params):
        return layer(params, seg_ids, chosen)
    output, pullback = jax.vjp(forward, *floats)
    grads = pullback(cotangent.astype(jnp.float32))
    return (output, grads[0], grads[1], grads[2], grads[3], grads[4], grads[5], grads[6], grads[7], grads[8], grads[9], grads[10], grads[11], grads[12], grads[13], grads[14], grads[15], grads[16], grads[17])
```

```python
import functools
import math

import jax
import jax.numpy as jnp
from jax import lax
from jax.experimental import pallas as pl
from jax.experimental.pallas import tpu as pltpu
from jax.sharding import PartitionSpec as P

HEAD = 64
LONGEST = 256
EPSILON = 1e-05
MASKED = -1000000000.0
GELU_A = math.sqrt(2.0 / math.pi)
GELU_B = 0.044715
F32 = jnp.float32
BF16 = jnp.bfloat16
MESH = pl.DeviceIdType.MESH


def dot(a, b):
    return lax.dot_general(a, b, (((1,), (0,)), ((), ())), preferred_element_type=F32)


def dot_nt(a, b):
    return lax.dot_general(a, b, (((1,), (1,)), ((), ())), preferred_element_type=F32)


def dot_tn(a, b):
    return lax.dot_general(a, b, (((0,), (0,)), ((), ())), preferred_element_type=F32)


def norm_stats(x):
    centred = x - jnp.mean(x, axis=1, keepdims=True)
    inverse = lax.rsqrt(jnp.mean(centred * centred, axis=1, keepdims=True) + EPSILON)
    return centred * inverse, inverse


def rem(a, b):
    return lax.rem(a, b)


class Sizes:
    def __init__(self, dp, expert, narrow, tokens, width, row_len, local_experts, ff_local):
        self.dp, self.expert, self.narrow = dp, expert, narrow
        self.tokens, self.width, self.row_len = tokens, width, row_len
        self.local_experts = local_experts
        self.experts = local_experts * expert
        self.group = expert * narrow
        self.block = tokens // self.group
        self.rows_y = dp // 2
        self.plane = self.rows_y * expert
        self.ff_local = ff_local
        self.head_part = HEAD // narrow
        self.shard = local_experts * self.head_part
        self.per_row = row_len // self.block
        spans = [
            min(row_len, (j + 1) * self.block + LONGEST) - max(0, j * self.block - LONGEST)
            for j in range(self.per_row)
        ]
        self.window = max(spans)
        self.reach = max(1, LONGEST // self.block) if self.per_row > 1 else 0
        self.piece = min(self.block, LONGEST)
        self.tile = min(256, self.block)
        self.up_rows = narrow * ff_local // width
        self.small_rows = 24


def kernel(
    z,
    x_any,
    seg_ref,
    chosen_ref,
    vec_ref,
    q_ref,
    k_ref,
    v_ref,
    o_ref,
    r_ref,
    up_any,
    down_any,
    cot_ref,
    out_ref,
    ig_ref,
    gq_ref,
    go_ref,
    gk_ref,
    gv_ref,
    gup_ref,
    gdown_ref,
    small_ref,
    xw,
    xcols,
    rw,
    wq,
    wo,
    wk,
    wv,
    bias,
    ffw,
    cot,
    segs,
    segc,
    kn,
    vn,
    kt,
    vt,
    qt,
    qk,
    prob,
    mix,
    mixg,
    hid,
    acc,
    second,
    active,
    ugrad,
    sgrad,
    hgrad,
    hgb,
    mgk,
    dk,
    dv,
    dq,
    dqt,
    halo_out,
    halo_in,
    delta,
    outd,
    gsend,
    crecv,
    psend,
    precv,
    zsend,
    zrecv,
    fin,
    gqo,
    cqo,
    pqo,
    rqo,
    zqo,
    yqo,
    fqo,
    gkv,
    ckv,
    pkv,
    rkv,
    zkv,
    ykv,
    fkv,
    sp,
    csp,
    psp,
    rsp,
    zsp,
    ysp,
    loc_sem,
    q_s,
    q_r,
    o_s,
    o_r,
    w_s,
    w_r,
    b_s,
    b_r,
    m_s,
    m_r,
    fz_s,
    fz_r,
    fp_s,
    fp_r,
    fm_s,
    fm_r,
    ct_s,
    ct_r,
    od_s,
    od_r,
    hl_s,
    hl_r,
    gc_s,
    gc_r,
    gp_s,
    gp_r,
    gz_s,
    gz_r,
    ga_s,
    ga_r,
    qc_s,
    qc_r,
    qp_s,
    qp_r,
    qz_s,
    qz_r,
    qa_s,
    qa_r,
):
    d, e, n = lax.axis_index("dp"), lax.axis_index("expert"), lax.axis_index("narrow")
    c, y = rem(d, 2), lax.div(d, 2)
    N, G, NP, NE, NY = z.narrow, z.group, z.plane, z.expert, z.rows_y
    T, W, D, R, HP, LE = z.block, z.window, z.width, z.shard, z.head_part, z.local_experts
    FL = z.ff_local
    half = D // 2
    here = e * N + n
    spot = y * NE + e
    mate = (d + 1 - 2 * c, e, n)

    def in_group(j):
        at = rem(here + j + G, G)
        return at, (d, lax.div(at, N), rem(at, N))

    def in_plane(j):
        at = rem(spot + j + NP, NP)
        return at, (2 * lax.div(at, NE) + c, rem(at, NE), n)

    def in_line(j):
        at = rem(n + j + N, N)
        return at, (d, e, at)

    def in_rows(j):
        at = rem(y + j + NY, NY)
        return at, (2 * at + c, e, n)

    started = []

    def push(src, dst, send, recv, device):
        copy = pltpu.make_async_remote_copy(
            src_ref=src,
            dst_ref=dst,
            send_sem=send,
            recv_sem=recv,
            device_id=device,
            device_id_type=MESH,
        )
        copy.start()
        started.append(copy)

    def landed(dst, send, recv):
        pltpu.make_async_remote_copy(
            src_ref=dst,
            dst_ref=dst,
            send_sem=send,
            recv_sem=recv,
            device_id=mate,
            device_id_type=MESH,
        ).wait_recv()

    def rows(start, size, step=16):
        return pl.ds(pl.multiple_of(start, step), size)

    start = here * T
    row = lax.div(start, z.row_len)
    spot_in_row = rem(here, z.per_row)
    base = row * z.row_len
    ws = jnp.minimum(jnp.maximum(spot_in_row * T - LONGEST, 0), z.row_len - W)
    off = spot_in_row * T - ws
    own = rows(off, T, 128)

    x_copy = pltpu.make_async_copy(x_any.at[rows(base + ws, W, 128)], xw, loc_sem.at[0])
    x_copy.start()
    up_copy = pltpu.make_async_copy(up_any, ffw.at[n, pl.ds(0, D)], loc_sem.at[1])
    up_copy.start()
    down_copy = pltpu.make_async_copy(down_any, ffw.at[n, pl.ds(D, FL)], loc_sem.at[2])
    down_copy.start()
    cols_copy = pltpu.make_async_copy(
        x_any.at[rows(e * N * T, N * T, 128), rows(n * (D // N), D // N, 128)], xcols, loc_sem.at[3]
    )
    cols_copy.start()

    wq[rows(here * R, R)] = q_ref[...]
    wo[rows(here * R, R)] = o_ref[...]
    wk[rows(n * HP, HP)] = k_ref[...]
    wv[rows(n * HP, HP)] = v_ref[...]
    bias[here] = vec_ref[8:16, :]

    barrier = pltpu.get_barrier_semaphore()
    pl.semaphore_signal(barrier, inc=1, device_id=mate, device_id_type=MESH)
    for j in range(1, NP):
        pl.semaphore_signal(barrier, inc=1, device_id=in_plane(j)[1], device_id_type=MESH)
    for j in range(1, G):
        pl.semaphore_signal(barrier, inc=1, device_id=in_group(j)[1], device_id_type=MESH)
    pl.semaphore_wait(barrier, NP + G - 1)

    mine_cols = rows(c * half, half, 128)
    for j in range(1, N):
        _, to = in_line(j)
        at = rows(n * HP, HP)
        push(wk.at[at], wk.at[at], w_s.at[0, j], w_r.at[0, j], to)
        push(wv.at[at], wv.at[at], w_s.at[1, j], w_r.at[1, j], to)
    for j in range(1, G):
        _, to = in_group(j)
        push(bias.at[here], bias.at[here], b_s.at[j], b_r.at[j], to)
    for j in range(1, G):
        _, to = in_group(j)
        at = wq.at[rows(here * R, R), mine_cols]
        push(at, at, q_s.at[j], q_r.at[j], to)
    for j in range(1, G):
        _, to = in_group(j)
        at = wo.at[rows(here * R, R), mine_cols]
        push(at, at, o_s.at[j], o_r.at[j], to)
    up_copy.wait()
    down_copy.wait()
    FR = D + FL
    SR = FR // (2 * NP)
    slot_rows = rows((c * NP + spot) * SR, SR)
    for j in range(1, N):
        _, to = in_line(j)
        at = ffw.at[n, slot_rows]
        push(at, at, fz_s.at[j], fz_r.at[j], to)
    CW = D // N
    cot[:, rows(n * CW, CW, 128)] = cot_ref[rows(n * T, T, 128), :]
    for j in range(1, N):
        there, to = in_line(j)
        push(
            cot_ref.at[rows(there * T, T, 128)],
            cot.at[:, rows(n * CW, CW, 128)],
            ct_s.at[j],
            ct_r.at[j],
            to,
        )

    x_copy.wait()
    gain_one, shift_one = vec_ref[0:1, :], vec_ref[1:2, :]

    def norm_one(i, carry):
        at = rows(i * 128, 128, 128)
        unit, _ = norm_stats(xw[at, :])
        rw[at, :] = (unit * gain_one + shift_one).astype(BF16)
        return carry

    lax.fori_loop(0, W // 128, norm_one, 0)

    seg_all = seg_ref[...].astype(F32)
    row_id = lax.broadcasted_iota(jnp.int32, seg_all.shape, 0)
    seg_here = jnp.sum(jnp.where(row_id == row, seg_all, 0.0), axis=0, keepdims=True)
    segs[...] = jnp.broadcast_to(seg_here, segs.shape)
    segc[...] = jnp.transpose(segs[:, rows(ws, W, 128)])
    seg_own = segs[0:1, rows(spot_in_row * T, T, 128)]
    logits = dot_nt(r_ref[...], rw[own, :]) + vec_ref[16:24, 0:1]
    expert_id = lax.broadcasted_iota(jnp.int32, (z.experts, T), 0)
    hot, picked = [], []
    for k in range(2):
        chosen = chosen_ref[k : k + 1, rows(start, T, 128)]
        hot.append((expert_id == chosen).astype(F32))
        picked.append(jnp.sum(logits * hot[k], axis=0, keepdims=True))
    top = jnp.maximum(picked[0], picked[1])
    raised = [jnp.exp(p - top) for p in picked]
    total = raised[0] + raised[1]
    gate = [r / total for r in raised]

    for j in range(1, N):
        there, _ = in_line(-j)
        at = rows(there * HP, HP)
        landed(wk.at[at], w_s.at[0, j], w_r.at[0, j])
        landed(wv.at[at], w_s.at[1, j], w_r.at[1, j])
    for j in range(1, G):
        there, _ = in_group(-j)
        landed(bias.at[there], b_s.at[j], b_r.at[j])
    value_b = bias[0, 2:3, 0:HEAD]
    for j in range(1, N):
        value_b = value_b + bias[j, 2:3, 0:HEAD]
    value_col = jnp.transpose(jnp.broadcast_to(value_b, (8, HEAD)))[:, 0:1]
    kn[...] = dot_nt(rw[...], wk[...]).astype(BF16)
    kt[...] = dot_nt(wk[...], rw[...]).astype(BF16)
    vn[...] = (dot_nt(rw[...], wv[...]) + value_b).astype(BF16)
    vt[...] = (dot_nt(wv[...], rw[...]) + value_col).astype(BF16)

    other_cols = rows((1 - c) * half, half, 128)
    for j in range(1, G):
        there, _ = in_group(-j)
        at = wq.at[rows(there * R, R), mine_cols]
        landed(at, q_s.at[j], q_r.at[j])
        push(at, at, m_s.at[0, j], m_r.at[0, j], mate)
    for j in range(1, G):
        there, _ = in_group(-j)
        landed(wq.at[rows(there * R, R), other_cols], m_s.at[0, j], m_r.at[0, j])
    qt[...] = dot_nt(wq[...], rw[own, :])

    def expert_rows(at, i, part):
        return ((at * N + part) * LE + i) * HP

    for part in range(N):
        chosen_rows = [jnp.zeros((HP, T), F32), jnp.zeros((HP, T), F32)]
        for at in range(NE):
            g = at * N + part
            column = jnp.transpose(jnp.broadcast_to(bias[g, 1:2, 0:128], (8, 128)))
            for i in range(LE):
                lo = expert_rows(at, i, part)
                one = qt[lo : lo + HP, :] + column[i * HP : (i + 1) * HP, 0:1]
                for k in range(2):
                    chosen_rows[k] = chosen_rows[k] + one * hot[k][at * LE + i : at * LE + i + 1, :]
        for k in range(2):
            qk[k, part * HP : (part + 1) * HP, :] = chosen_rows[k].astype(BF16)

    for j in range(1, G):
        there, _ = in_group(-j)
        at = wo.at[rows(there * R, R), mine_cols]
        landed(at, o_s.at[j], o_r.at[j])
        push(at, at, m_s.at[1, j], m_r.at[1, j], mate)

    scale = 1.0 / math.sqrt(HEAD)
    TL = z.tile
    tiles = T // TL
    seg_tiles = [seg_own[:, i * TL : (i + 1) * TL] for i in range(tiles)]

    def attend(k):
        for i in range(tiles):
            at = pl.ds(i * TL, TL)
            scores = dot(kn[...], qk[k, :, at]) * scale
            scores = jnp.where(segc[:, 0:1] == seg_tiles[i], scores, MASKED)
            high = jnp.max(scores, axis=0, keepdims=True)
            raised_scores = jnp.exp(scores - high)
            low = (raised_scores * (1.0 / jnp.sum(raised_scores, axis=0, keepdims=True))).astype(BF16)
            prob[k, :, at] = low
            mix[k, :, at] = dot(vt[...], low)

    attend(0)
    for j in range(1, N):
        there, _ = in_line(-j)
        at = ffw.at[there, slot_rows]
        landed(at, fz_s.at[j], fz_r.at[j])
        for i in range(1, NP):
            _, to = in_plane(i)
            push(at, at, fp_s.at[j, i], fp_r.at[j, i], to)
    attend(1)

    for part in range(N):
        for at in range(NE):
            for i in range(LE):
                lo = expert_rows(at, i, part)
                x = at * LE + i
                gated = jnp.zeros((HP, T), F32)
                for k in range(2):
                    rounded_mix = mix[k, part * HP : (part + 1) * HP, :].astype(BF16).astype(F32)
                    gated = gated + rounded_mix * (hot[k][x : x + 1, :] * gate[k])
                mixg[lo : lo + HP, :] = gated.astype(BF16)
    for j in range(1, G):
        there, _ = in_group(-j)
        landed(wo.at[rows(there * R, R), other_cols], m_s.at[1, j], m_r.at[1, j])
    out_b, down_b = vec_ref[2:3, :], vec_ref[5:6, :]
    gain_two, shift_two = vec_ref[3:4, :], vec_ref[4:5, :]
    attention = dot_tn(mixg[...], wo[...]) + out_b
    acc[...] = attention + down_b
    hid[...] = xw[own, :] + attention

    def norm_two(i, carry):
        at = rows(i * 128, 128, 128)
        unit, _ = norm_stats(hid[at, :])
        second[at, :] = (unit * gain_two + shift_two).astype(BF16)
        return carry

    lax.fori_loop(0, T // 128, norm_two, 0)
    sgrad[...] = jnp.zeros_like(sgrad)

    for j in range(1, N):
        there, _ = in_line(-j)
        landed(cot.at[:, rows(there * CW, CW, 128)], ct_s.at[j], ct_r.at[j])

    HR = FR // 2
    HS = HR // NP

    def core_start(j):
        push(
            gsend.at[j, rows((1 - c) * HR, HR)], crecv.at[j], gc_s.at[j], gc_r.at[j], mate
        )

    def plane_start(j):
        landed(crecv.at[j], gc_s.at[j], gc_r.at[j])
        psend[j] = (
            gsend[j, rows(c * HR, HR), :].astype(F32) + crecv[j].astype(F32)
        ).astype(BF16)
        for i in range(1, NP):
            there, to = in_plane(i)
            push(psend.at[j, rows(there * HS, HS)], precv.at[j, i], gp_s.at[j, i], gp_r.at[j, i], to)

    def line_start(j):
        whole = psend[j, rows(spot * HS, HS), :].astype(F32)
        for i in range(1, NP):
            landed(precv.at[j, i], gp_s.at[j, i], gp_r.at[j, i])
            whole = whole + precv[j, i].astype(F32)
        zsend[j] = whole.astype(BF16)
        if j:
            _, to = in_line(-j)
            push(zsend.at[j], zrecv.at[j], gz_s.at[j], gz_r.at[j], to)

    for j in range(N):
        there, _ = in_line(-j)
        if j:
            for i in range(1, NP):
                near, _ = in_plane(-i)
                landed(ffw.at[there, rows((c * NP + near) * SR, SR)], fp_s.at[j, i], fp_r.at[j, i])
            at = ffw.at[there, rows(c * HR, HR)]
            push(at, at, fm_s.at[j], fm_r.at[j], mate)
            landed(ffw.at[there, rows((1 - c) * HR, HR)], fm_s.at[j], fm_r.at[j])
        up_b = bias[there, 0:1, :]

        def feed(i, carry):
            at = rows(i * TL, TL, 128)
            upper = dot(second[at, :], ffw[there, 0:D, :]) + up_b
            square = upper * upper
            t = jnp.tanh(upper * (GELU_A + (GELU_A * GELU_B) * square))
            one = 0.5 + 0.5 * t
            low = (upper * one).astype(BF16)
            active[at, :] = low
            slope_here = one + (0.5 * upper) * (1.0 - t * t) * (
                GELU_A + (3.0 * GELU_A * GELU_B) * square
            )
            acc[at, :] = acc[at, :] + dot(low, ffw[there, D : D + FL, :])
            back = (dot_nt(cot[at, :], ffw[there, D : D + FL, :]) * slope_here).astype(BF16)
            ugrad[at, :] = back
            sgrad[at, :] = sgrad[at, :] + dot_nt(back, ffw[there, 0:D, :])
            return carry

        lax.fori_loop(0, T // TL, feed, 0)
        sp[pl.ds(8 + there, 1), :] = jnp.sum(ugrad[...].astype(F32), axis=0, keepdims=True)
        gsend[j, 0:D, :] = dot_tn(second[...], ugrad[...]).astype(BF16)
        gsend[j, D : D + FL, :] = dot_tn(active[...], cot[...]).astype(BF16)
        core_start(j)
        if j:
            plane_start(j - 1)

    delta[...] = acc[...].astype(BF16)
    outd[n] = delta[:, rows(n * CW, CW, 128)]
    for j in range(1, N):
        there, to = in_line(j)
        push(delta.at[:, rows(there * CW, CW, 128)], outd.at[n], od_s.at[j], od_r.at[j], to)

    zero_row = jnp.zeros((1, D), F32)

    def norm_two_back(i, carry):
        at = rows(i * 128, 128, 128)
        unit, inverse = norm_stats(hid[at, :])
        grad = sgrad[at, :]
        scaled = grad * gain_two
        back = inverse * (
            scaled
            - jnp.mean(scaled, axis=1, keepdims=True)
            - unit * jnp.mean(scaled * unit, axis=1, keepdims=True)
        )
        top_grad = cot[at, :].astype(F32)
        whole = top_grad + back
        hgrad[at, :] = whole
        hgb[at, :] = whole.astype(BF16)
        parts = (grad * unit, grad, whole, top_grad)
        return tuple(a + jnp.sum(b, axis=0, keepdims=True) for a, b in zip(carry, parts))

    sums = lax.fori_loop(0, T // 128, norm_two_back, (zero_row,) * 4)
    sp[3:4, :] = sums[0]
    sp[4:5, :] = sums[1]
    sp[2:3, :] = sums[2]
    sp[5:6, :] = sums[3]

    plane_start(N - 1)

    gqo[1] = dot(mixg[...], hgb[...]).astype(BF16)
    qt[...] = dot_nt(wo[...], hgb[...])
    gate_grad = [jnp.zeros((1, T), F32), jnp.zeros((1, T), F32)]
    for part in range(N):
        picked_rows = [jnp.zeros((HP, T), F32), jnp.zeros((HP, T), F32)]
        for at in range(NE):
            for i in range(LE):
                lo = expert_rows(at, i, part)
                one = qt[lo : lo + HP, :]
                x = at * LE + i
                for k in range(2):
                    picked_rows[k] = picked_rows[k] + one * hot[k][x : x + 1, :]
        for k in range(2):
            span = slice(part * HP, (part + 1) * HP)
            rounded_mix = mix[k, span, :].astype(BF16).astype(F32)
            gate_grad[k] = gate_grad[k] + jnp.sum(picked_rows[k] * rounded_mix, axis=0, keepdims=True)
            mgk[k, span, :] = (picked_rows[k] * gate[k]).astype(BF16)
    middle = gate[0] * gate_grad[0] + gate[1] * gate_grad[1]
    logit_grad = sum(hot[k] * (gate[k] * (gate_grad[k] - middle)) for k in range(2))
    logit_low = logit_grad.astype(BF16)

    def attend_back(k):
        for i in range(tiles):
            at = pl.ds(i * TL, TL)
            low = prob[k, :, at]
            p = low.astype(F32)
            prob_grad = dot(vn[...], mgk[k, :, at])
            inner = jnp.sum(p * prob_grad, axis=0, keepdims=True)
            score = (p * (prob_grad - inner)).astype(BF16)
            dq[k, :, at] = (dot(kt[...], score) * scale).astype(BF16)
            key_part = dot_nt(score, qk[k, :, at])
            value_part = dot_nt(low, mgk[k, :, at])
            if k == 0 and i == 0:
                dk[...] = key_part
                dv[...] = value_part
            else:
                dk[...] = dk[...] + key_part
                dv[...] = dv[...] + value_part

    attend_back(0)
    for j in range(N):
        line_start(j)
    attend_back(1)

    H, PC = z.reach, z.piece
    offsets = [o for o in range(-H, H + 1) if o]
    inside = T >= LONGEST

    def halo_source(o):
        if inside:
            return (spot_in_row + 1) * T - ws if o > 0 else spot_in_row * T - LONGEST - ws
        return (spot_in_row + o) * T - ws

    def halo_copy(s, o):
        to = rem(here + o + G, G)
        return pltpu.make_async_remote_copy(
            src_ref=halo_out.at[s],
            dst_ref=halo_in.at[s],
            send_sem=hl_s.at[s],
            recv_sem=hl_r.at[s],
            device_id=(d, lax.div(to, N), rem(to, N)),
            device_id_type=MESH,
        )

    for s, o in enumerate(offsets):
        valid = jnp.logical_and(spot_in_row + o >= 0, spot_in_row + o < z.per_row)

        @pl.when(valid)
        def _(s=s, o=o):
            at = rows(halo_source(o), PC, 128)
            halo_out[s, 0] = (dk[at, :] * scale).astype(BF16)
            halo_out[s, 1] = dv[at, :].astype(BF16)
            halo_copy(s, o).start()

    for part in range(N):
        for at in range(NE):
            for i in range(LE):
                lo = expert_rows(at, i, part)
                x = at * LE + i
                span = slice(part * HP, (part + 1) * HP)
                one = dq[0, span, :].astype(F32) * hot[0][x : x + 1, :]
                one = one + dq[1, span, :].astype(F32) * hot[1][x : x + 1, :]
                dqt[lo : lo + HP, :] = one.astype(BF16)
    gqo[0] = dot(dqt[...], rw[own, :]).astype(BF16)
    push(gqo.at[1 - c], cqo, qc_s.at[0], qc_r.at[0], mate)
    ones = jnp.ones((8, T), BF16)
    sp[6:7, :] = dot_nt(ones, dqt[...])[0:1, :]
    sp[7:8, :] = jnp.zeros((1, D), F32)
    sp[7:8, 0 : z.experts] = jnp.transpose(
        jnp.broadcast_to(jnp.sum(logit_grad, axis=1, keepdims=True), (z.experts, 128))
    )[0:1, :]
    acc[...] = dot_tn(dqt[...], wq[...]) + dot_tn(logit_low, r_ref[...])
    sp[16:24, :] = dot(logit_low, rw[own, :])

    whole = zsend[0].astype(F32)
    for j in range(1, N):
        landed(zrecv.at[j], gz_s.at[j], gz_r.at[j])
        whole = whole + zrecv[j].astype(F32)
    fin_at = rows(c * HR + spot * HS, HS)
    fin[fin_at, :] = whole.astype(BF16)
    for i in range(1, NP):
        _, to = in_plane(i)
        push(fin.at[fin_at], fin.at[fin_at], ga_s.at[i], ga_r.at[i], to)

    dk[...] = dk[...] * scale
    for s, o in enumerate(offsets):
        back_valid = jnp.logical_and(spot_in_row - o >= 0, spot_in_row - o < z.per_row)

        @pl.when(back_valid)
        def _(s=s, o=o):
            halo_copy(s, o).wait_recv()
            at = off if (not inside or o > 0) else off + T - LONGEST
            at = rows(at, PC, 128)
            dk[at, :] = dk[at, :] + halo_in[s, 0].astype(F32)
            dv[at, :] = dv[at, :] + halo_in[s, 1].astype(F32)

    key_grad = dk[own, :]
    value_grad = dv[own, :]
    key_low, value_low = key_grad.astype(BF16), value_grad.astype(BF16)
    gkv[0] = dot_tn(key_low, rw[own, :]).astype(BF16)
    gkv[1] = dot_tn(value_low, rw[own, :]).astype(BF16)
    push(gkv.at[1 - c], ckv, qc_s.at[1], qc_r.at[1], mate)
    sp[15:16, :] = jnp.zeros((1, D), F32)
    sp[15:16, 0:HEAD] = jnp.sum(value_grad, axis=0, keepdims=True)
    acc[...] = acc[...] + dot(key_low, wk[...]) + dot(value_low, wv[...])

    def norm_one_back(i, carry):
        at = rows(i * 128, 128, 128)
        unit, inverse = norm_stats(xw[rows(off + i * 128, 128, 128), :])
        grad = acc[at, :]
        scaled = grad * gain_one
        back = inverse * (
            scaled
            - jnp.mean(scaled, axis=1, keepdims=True)
            - unit * jnp.mean(scaled * unit, axis=1, keepdims=True)
        )
        ig_ref[at, :] = hgrad[at, :] + back
        parts = (grad * unit, grad)
        return tuple(a + jnp.sum(b, axis=0, keepdims=True) for a, b in zip(carry, parts))

    sums = lax.fori_loop(0, T // 128, norm_one_back, (zero_row,) * 2)
    sp[0:1, :] = sums[0]
    sp[1:2, :] = sums[1]
    for j in range(8 + N, 15):
        sp[j : j + 1, :] = zero_row
    push(sp, csp, qc_s.at[2], qc_r.at[2], mate)

    YW = D // NY
    ER = N * R
    landed(cqo, qc_s.at[0], qc_r.at[0])
    pqo[...] = (gqo[c].astype(F32) + cqo[...].astype(F32)).astype(BF16)
    for i in range(1, NP):
        there, to = in_plane(i)
        src = pqo.at[rows(rem(there, NE) * ER, ER), rows(lax.div(there, NE) * YW, YW, 128)]
        push(src, rqo.at[i], qp_s.at[0, i], qp_r.at[0, i], to)
    landed(ckv, qc_s.at[1], qc_r.at[1])
    pkv[...] = (gkv[c].astype(F32) + ckv[...].astype(F32)).astype(BF16)
    for i in range(1, NP):
        _, to = in_plane(i)
        push(pkv, rkv.at[i], qp_s.at[1, i], qp_r.at[1, i], to)
    landed(csp, qc_s.at[2], qc_r.at[2])
    psp[...] = sp[...] + csp[...]
    for i in range(1, NP):
        _, to = in_plane(i)
        push(psp, rsp.at[i], qp_s.at[2, i], qp_r.at[2, i], to)

    for i in range(1, NP):
        near, _ = in_plane(-i)
        landed(fin.at[rows(c * HR + near * HS, HS)], ga_s.at[i], ga_r.at[i])
    at = fin.at[rows(c * HR, HR)]
    push(at, at, ga_s.at[0], ga_r.at[0], mate)

    whole = pqo[rows(e * ER, ER), rows(y * YW, YW, 128)].astype(F32)
    for i in range(1, NP):
        landed(rqo.at[i], qp_s.at[0, i], qp_r.at[0, i])
        whole = whole + rqo[i].astype(F32)
    zqo[...] = whole.astype(BF16)
    for j in range(1, N):
        there, to = in_line(j)
        push(zqo.at[rows(there * R, R)], yqo.at[j], qz_s.at[0, j], qz_r.at[0, j], to)
    whole = pkv[...].astype(F32)
    for i in range(1, NP):
        landed(rkv.at[i], qp_s.at[1, i], qp_r.at[1, i])
        whole = whole + rkv[i].astype(F32)
    zkv[...] = whole.astype(BF16)
    for j in range(1, N):
        there, to = in_line(j)
        push(zkv.at[rows(there * HP, HP)], ykv.at[j], qz_s.at[1, j], qz_r.at[1, j], to)
    whole = psp[...]
    for i in range(1, NP):
        landed(rsp.at[i], qp_s.at[2, i], qp_r.at[2, i])
        whole = whole + rsp[i]
    zsp[...] = whole
    for j in range(1, N):
        _, to = in_line(j)
        push(zsp, ysp.at[j], qz_s.at[2, j], qz_r.at[2, j], to)

    for j in range(1, N):
        there, _ = in_line(-j)
        landed(outd.at[there], od_s.at[j], od_r.at[j])
    cols_copy.wait()
    for j in range(N):
        out_ref[j * T : (j + 1) * T, :] = xcols[j * T : (j + 1) * T, :] + outd[j].astype(F32)

    landed(fin.at[rows((1 - c) * HR, HR)], ga_s.at[0], ga_r.at[0])
    gup_ref[...] = fin[0:D, :].astype(F32)
    gdown_ref[...] = fin[D : D + FL, :].astype(F32)

    whole = zqo[rows(n * R, R), :].astype(F32)
    for j in range(1, N):
        landed(yqo.at[j], qz_s.at[0, j], qz_r.at[0, j])
        whole = whole + yqo[j].astype(F32)
    my_cols = rows(y * YW, YW, 128)
    fqo[c, :, my_cols] = whole.astype(BF16)
    for i in range(1, NY):
        _, to = in_rows(i)
        at = fqo.at[c, :, my_cols]
        push(at, at, qa_s.at[0, i], qa_r.at[0, i], to)
    whole = zkv[rows(n * HP, HP), :].astype(F32)
    for j in range(1, N):
        landed(ykv.at[j], qz_s.at[1, j], qz_r.at[1, j])
        whole = whole + ykv[j].astype(F32)
    fkv[c] = whole.astype(BF16)
    push(fkv.at[c], fkv.at[c], qa_s.at[1, 0], qa_r.at[1, 0], mate)
    whole = zsp[...]
    for j in range(1, N):
        landed(ysp.at[j], qz_s.at[2, j], qz_r.at[2, j])
        whole = whole + ysp[j]
    small_ref[...] = whole
    for i in range(1, NY):
        near, _ = in_rows(-i)
        landed(fqo.at[c, :, rows(near * YW, YW, 128)], qa_s.at[0, i], qa_r.at[0, i])
    push(fqo.at[c], fqo.at[c], qa_s.at[0, 0], qa_r.at[0, 0], mate)
    landed(fkv.at[1 - c], qa_s.at[1, 0], qa_r.at[1, 0])
    gk_ref[...] = fkv[0].astype(F32)
    gv_ref[...] = fkv[1].astype(F32)
    landed(fqo.at[1 - c], qa_s.at[0, 0], qa_r.at[0, 0])
    gq_ref[...] = fqo[0].astype(F32)
    go_ref[...] = fqo[1].astype(F32)

    for copy in started:
        copy.wait_send()
    for s, o in enumerate(offsets):
        valid = jnp.logical_and(spot_in_row + o >= 0, spot_in_row + o < z.per_row)

        @pl.when(valid)
        def _(s=s, o=o):
            halo_copy(s, o).wait_send()


def run(z, x, seg, chosen, vec, q, k, v, o, r, up, down, cot):
    N, G, NP, NY = z.narrow, z.group, z.plane, z.rows_y
    T, W, D, R, HP = z.block, z.window, z.width, z.shard, z.head_part
    FL = z.ff_local
    FR = D + FL
    HR = FR // 2
    HS = HR // NP
    YW = D // NY
    ER = N * R
    QR = G * R
    S = 2 * z.reach
    SMALL = z.small_rows
    vmem = pl.BlockSpec(memory_space=pltpu.VMEM)
    anywhere = pl.BlockSpec(memory_space=pl.ANY)
    scratch = [
        ((W, D), F32),
        ((N * T, D // N), F32),
        ((W, D), BF16),
        ((QR, D), BF16),
        ((QR, D), BF16),
        ((HEAD, D), BF16),
        ((HEAD, D), BF16),
        ((G, 8, D), F32),
        ((N, FR, D), BF16),
        ((T, D), BF16),
        ((8, z.row_len), F32),
        ((W, 8), F32),
        ((W, HEAD), BF16),
        ((W, HEAD), BF16),
        ((HEAD, W), BF16),
        ((HEAD, W), BF16),
        ((QR, T), F32),
        ((2, HEAD, T), BF16),
        ((2, W, T), BF16),
        ((2, HEAD, T), F32),
        ((QR, T), BF16),
        ((T, D), F32),
        ((T, D), F32),
        ((T, D), BF16),
        ((T, FL), BF16),
        ((T, FL), BF16),
        ((T, D), F32),
        ((T, D), F32),
        ((T, D), BF16),
        ((2, HEAD, T), BF16),
        ((W, HEAD), F32),
        ((W, HEAD), F32),
        ((2, HEAD, T), BF16),
        ((QR, T), BF16),
        ((max(S, 1), 2, z.piece, HEAD), BF16),
        ((max(S, 1), 2, z.piece, HEAD), BF16),
        ((T, D), BF16),
        ((N, T, D // N), BF16),
        ((N, FR, D), BF16),
        ((N, HR, D), BF16),
        ((N, HR, D), BF16),
        ((N, NP, HS, D), BF16),
        ((N, HS, D), BF16),
        ((N, HS, D), BF16),
        ((FR, D), BF16),
        ((2, QR, D), BF16),
        ((QR, D), BF16),
        ((QR, D), BF16),
        ((NP, ER, YW), BF16),
        ((ER, YW), BF16),
        ((N, R, YW), BF16),
        ((2, R, D), BF16),
        ((2, HEAD, D), BF16),
        ((HEAD, D), BF16),
        ((HEAD, D), BF16),
        ((NP, HEAD, D), BF16),
        ((HEAD, D), BF16),
        ((N, HP, D), BF16),
        ((2, HP, D), BF16),
        ((SMALL, D), F32),
        ((SMALL, D), F32),
        ((SMALL, D), F32),
        ((NP, SMALL, D), F32),
        ((SMALL, D), F32),
        ((N, SMALL, D), F32),
    ]
    pairs = [
        (G,),
        (G,),
        (2, N),
        (G,),
        (2, G),
        (N,),
        (N, NP),
        (N,),
        (N,),
        (N,),
        (max(S, 1),),
        (N,),
        (N, NP),
        (N,),
        (NP,),
        (3,),
        (3, NP),
        (3, N),
        (2, NY),
    ]
    sems = [pltpu.SemaphoreType.DMA((4,))]
    for shape in pairs:
        sems += [pltpu.SemaphoreType.DMA(shape)] * 2
    outs = [
        ((N * T, D // N), F32),
        ((T, D), F32),
        ((R, D), F32),
        ((R, D), F32),
        ((HP, D), F32),
        ((HP, D), F32),
        ((D, FL), F32),
        ((FL, D), F32),
        ((SMALL, D), F32),
    ]
    return pl.pallas_call(
        functools.partial(kernel, z),
        out_shape=[jax.ShapeDtypeStruct(s, t) for s, t in outs],
        in_specs=[anywhere] + [vmem] * 8 + [anywhere] * 2 + [vmem],
        out_specs=[vmem] * len(outs),
        scratch_shapes=[pltpu.VMEM(s, t) for s, t in scratch] + sems,
        compiler_params=pltpu.CompilerParams(
            collective_id=0, has_side_effects=True, vmem_limit_bytes=60 * 2**20
        ),
        name="layer",
    )(x, seg, chosen, vec, q, k, v, o, r, up, down, cot)


def per_device(
    inputs,
    seg_ids,
    chosen,
    gain_one,
    shift_one,
    query_w,
    query_b,
    key_w,
    value_w,
    value_b,
    out_w,
    out_b,
    router_w,
    router_b,
    gain_two,
    shift_two,
    up_w,
    up_b,
    down_w,
    down_b,
    cotangent,
):
    narrow = lax.axis_size("narrow")
    e, n = lax.axis_index("expert"), lax.axis_index("narrow")
    z = Sizes(
        lax.axis_size("dp"),
        lax.axis_size("expert"),
        narrow,
        inputs.shape[0],
        inputs.shape[1],
        seg_ids.shape[1],
        query_w.shape[0],
        up_w.shape[1],
    )
    D, R, HP = z.width, z.shard, z.head_part
    zero = jnp.zeros((D,), F32)
    spread = jnp.where(
        jnp.arange(HEAD) // HP == n, jnp.tile(value_b, narrow), 0.0
    )
    vec = jnp.stack(
        [
            gain_one,
            shift_one,
            out_b,
            gain_two,
            shift_two,
            down_b,
            zero,
            zero,
            up_b,
            jnp.pad(query_b.reshape(-1), (0, D - R)),
            jnp.pad(spread, (0, D - HEAD)),
            zero,
            zero,
            zero,
            zero,
            zero,
        ]
    )
    vec = jnp.concatenate([vec, jnp.broadcast_to(router_b[:, None], (z.experts, D))])
    out, ig, gq, go, gk, gv, gup, gdown, small = run(
        z,
        inputs,
        seg_ids,
        jnp.transpose(chosen),
        vec,
        jnp.transpose(query_w, (0, 2, 1)).reshape(R, D),
        jnp.transpose(key_w),
        jnp.transpose(value_w),
        out_w.reshape(R, D),
        jnp.transpose(router_w),
        up_w,
        down_w,
        cotangent,
    )
    up_b_grad = lax.dynamic_index_in_dim(small[8 : 8 + narrow], n, 0, keepdims=False)
    query_b_grad = lax.dynamic_slice_in_dim(small[6], (e * narrow + n) * R, R).reshape(query_b.shape)
    value_b_grad = lax.dynamic_slice_in_dim(small[15], n * HP, HP)
    return (
        out,
        ig,
        small[0],
        small[1],
        jnp.transpose(gq.reshape(z.local_experts, HP, D), (0, 2, 1)),
        query_b_grad,
        jnp.transpose(gk),
        jnp.transpose(gv),
        value_b_grad,
        go.reshape(z.local_experts, HP, D),
        small[2],
        jnp.transpose(small[16 : 16 + z.experts]),
        small[7, : z.experts],
        small[3],
        small[4],
        gup,
        up_b_grad,
        gdown,
        small[5],
    )


def solution(mesh):
    return jax.shard_map(
        per_device,
        mesh=mesh,
        in_specs=(
            P("dp", None),
            P("dp", None),
            P("dp", None),
            P(),
            P(),
            P("expert", None, "narrow"),
            P("expert", "narrow"),
            P(None, "narrow"),
            P(None, "narrow"),
            P("narrow"),
            P("expert", "narrow", None),
            P(),
            P(),
            P(),
            P(),
            P(),
            P(None, "narrow"),
            P("narrow"),
            P("narrow", None),
            P(),
            P(("dp", "expert"), "narrow"),
        ),
        out_specs=(
            P(("dp", "expert"), "narrow"),
            P(("dp", "expert", "narrow"), None),
            P(),
            P(),
            P("expert", None, "narrow"),
            P("expert", "narrow"),
            P(None, "narrow"),
            P(None, "narrow"),
            P("narrow"),
            P("expert", "narrow", None),
            P(),
            P(),
            P(),
            P(),
            P(),
            P(None, "narrow"),
            P("narrow"),
            P("narrow", None),
            P(),
        ),
        check_vma=False,
    )
```

```python
import functools
import math

import jax
import jax.numpy as jnp
from jax import lax
from jax.experimental import pallas as pl
from jax.experimental.pallas import tpu as pltpu
from jax.sharding import PartitionSpec as P

HEAD = 64
LONGEST = 256
EPSILON = 1e-05
MASKED = -1000000000.0
GELU_A = math.sqrt(2.0 / math.pi)
GELU_B = 0.044715
F32 = jnp.float32
BF16 = jnp.bfloat16
MESH = pl.DeviceIdType.MESH


def dot(a, b):
    return lax.dot_general(a, b, (((1,), (0,)), ((), ())), preferred_element_type=F32)


def dot_nt(a, b):
    return lax.dot_general(a, b, (((1,), (1,)), ((), ())), preferred_element_type=F32)


def dot_tn(a, b):
    return lax.dot_general(a, b, (((0,), (0,)), ((), ())), preferred_element_type=F32)


def norm_stats(x):
    centred = x - jnp.mean(x, axis=1, keepdims=True)
    inverse = lax.rsqrt(jnp.mean(centred * centred, axis=1, keepdims=True) + EPSILON)
    return centred * inverse, inverse


def rem(a, b):
    return lax.rem(a, b)


class Sizes:
    def __init__(self, dp, expert, narrow, tokens, width, row_len, local_experts, ff_local):
        self.dp, self.expert, self.narrow = dp, expert, narrow
        self.tokens, self.width, self.row_len = tokens, width, row_len
        self.local_experts = local_experts
        self.experts = local_experts * expert
        self.group = expert * narrow
        self.block = tokens // self.group
        self.rows_y = dp // 2
        self.plane = self.rows_y * expert
        self.ff_local = ff_local
        self.head_part = HEAD // narrow
        self.shard = local_experts * self.head_part
        self.per_row = row_len // self.block
        spans = [
            min(row_len, (j + 1) * self.block + LONGEST) - max(0, j * self.block - LONGEST)
            for j in range(self.per_row)
        ]
        self.window = max(spans)
        self.reach = max(1, LONGEST // self.block) if self.per_row > 1 else 0
        self.piece = min(self.block, LONGEST)
        self.tile = min(256, self.block)
        self.up_rows = narrow * ff_local // width
        self.small_rows = 24


def kernel(
    z,
    x_any,
    seg_ref,
    chosen_ref,
    g1_ref,
    s1_ref,
    ob_ref,
    g2_ref,
    s2_ref,
    db_ref,
    ub_ref,
    qb_ref,
    vb_ref,
    rb_ref,
    q_ref,
    k_ref,
    v_ref,
    o_ref,
    r_ref,
    up_any,
    down_any,
    cot_ref,
    out_ref,
    ig_ref,
    fin_ref,
    fqo_ref,
    small_ref,
    xw,
    rw,
    wq,
    wo,
    wkv,
    bias,
    corner,
    vcol,
    ffw,
    cot,
    segs,
    segc,
    kn,
    vn,
    kt,
    vt,
    qt,
    qk,
    prob,
    mix,
    mixg,
    hid,
    acc,
    second,
    active,
    slope,
    ugrad,
    sgrad,
    hgrad,
    hgb,
    mgk,
    dk,
    dv,
    dq,
    dqt,
    halo_out,
    halo_in,
    delta,
    outd,
    gsend,
    crecv,
    psend,
    pea,
    pya,
    mea,
    mya,
    pyb,
    peb,
    zsend,
    zrecv,
    fin,
    gqo,
    cqo,
    pqo,
    rqo,
    zqo,
    yqo,
    fqo,
    sp,
    csp,
    psp,
    rsp,
    zsp,
    ysp,
    fsp,
    loc_sem,
    w_s,
    w_r,
    wm_s,
    wm_r,
    b_s,
    b_r,
    q_s,
    q_r,
    qm_s,
    qm_r,
    o_s,
    o_r,
    om_s,
    om_r,
    fz_s,
    fz_r,
    fp_s,
    fp_r,
    fm_s,
    fm_r,
    ct_s,
    ct_r,
    od_s,
    od_r,
    hl_s,
    hl_r,
    gc_s,
    gc_r,
    gp_s,
    gp_r,
    gz_s,
    gz_r,
    ga_s,
    ga_r,
    qc_s,
    qc_r,
    qp_s,
    qp_r,
    qz_s,
    qz_r,
    qa_s,
    qa_r,
):
    d, e, n = lax.axis_index("dp"), lax.axis_index("expert"), lax.axis_index("narrow")
    c, y = rem(d, 2), lax.div(d, 2)
    N, G, NP, NE, NY = z.narrow, z.group, z.plane, z.expert, z.rows_y
    T, W, D, R, HP, LE = z.block, z.window, z.width, z.shard, z.head_part, z.local_experts
    FL = z.ff_local
    half = D // 2
    here = e * N + n
    spot = y * NE + e
    mate = (d + 1 - 2 * c, e, n)

    def in_group(j):
        at = rem(here + j + G, G)
        return at, (d, lax.div(at, N), rem(at, N))

    def in_plane(j):
        at = rem(spot + j + NP, NP)
        return at, (2 * lax.div(at, NE) + c, rem(at, NE), n)

    def in_line(j):
        at = rem(n + j + N, N)
        return at, (d, e, at)

    def in_rows(j):
        at = rem(y + j + NY, NY)
        return at, (2 * at + c, e, n)

    started = []

    def push(src, dst, send, recv, device):
        copy = pltpu.make_async_remote_copy(
            src_ref=src,
            dst_ref=dst,
            send_sem=send,
            recv_sem=recv,
            device_id=device,
            device_id_type=MESH,
        )
        copy.start()
        started.append(copy)

    def landed(dst, send, recv):
        pltpu.make_async_remote_copy(
            src_ref=dst,
            dst_ref=dst,
            send_sem=send,
            recv_sem=recv,
            device_id=mate,
            device_id_type=MESH,
        ).wait_recv()

    def rows(start, size, step=16):
        return pl.ds(pl.multiple_of(start, step), size)

    start = here * T
    row = lax.div(start, z.row_len)
    spot_in_row = rem(here, z.per_row)
    base = row * z.row_len
    ws = jnp.minimum(jnp.maximum(spot_in_row * T - LONGEST, 0), z.row_len - W)
    off = spot_in_row * T - ws
    own = rows(off, T, 128)

    x_copy = pltpu.make_async_copy(x_any.at[rows(base + ws, W, 128)], xw, loc_sem.at[0])
    x_copy.start()
    up_copy = pltpu.make_async_copy(up_any, ffw.at[n, pl.ds(0, D)], loc_sem.at[1])
    up_copy.start()
    down_copy = pltpu.make_async_copy(down_any, ffw.at[n, pl.ds(D, FL)], loc_sem.at[2])
    down_copy.start()
    cols_copy = pltpu.make_async_copy(
        x_any.at[rows(e * N * T, N * T, 128), rows(n * (D // N), D // N, 128)], out_ref, loc_sem.at[3]
    )
    cols_copy.start()
    wq[rows(here * R, R)] = q_ref[...]
    wo[rows(here * R, R)] = o_ref[...]
    wkv[0, rows(n * HP, HP)] = k_ref[...]
    wkv[1, rows(n * HP, HP)] = v_ref[...]
    bias[here] = jnp.zeros((16, 128), F32)
    for i in range(FL // 128):
        bias[here, i : i + 1, :] = ub_ref[0:1, i * 128 : (i + 1) * 128]
    bias[here, 8 : 8 + LE, 0:HP] = qb_ref[...]
    bias[here, 7:8, 0:HP] = vb_ref[...]

    barrier = pltpu.get_barrier_semaphore()
    pl.semaphore_signal(barrier, inc=1, device_id=mate, device_id_type=MESH)
    for j in range(1, NP):
        pl.semaphore_signal(barrier, inc=1, device_id=in_plane(j)[1], device_id_type=MESH)
    for j in range(1, G):
        pl.semaphore_signal(barrier, inc=1, device_id=in_group(j)[1], device_id_type=MESH)
    pl.semaphore_wait(barrier, NP + G - 1)

    mine_cols = rows(c * half, half, 128)
    other_cols = rows((1 - c) * half, half, 128)

    def in_expert(i):
        at = rem(e + i + NE, NE)
        return at, (d, at, n)

    def shard_at(i, j):
        return rem(e - i + NE, NE) * N + rem(n - j + N, N)

    def spread_start(part, send, recv):
        for j in range(1, N):
            at = part(here)
            push(at, at, send.at[0, j], recv.at[0, j], in_line(j)[1])
        for i in range(1, NE):
            at = part(here)
            push(at, at, send.at[i, 0], recv.at[i, 0], in_expert(i)[1])

    def spread_on(part, send, recv, to_mate):
        for j in range(1, N):
            at = part(shard_at(0, j))
            landed(at, send.at[0, j], recv.at[0, j])
            for i in range(1, NE):
                push(at, at, send.at[i, j], recv.at[i, j], in_expert(i)[1])
            if to_mate is not None:
                push(at, at, to_mate[0].at[0, j], to_mate[1].at[0, j], mate)

    def spread_end(part, send, recv, to_mate):
        for i in range(1, NE):
            for j in range(N):
                at = part(shard_at(i, j))
                landed(at, send.at[i, j], recv.at[i, j])
                if to_mate is not None:
                    push(at, at, to_mate[0].at[i, j], to_mate[1].at[i, j], mate)

    def spread_wait(part, to_mate):
        for i in range(NE):
            for j in range(N):
                if i or j:
                    landed(part(shard_at(i, j)), to_mate[0].at[i, j], to_mate[1].at[i, j])

    def bias_part(g):
        return bias.at[g]

    def q_part(g):
        return wq.at[rows(g * R, R), mine_cols]

    def q_other(g):
        return wq.at[rows(g * R, R), other_cols]

    def o_part(g):
        return wo.at[rows(g * R, R), mine_cols]

    def o_other(g):
        return wo.at[rows(g * R, R), other_cols]

    for j in range(1, N):
        at = wkv.at[c, rows(n * HP, HP)]
        push(at, at, w_s.at[j], w_r.at[j], in_line(j)[1])
    spread_start(q_part, q_s, q_r)
    spread_start(bias_part, b_s, b_r)
    up_copy.wait()
    down_copy.wait()
    FR = D + FL

    left, right = pl.ds(0, half), pl.ds(half, half)
    HR = FR // 2
    HS = HR // NP
    HA, HB = HR // NE, HR // NY
    near_first = sorted(range(1, N), key=lambda j: (min(j, N - j), j))
    first, last = near_first[: N // 2], near_first[N // 2 :]

    def left_slice(of, ys, es):
        return ffw.at[of, rows(c * HR + (es * NY + ys) * HS, HS), left]

    def right_slice(of, ys, es):
        return ffw.at[of, rows(c * HR + (ys * NE + es) * HS, HS), right]

    def left_half(of, es):
        return ffw.at[of, rows(c * HR + es * HA, HA), left]

    def right_half(of, ys):
        return ffw.at[of, rows(c * HR + ys * HB, HB), right]

    def shard_start(j):
        to = in_line(j)[1]
        at = left_slice(n, y, e)
        push(at, at, fz_s.at[0, j], fz_r.at[0, j], to)
        at = right_slice(n, y, e)
        push(at, at, fz_s.at[1, j], fz_r.at[1, j], to)

    def plane_on(j):
        there, _ = in_line(-j)
        at = left_slice(there, y, e)
        landed(at, fz_s.at[0, j], fz_r.at[0, j])
        for i in range(1, NY):
            push(at, at, fp_s.at[0, j, i], fp_r.at[0, j, i], in_rows(i)[1])
        at = right_slice(there, y, e)
        landed(at, fz_s.at[1, j], fz_r.at[1, j])
        for i in range(1, NE):
            push(at, at, fp_s.at[1, j, i], fp_r.at[1, j, i], in_expert(i)[1])

    def plane_turn(j):
        there, _ = in_line(-j)
        for i in range(1, NY):
            near, _ = in_rows(-i)
            landed(left_slice(there, near, e), fp_s.at[0, j, i], fp_r.at[0, j, i])
        at = left_half(there, e)
        for i in range(1, NE):
            push(at, at, fp_s.at[2, j, i], fp_r.at[2, j, i], in_expert(i)[1])
        for i in range(1, NE):
            near, _ = in_expert(-i)
            landed(right_slice(there, y, near), fp_s.at[1, j, i], fp_r.at[1, j, i])
        at = right_half(there, y)
        for i in range(1, NY):
            push(at, at, fp_s.at[3, j, i], fp_r.at[3, j, i], in_rows(i)[1])

    def mate_on(j):
        there, _ = in_line(-j)
        for i in range(1, NE):
            near, _ = in_expert(-i)
            landed(left_half(there, near), fp_s.at[2, j, i], fp_r.at[2, j, i])
        for i in range(1, NY):
            near, _ = in_rows(-i)
            landed(right_half(there, near), fp_s.at[3, j, i], fp_r.at[3, j, i])
        at = ffw.at[there, rows(c * HR, HR)]
        push(at, at, fm_s.at[j], fm_r.at[j], mate)

    x_copy.wait()
    gain_one, shift_one = g1_ref[...], s1_ref[...]

    def norm_one(i, carry):
        at = rows(i * 128, 128, 128)
        unit, _ = norm_stats(xw[at, :])
        rw[at, :] = (unit * gain_one + shift_one).astype(BF16)
        return carry

    lax.fori_loop(0, W // 128, norm_one, 0)

    seg_all = seg_ref[...].astype(F32)
    row_id = lax.broadcasted_iota(jnp.int32, seg_all.shape, 0)
    seg_here = jnp.sum(jnp.where(row_id == row, seg_all, 0.0), axis=0, keepdims=True)
    segs[...] = jnp.broadcast_to(seg_here, segs.shape)
    segc[...] = jnp.transpose(segs[:, rows(ws, W, 128)])
    seg_own = segs[0:1, rows(spot_in_row * T, T, 128)]
    corner[...] = jnp.zeros_like(corner)
    corner[:, 0 : z.experts] = jnp.broadcast_to(rb_ref[...], (8, z.experts))
    router_col = jnp.transpose(corner[...])[0 : z.experts, 0:1]
    logits = dot_nt(r_ref[...], rw[own, :]) + router_col
    expert_id = lax.broadcasted_iota(jnp.int32, (z.experts, T), 0)
    hot, picked = [], []
    for k in range(2):
        chosen = chosen_ref[k : k + 1, rows(start, T, 128)]
        hot.append((expert_id == chosen).astype(F32))
        picked.append(jnp.sum(logits * hot[k], axis=0, keepdims=True))
    top = jnp.maximum(picked[0], picked[1])
    raised = [jnp.exp(p - top) for p in picked]
    total = raised[0] + raised[1]
    gate = [r / total for r in raised]

    for j in range(1, N):
        there, _ = in_line(-j)
        at = wkv.at[c, rows(there * HP, HP)]
        landed(at, w_s.at[j], w_r.at[j])
        push(at, at, wm_s.at[j], wm_r.at[j], mate)
    spread_on(q_part, q_s, q_r, (qm_s, qm_r))
    spread_on(bias_part, b_s, b_r, None)
    for j in first:
        shard_start(j)
    spread_start(o_part, o_s, o_r)

    for j in range(1, N):
        there, _ = in_line(-j)
        landed(wkv.at[1 - c, rows(there * HP, HP)], wm_s.at[j], wm_r.at[j])
    kn[...] = dot_nt(rw[...], wkv[0]).astype(BF16)
    kt[...] = dot_nt(wkv[0], rw[...]).astype(BF16)
    spread_end(q_part, q_s, q_r, (qm_s, qm_r))
    spread_end(bias_part, b_s, b_r, None)
    columns = [jnp.transpose(bias[g, 0:16, :]) for g in range(G)]
    for part in range(N):
        vcol[part * HP : (part + 1) * HP, :] = jnp.broadcast_to(columns[part][0:HP, 7:8], (HP, 128))
    value_row = jnp.transpose(vcol[...])[0:1, :]
    vn[...] = (dot_nt(rw[...], wkv[1]) + value_row).astype(BF16)
    vt[...] = (dot_nt(wkv[1], rw[...]) + vcol[:, 0:1]).astype(BF16)

    spread_wait(q_other, (qm_s, qm_r))
    qt[...] = dot_nt(wq[...], rw[own, :])

    def expert_rows(at, i, part):
        return ((at * N + part) * LE + i) * HP

    for part in range(N):
        chosen_rows = [jnp.zeros((HP, T), F32), jnp.zeros((HP, T), F32)]
        for at in range(NE):
            g = at * N + part
            for i in range(LE):
                lo = expert_rows(at, i, part)
                one = qt[lo : lo + HP, :] + columns[g][0:HP, 8 + i : 9 + i]
                for k in range(2):
                    chosen_rows[k] = chosen_rows[k] + one * hot[k][at * LE + i : at * LE + i + 1, :]
        for k in range(2):
            qk[k, part * HP : (part + 1) * HP, :] = chosen_rows[k].astype(BF16)

    scale = 1.0 / math.sqrt(HEAD)
    TL = z.tile
    tiles = T // TL
    seg_tiles = [seg_own[:, i * TL : (i + 1) * TL] for i in range(tiles)]

    def attend(k):
        for i in range(tiles):
            at = pl.ds(i * TL, TL)
            scores = dot(kn[...], qk[k, :, at]) * scale
            scores = jnp.where(segc[:, 0:1] == seg_tiles[i], scores, MASKED)
            high = jnp.max(scores, axis=0, keepdims=True)
            raised_scores = jnp.exp(scores - high)
            low = (raised_scores * (1.0 / jnp.sum(raised_scores, axis=0, keepdims=True))).astype(BF16)
            prob[k, :, at] = low
            mix[k, :, at] = dot(vt[...], low)

    for j in last:
        shard_start(j)
    attend(0)
    attend(1)
    plane_on(first[0])
    for j in first[1:]:
        plane_on(j)
    spread_on(o_part, o_s, o_r, (om_s, om_r))
    for j in first:
        plane_turn(j)
    CW = D // N
    cot[:, rows(n * CW, CW, 128)] = cot_ref[rows(n * T, T, 128), :]
    for j in range(1, N):
        there, to = in_line(j)
        push(
            cot_ref.at[rows(there * T, T, 128)],
            cot.at[:, rows(n * CW, CW, 128)],
            ct_s.at[j],
            ct_r.at[j],
            to,
        )
    for j in last:
        plane_on(j)
    spread_end(o_part, o_s, o_r, (om_s, om_r))

    for part in range(N):
        for at in range(NE):
            for i in range(LE):
                lo = expert_rows(at, i, part)
                x = at * LE + i
                gated = jnp.zeros((HP, T), F32)
                for k in range(2):
                    rounded_mix = mix[k, part * HP : (part + 1) * HP, :].astype(BF16).astype(F32)
                    gated = gated + rounded_mix * (hot[k][x : x + 1, :] * gate[k])
                mixg[lo : lo + HP, :] = gated.astype(BF16)
    spread_wait(o_other, (om_s, om_r))
    out_b, down_b = ob_ref[...], db_ref[...]
    gain_two, shift_two = g2_ref[...], s2_ref[...]
    attention = dot_tn(mixg[...], wo[...]) + out_b
    acc[...] = attention + down_b
    hid[...] = xw[own, :] + attention

    def norm_two(i, carry):
        at = rows(i * 128, 128, 128)
        unit, _ = norm_stats(hid[at, :])
        second[at, :] = (unit * gain_two + shift_two).astype(BF16)
        return carry

    lax.fori_loop(0, T // 128, norm_two, 0)
    sgrad[...] = jnp.zeros_like(sgrad)

    def core_start(j):
        push(
            gsend.at[j, rows((1 - c) * HR, HR)], crecv.at[j], gc_s.at[j], gc_r.at[j], mate
        )

    def plane_start(j):
        landed(crecv.at[j], gc_s.at[j], gc_r.at[j])
        psend[j] = (
            gsend[j, rows(c * HR, HR), :].astype(F32) + crecv[j].astype(F32)
        ).astype(BF16)
        for i in range(1, NE):
            there, to = in_expert(i)
            src = psend.at[j, rows(there * HA, HA), left]
            push(src, pea.at[j, i], gp_s.at[0, j, i], gp_r.at[0, j, i], to)
        for i in range(1, NY):
            there, to = in_rows(i)
            src = psend.at[j, rows(there * HB, HB), right]
            push(src, pya.at[j, i], gp_s.at[1, j, i], gp_r.at[1, j, i], to)

    def plane_middle(j):
        whole = psend[j, rows(e * HA, HA), left].astype(F32)
        for i in range(1, NE):
            landed(pea.at[j, i], gp_s.at[0, j, i], gp_r.at[0, j, i])
            whole = whole + pea[j, i].astype(F32)
        mea[j] = whole.astype(BF16)
        for i in range(1, NY):
            there, to = in_rows(i)
            src = mea.at[j, rows(there * HS, HS)]
            push(src, pyb.at[j, i], gp_s.at[2, j, i], gp_r.at[2, j, i], to)
        whole = psend[j, rows(y * HB, HB), right].astype(F32)
        for i in range(1, NY):
            landed(pya.at[j, i], gp_s.at[1, j, i], gp_r.at[1, j, i])
            whole = whole + pya[j, i].astype(F32)
        mya[j] = whole.astype(BF16)
        for i in range(1, NE):
            there, to = in_expert(i)
            src = mya.at[j, rows(there * HS, HS)]
            push(src, peb.at[j, i], gp_s.at[3, j, i], gp_r.at[3, j, i], to)

    def line_start(j):
        whole = mea[j, rows(y * HS, HS), :].astype(F32)
        for i in range(1, NY):
            landed(pyb.at[j, i], gp_s.at[2, j, i], gp_r.at[2, j, i])
            whole = whole + pyb[j, i].astype(F32)
        zsend[j, :, left] = whole.astype(BF16)
        whole = mya[j, rows(e * HS, HS), :].astype(F32)
        for i in range(1, NE):
            landed(peb.at[j, i], gp_s.at[3, j, i], gp_r.at[3, j, i])
            whole = whole + peb[j, i].astype(F32)
        zsend[j, :, right] = whole.astype(BF16)
        if j:
            _, to = in_line(-j)
            push(zsend.at[j], zrecv.at[j], gz_s.at[j], gz_r.at[j], to)

    for step, j in enumerate([0] + near_first):
        there, _ = in_line(-j)
        if j:
            if step == 1:
                mate_on(j)
            if step + 1 < N:
                mate_on(near_first[step])
            landed(ffw.at[there, rows((1 - c) * HR, HR)], fm_s.at[j], fm_r.at[j])
        up_b = jnp.concatenate(
            [bias[e * N + there, i : i + 1, :] for i in range(FL // 128)], axis=1
        )

        def feed(i, carry):
            at = rows(i * TL, TL, 128)
            upper = dot(second[at, :], ffw[there, 0:D, :]) + up_b
            square = upper * upper
            t = jnp.tanh(upper * (GELU_A + (GELU_A * GELU_B) * square))
            one = 0.5 + 0.5 * t
            low = (upper * one).astype(BF16)
            active[j, at, :] = low
            slope[j, at, :] = (
                one + (0.5 * upper) * (1.0 - t * t) * (GELU_A + (3.0 * GELU_A * GELU_B) * square)
            ).astype(BF16)
            acc[at, :] = acc[at, :] + dot(low, ffw[there, D : D + FL, :])
            return carry

        lax.fori_loop(0, T // TL, feed, 0)
        if step == 0:
            for j in last:
                plane_turn(j)
    delta[...] = acc[...].astype(BF16)

    for j in range(1, N):
        there, _ = in_line(-j)
        landed(cot.at[:, rows(there * CW, CW, 128)], ct_s.at[j], ct_r.at[j])


    outd[n] = delta[:, rows(n * CW, CW, 128)]
    for j in range(1, N):
        there, to = in_line(j)
        push(delta.at[:, rows(there * CW, CW, 128)], outd.at[n], od_s.at[j], od_r.at[j], to)

    order = list(range(1, N)) + [0]
    for step, j in enumerate(order):
        there, _ = in_line(-j)

        def feed_back(i, carry):
            at = rows(i * TL, TL, 128)
            back = dot_nt(cot[at, :], ffw[there, D : D + FL, :]) * slope[j, at, :].astype(F32)
            back = back.astype(BF16)
            ugrad[at, :] = back
            sgrad[at, :] = sgrad[at, :] + dot_nt(back, ffw[there, 0:D, :])
            return carry

        lax.fori_loop(0, T // TL, feed_back, 0)
        sp[pl.ds(8 + there, 1), :] = jnp.sum(ugrad[...].astype(F32), axis=0, keepdims=True)
        gsend[j, 0:D, :] = dot_tn(second[...], ugrad[...]).astype(BF16)
        gsend[j, D : D + FL, :] = dot_tn(active[j], cot[...]).astype(BF16)
        core_start(j)
        if step:
            plane_start(order[step - 1])

    zero_row = jnp.zeros((1, D), F32)

    def norm_two_back(i, carry):
        at = rows(i * 128, 128, 128)
        unit, inverse = norm_stats(hid[at, :])
        grad = sgrad[at, :]
        scaled = grad * gain_two
        back = inverse * (
            scaled
            - jnp.mean(scaled, axis=1, keepdims=True)
            - unit * jnp.mean(scaled * unit, axis=1, keepdims=True)
        )
        top_grad = cot[at, :].astype(F32)
        whole = top_grad + back
        hgrad[at, :] = whole
        hgb[at, :] = whole.astype(BF16)
        parts = (grad * unit, grad, whole, top_grad)
        return tuple(a + jnp.sum(b, axis=0, keepdims=True) for a, b in zip(carry, parts))

    sums = lax.fori_loop(0, T // 128, norm_two_back, (zero_row,) * 4)
    sp[3:4, :] = sums[0]
    sp[4:5, :] = sums[1]
    sp[2:3, :] = sums[2]
    sp[5:6, :] = sums[3]

    plane_start(order[N - 1])
    plane_middle(order[0])

    SH = R + HP
    out_grad = dot(mixg[...], hgb[...]).astype(BF16)
    for g in range(G):
        gqo[1, g * SH : g * SH + R, :] = out_grad[g * R : (g + 1) * R, :]
    qt[...] = dot_nt(wo[...], hgb[...])
    gate_grad = [jnp.zeros((1, T), F32), jnp.zeros((1, T), F32)]
    for part in range(N):
        picked_rows = [jnp.zeros((HP, T), F32), jnp.zeros((HP, T), F32)]
        for at in range(NE):
            for i in range(LE):
                lo = expert_rows(at, i, part)
                one = qt[lo : lo + HP, :]
                x = at * LE + i
                for k in range(2):
                    picked_rows[k] = picked_rows[k] + one * hot[k][x : x + 1, :]
        for k in range(2):
            span = slice(part * HP, (part + 1) * HP)
            rounded_mix = mix[k, span, :].astype(BF16).astype(F32)
            gate_grad[k] = gate_grad[k] + jnp.sum(picked_rows[k] * rounded_mix, axis=0, keepdims=True)
            mgk[k, span, :] = (picked_rows[k] * gate[k]).astype(BF16)
    middle = gate[0] * gate_grad[0] + gate[1] * gate_grad[1]
    logit_grad = sum(hot[k] * (gate[k] * (gate_grad[k] - middle)) for k in range(2))
    logit_low = logit_grad.astype(BF16)

    def attend_back(k):
        for i in range(tiles):
            at = pl.ds(i * TL, TL)
            low = prob[k, :, at]
            p = low.astype(F32)
            prob_grad = dot(vn[...], mgk[k, :, at])
            inner = jnp.sum(p * prob_grad, axis=0, keepdims=True)
            score = (p * (prob_grad - inner)).astype(BF16)
            dq[k, :, at] = (dot(kt[...], score) * scale).astype(BF16)
            key_part = dot_nt(score, qk[k, :, at])
            value_part = dot_nt(low, mgk[k, :, at])
            if k == 0 and i == 0:
                dk[...] = key_part
                dv[...] = value_part
            else:
                dk[...] = dk[...] + key_part
                dv[...] = dv[...] + value_part

    attend_back(0)
    attend_back(1)
    plane_middle(order[1])

    H, PC = z.reach, z.piece
    offsets = [o for o in range(-H, H + 1) if o]
    inside = T >= LONGEST

    def halo_source(o):
        if inside:
            return (spot_in_row + 1) * T - ws if o > 0 else spot_in_row * T - LONGEST - ws
        return (spot_in_row + o) * T - ws

    def halo_copy(s, o):
        to = rem(here + o + G, G)
        return pltpu.make_async_remote_copy(
            src_ref=halo_out.at[s],
            dst_ref=halo_in.at[s],
            send_sem=hl_s.at[s],
            recv_sem=hl_r.at[s],
            device_id=(d, lax.div(to, N), rem(to, N)),
            device_id_type=MESH,
        )

    for s, o in enumerate(offsets):
        valid = jnp.logical_and(spot_in_row + o >= 0, spot_in_row + o < z.per_row)

        @pl.when(valid)
        def _(s=s, o=o):
            at = rows(halo_source(o), PC, 128)
            halo_out[s, 0] = (dk[at, :] * scale).astype(BF16)
            halo_out[s, 1] = dv[at, :].astype(BF16)
            halo_copy(s, o).start()

    for part in range(N):
        for at in range(NE):
            for i in range(LE):
                lo = expert_rows(at, i, part)
                x = at * LE + i
                span = slice(part * HP, (part + 1) * HP)
                one = dq[0, span, :].astype(F32) * hot[0][x : x + 1, :]
                one = one + dq[1, span, :].astype(F32) * hot[1][x : x + 1, :]
                dqt[lo : lo + HP, :] = one.astype(BF16)
    query_w_grad = dot(dqt[...], rw[own, :]).astype(BF16)
    key_w_grad = dot_tn((dk[...] * scale).astype(BF16), rw[...]).astype(BF16)
    value_w_grad = dot_tn(dv[...].astype(BF16), rw[...]).astype(BF16)
    for g in range(G):
        shared = slice((g % N) * HP, (g % N + 1) * HP)
        gqo[0, g * SH : g * SH + R, :] = query_w_grad[g * R : (g + 1) * R, :]
        gqo[0, g * SH + R : (g + 1) * SH, :] = key_w_grad[shared, :]
        gqo[1, g * SH + R : (g + 1) * SH, :] = value_w_grad[shared, :]
    push(gqo.at[1 - c], cqo, qc_s.at[0], qc_r.at[0], mate)
    plane_middle(order[2])
    line_start(order[0])
    ones = jnp.ones((8, T), BF16)
    sp[6:7, :] = dot_nt(ones, dqt[...])[0:1, :]
    sp[7:8, :] = jnp.zeros((1, D), F32)
    sp[7:8, 0 : z.experts] = jnp.transpose(
        jnp.broadcast_to(jnp.sum(logit_grad, axis=1, keepdims=True), (z.experts, 128))
    )[0:1, :]
    acc[...] = dot_tn(dqt[...], wq[...]) + dot_tn(logit_low, r_ref[...])
    sp[16:24, :] = dot(logit_low, rw[own, :])
    sp[15:16, :] = jnp.zeros((1, D), F32)
    sp[15:16, 0:HEAD] = jnp.sum(dv[...], axis=0, keepdims=True)
    for j in order[3:]:
        plane_middle(j)
    YW = D // NY
    ER = N * SH
    landed(cqo, qc_s.at[0], qc_r.at[0])
    pqo[...] = (gqo[c].astype(F32) + cqo[...].astype(F32)).astype(BF16)
    for i in range(1, NP):
        there, to = in_plane(i)
        src = pqo.at[rows(rem(there, NE) * ER, ER), rows(lax.div(there, NE) * YW, YW, 128)]
        push(src, rqo.at[i], qp_s.at[0, i], qp_r.at[0, i], to)
    line_start(order[1])

    dk[...] = dk[...] * scale
    for s, o in enumerate(offsets):
        back_valid = jnp.logical_and(spot_in_row - o >= 0, spot_in_row - o < z.per_row)

        @pl.when(back_valid)
        def _(s=s, o=o):
            halo_copy(s, o).wait_recv()
            at = off if (not inside or o > 0) else off + T - LONGEST
            at = rows(at, PC, 128)
            dk[at, :] = dk[at, :] + halo_in[s, 0].astype(F32)
            dv[at, :] = dv[at, :] + halo_in[s, 1].astype(F32)

    key_grad = dk[own, :]
    value_grad = dv[own, :]
    key_low, value_low = key_grad.astype(BF16), value_grad.astype(BF16)
    acc[...] = acc[...] + dot(key_low, wkv[0]) + dot(value_low, wkv[1])

    def norm_one_back(i, carry):
        at = rows(i * 128, 128, 128)
        unit, inverse = norm_stats(xw[rows(off + i * 128, 128, 128), :])
        grad = acc[at, :]
        scaled = grad * gain_one
        back = inverse * (
            scaled
            - jnp.mean(scaled, axis=1, keepdims=True)
            - unit * jnp.mean(scaled * unit, axis=1, keepdims=True)
        )
        ig_ref[at, :] = hgrad[at, :] + back
        parts = (grad * unit, grad)
        return tuple(a + jnp.sum(b, axis=0, keepdims=True) for a, b in zip(carry, parts))

    sums = lax.fori_loop(0, T // 128, norm_one_back, (zero_row,) * 2)
    sp[0:1, :] = sums[0]
    sp[1:2, :] = sums[1]
    for j in range(8 + N, 15):
        sp[j : j + 1, :] = zero_row
    push(sp.at[:, other_cols], csp, qc_s.at[2], qc_r.at[2], mate)
    for j in order[2:]:
        line_start(j)

    landed(csp, qc_s.at[2], qc_r.at[2])
    psp[...] = sp[:, mine_cols] + csp[...]
    for i in range(1, NP):
        _, to = in_plane(i)
        push(psp, rsp.at[i], qp_s.at[2, i], qp_r.at[2, i], to)

    whole = pqo[rows(e * ER, ER), rows(y * YW, YW, 128)].astype(F32)
    for i in range(1, NP):
        landed(rqo.at[i], qp_s.at[0, i], qp_r.at[0, i])
        whole = whole + rqo[i].astype(F32)
    zqo[...] = whole.astype(BF16)
    for j in range(1, N):
        there, to = in_line(j)
        push(zqo.at[rows(there * SH, SH)], yqo.at[j], qz_s.at[0, j], qz_r.at[0, j], to)
    whole = psp[...]
    for i in range(1, NP):
        landed(rsp.at[i], qp_s.at[2, i], qp_r.at[2, i])
        whole = whole + rsp[i]
    zsp[...] = whole
    for j in range(1, N):
        _, to = in_line(j)
        push(zsp, ysp.at[j], qz_s.at[2, j], qz_r.at[2, j], to)

    whole = zsend[0].astype(F32)
    for j in range(1, N):
        landed(zrecv.at[j], gz_s.at[j], gz_r.at[j])
        whole = whole + zrecv[j].astype(F32)

    def fin_left(ys, es):
        return fin.at[rows(c * HR + (es * NY + ys) * HS, HS), left]

    def fin_right(ys, es):
        return fin.at[rows(c * HR + (ys * NE + es) * HS, HS), right]

    fin[rows(c * HR + (e * NY + y) * HS, HS), left] = whole[:, 0:half].astype(BF16)
    fin[rows(c * HR + (y * NE + e) * HS, HS), right] = whole[:, half:].astype(BF16)
    for i in range(1, NP):
        _, to = in_plane(i)
        push(fin_left(y, e), fin_left(y, e), ga_s.at[0, i], ga_r.at[0, i], to)
        push(fin_right(y, e), fin_right(y, e), ga_s.at[1, i], ga_r.at[1, i], to)

    cols_copy.wait()
    for j in range(1, N):
        there, _ = in_line(-j)
        landed(outd.at[there], od_s.at[j], od_r.at[j])
    for j in range(N):
        at = pl.ds(j * T, T)
        out_ref[at, :] = out_ref[at, :] + outd[j].astype(F32)

    whole = zqo[rows(n * SH, SH), :].astype(F32)
    for j in range(1, N):
        landed(yqo.at[j], qz_s.at[0, j], qz_r.at[0, j])
        whole = whole + yqo[j].astype(F32)
    my_cols = rows(y * YW, YW, 128)
    fqo[c, :, my_cols] = whole.astype(BF16)
    for i in range(1, NY):
        _, to = in_rows(i)
        at = fqo.at[c, :, my_cols]
        push(at, at, qa_s.at[0, i], qa_r.at[0, i], to)
    whole = zsp[...]
    for j in range(1, N):
        landed(ysp.at[j], qz_s.at[2, j], qz_r.at[2, j])
        whole = whole + ysp[j]
    fsp[:, mine_cols] = whole
    at = fsp.at[:, mine_cols]
    push(at, at, qa_s.at[2, 0], qa_r.at[2, 0], mate)
    for i in range(1, NY):
        near, _ = in_rows(-i)
        landed(fqo.at[c, :, rows(near * YW, YW, 128)], qa_s.at[0, i], qa_r.at[0, i])
    push(fqo.at[c], fqo.at[c], qa_s.at[0, 0], qa_r.at[0, 0], mate)

    for i in range(1, NP):
        near, _ = in_plane(-i)
        ys, es = lax.div(near, NE), rem(near, NE)
        landed(fin_left(ys, es), ga_s.at[0, i], ga_r.at[0, i])
        landed(fin_right(ys, es), ga_s.at[1, i], ga_r.at[1, i])
    at = fin.at[rows(c * HR, HR)]
    push(at, at, ga_s.at[0, 0], ga_r.at[0, 0], mate)
    landed(fsp.at[:, other_cols], qa_s.at[2, 0], qa_r.at[2, 0])
    small_ref[...] = fsp[...]
    landed(fqo.at[1 - c], qa_s.at[0, 0], qa_r.at[0, 0])
    fqo_ref[...] = fqo[...]
    landed(fin.at[rows((1 - c) * HR, HR)], ga_s.at[0, 0], ga_r.at[0, 0])
    fin_ref[...] = fin[...]

    for copy in started:
        copy.wait_send()
    for s, o in enumerate(offsets):
        valid = jnp.logical_and(spot_in_row + o >= 0, spot_in_row + o < z.per_row)

        @pl.when(valid)
        def _(s=s, o=o):
            halo_copy(s, o).wait_send()


def run(z, x, seg, chosen, vectors, q, k, v, o, r, up, down, cot):
    N, G, NP, NY, NE = z.narrow, z.group, z.plane, z.rows_y, z.expert
    T, W, D, R, HP = z.block, z.window, z.width, z.shard, z.head_part
    FL = z.ff_local
    FR = D + FL
    HR = FR // 2
    HS = HR // NP
    YW = D // NY
    SH = R + HP
    ER = N * SH
    QR = G * R
    GR = G * SH
    S = 2 * z.reach
    SMALL = z.small_rows
    vmem = pl.BlockSpec(memory_space=pltpu.VMEM)
    anywhere = pl.BlockSpec(memory_space=pltpu.HBM)
    scratch = [
        ((W, D), F32),
        ((W, D), BF16),
        ((QR, D), BF16),
        ((QR, D), BF16),
        ((2, HEAD, D), BF16),
        ((G, 16, 128), F32),
        ((8, 128), F32),
        ((HEAD, 128), F32),
        ((N, FR, D), BF16),
        ((T, D), BF16),
        ((8, z.row_len), F32),
        ((W, 8), F32),
        ((W, HEAD), BF16),
        ((W, HEAD), BF16),
        ((HEAD, W), BF16),
        ((HEAD, W), BF16),
        ((QR, T), F32),
        ((2, HEAD, T), BF16),
        ((2, W, T), BF16),
        ((2, HEAD, T), F32),
        ((QR, T), BF16),
        ((T, D), F32),
        ((T, D), F32),
        ((T, D), BF16),
        ((N, T, FL), BF16),
        ((N, T, FL), BF16),
        ((T, FL), BF16),
        ((T, D), F32),
        ((T, D), F32),
        ((T, D), BF16),
        ((2, HEAD, T), BF16),
        ((W, HEAD), F32),
        ((W, HEAD), F32),
        ((2, HEAD, T), BF16),
        ((QR, T), BF16),
        ((max(S, 1), 2, z.piece, HEAD), BF16),
        ((max(S, 1), 2, z.piece, HEAD), BF16),
        ((T, D), BF16),
        ((N, T, D // N), BF16),
        ((N, FR, D), BF16),
        ((N, HR, D), BF16),
        ((N, HR, D), BF16),
        ((N, NE, HR // NE, D // 2), BF16),
        ((N, NY, HR // NY, D // 2), BF16),
        ((N, HR // NE, D // 2), BF16),
        ((N, HR // NY, D // 2), BF16),
        ((N, NY, HS, D // 2), BF16),
        ((N, NE, HS, D // 2), BF16),
        ((N, HS, D), BF16),
        ((N, HS, D), BF16),
        ((FR, D), BF16),
        ((2, GR, D), BF16),
        ((GR, D), BF16),
        ((GR, D), BF16),
        ((NP, ER, YW), BF16),
        ((ER, YW), BF16),
        ((N, SH, YW), BF16),
        ((2, SH, D), BF16),
        ((SMALL, D), F32),
        ((SMALL, D // 2), F32),
        ((SMALL, D // 2), F32),
        ((NP, SMALL, D // 2), F32),
        ((SMALL, D // 2), F32),
        ((N, SMALL, D // 2), F32),
        ((SMALL, D), F32),
    ]
    pairs = [
        (N,),
        (N,),
        (NE, N),
        (NE, N),
        (NE, N),
        (NE, N),
        (NE, N),
        (2, N),
        (4, N, max(NE, NY)),
        (N,),
        (N,),
        (N,),
        (max(S, 1),),
        (N,),
        (4, N, max(NE, NY)),
        (N,),
        (2, NP),
        (3,),
        (3, NP),
        (3, N),
        (3, NY),
    ]
    sems = [pltpu.SemaphoreType.DMA((4,))]
    for shape in pairs:
        sems += [pltpu.SemaphoreType.DMA(shape)] * 2
    outs = [
        ((N * T, D // N), F32),
        ((T, D), F32),
        ((FR, D), BF16),
        ((2, SH, D), BF16),
        ((SMALL, D), F32),
    ]
    return pl.pallas_call(
        functools.partial(kernel, z),
        out_shape=[pltpu.VMEM(s, t) for s, t in outs],
        in_specs=[anywhere] + [vmem] * (7 + len(vectors)) + [anywhere] * 2 + [vmem],
        out_specs=[vmem] * len(outs),
        scratch_shapes=[pltpu.VMEM(s, t) for s, t in scratch] + sems,
        compiler_params=pltpu.CompilerParams(
            collective_id=0, has_side_effects=True, vmem_limit_bytes=58 * 2**20
        ),
        name="layer",
    )(x, seg, chosen, *vectors, q, k, v, o, r, up, down, cot)


def finish_kernel(
    z,
    out_in,
    ig_in,
    fin_ref,
    fqo_ref,
    small_ref,
    out_any,
    ig_out,
    g1_ref,
    s1_ref,
    gq_ref,
    qb_ref,
    gk_ref,
    gv_ref,
    vb_ref,
    go_ref,
    ob_ref,
    rw_ref,
    rb_ref,
    g2_ref,
    s2_ref,
    gup_any,
    ub_ref,
    gdown_any,
    db_ref,
    gup,
    gdown,
    sems,
):
    e, n = lax.axis_index("expert"), lax.axis_index("narrow")
    N, T, D, R, HP, LE = z.narrow, z.block, z.width, z.shard, z.head_part, z.local_experts
    copies = []

    def put(src, dst):
        copies.append(pltpu.make_async_copy(src, dst, sems.at[len(copies)]))
        copies[-1].start()

    put(out_in, out_any)
    put(ig_in, ig_out)
    gup[...] = fin_ref[0:D, :].astype(F32)
    put(gup, gup_any)
    gdown[...] = fin_ref[D : D + z.ff_local, :].astype(F32)
    put(gdown, gdown_any)
    gq_ref[...] = fqo_ref[0, 0:R, :].astype(F32)
    go_ref[...] = fqo_ref[1, 0:R, :].astype(F32)
    gk_ref[...] = fqo_ref[0, R : R + HP, :].astype(F32)
    gv_ref[...] = fqo_ref[1, R : R + HP, :].astype(F32)
    g1_ref[...] = small_ref[0:1, :]
    s1_ref[...] = small_ref[1:2, :]
    ob_ref[...] = small_ref[2:3, :]
    g2_ref[...] = small_ref[3:4, :]
    s2_ref[...] = small_ref[4:5, :]
    db_ref[...] = small_ref[5:6, :]
    rb_ref[...] = small_ref[7:8, 0 : z.experts]
    rw_ref[...] = small_ref[16 : 16 + z.experts, :]
    upper = jnp.zeros((1, D), F32)
    for j in range(N):
        upper = jnp.where(n == j, small_ref[8 + j : 9 + j, :], upper)
    ub_ref[...] = upper
    here = e * N + n
    query = pltpu.roll(small_ref[0:8, :], lax.rem(D - here * R, D), 1)
    for i in range(LE):
        qb_ref[i : i + 1, :] = query[6:7, i * HP : (i + 1) * HP]
    value = pltpu.roll(small_ref[8:16, :], lax.rem(D - n * HP, D), 1)
    vb_ref[...] = value[7:8, 0:HP]
    for copy in copies:
        copy.wait()


def finish(z, out, ig, fin, fqo, small):
    N, T, D, R, HP = z.narrow, z.block, z.width, z.shard, z.head_part
    FL = z.ff_local
    vmem = pl.BlockSpec(memory_space=pltpu.VMEM)
    anywhere = pl.BlockSpec(memory_space=pltpu.HBM)
    shapes = [
        (N * T, D // N),
        (T, D),
        (1, D),
        (1, D),
        (R, D),
        (z.local_experts, HP),
        (HP, D),
        (HP, D),
        (1, HP),
        (R, D),
        (1, D),
        (z.experts, D),
        (1, z.experts),
        (1, D),
        (1, D),
        (D, FL),
        (1, FL),
        (FL, D),
        (1, D),
    ]
    return pl.pallas_call(
        functools.partial(finish_kernel, z),
        out_shape=[jax.ShapeDtypeStruct(s, F32) for s in shapes],
        in_specs=[vmem] * 5,
        out_specs=[anywhere] * 2 + [vmem] * 13 + [anywhere, vmem, anywhere, vmem],
        scratch_shapes=[
            pltpu.VMEM((D, FL), F32),
            pltpu.VMEM((FL, D), F32),
            pltpu.SemaphoreType.DMA((4,)),
        ],
        compiler_params=pltpu.CompilerParams(vmem_limit_bytes=16 * 2**20),
        name="finish",
    )(out, ig, fin, fqo, small)


def per_device(
    inputs,
    seg_ids,
    chosen,
    gain_one,
    shift_one,
    query_w,
    query_b,
    key_w,
    value_w,
    value_b,
    out_w,
    out_b,
    router_w,
    router_b,
    gain_two,
    shift_two,
    up_w,
    up_b,
    down_w,
    down_b,
    cotangent,
):
    narrow = lax.axis_size("narrow")
    e, n = lax.axis_index("expert"), lax.axis_index("narrow")
    z = Sizes(
        lax.axis_size("dp"),
        lax.axis_size("expert"),
        narrow,
        inputs.shape[0],
        inputs.shape[1],
        seg_ids.shape[1],
        query_w.shape[0],
        up_w.shape[1],
    )
    D, R, HP = z.width, z.shard, z.head_part
    vectors = [gain_one, shift_one, out_b, gain_two, shift_two, down_b, up_b]
    vectors = [v.reshape(1, -1) for v in vectors]
    vectors += [query_b, value_b.reshape(1, -1), router_b.reshape(1, -1)]
    parts = run(
        z,
        inputs,
        seg_ids,
        jnp.transpose(chosen),
        vectors,
        jnp.transpose(query_w, (0, 2, 1)).reshape(R, D),
        jnp.transpose(key_w),
        jnp.transpose(value_w),
        out_w.reshape(R, D),
        jnp.transpose(router_w),
        up_w,
        down_w,
        cotangent,
    )
    out, ig, g1, s1, gq, qb, gk, gv, vb, go, ob, rw, rb, g2, s2, gup, ub, gdown, db = finish(
        z, *parts
    )
    return (
        out,
        ig,
        g1.reshape(-1),
        s1.reshape(-1),
        jnp.transpose(gq.reshape(z.local_experts, HP, D), (0, 2, 1)),
        qb,
        jnp.transpose(gk),
        jnp.transpose(gv),
        vb.reshape(-1),
        go.reshape(z.local_experts, HP, D),
        ob.reshape(-1),
        jnp.transpose(rw),
        rb.reshape(-1),
        g2.reshape(-1),
        s2.reshape(-1),
        gup,
        ub.reshape(-1),
        gdown,
        db.reshape(-1),
    )


def solution(mesh):
    return jax.shard_map(
        per_device,
        mesh=mesh,
        in_specs=(
            P("dp", None),
            P("dp", None),
            P("dp", None),
            P(),
            P(),
            P("expert", None, "narrow"),
            P("expert", "narrow"),
            P(None, "narrow"),
            P(None, "narrow"),
            P("narrow"),
            P("expert", "narrow", None),
            P(),
            P(),
            P(),
            P(),
            P(),
            P(None, "narrow"),
            P("narrow"),
            P("narrow", None),
            P(),
            P(("dp", "expert"), "narrow"),
        ),
        out_specs=(
            P(("dp", "expert"), "narrow"),
            P(("dp", "expert", "narrow"), None),
            P(),
            P(),
            P("expert", None, "narrow"),
            P("expert", "narrow"),
            P(None, "narrow"),
            P(None, "narrow"),
            P("narrow"),
            P("expert", "narrow", None),
            P(),
            P(),
            P(),
            P(),
            P(),
            P(None, "narrow"),
            P("narrow"),
            P("narrow", None),
            P(),
        ),
        check_vma=False,
    )
```

```python
import functools
import math

import jax
import jax.numpy as jnp
from jax import lax
from jax.experimental import pallas as pl
from jax.experimental.pallas import tpu as pltpu
from jax.sharding import PartitionSpec as P

HEAD = 64
LONGEST = 256
EPSILON = 1e-05
MASKED = -1000000000.0
GELU_A = math.sqrt(2.0 / math.pi)
GELU_B = 0.044715
F32 = jnp.float32
BF16 = jnp.bfloat16
MESH = pl.DeviceIdType.MESH


def dot(a, b):
    return lax.dot_general(a, b, (((1,), (0,)), ((), ())), preferred_element_type=F32)


def dot_nt(a, b):
    return lax.dot_general(a, b, (((1,), (1,)), ((), ())), preferred_element_type=F32)


def dot_tn(a, b):
    return lax.dot_general(a, b, (((0,), (0,)), ((), ())), preferred_element_type=F32)


def norm_stats(x):
    centred = x - jnp.mean(x, axis=1, keepdims=True)
    inverse = lax.rsqrt(jnp.mean(centred * centred, axis=1, keepdims=True) + EPSILON)
    return centred * inverse, inverse


def rem(a, b):
    return lax.rem(a, b)


class Sizes:
    def __init__(self, dp, expert, narrow, tokens, width, row_len, local_experts, ff_local):
        self.dp, self.expert, self.narrow = dp, expert, narrow
        self.tokens, self.width, self.row_len = tokens, width, row_len
        self.local_experts = local_experts
        self.experts = local_experts * expert
        self.group = expert * narrow
        self.block = tokens // self.group
        self.rows_y = dp // 2
        self.plane = self.rows_y * expert
        self.ff_local = ff_local
        self.head_part = HEAD // narrow
        self.shard = local_experts * self.head_part
        self.per_row = row_len // self.block
        spans = [
            min(row_len, (j + 1) * self.block + LONGEST) - max(0, j * self.block - LONGEST)
            for j in range(self.per_row)
        ]
        self.window = max(spans)
        self.reach = max(1, LONGEST // self.block) if self.per_row > 1 else 0
        self.piece = min(self.block, LONGEST)
        self.tile = min(256, self.block)
        self.up_rows = narrow * ff_local // width
        self.small_rows = 24


def kernel(
    z,
    x_any,
    seg_ref,
    chosen_ref,
    g1_ref,
    s1_ref,
    ob_ref,
    g2_ref,
    s2_ref,
    db_ref,
    ub_ref,
    qb_ref,
    vb_ref,
    rb_ref,
    q_ref,
    k_ref,
    v_ref,
    o_ref,
    r_ref,
    up_any,
    down_any,
    cot_ref,
    out_any,
    ig_any,
    fin_any,
    fqo_ref,
    small_ref,
    out_ref,
    ig_ref,
    xw,
    rw,
    wq,
    wo,
    wkv,
    bias,
    corner,
    vcol,
    ffw,
    cot,
    segs,
    segc,
    kn,
    vn,
    kt,
    vt,
    qt,
    qk,
    prob,
    mix,
    mixg,
    hid,
    acc,
    second,
    active,
    slope,
    ugrad,
    sgrad,
    hgrad,
    hgb,
    mgk,
    dk,
    dv,
    dq,
    dqt,
    halo_out,
    halo_in,
    delta,
    outd,
    gsend,
    crecv,
    psend,
    pea,
    pya,
    mea,
    mya,
    pyb,
    peb,
    zsend,
    zrecv,
    fin,
    gqo,
    cqo,
    pqo,
    rqo,
    zqo,
    yqo,
    fqo,
    sp,
    csp,
    psp,
    rsp,
    zsp,
    ysp,
    fsp,
    loc_sem,
    w_s,
    w_r,
    wm_s,
    wm_r,
    b_s,
    b_r,
    q_s,
    q_r,
    qm_s,
    qm_r,
    o_s,
    o_r,
    om_s,
    om_r,
    fp_s,
    fp_r,
    fm_s,
    fm_r,
    ct_s,
    ct_r,
    od_s,
    od_r,
    hl_s,
    hl_r,
    gc_s,
    gc_r,
    gp_s,
    gp_r,
    gz_s,
    gz_r,
    ga_s,
    ga_r,
    qc_s,
    qc_r,
    qp_s,
    qp_r,
    qz_s,
    qz_r,
    qa_s,
    qa_r,
    fz_s,
    fz_r,
):
    d, e, n = lax.axis_index("dp"), lax.axis_index("expert"), lax.axis_index("narrow")
    c, y = rem(d, 2), lax.div(d, 2)
    N, G, NP, NE, NY = z.narrow, z.group, z.plane, z.expert, z.rows_y
    T, W, D, R, HP, LE = z.block, z.window, z.width, z.shard, z.head_part, z.local_experts
    FL = z.ff_local
    half = D // 2
    here = e * N + n
    spot = y * NE + e
    mate = (d + 1 - 2 * c, e, n)

    def in_group(j):
        at = rem(here + j + G, G)
        return at, (d, lax.div(at, N), rem(at, N))

    def in_plane(j):
        at = rem(spot + j + NP, NP)
        return at, (2 * lax.div(at, NE) + c, rem(at, NE), n)

    def in_line(j):
        at = rem(n + j + N, N)
        return at, (d, e, at)

    def in_rows(j):
        at = rem(y + j + NY, NY)
        return at, (2 * at + c, e, n)

    started = []

    def push(src, dst, send, recv, device):
        copy = pltpu.make_async_remote_copy(
            src_ref=src,
            dst_ref=dst,
            send_sem=send,
            recv_sem=recv,
            device_id=device,
            device_id_type=MESH,
        )
        copy.start()
        started.append(copy)

    def landed(dst, send, recv):
        pltpu.make_async_remote_copy(
            src_ref=dst,
            dst_ref=dst,
            send_sem=send,
            recv_sem=recv,
            device_id=mate,
            device_id_type=MESH,
        ).wait_recv()

    def rows(start, size, step=16):
        return pl.ds(pl.multiple_of(start, step), size)

    start = here * T
    row = lax.div(start, z.row_len)
    spot_in_row = rem(here, z.per_row)
    base = row * z.row_len
    ws = jnp.minimum(jnp.maximum(spot_in_row * T - LONGEST, 0), z.row_len - W)
    off = spot_in_row * T - ws
    own = rows(off, T, 128)

    x_copy = pltpu.make_async_copy(x_any.at[rows(base + ws, W, 128)], xw, loc_sem.at[0])
    x_copy.start()
    up_copy = pltpu.make_async_copy(up_any, ffw.at[n, pl.ds(0, D)], loc_sem.at[1])
    up_copy.start()
    down_copy = pltpu.make_async_copy(down_any, ffw.at[n, pl.ds(D, FL)], loc_sem.at[2])
    down_copy.start()
    cols_copy = pltpu.make_async_copy(
        x_any.at[rows(e * N * T, N * T, 128), rows(n * (D // N), D // N, 128)], out_ref, loc_sem.at[3]
    )
    cols_copy.start()
    wq[rows(here * R, R)] = q_ref[...]
    wo[rows(here * R, R)] = o_ref[...]
    wkv[0, rows(n * HP, HP)] = k_ref[...]
    wkv[1, rows(n * HP, HP)] = v_ref[...]
    bias[here] = jnp.zeros((16, 128), F32)
    for i in range(FL // 128):
        bias[here, i : i + 1, :] = ub_ref[0:1, i * 128 : (i + 1) * 128]
    bias[here, 8 : 8 + LE, 0:HP] = qb_ref[...]
    bias[here, 7:8, 0:HP] = vb_ref[...]

    barrier = pltpu.get_barrier_semaphore()
    pl.semaphore_signal(barrier, inc=1, device_id=mate, device_id_type=MESH)
    for j in range(1, NP):
        pl.semaphore_signal(barrier, inc=1, device_id=in_plane(j)[1], device_id_type=MESH)
    for j in range(1, G):
        pl.semaphore_signal(barrier, inc=1, device_id=in_group(j)[1], device_id_type=MESH)
    pl.semaphore_wait(barrier, NP + G - 1)

    mine_cols = rows(c * half, half, 128)
    other_cols = rows((1 - c) * half, half, 128)

    def in_expert(i):
        at = rem(e + i + NE, NE)
        return at, (d, at, n)

    def shard_at(i, j):
        return rem(e - i + NE, NE) * N + rem(n - j + N, N)

    def spread_start(part, send, recv):
        for j in range(1, N):
            at = part(here)
            push(at, at, send.at[j - 1], recv.at[j - 1], in_line(j)[1])
        for i in range(1, NE):
            at = part(here)
            push(at, at, send.at[i * N - 1], recv.at[i * N - 1], in_expert(i)[1])

    def spread_on(part, send, recv, to_mate):
        for j in range(1, N):
            at = part(shard_at(0, j))
            landed(at, send.at[j - 1], recv.at[j - 1])
            for i in range(1, NE):
                push(at, at, send.at[i * N + j - 1], recv.at[i * N + j - 1], in_expert(i)[1])
            if to_mate is not None:
                push(at, at, to_mate[0].at[j - 1], to_mate[1].at[j - 1], mate)

    def spread_end(part, send, recv, to_mate):
        for i in range(1, NE):
            for j in range(N):
                at = part(shard_at(i, j))
                landed(at, send.at[i * N + j - 1], recv.at[i * N + j - 1])
                if to_mate is not None:
                    push(at, at, to_mate[0].at[i * N + j - 1], to_mate[1].at[i * N + j - 1], mate)

    def spread_wait(part, to_mate):
        for i in range(NE):
            for j in range(N):
                if i or j:
                    landed(part(shard_at(i, j)), to_mate[0].at[i * N + j - 1], to_mate[1].at[i * N + j - 1])

    def bias_part(g):
        return bias.at[g]

    def q_part(g):
        return wq.at[rows(g * R, R), mine_cols]

    def q_other(g):
        return wq.at[rows(g * R, R), other_cols]

    def o_part(g):
        return wo.at[rows(g * R, R), mine_cols]

    def o_other(g):
        return wo.at[rows(g * R, R), other_cols]

    for j in range(1, N):
        at = wkv.at[c, rows(n * HP, HP)]
        push(at, at, w_s.at[j - 1], w_r.at[j - 1], in_line(j)[1])
    spread_start(q_part, q_s, q_r)
    spread_start(bias_part, b_s, b_r)
    up_copy.wait()
    down_copy.wait()
    FR = D + FL

    left, right = pl.ds(0, half), pl.ds(half, half)
    HR = FR // 2
    HS = HR // NP
    HA, HB = HR // NE, HR // NY
    def left_slice(of, ys, es):
        return ffw.at[of, rows(c * HR + (es * NY + ys) * HS, HS), left]

    def right_slice(of, ys, es):
        return ffw.at[of, rows(c * HR + (ys * NE + es) * HS, HS), right]

    def left_half(of, es):
        return ffw.at[of, rows(c * HR + es * HA, HA), left]

    def right_half(of, ys):
        return ffw.at[of, rows(c * HR + ys * HB, HB), right]

    def by_distance(at):
        return sorted((o for o in range(N) if o != at), key=lambda o: (abs(o - at), o))

    def pick(choices):
        value = choices[0]
        for at in range(1, N):
            value = jnp.where(n == at, choices[at], value)
        return value

    shard_of = [n] + [pick([by_distance(at)[k] for at in range(N)]) for k in range(N - 1)]
    maybe_started = []

    def line_push(of, step, valid):
        of = jnp.clip(of, 0, N - 1)
        to = (d, e, jnp.clip(n + step, 0, N - 1))
        way = (step + 1) // 2
        copies = [
            pltpu.make_async_remote_copy(
                src_ref=at,
                dst_ref=at,
                send_sem=fz_s.at[part, way, of],
                recv_sem=fz_r.at[part, of],
                device_id=to,
                device_id_type=MESH,
            )
            for part, at in enumerate((left_slice(of, y, e), right_slice(of, y, e)))
        ]

        @pl.when(valid)
        def _():
            for copy in copies:
                copy.start()

        maybe_started.append((valid, copies))

    def line_landed(of, valid):
        of = jnp.clip(of, 0, N - 1)

        @pl.when(valid)
        def _():
            landed(left_slice(of, y, e), fz_s.at[0, 0, of], fz_r.at[0, of])
            landed(right_slice(of, y, e), fz_s.at[1, 0, of], fz_r.at[1, of])

    def shards_start():
        line_push(n, 1, n + 1 < N)
        line_push(n, -1, n > 0)

    def shards_on(hop):
        line_landed(n - hop, n >= hop)
        line_push(n - hop, 1, jnp.logical_and(n >= hop, n + 1 < N))
        line_landed(n + hop, n + hop < N)
        line_push(n + hop, -1, jnp.logical_and(n + hop < N, n > 0))

    def plane_on(j):
        there = shard_of[j]
        at = left_slice(there, y, e)
        for i in range(1, NY):
            push(at, at, fp_s.at[0, j - 1, i - 1], fp_r.at[0, j - 1, i - 1], in_rows(i)[1])
        at = right_slice(there, y, e)
        for i in range(1, NE):
            push(at, at, fp_s.at[1, j - 1, i - 1], fp_r.at[1, j - 1, i - 1], in_expert(i)[1])

    def plane_turn(j):
        there = shard_of[j]
        for i in range(1, NY):
            near, _ = in_rows(-i)
            landed(left_slice(there, near, e), fp_s.at[0, j - 1, i - 1], fp_r.at[0, j - 1, i - 1])
        at = left_half(there, e)
        for i in range(1, NE):
            push(at, at, fp_s.at[2, j - 1, i - 1], fp_r.at[2, j - 1, i - 1], in_expert(i)[1])
        for i in range(1, NE):
            near, _ = in_expert(-i)
            landed(right_slice(there, y, near), fp_s.at[1, j - 1, i - 1], fp_r.at[1, j - 1, i - 1])
        at = right_half(there, y)
        for i in range(1, NY):
            push(at, at, fp_s.at[3, j - 1, i - 1], fp_r.at[3, j - 1, i - 1], in_rows(i)[1])

    def mate_on(j):
        there = shard_of[j]
        for i in range(1, NE):
            near, _ = in_expert(-i)
            landed(left_half(there, near), fp_s.at[2, j - 1, i - 1], fp_r.at[2, j - 1, i - 1])
        for i in range(1, NY):
            near, _ = in_rows(-i)
            landed(right_half(there, near), fp_s.at[3, j - 1, i - 1], fp_r.at[3, j - 1, i - 1])
        at = ffw.at[there, rows(c * HR, HR)]
        push(at, at, fm_s.at[j - 1], fm_r.at[j - 1], mate)

    x_copy.wait()
    gain_one, shift_one = g1_ref[...], s1_ref[...]

    def norm_one(i, carry):
        at = rows(i * 128, 128, 128)
        unit, _ = norm_stats(xw[at, :])
        rw[at, :] = (unit * gain_one + shift_one).astype(BF16)
        return carry

    lax.fori_loop(0, W // 128, norm_one, 0)

    seg_all = seg_ref[...].astype(F32)
    row_id = lax.broadcasted_iota(jnp.int32, seg_all.shape, 0)
    seg_here = jnp.sum(jnp.where(row_id == row, seg_all, 0.0), axis=0, keepdims=True)
    segs[...] = jnp.broadcast_to(seg_here, segs.shape)
    segc[...] = jnp.transpose(segs[:, rows(ws, W, 128)])
    seg_own = segs[0:1, rows(spot_in_row * T, T, 128)]
    corner[...] = jnp.zeros_like(corner)
    corner[:, 0 : z.experts] = jnp.broadcast_to(rb_ref[...], (8, z.experts))
    router_col = jnp.transpose(corner[...])[0 : z.experts, 0:1]
    logits = dot_nt(r_ref[...], rw[own, :]) + router_col
    expert_id = lax.broadcasted_iota(jnp.int32, (z.experts, T), 0)
    hot, picked = [], []
    for k in range(2):
        chosen = chosen_ref[k : k + 1, rows(start, T, 128)]
        hot.append((expert_id == chosen).astype(F32))
        picked.append(jnp.sum(logits * hot[k], axis=0, keepdims=True))
    top = jnp.maximum(picked[0], picked[1])
    raised = [jnp.exp(p - top) for p in picked]
    total = raised[0] + raised[1]
    gate = [r / total for r in raised]

    for j in range(1, N):
        there, _ = in_line(-j)
        at = wkv.at[c, rows(there * HP, HP)]
        landed(at, w_s.at[j - 1], w_r.at[j - 1])
        push(at, at, wm_s.at[j - 1], wm_r.at[j - 1], mate)
    spread_on(q_part, q_s, q_r, (qm_s, qm_r))
    spread_on(bias_part, b_s, b_r, None)
    shards_start()
    spread_start(o_part, o_s, o_r)

    for j in range(1, N):
        there, _ = in_line(-j)
        landed(wkv.at[1 - c, rows(there * HP, HP)], wm_s.at[j - 1], wm_r.at[j - 1])
    kn[...] = dot_nt(rw[...], wkv[0]).astype(BF16)
    kt[...] = dot_nt(wkv[0], rw[...]).astype(BF16)
    spread_end(q_part, q_s, q_r, (qm_s, qm_r))
    spread_end(bias_part, b_s, b_r, None)
    columns = [jnp.transpose(bias[g, 0:16, :]) for g in range(G)]
    for part in range(N):
        vcol[part * HP : (part + 1) * HP, :] = jnp.broadcast_to(columns[part][0:HP, 7:8], (HP, 128))
    value_row = jnp.transpose(vcol[...])[0:1, :]
    vn[...] = (dot_nt(rw[...], wkv[1]) + value_row).astype(BF16)
    vt[...] = (dot_nt(wkv[1], rw[...]) + vcol[:, 0:1]).astype(BF16)

    spread_wait(q_other, (qm_s, qm_r))
    qt[...] = dot_nt(wq[...], rw[own, :])

    def expert_rows(at, i, part):
        return ((at * N + part) * LE + i) * HP

    for part in range(N):
        chosen_rows = [jnp.zeros((HP, T), F32), jnp.zeros((HP, T), F32)]
        for at in range(NE):
            g = at * N + part
            for i in range(LE):
                lo = expert_rows(at, i, part)
                one = qt[lo : lo + HP, :] + columns[g][0:HP, 8 + i : 9 + i]
                for k in range(2):
                    chosen_rows[k] = chosen_rows[k] + one * hot[k][at * LE + i : at * LE + i + 1, :]
        for k in range(2):
            qk[k, part * HP : (part + 1) * HP, :] = chosen_rows[k].astype(BF16)

    scale = 1.0 / math.sqrt(HEAD)
    TL = z.tile
    tiles = T // TL
    seg_tiles = [seg_own[:, i * TL : (i + 1) * TL] for i in range(tiles)]

    def attend(k):
        for i in range(tiles):
            at = pl.ds(i * TL, TL)
            scores = dot(kn[...], qk[k, :, at]) * scale
            scores = jnp.where(segc[:, 0:1] == seg_tiles[i], scores, MASKED)
            high = jnp.max(scores, axis=0, keepdims=True)
            raised_scores = jnp.exp(scores - high)
            low = (raised_scores * (1.0 / jnp.sum(raised_scores, axis=0, keepdims=True))).astype(BF16)
            prob[k, :, at] = low
            mix[k, :, at] = dot(vt[...], low)

    attend(0)
    attend(1)
    shards_on(1)
    plane_on(1)
    spread_on(o_part, o_s, o_r, (om_s, om_r))
    plane_turn(1)
    shards_on(2)
    plane_on(2)
    CW = D // N
    cot[:, rows(n * CW, CW, 128)] = cot_ref[rows(n * T, T, 128), :]
    for j in range(1, N):
        there, to = in_line(j)
        push(
            cot_ref.at[rows(there * T, T, 128)],
            cot.at[:, rows(n * CW, CW, 128)],
            ct_s.at[j - 1],
            ct_r.at[j - 1],
            to,
        )
    spread_end(o_part, o_s, o_r, (om_s, om_r))

    for part in range(N):
        for at in range(NE):
            for i in range(LE):
                lo = expert_rows(at, i, part)
                x = at * LE + i
                gated = jnp.zeros((HP, T), F32)
                for k in range(2):
                    rounded_mix = mix[k, part * HP : (part + 1) * HP, :].astype(BF16).astype(F32)
                    gated = gated + rounded_mix * (hot[k][x : x + 1, :] * gate[k])
                mixg[lo : lo + HP, :] = gated.astype(BF16)
    spread_wait(o_other, (om_s, om_r))
    out_b, down_b = ob_ref[...], db_ref[...]
    gain_two, shift_two = g2_ref[...], s2_ref[...]
    attention = dot_tn(mixg[...], wo[...]) + out_b
    acc[...] = attention + down_b
    hid[...] = xw[own, :] + attention

    def norm_two(i, carry):
        at = rows(i * 128, 128, 128)
        unit, _ = norm_stats(hid[at, :])
        second[at, :] = (unit * gain_two + shift_two).astype(BF16)
        return carry

    lax.fori_loop(0, T // 128, norm_two, 0)
    sgrad[...] = jnp.zeros_like(sgrad)

    def core_start(j):
        push(
            gsend.at[j, rows((1 - c) * HR, HR)], crecv.at[j], gc_s.at[j], gc_r.at[j], mate
        )

    def plane_start(j):
        landed(crecv.at[j], gc_s.at[j], gc_r.at[j])
        psend[j] = (
            gsend[j, rows(c * HR, HR), :].astype(F32) + crecv[j].astype(F32)
        ).astype(BF16)
        for i in range(1, NE):
            there, to = in_expert(i)
            src = psend.at[j, rows(there * HA, HA), left]
            push(src, pea.at[j, i], gp_s.at[0, j, i - 1], gp_r.at[0, j, i - 1], to)
        for i in range(1, NY):
            there, to = in_rows(i)
            src = psend.at[j, rows(there * HB, HB), right]
            push(src, pya.at[j, i], gp_s.at[1, j, i - 1], gp_r.at[1, j, i - 1], to)

    def plane_middle(j):
        whole = psend[j, rows(e * HA, HA), left].astype(F32)
        for i in range(1, NE):
            landed(pea.at[j, i], gp_s.at[0, j, i - 1], gp_r.at[0, j, i - 1])
            whole = whole + pea[j, i].astype(F32)
        mea[j] = whole.astype(BF16)
        for i in range(1, NY):
            there, to = in_rows(i)
            src = mea.at[j, rows(there * HS, HS)]
            push(src, pyb.at[j, i], gp_s.at[2, j, i - 1], gp_r.at[2, j, i - 1], to)
        whole = psend[j, rows(y * HB, HB), right].astype(F32)
        for i in range(1, NY):
            landed(pya.at[j, i], gp_s.at[1, j, i - 1], gp_r.at[1, j, i - 1])
            whole = whole + pya[j, i].astype(F32)
        mya[j] = whole.astype(BF16)
        for i in range(1, NE):
            there, to = in_expert(i)
            src = mya.at[j, rows(there * HS, HS)]
            push(src, peb.at[j, i], gp_s.at[3, j, i - 1], gp_r.at[3, j, i - 1], to)

    def line_start(j):
        whole = mea[j, rows(y * HS, HS), :].astype(F32)
        for i in range(1, NY):
            landed(pyb.at[j, i], gp_s.at[2, j, i - 1], gp_r.at[2, j, i - 1])
            whole = whole + pyb[j, i].astype(F32)
        zsend[j, :, left] = whole.astype(BF16)
        whole = mya[j, rows(e * HS, HS), :].astype(F32)
        for i in range(1, NE):
            landed(peb.at[j, i], gp_s.at[3, j, i - 1], gp_r.at[3, j, i - 1])
            whole = whole + peb[j, i].astype(F32)
        zsend[j, :, right] = whole.astype(BF16)
        if j:
            push(zsend.at[j], zrecv.at[n], gz_s.at[j], gz_r.at[n], (d, e, shard_of[j]))

    def forward(j):
        there = shard_of[j]
        if j:
            landed(ffw.at[there, rows((1 - c) * HR, HR)], fm_s.at[j - 1], fm_r.at[j - 1])
        up_b = jnp.concatenate(
            [bias[e * N + there, i : i + 1, :] for i in range(FL // 128)], axis=1
        )

        def feed(i, carry):
            at = rows(i * TL, TL, 128)
            upper = dot(second[at, :], ffw[there, 0:D, :]) + up_b
            square = upper * upper
            t = jnp.tanh(upper * (GELU_A + (GELU_A * GELU_B) * square))
            one = 0.5 + 0.5 * t
            low = (upper * one).astype(BF16)
            active[j, at, :] = low
            slope[j, at, :] = (
                one + (0.5 * upper) * (1.0 - t * t) * (GELU_A + (3.0 * GELU_A * GELU_B) * square)
            ).astype(BF16)
            acc[at, :] = acc[at, :] + dot(low, ffw[there, D : D + FL, :])
            return carry

        lax.fori_loop(0, T // TL, feed, 0)

    def backward(j):
        there = shard_of[j]

        def feed_back(i, carry):
            at = rows(i * TL, TL, 128)
            back = dot_nt(cot[at, :], ffw[there, D : D + FL, :]) * slope[j, at, :].astype(F32)
            back = back.astype(BF16)
            ugrad[at, :] = back
            sgrad[at, :] = sgrad[at, :] + dot_nt(back, ffw[there, 0:D, :])
            return carry

        lax.fori_loop(0, T // TL, feed_back, 0)
        sp[pl.ds(8 + there, 1), :] = jnp.sum(ugrad[...].astype(F32), axis=0, keepdims=True)
        gsend[j, 0:D, :] = dot_tn(second[...], ugrad[...]).astype(BF16)
        gsend[j, D : D + FL, :] = dot_tn(active[j], cot[...]).astype(BF16)
        core_start(j)

    def cotangent_wait():
        for j in range(1, N):
            there, _ = in_line(-j)
            landed(cot.at[:, rows(there * CW, CW, 128)], ct_s.at[j - 1], ct_r.at[j - 1])

    forward(0)
    plane_turn(2)
    mate_on(1)
    shards_on(3)
    plane_on(3)
    forward(1)
    mate_on(2)
    plane_turn(3)
    forward(2)
    cotangent_wait()
    backward(1)
    backward(2)
    plane_start(1)
    mate_on(3)
    forward(3)
    delta[...] = acc[...].astype(BF16)
    outd[n] = delta[:, rows(n * CW, CW, 128)]
    for j in range(1, N):
        there, to = in_line(j)
        push(delta.at[:, rows(there * CW, CW, 128)], outd.at[n], od_s.at[j - 1], od_r.at[j - 1], to)

    backward(3)
    plane_start(2)
    backward(0)
    plane_start(3)
    plane_middle(1)

    zero_row = jnp.zeros((1, D), F32)

    def norm_two_back(i, carry):
        at = rows(i * 128, 128, 128)
        unit, inverse = norm_stats(hid[at, :])
        grad = sgrad[at, :]
        scaled = grad * gain_two
        back = inverse * (
            scaled
            - jnp.mean(scaled, axis=1, keepdims=True)
            - unit * jnp.mean(scaled * unit, axis=1, keepdims=True)
        )
        top_grad = cot[at, :].astype(F32)
        whole = top_grad + back
        hgrad[at, :] = whole
        hgb[at, :] = whole.astype(BF16)
        parts = (grad * unit, grad, whole, top_grad)
        return tuple(a + jnp.sum(b, axis=0, keepdims=True) for a, b in zip(carry, parts))

    sums = lax.fori_loop(0, T // 128, norm_two_back, (zero_row,) * 4)
    sp[3:4, :] = sums[0]
    sp[4:5, :] = sums[1]
    sp[2:3, :] = sums[2]
    sp[5:6, :] = sums[3]

    plane_start(0)

    SH = R + HP
    out_grad = dot(mixg[...], hgb[...]).astype(BF16)
    for g in range(G):
        gqo[1, g * SH : g * SH + R, :] = out_grad[g * R : (g + 1) * R, :]
    qt[...] = dot_nt(wo[...], hgb[...])
    gate_grad = [jnp.zeros((1, T), F32), jnp.zeros((1, T), F32)]
    for part in range(N):
        picked_rows = [jnp.zeros((HP, T), F32), jnp.zeros((HP, T), F32)]
        for at in range(NE):
            for i in range(LE):
                lo = expert_rows(at, i, part)
                one = qt[lo : lo + HP, :]
                x = at * LE + i
                for k in range(2):
                    picked_rows[k] = picked_rows[k] + one * hot[k][x : x + 1, :]
        for k in range(2):
            span = slice(part * HP, (part + 1) * HP)
            rounded_mix = mix[k, span, :].astype(BF16).astype(F32)
            gate_grad[k] = gate_grad[k] + jnp.sum(picked_rows[k] * rounded_mix, axis=0, keepdims=True)
            mgk[k, span, :] = (picked_rows[k] * gate[k]).astype(BF16)
    middle = gate[0] * gate_grad[0] + gate[1] * gate_grad[1]
    logit_grad = sum(hot[k] * (gate[k] * (gate_grad[k] - middle)) for k in range(2))
    logit_low = logit_grad.astype(BF16)

    def attend_back(k):
        for i in range(tiles):
            at = pl.ds(i * TL, TL)
            low = prob[k, :, at]
            p = low.astype(F32)
            prob_grad = dot(vn[...], mgk[k, :, at])
            inner = jnp.sum(p * prob_grad, axis=0, keepdims=True)
            score = (p * (prob_grad - inner)).astype(BF16)
            dq[k, :, at] = (dot(kt[...], score) * scale).astype(BF16)
            key_part = dot_nt(score, qk[k, :, at])
            value_part = dot_nt(low, mgk[k, :, at])
            if k == 0 and i == 0:
                dk[...] = key_part
                dv[...] = value_part
            else:
                dk[...] = dk[...] + key_part
                dv[...] = dv[...] + value_part

    attend_back(0)
    attend_back(1)
    plane_middle(2)

    H, PC = z.reach, z.piece
    offsets = [o for o in range(-H, H + 1) if o]
    inside = T >= LONGEST

    def halo_source(o):
        if inside:
            return (spot_in_row + 1) * T - ws if o > 0 else spot_in_row * T - LONGEST - ws
        return (spot_in_row + o) * T - ws

    def halo_copy(s, o):
        to = rem(here + o + G, G)
        return pltpu.make_async_remote_copy(
            src_ref=halo_out.at[s],
            dst_ref=halo_in.at[s],
            send_sem=hl_s.at[s],
            recv_sem=hl_r.at[s],
            device_id=(d, lax.div(to, N), rem(to, N)),
            device_id_type=MESH,
        )

    for s, o in enumerate(offsets):
        valid = jnp.logical_and(spot_in_row + o >= 0, spot_in_row + o < z.per_row)

        @pl.when(valid)
        def _(s=s, o=o):
            at = rows(halo_source(o), PC, 128)
            halo_out[s, 0] = (dk[at, :] * scale).astype(BF16)
            halo_out[s, 1] = dv[at, :].astype(BF16)
            halo_copy(s, o).start()

    for part in range(N):
        for at in range(NE):
            for i in range(LE):
                lo = expert_rows(at, i, part)
                x = at * LE + i
                span = slice(part * HP, (part + 1) * HP)
                one = dq[0, span, :].astype(F32) * hot[0][x : x + 1, :]
                one = one + dq[1, span, :].astype(F32) * hot[1][x : x + 1, :]
                dqt[lo : lo + HP, :] = one.astype(BF16)
    query_w_grad = dot(dqt[...], rw[own, :]).astype(BF16)
    key_w_grad = dot_tn((dk[...] * scale).astype(BF16), rw[...]).astype(BF16)
    value_w_grad = dot_tn(dv[...].astype(BF16), rw[...]).astype(BF16)
    for g in range(G):
        shared = slice((g % N) * HP, (g % N + 1) * HP)
        gqo[0, g * SH : g * SH + R, :] = query_w_grad[g * R : (g + 1) * R, :]
        gqo[0, g * SH + R : (g + 1) * SH, :] = key_w_grad[shared, :]
        gqo[1, g * SH + R : (g + 1) * SH, :] = value_w_grad[shared, :]
    push(gqo.at[1 - c], cqo, qc_s.at[0], qc_r.at[0], mate)
    plane_middle(3)
    line_start(1)
    ones = jnp.ones((8, T), BF16)
    sp[6:7, :] = dot_nt(ones, dqt[...])[0:1, :]
    sp[7:8, :] = jnp.zeros((1, D), F32)
    sp[7:8, 0 : z.experts] = jnp.transpose(
        jnp.broadcast_to(jnp.sum(logit_grad, axis=1, keepdims=True), (z.experts, 128))
    )[0:1, :]
    acc[...] = dot_tn(dqt[...], wq[...]) + dot_tn(logit_low, r_ref[...])
    sp[16:24, :] = dot(logit_low, rw[own, :])
    sp[15:16, :] = jnp.zeros((1, D), F32)
    sp[15:16, 0:HEAD] = jnp.sum(dv[...], axis=0, keepdims=True)
    YW = D // NY
    ER = N * SH
    landed(cqo, qc_s.at[0], qc_r.at[0])
    pqo[...] = (gqo[c].astype(F32) + cqo[...].astype(F32)).astype(BF16)
    for i in range(1, NP):
        there, to = in_plane(i)
        src = pqo.at[rows(rem(there, NE) * ER, ER), rows(lax.div(there, NE) * YW, YW, 128)]
        push(src, rqo.at[i], qp_s.at[0, i - 1], qp_r.at[0, i - 1], to)
    plane_middle(0)
    line_start(2)
    line_start(3)

    dk[...] = dk[...] * scale
    for s, o in enumerate(offsets):
        back_valid = jnp.logical_and(spot_in_row - o >= 0, spot_in_row - o < z.per_row)

        @pl.when(back_valid)
        def _(s=s, o=o):
            halo_copy(s, o).wait_recv()
            at = off if (not inside or o > 0) else off + T - LONGEST
            at = rows(at, PC, 128)
            dk[at, :] = dk[at, :] + halo_in[s, 0].astype(F32)
            dv[at, :] = dv[at, :] + halo_in[s, 1].astype(F32)

    key_grad = dk[own, :]
    value_grad = dv[own, :]
    key_low, value_low = key_grad.astype(BF16), value_grad.astype(BF16)
    acc[...] = acc[...] + dot(key_low, wkv[0]) + dot(value_low, wkv[1])

    def norm_one_back(i, carry):
        at = rows(i * 128, 128, 128)
        unit, inverse = norm_stats(xw[rows(off + i * 128, 128, 128), :])
        grad = acc[at, :]
        scaled = grad * gain_one
        back = inverse * (
            scaled
            - jnp.mean(scaled, axis=1, keepdims=True)
            - unit * jnp.mean(scaled * unit, axis=1, keepdims=True)
        )
        ig_ref[at, :] = hgrad[at, :] + back
        parts = (grad * unit, grad)
        return tuple(a + jnp.sum(b, axis=0, keepdims=True) for a, b in zip(carry, parts))

    sums = lax.fori_loop(0, T // 128, norm_one_back, (zero_row,) * 2)
    ig_copy = pltpu.make_async_copy(ig_ref, ig_any, loc_sem.at[4])
    ig_copy.start()
    sp[0:1, :] = sums[0]
    sp[1:2, :] = sums[1]
    for j in range(8 + N, 15):
        sp[j : j + 1, :] = zero_row
    push(sp.at[:, other_cols], csp, qc_s.at[1], qc_r.at[1], mate)

    landed(csp, qc_s.at[1], qc_r.at[1])
    psp[...] = sp[:, mine_cols] + csp[...]
    for i in range(1, NP):
        _, to = in_plane(i)
        push(psp, rsp.at[i], qp_s.at[1, i - 1], qp_r.at[1, i - 1], to)

    line_start(0)

    whole = zsend[0].astype(F32)
    for j in range(1, N):
        there, _ = in_line(-j)
        landed(zrecv.at[there], gz_s.at[j], gz_r.at[there])
        whole = whole + zrecv[there].astype(F32)

    def fin_left(ys, es):
        return fin.at[rows(c * HR + (es * NY + ys) * HS, HS), left]

    def fin_right(ys, es):
        return fin.at[rows(c * HR + (ys * NE + es) * HS, HS), right]

    fin[rows(c * HR + (e * NY + y) * HS, HS), left] = whole[:, 0:half].astype(BF16)
    fin[rows(c * HR + (y * NE + e) * HS, HS), right] = whole[:, half:].astype(BF16)
    for i in range(1, NP):
        _, to = in_plane(i)
        push(fin_left(y, e), fin_left(y, e), ga_s.at[i], ga_r.at[i], to)
        push(fin_right(y, e), fin_right(y, e), ga_s.at[NP - 1 + i], ga_r.at[NP - 1 + i], to)

    whole = pqo[rows(e * ER, ER), rows(y * YW, YW, 128)].astype(F32)
    for i in range(1, NP):
        landed(rqo.at[i], qp_s.at[0, i - 1], qp_r.at[0, i - 1])
        whole = whole + rqo[i].astype(F32)
    zqo[...] = whole.astype(BF16)
    for j in range(1, N):
        there, to = in_line(j)
        push(zqo.at[rows(there * SH, SH)], yqo.at[j], qz_s.at[0, j - 1], qz_r.at[0, j - 1], to)
    whole = psp[...]
    for i in range(1, NP):
        landed(rsp.at[i], qp_s.at[1, i - 1], qp_r.at[1, i - 1])
        whole = whole + rsp[i]
    zsp[...] = whole
    for j in range(1, N):
        _, to = in_line(j)
        push(zsp, ysp.at[j], qz_s.at[1, j - 1], qz_r.at[1, j - 1], to)

    cols_copy.wait()
    for j in range(1, N):
        there, _ = in_line(-j)
        landed(outd.at[there], od_s.at[j - 1], od_r.at[j - 1])
    for j in range(N):
        at = pl.ds(j * T, T)
        out_ref[at, :] = out_ref[at, :] + outd[j].astype(F32)
    out_copy = pltpu.make_async_copy(out_ref, out_any, loc_sem.at[5])
    out_copy.start()

    whole = zqo[rows(n * SH, SH), :].astype(F32)
    for j in range(1, N):
        landed(yqo.at[j], qz_s.at[0, j - 1], qz_r.at[0, j - 1])
        whole = whole + yqo[j].astype(F32)
    my_cols = rows(y * YW, YW, 128)
    fqo[c, :, my_cols] = whole.astype(BF16)
    for i in range(1, NY):
        _, to = in_rows(i)
        at = fqo.at[c, :, my_cols]
        push(at, at, qa_s.at[1 + i], qa_r.at[1 + i], to)
    whole = zsp[...]
    for j in range(1, N):
        landed(ysp.at[j], qz_s.at[1, j - 1], qz_r.at[1, j - 1])
        whole = whole + ysp[j]
    fsp[:, mine_cols] = whole
    at = fsp.at[:, mine_cols]
    push(at, at, qa_s.at[1], qa_r.at[1], mate)
    for i in range(1, NY):
        near, _ = in_rows(-i)
        landed(fqo.at[c, :, rows(near * YW, YW, 128)], qa_s.at[1 + i], qa_r.at[1 + i])
    push(fqo.at[c], fqo.at[c], qa_s.at[0], qa_r.at[0], mate)

    for i in range(1, NP):
        near, _ = in_plane(-i)
        ys, es = lax.div(near, NE), rem(near, NE)
        landed(fin_left(ys, es), ga_s.at[i], ga_r.at[i])
        landed(fin_right(ys, es), ga_s.at[NP - 1 + i], ga_r.at[NP - 1 + i])
    at = rows(c * HR, HR)
    push(fin.at[at], fin_any.at[at], ga_s.at[0], ga_r.at[0], mate)
    fin_copy = pltpu.make_async_copy(fin.at[at], fin_any.at[at], loc_sem.at[6])
    fin_copy.start()
    landed(fsp.at[:, other_cols], qa_s.at[1], qa_r.at[1])
    small_ref[...] = fsp[...]
    landed(fqo.at[1 - c], qa_s.at[0], qa_r.at[0])
    fqo_ref[...] = fqo[...]
    ig_copy.wait()
    out_copy.wait()
    fin_copy.wait()
    landed(fin_any.at[rows((1 - c) * HR, HR)], ga_s.at[0], ga_r.at[0])

    for copy in started:
        copy.wait_send()
    for valid, copies in maybe_started:

        @pl.when(valid)
        def _(copies=copies):
            for copy in copies:
                copy.wait_send()

    for s, o in enumerate(offsets):
        valid = jnp.logical_and(spot_in_row + o >= 0, spot_in_row + o < z.per_row)

        @pl.when(valid)
        def _(s=s, o=o):
            halo_copy(s, o).wait_send()


def run(z, x, seg, chosen, vectors, q, k, v, o, r, up, down, cot):
    N, G, NP, NY, NE = z.narrow, z.group, z.plane, z.rows_y, z.expert
    T, W, D, R, HP = z.block, z.window, z.width, z.shard, z.head_part
    FL = z.ff_local
    FR = D + FL
    HR = FR // 2
    HS = HR // NP
    YW = D // NY
    SH = R + HP
    ER = N * SH
    QR = G * R
    GR = G * SH
    S = 2 * z.reach
    SMALL = z.small_rows
    vmem = pl.BlockSpec(memory_space=pltpu.VMEM)
    anywhere = pl.BlockSpec(memory_space=pltpu.HBM)
    scratch = [
        ((N * T, D // N), F32),
        ((T, D), F32),
        ((W, D), F32),
        ((W, D), BF16),
        ((QR, D), BF16),
        ((QR, D), BF16),
        ((2, HEAD, D), BF16),
        ((G, 16, 128), F32),
        ((8, 128), F32),
        ((HEAD, 128), F32),
        ((N, FR, D), BF16),
        ((T, D), BF16),
        ((8, z.row_len), F32),
        ((W, 8), F32),
        ((W, HEAD), BF16),
        ((W, HEAD), BF16),
        ((HEAD, W), BF16),
        ((HEAD, W), BF16),
        ((QR, T), F32),
        ((2, HEAD, T), BF16),
        ((2, W, T), BF16),
        ((2, HEAD, T), F32),
        ((QR, T), BF16),
        ((T, D), F32),
        ((T, D), F32),
        ((T, D), BF16),
        ((N, T, FL), BF16),
        ((N, T, FL), BF16),
        ((T, FL), BF16),
        ((T, D), F32),
        ((T, D), F32),
        ((T, D), BF16),
        ((2, HEAD, T), BF16),
        ((W, HEAD), F32),
        ((W, HEAD), F32),
        ((2, HEAD, T), BF16),
        ((QR, T), BF16),
        ((max(S, 1), 2, z.piece, HEAD), BF16),
        ((max(S, 1), 2, z.piece, HEAD), BF16),
        ((T, D), BF16),
        ((N, T, D // N), BF16),
        ((N, FR, D), BF16),
        ((N, HR, D), BF16),
        ((N, HR, D), BF16),
        ((N, NE, HR // NE, D // 2), BF16),
        ((N, NY, HR // NY, D // 2), BF16),
        ((N, HR // NE, D // 2), BF16),
        ((N, HR // NY, D // 2), BF16),
        ((N, NY, HS, D // 2), BF16),
        ((N, NE, HS, D // 2), BF16),
        ((N, HS, D), BF16),
        ((N, HS, D), BF16),
        ((FR, D), BF16),
        ((2, GR, D), BF16),
        ((GR, D), BF16),
        ((GR, D), BF16),
        ((NP, ER, YW), BF16),
        ((ER, YW), BF16),
        ((N, SH, YW), BF16),
        ((2, SH, D), BF16),
        ((SMALL, D), F32),
        ((SMALL, D // 2), F32),
        ((SMALL, D // 2), F32),
        ((NP, SMALL, D // 2), F32),
        ((SMALL, D // 2), F32),
        ((N, SMALL, D // 2), F32),
        ((SMALL, D), F32),
    ]
    pairs = [
        (N - 1,),
        (N - 1,),
        (G - 1,),
        (G - 1,),
        (G - 1,),
        (G - 1,),
        (G - 1,),
        (4, N - 1, max(NE, NY) - 1),
        (N - 1,),
        (N - 1,),
        (N - 1,),
        (max(S, 1),),
        (N,),
        (4, N, max(NE, NY) - 1),
        (N,),
        (2 * NP - 1,),
        (2,),
        (2, NP - 1),
        (2, N - 1),
        (NY + 1,),
    ]
    sems = [pltpu.SemaphoreType.DMA((7,))]
    for shape in pairs:
        sems += [pltpu.SemaphoreType.DMA(shape)] * 2
    sems += [pltpu.SemaphoreType.DMA((2, 2, N)), pltpu.SemaphoreType.DMA((2, N))]
    outs = [
        ((N * T, D // N), F32),
        ((T, D), F32),
        ((FR, D), BF16),
        ((2, SH, D), BF16),
        ((SMALL, D), F32),
    ]
    return pl.pallas_call(
        functools.partial(kernel, z),
        out_shape=[pltpu.VMEM(s, t) for s, t in outs],
        in_specs=[anywhere] + [vmem] * (7 + len(vectors)) + [anywhere] * 2 + [vmem],
        out_specs=[pl.BlockSpec(memory_space=pl.ANY)] * 3 + [vmem] * 2,
        scratch_shapes=[pltpu.VMEM(s, t) for s, t in scratch] + sems,
        compiler_params=pltpu.CompilerParams(
            collective_id=0, has_side_effects=True, vmem_limit_bytes=58 * 2**20
        ),
        name="layer",
    )(x, seg, chosen, *vectors, q, k, v, o, r, up, down, cot)


def finish_kernel(
    z,
    out_in,
    ig_in,
    fin_ref,
    fqo_ref,
    small_ref,
    out_any,
    ig_out,
    g1_ref,
    s1_ref,
    gq_ref,
    qb_ref,
    gk_ref,
    gv_ref,
    vb_ref,
    go_ref,
    ob_ref,
    rw_ref,
    rb_ref,
    g2_ref,
    s2_ref,
    gup_any,
    ub_ref,
    gdown_any,
    db_ref,
    gup,
    gdown,
    sems,
):
    e, n = lax.axis_index("expert"), lax.axis_index("narrow")
    N, T, D, R, HP, LE = z.narrow, z.block, z.width, z.shard, z.head_part, z.local_experts
    copies = []

    def put(src, dst):
        copies.append(pltpu.make_async_copy(src, dst, sems.at[len(copies)]))
        copies[-1].start()

    put(out_in, out_any)
    put(ig_in, ig_out)
    gup[...] = fin_ref[0:D, :].astype(F32)
    put(gup, gup_any)
    gdown[...] = fin_ref[D : D + z.ff_local, :].astype(F32)
    put(gdown, gdown_any)
    gq_ref[...] = fqo_ref[0, 0:R, :].astype(F32)
    go_ref[...] = fqo_ref[1, 0:R, :].astype(F32)
    gk_ref[...] = fqo_ref[0, R : R + HP, :].astype(F32)
    gv_ref[...] = fqo_ref[1, R : R + HP, :].astype(F32)
    g1_ref[...] = small_ref[0:1, :]
    s1_ref[...] = small_ref[1:2, :]
    ob_ref[...] = small_ref[2:3, :]
    g2_ref[...] = small_ref[3:4, :]
    s2_ref[...] = small_ref[4:5, :]
    db_ref[...] = small_ref[5:6, :]
    rb_ref[...] = small_ref[7:8, 0 : z.experts]
    rw_ref[...] = small_ref[16 : 16 + z.experts, :]
    upper = jnp.zeros((1, D), F32)
    for j in range(N):
        upper = jnp.where(n == j, small_ref[8 + j : 9 + j, :], upper)
    ub_ref[...] = upper
    here = e * N + n
    query = pltpu.roll(small_ref[0:8, :], lax.rem(D - here * R, D), 1)
    for i in range(LE):
        qb_ref[i : i + 1, :] = query[6:7, i * HP : (i + 1) * HP]
    value = pltpu.roll(small_ref[8:16, :], lax.rem(D - n * HP, D), 1)
    vb_ref[...] = value[7:8, 0:HP]
    for copy in copies:
        copy.wait()


def finish(z, out, ig, fin, fqo, small):
    N, T, D, R, HP = z.narrow, z.block, z.width, z.shard, z.head_part
    FL = z.ff_local
    vmem = pl.BlockSpec(memory_space=pltpu.VMEM)
    anywhere = pl.BlockSpec(memory_space=pltpu.HBM)
    shapes = [
        (N * T, D // N),
        (T, D),
        (1, D),
        (1, D),
        (R, D),
        (z.local_experts, HP),
        (HP, D),
        (HP, D),
        (1, HP),
        (R, D),
        (1, D),
        (z.experts, D),
        (1, z.experts),
        (1, D),
        (1, D),
        (D, FL),
        (1, FL),
        (FL, D),
        (1, D),
    ]
    return pl.pallas_call(
        functools.partial(finish_kernel, z),
        out_shape=[jax.ShapeDtypeStruct(s, F32) for s in shapes],
        in_specs=[pl.BlockSpec(memory_space=pl.ANY)] * 2 + [vmem] * 3,
        out_specs=[anywhere] * 2 + [vmem] * 13 + [anywhere, vmem, anywhere, vmem],
        scratch_shapes=[
            pltpu.VMEM((D, FL), F32),
            pltpu.VMEM((FL, D), F32),
            pltpu.SemaphoreType.DMA((4,)),
        ],
        compiler_params=pltpu.CompilerParams(vmem_limit_bytes=16 * 2**20),
        name="finish",
    )(out, ig, fin, fqo, small)


def per_device(
    inputs,
    seg_ids,
    chosen,
    gain_one,
    shift_one,
    query_w,
    query_b,
    key_w,
    value_w,
    value_b,
    out_w,
    out_b,
    router_w,
    router_b,
    gain_two,
    shift_two,
    up_w,
    up_b,
    down_w,
    down_b,
    cotangent,
):
    narrow = lax.axis_size("narrow")
    e, n = lax.axis_index("expert"), lax.axis_index("narrow")
    z = Sizes(
        lax.axis_size("dp"),
        lax.axis_size("expert"),
        narrow,
        inputs.shape[0],
        inputs.shape[1],
        seg_ids.shape[1],
        query_w.shape[0],
        up_w.shape[1],
    )
    D, R, HP = z.width, z.shard, z.head_part
    vectors = [gain_one, shift_one, out_b, gain_two, shift_two, down_b, up_b]
    vectors = [v.reshape(1, -1) for v in vectors]
    vectors += [query_b, value_b.reshape(1, -1), router_b.reshape(1, -1)]
    parts = run(
        z,
        inputs,
        seg_ids,
        jnp.transpose(chosen),
        vectors,
        jnp.transpose(query_w, (0, 2, 1)).reshape(R, D),
        jnp.transpose(key_w),
        jnp.transpose(value_w),
        out_w.reshape(R, D),
        jnp.transpose(router_w),
        up_w,
        down_w,
        cotangent,
    )
    out, ig, g1, s1, gq, qb, gk, gv, vb, go, ob, rw, rb, g2, s2, gup, ub, gdown, db = finish(
        z, *parts
    )
    return (
        out,
        ig,
        g1.reshape(-1),
        s1.reshape(-1),
        jnp.transpose(gq.reshape(z.local_experts, HP, D), (0, 2, 1)),
        qb,
        jnp.transpose(gk),
        jnp.transpose(gv),
        vb.reshape(-1),
        go.reshape(z.local_experts, HP, D),
        ob.reshape(-1),
        jnp.transpose(rw),
        rb.reshape(-1),
        g2.reshape(-1),
        s2.reshape(-1),
        gup,
        ub.reshape(-1),
        gdown,
        db.reshape(-1),
    )


def solution(mesh):
    return jax.shard_map(
        per_device,
        mesh=mesh,
        in_specs=(
            P("dp", None),
            P("dp", None),
            P("dp", None),
            P(),
            P(),
            P("expert", None, "narrow"),
            P("expert", "narrow"),
            P(None, "narrow"),
            P(None, "narrow"),
            P("narrow"),
            P("expert", "narrow", None),
            P(),
            P(),
            P(),
            P(),
            P(),
            P(None, "narrow"),
            P("narrow"),
            P("narrow", None),
            P(),
            P(("dp", "expert"), "narrow"),
        ),
        out_specs=(
            P(("dp", "expert"), "narrow"),
            P(("dp", "expert", "narrow"), None),
            P(),
            P(),
            P("expert", None, "narrow"),
            P("expert", "narrow"),
            P(None, "narrow"),
            P(None, "narrow"),
            P("narrow"),
            P("expert", "narrow", None),
            P(),
            P(),
            P(),
            P(),
            P(),
            P(None, "narrow"),
            P("narrow"),
            P("narrow", None),
            P(),
        ),
        check_vma=False,
    )
```

```python
import functools
import math

import jax
import jax.numpy as jnp
from jax import lax
from jax.experimental import pallas as pl
from jax.experimental.pallas import tpu as pltpu
from jax.sharding import PartitionSpec as P

HEAD = 64
LONGEST = 256
EPSILON = 1e-05
MASKED = -1000000000.0
GELU_A = math.sqrt(2.0 / math.pi)
GELU_B = 0.044715
F32 = jnp.float32
BF16 = jnp.bfloat16
MESH = pl.DeviceIdType.MESH


def dot(a, b):
    return lax.dot_general(a, b, (((1,), (0,)), ((), ())), preferred_element_type=F32)


def dot_nt(a, b):
    return lax.dot_general(a, b, (((1,), (1,)), ((), ())), preferred_element_type=F32)


def dot_tn(a, b):
    return lax.dot_general(a, b, (((0,), (0,)), ((), ())), preferred_element_type=F32)


def norm_stats(x):
    centred = x - jnp.mean(x, axis=1, keepdims=True)
    inverse = lax.rsqrt(jnp.mean(centred * centred, axis=1, keepdims=True) + EPSILON)
    return centred * inverse, inverse


def rem(a, b):
    return lax.rem(a, b)


class Sizes:
    def __init__(self, dp, expert, narrow, tokens, width, row_len, local_experts, ff_local):
        self.dp, self.expert, self.narrow = dp, expert, narrow
        self.tokens, self.width, self.row_len = tokens, width, row_len
        self.local_experts = local_experts
        self.experts = local_experts * expert
        self.group = expert * narrow
        self.block = tokens // self.group
        self.rows_y = dp // 2
        self.plane = self.rows_y * expert
        self.ff_local = ff_local
        self.head_part = HEAD // narrow
        self.shard = local_experts * self.head_part
        self.per_row = row_len // self.block
        spans = [
            min(row_len, (j + 1) * self.block + LONGEST) - max(0, j * self.block - LONGEST)
            for j in range(self.per_row)
        ]
        self.window = max(spans)
        self.reach = max(1, LONGEST // self.block) if self.per_row > 1 else 0
        self.piece = min(self.block, LONGEST)
        self.tile = min(256, self.block)
        self.up_rows = narrow * ff_local // width
        self.small_rows = 24


def kernel(
    z,
    x_any,
    seg_ref,
    chosen_ref,
    g1_ref,
    s1_ref,
    ob_ref,
    g2_ref,
    s2_ref,
    db_ref,
    ub_ref,
    qb_ref,
    vb_ref,
    rb_ref,
    q_ref,
    k_ref,
    v_ref,
    o_ref,
    r_ref,
    up_any,
    down_any,
    cot_ref,
    out_any,
    ig_any,
    fin_any,
    fqo_ref,
    small_ref,
    out_ref,
    ig_ref,
    xw,
    rw,
    wq,
    wo,
    wkv,
    bias,
    corner,
    vcol,
    ffw,
    cot,
    segs,
    segc,
    kn,
    vn,
    kt,
    vt,
    qt,
    qk,
    prob,
    mix,
    mixg,
    hid,
    acc,
    second,
    active,
    slope,
    ugrad,
    sgrad,
    hgrad,
    hgb,
    mgk,
    dk,
    dv,
    dq,
    dqt,
    halo_out,
    halo_in,
    delta,
    outd,
    gsend,
    crecv,
    psend,
    pea,
    pya,
    mea,
    mya,
    pyb,
    peb,
    zsend,
    zrecv,
    fin,
    gqo,
    cqo,
    pqo,
    rqo,
    zqo,
    yqo,
    fqo,
    sp,
    csp,
    psp,
    rsp,
    zsp,
    ysp,
    fsp,
    loc_sem,
    w_s,
    w_r,
    wm_s,
    wm_r,
    b_s,
    b_r,
    q_s,
    q_r,
    qm_s,
    qm_r,
    o_s,
    o_r,
    om_s,
    om_r,
    fp_s,
    fp_r,
    fm_s,
    fm_r,
    ct_s,
    ct_r,
    od_s,
    od_r,
    hl_s,
    hl_r,
    gc_s,
    gc_r,
    gp_s,
    gp_r,
    gz_s,
    gz_r,
    ga_s,
    ga_r,
    qc_s,
    qc_r,
    qp_s,
    qp_r,
    qz_s,
    qz_r,
    qa_s,
    qa_r,
    fz_s,
    fz_r,
):
    d, e, n = lax.axis_index("dp"), lax.axis_index("expert"), lax.axis_index("narrow")
    c, y = rem(d, 2), lax.div(d, 2)
    N, G, NP, NE, NY = z.narrow, z.group, z.plane, z.expert, z.rows_y
    T, W, D, R, HP, LE = z.block, z.window, z.width, z.shard, z.head_part, z.local_experts
    FL = z.ff_local
    half = D // 2
    here = e * N + n
    spot = y * NE + e
    mate = (d + 1 - 2 * c, e, n)

    def in_group(j):
        at = rem(here + j + G, G)
        return at, (d, lax.div(at, N), rem(at, N))

    def in_plane(j):
        at = rem(spot + j + NP, NP)
        return at, (2 * lax.div(at, NE) + c, rem(at, NE), n)

    def in_line(j):
        at = rem(n + j + N, N)
        return at, (d, e, at)

    def in_rows(j):
        at = rem(y + j + NY, NY)
        return at, (2 * at + c, e, n)

    started = []

    def push(src, dst, send, recv, device):
        copy = pltpu.make_async_remote_copy(
            src_ref=src,
            dst_ref=dst,
            send_sem=send,
            recv_sem=recv,
            device_id=device,
            device_id_type=MESH,
        )
        copy.start()
        started.append(copy)

    def landed(dst, send, recv):
        pltpu.make_async_remote_copy(
            src_ref=dst,
            dst_ref=dst,
            send_sem=send,
            recv_sem=recv,
            device_id=mate,
            device_id_type=MESH,
        ).wait_recv()

    def rows(start, size, step=16):
        return pl.ds(pl.multiple_of(start, step), size)

    start = here * T
    row = lax.div(start, z.row_len)
    spot_in_row = rem(here, z.per_row)
    base = row * z.row_len
    ws = jnp.minimum(jnp.maximum(spot_in_row * T - LONGEST, 0), z.row_len - W)
    off = spot_in_row * T - ws
    own = rows(off, T, 128)

    x_copy = pltpu.make_async_copy(x_any.at[rows(base + ws, W, 128)], xw, loc_sem.at[0])
    x_copy.start()
    up_copy = pltpu.make_async_copy(up_any, ffw.at[n, pl.ds(0, D)], loc_sem.at[1])
    up_copy.start()
    down_copy = pltpu.make_async_copy(down_any, ffw.at[n, pl.ds(D, FL)], loc_sem.at[2])
    down_copy.start()
    cols_copy = pltpu.make_async_copy(
        x_any.at[rows(e * N * T, N * T, 128), rows(n * (D // N), D // N, 128)], out_ref, loc_sem.at[3]
    )
    cols_copy.start()
    wq[rows(here * R, R)] = q_ref[...]
    wo[rows(here * R, R)] = o_ref[...]
    wkv[0, rows(n * HP, HP)] = k_ref[...]
    wkv[1, rows(n * HP, HP)] = v_ref[...]
    bias[here] = jnp.zeros((16, 128), F32)
    for i in range(FL // 128):
        bias[here, i : i + 1, :] = ub_ref[0:1, i * 128 : (i + 1) * 128]
    bias[here, 8 : 8 + LE, 0:HP] = qb_ref[...]
    bias[here, 7:8, 0:HP] = vb_ref[...]

    barrier = pltpu.get_barrier_semaphore()
    pl.semaphore_signal(barrier, inc=1, device_id=mate, device_id_type=MESH)
    for j in range(1, NP):
        pl.semaphore_signal(barrier, inc=1, device_id=in_plane(j)[1], device_id_type=MESH)
    for j in range(1, G):
        pl.semaphore_signal(barrier, inc=1, device_id=in_group(j)[1], device_id_type=MESH)
    for j in range(1, NY):
        to = (2 * in_rows(j)[0] + 1 - c, e, n)
        pl.semaphore_signal(barrier, inc=1, device_id=to, device_id_type=MESH)
    pl.semaphore_wait(barrier, NP + G + NY - 2)

    mine_cols = rows(c * half, half, 128)
    other_cols = rows((1 - c) * half, half, 128)

    def in_expert(i):
        at = rem(e + i + NE, NE)
        return at, (d, at, n)

    def shard_at(i, j):
        return rem(e - i + NE, NE) * N + rem(n - j + N, N)

    def spread_start(part, send, recv):
        for j in range(1, N):
            at = part(here)
            push(at, at, send.at[j - 1], recv.at[j - 1], in_line(j)[1])
        for i in range(1, NE):
            at = part(here)
            push(at, at, send.at[i * N - 1], recv.at[i * N - 1], in_expert(i)[1])

    def spread_on(part, send, recv, to_mate):
        for j in range(1, N):
            at = part(shard_at(0, j))
            landed(at, send.at[j - 1], recv.at[j - 1])
            for i in range(1, NE):
                push(at, at, send.at[i * N + j - 1], recv.at[i * N + j - 1], in_expert(i)[1])
            if to_mate is not None:
                push(at, at, to_mate[0].at[j - 1], to_mate[1].at[j - 1], mate)

    def spread_end(part, send, recv, to_mate):
        for i in range(1, NE):
            for j in range(N):
                at = part(shard_at(i, j))
                landed(at, send.at[i * N + j - 1], recv.at[i * N + j - 1])
                if to_mate is not None:
                    push(at, at, to_mate[0].at[i * N + j - 1], to_mate[1].at[i * N + j - 1], mate)

    def spread_wait(part, to_mate):
        for i in range(NE):
            for j in range(N):
                if i or j:
                    landed(part(shard_at(i, j)), to_mate[0].at[i * N + j - 1], to_mate[1].at[i * N + j - 1])

    def bias_part(g):
        return bias.at[g]

    def q_part(g):
        return wq.at[rows(g * R, R), mine_cols]

    def q_other(g):
        return wq.at[rows(g * R, R), other_cols]

    def o_part(g):
        return wo.at[rows(g * R, R), mine_cols]

    def o_other(g):
        return wo.at[rows(g * R, R), other_cols]

    for j in range(1, N):
        at = wkv.at[c, rows(n * HP, HP)]
        push(at, at, w_s.at[j - 1], w_r.at[j - 1], in_line(j)[1])
    spread_start(q_part, q_s, q_r)
    spread_start(bias_part, b_s, b_r)
    up_copy.wait()
    down_copy.wait()
    FR = D + FL

    left, right = pl.ds(0, half), pl.ds(half, half)
    HR = FR // 2
    HS = HR // NP
    HA, HB = HR // NE, HR // NY
    def left_slice(of, ys, es):
        return ffw.at[of, rows(c * HR + (es * NY + ys) * HS, HS), left]

    def right_slice(of, ys, es):
        return ffw.at[of, rows(c * HR + (ys * NE + es) * HS, HS), right]

    def left_half(of, es):
        return ffw.at[of, rows(c * HR + es * HA, HA), left]

    def right_half(of, ys):
        return ffw.at[of, rows(c * HR + ys * HB, HB), right]

    def by_distance(at):
        return sorted((o for o in range(N) if o != at), key=lambda o: (abs(o - at), o if 2 * at >= N else -o))

    def pick(choices):
        value = choices[0]
        for at in range(1, N):
            value = jnp.where(n == at, choices[at], value)
        return value

    shard_of = [n] + [pick([by_distance(at)[k] for at in range(N)]) for k in range(N - 1)]
    maybe_started = []

    def line_push(of, step, valid):
        of = jnp.clip(of, 0, N - 1)
        to = (d, e, jnp.clip(n + step, 0, N - 1))
        way = (step + 1) // 2
        copies = [
            pltpu.make_async_remote_copy(
                src_ref=at,
                dst_ref=at,
                send_sem=fz_s.at[part, way, of],
                recv_sem=fz_r.at[part, of],
                device_id=to,
                device_id_type=MESH,
            )
            for part, at in enumerate((left_slice(of, y, e), right_slice(of, y, e)))
        ]

        @pl.when(valid)
        def _():
            for copy in copies:
                copy.start()

        maybe_started.append((valid, copies))

    def line_landed(of, valid):
        of = jnp.clip(of, 0, N - 1)

        @pl.when(valid)
        def _():
            landed(left_slice(of, y, e), fz_s.at[0, 0, of], fz_r.at[0, of])
            landed(right_slice(of, y, e), fz_s.at[1, 0, of], fz_r.at[1, of])

    def shards_start():
        line_push(n, 1, n + 1 < N)
        line_push(n, -1, n > 0)

    def shards_on(hop):
        line_landed(n - hop, n >= hop)
        line_push(n - hop, 1, jnp.logical_and(n >= hop, n + 1 < N))
        line_landed(n + hop, n + hop < N)
        line_push(n + hop, -1, jnp.logical_and(n + hop < N, n > 0))

    def plane_on(j):
        there = shard_of[j]
        at = left_slice(there, y, e)
        for i in range(1, NY):
            push(at, at, fp_s.at[0, j - 1, i - 1], fp_r.at[0, j - 1, i - 1], in_rows(i)[1])
        at = right_slice(there, y, e)
        for i in range(1, NE):
            push(at, at, fp_s.at[1, j - 1, i - 1], fp_r.at[1, j - 1, i - 1], in_expert(i)[1])

    def plane_turn(j):
        there = shard_of[j]
        for i in range(1, NY):
            near, _ = in_rows(-i)
            landed(left_slice(there, near, e), fp_s.at[0, j - 1, i - 1], fp_r.at[0, j - 1, i - 1])
        at = left_half(there, e)
        for i in range(1, NE):
            push(at, at, fp_s.at[2, j - 1, i - 1], fp_r.at[2, j - 1, i - 1], in_expert(i)[1])
        for i in range(1, NE):
            near, _ = in_expert(-i)
            landed(right_slice(there, y, near), fp_s.at[1, j - 1, i - 1], fp_r.at[1, j - 1, i - 1])
        at = right_half(there, y)
        for i in range(1, NY):
            push(at, at, fp_s.at[3, j - 1, i - 1], fp_r.at[3, j - 1, i - 1], in_rows(i)[1])

    def mate_on(j):
        there = shard_of[j]
        for i in range(1, NE):
            near, _ = in_expert(-i)
            landed(left_half(there, near), fp_s.at[2, j - 1, i - 1], fp_r.at[2, j - 1, i - 1])
        for i in range(1, NY):
            near, _ = in_rows(-i)
            landed(right_half(there, near), fp_s.at[3, j - 1, i - 1], fp_r.at[3, j - 1, i - 1])
        at = ffw.at[there, rows(c * HR, HR)]
        push(at, at, fm_s.at[j - 1], fm_r.at[j - 1], mate)

    x_copy.wait()
    gain_one, shift_one = g1_ref[...], s1_ref[...]

    def norm_one(i, carry):
        at = rows(i * 128, 128, 128)
        unit, _ = norm_stats(xw[at, :])
        rw[at, :] = (unit * gain_one + shift_one).astype(BF16)
        return carry

    lax.fori_loop(0, W // 128, norm_one, 0)

    seg_all = seg_ref[...].astype(F32)
    row_id = lax.broadcasted_iota(jnp.int32, seg_all.shape, 0)
    seg_here = jnp.sum(jnp.where(row_id == row, seg_all, 0.0), axis=0, keepdims=True)
    segs[...] = jnp.broadcast_to(seg_here, segs.shape)
    segc[...] = jnp.transpose(segs[:, rows(ws, W, 128)])
    seg_own = segs[0:1, rows(spot_in_row * T, T, 128)]
    corner[...] = jnp.zeros_like(corner)
    corner[:, 0 : z.experts] = jnp.broadcast_to(rb_ref[...], (8, z.experts))
    router_col = jnp.transpose(corner[...])[0 : z.experts, 0:1]
    logits = dot_nt(r_ref[...], rw[own, :]) + router_col
    expert_id = lax.broadcasted_iota(jnp.int32, (z.experts, T), 0)
    hot, picked = [], []
    for k in range(2):
        chosen = chosen_ref[k : k + 1, rows(start, T, 128)]
        hot.append((expert_id == chosen).astype(F32))
        picked.append(jnp.sum(logits * hot[k], axis=0, keepdims=True))
    top = jnp.maximum(picked[0], picked[1])
    raised = [jnp.exp(p - top) for p in picked]
    total = raised[0] + raised[1]
    gate = [r / total for r in raised]

    for j in range(1, N):
        there, _ = in_line(-j)
        at = wkv.at[c, rows(there * HP, HP)]
        landed(at, w_s.at[j - 1], w_r.at[j - 1])
        push(at, at, wm_s.at[j - 1], wm_r.at[j - 1], mate)
    spread_on(q_part, q_s, q_r, (qm_s, qm_r))
    spread_on(bias_part, b_s, b_r, None)
    shards_start()
    spread_start(o_part, o_s, o_r)

    for j in range(1, N):
        there, _ = in_line(-j)
        landed(wkv.at[1 - c, rows(there * HP, HP)], wm_s.at[j - 1], wm_r.at[j - 1])
    kn[...] = dot_nt(rw[...], wkv[0]).astype(BF16)
    kt[...] = dot_nt(wkv[0], rw[...]).astype(BF16)
    spread_end(q_part, q_s, q_r, (qm_s, qm_r))
    spread_end(bias_part, b_s, b_r, None)
    columns = [jnp.transpose(bias[g, 0:16, :]) for g in range(G)]
    for part in range(N):
        vcol[part * HP : (part + 1) * HP, :] = jnp.broadcast_to(columns[part][0:HP, 7:8], (HP, 128))
    value_row = jnp.transpose(vcol[...])[0:1, :]
    vn[...] = (dot_nt(rw[...], wkv[1]) + value_row).astype(BF16)
    vt[...] = (dot_nt(wkv[1], rw[...]) + vcol[:, 0:1]).astype(BF16)

    spread_wait(q_other, (qm_s, qm_r))
    qt[...] = dot_nt(wq[...], rw[own, :])

    def expert_rows(at, i, part):
        return ((at * N + part) * LE + i) * HP

    for part in range(N):
        chosen_rows = [jnp.zeros((HP, T), F32), jnp.zeros((HP, T), F32)]
        for at in range(NE):
            g = at * N + part
            for i in range(LE):
                lo = expert_rows(at, i, part)
                one = qt[lo : lo + HP, :] + columns[g][0:HP, 8 + i : 9 + i]
                for k in range(2):
                    chosen_rows[k] = chosen_rows[k] + one * hot[k][at * LE + i : at * LE + i + 1, :]
        for k in range(2):
            qk[k, part * HP : (part + 1) * HP, :] = chosen_rows[k].astype(BF16)

    scale = 1.0 / math.sqrt(HEAD)
    TL = z.tile
    tiles = T // TL
    seg_tiles = [seg_own[:, i * TL : (i + 1) * TL] for i in range(tiles)]

    def attend(k):
        for i in range(tiles):
            at = pl.ds(i * TL, TL)
            scores = dot(kn[...], qk[k, :, at]) * scale
            scores = jnp.where(segc[:, 0:1] == seg_tiles[i], scores, MASKED)
            high = jnp.max(scores, axis=0, keepdims=True)
            raised_scores = jnp.exp(scores - high)
            low = (raised_scores * (1.0 / jnp.sum(raised_scores, axis=0, keepdims=True))).astype(BF16)
            prob[k, :, at] = low
            mix[k, :, at] = dot(vt[...], low)

    attend(0)
    attend(1)
    shards_on(1)
    plane_on(1)
    spread_on(o_part, o_s, o_r, (om_s, om_r))
    plane_turn(1)
    shards_on(2)
    plane_on(2)
    CW = D // N
    cot[:, rows(n * CW, CW, 128)] = cot_ref[rows(n * T, T, 128), :]
    for j in range(1, N):
        there, to = in_line(j)
        push(
            cot_ref.at[rows(there * T, T, 128)],
            cot.at[:, rows(n * CW, CW, 128)],
            ct_s.at[j - 1],
            ct_r.at[j - 1],
            to,
        )
    spread_end(o_part, o_s, o_r, (om_s, om_r))

    for part in range(N):
        for at in range(NE):
            for i in range(LE):
                lo = expert_rows(at, i, part)
                x = at * LE + i
                gated = jnp.zeros((HP, T), F32)
                for k in range(2):
                    rounded_mix = mix[k, part * HP : (part + 1) * HP, :].astype(BF16).astype(F32)
                    gated = gated + rounded_mix * (hot[k][x : x + 1, :] * gate[k])
                mixg[lo : lo + HP, :] = gated.astype(BF16)
    spread_wait(o_other, (om_s, om_r))
    out_b, down_b = ob_ref[...], db_ref[...]
    gain_two, shift_two = g2_ref[...], s2_ref[...]
    attention = dot_tn(mixg[...], wo[...]) + out_b
    acc[...] = attention + down_b
    hid[...] = xw[own, :] + attention

    def norm_two(i, carry):
        at = rows(i * 128, 128, 128)
        unit, _ = norm_stats(hid[at, :])
        second[at, :] = (unit * gain_two + shift_two).astype(BF16)
        return carry

    lax.fori_loop(0, T // 128, norm_two, 0)
    sgrad[...] = jnp.zeros_like(sgrad)

    def core_start(j):
        push(
            gsend.at[j, rows((1 - c) * HR, HR)], crecv.at[j], gc_s.at[j], gc_r.at[j], mate
        )

    def plane_start(j):
        landed(crecv.at[j], gc_s.at[j], gc_r.at[j])
        psend[j] = (
            gsend[j, rows(c * HR, HR), :].astype(F32) + crecv[j].astype(F32)
        ).astype(BF16)
        for i in range(1, NE):
            there, to = in_expert(i)
            src = psend.at[j, rows(there * HA, HA), left]
            push(src, pea.at[j, i], gp_s.at[0, j, i - 1], gp_r.at[0, j, i - 1], to)
        for i in range(1, NY):
            there, to = in_rows(i)
            src = psend.at[j, rows(there * HB, HB), right]
            push(src, pya.at[j, i], gp_s.at[1, j, i - 1], gp_r.at[1, j, i - 1], to)

    def plane_middle(j):
        whole = psend[j, rows(e * HA, HA), left].astype(F32)
        for i in range(1, NE):
            landed(pea.at[j, i], gp_s.at[0, j, i - 1], gp_r.at[0, j, i - 1])
            whole = whole + pea[j, i].astype(F32)
        mea[j] = whole.astype(BF16)
        for i in range(1, NY):
            there, to = in_rows(i)
            src = mea.at[j, rows(there * HS, HS)]
            push(src, pyb.at[j, i], gp_s.at[2, j, i - 1], gp_r.at[2, j, i - 1], to)
        whole = psend[j, rows(y * HB, HB), right].astype(F32)
        for i in range(1, NY):
            landed(pya.at[j, i], gp_s.at[1, j, i - 1], gp_r.at[1, j, i - 1])
            whole = whole + pya[j, i].astype(F32)
        mya[j] = whole.astype(BF16)
        for i in range(1, NE):
            there, to = in_expert(i)
            src = mya.at[j, rows(there * HS, HS)]
            push(src, peb.at[j, i], gp_s.at[3, j, i - 1], gp_r.at[3, j, i - 1], to)

    def line_start(j):
        whole = mea[j, rows(y * HS, HS), :].astype(F32)
        for i in range(1, NY):
            landed(pyb.at[j, i], gp_s.at[2, j, i - 1], gp_r.at[2, j, i - 1])
            whole = whole + pyb[j, i].astype(F32)
        zsend[j, :, left] = whole.astype(BF16)
        whole = mya[j, rows(e * HS, HS), :].astype(F32)
        for i in range(1, NE):
            landed(peb.at[j, i], gp_s.at[3, j, i - 1], gp_r.at[3, j, i - 1])
            whole = whole + peb[j, i].astype(F32)
        zsend[j, :, right] = whole.astype(BF16)
        if j:
            push(zsend.at[j], zrecv.at[n], gz_s.at[j], gz_r.at[n], (d, e, shard_of[j]))

    def forward(j):
        there = shard_of[j]
        if j:
            landed(ffw.at[there, rows((1 - c) * HR, HR)], fm_s.at[j - 1], fm_r.at[j - 1])
        up_b = jnp.concatenate(
            [bias[e * N + there, i : i + 1, :] for i in range(FL // 128)], axis=1
        )

        def feed(i, carry):
            at = rows(i * TL, TL, 128)
            upper = dot(second[at, :], ffw[there, 0:D, :]) + up_b
            square = upper * upper
            t = jnp.tanh(upper * (GELU_A + (GELU_A * GELU_B) * square))
            one = 0.5 + 0.5 * t
            low = (upper * one).astype(BF16)
            active[j, at, :] = low
            slope[j, at, :] = (
                one + (0.5 * upper) * (1.0 - t * t) * (GELU_A + (3.0 * GELU_A * GELU_B) * square)
            ).astype(BF16)
            acc[at, :] = acc[at, :] + dot(low, ffw[there, D : D + FL, :])
            return carry

        lax.fori_loop(0, T // TL, feed, 0)

    def backward(j):
        there = shard_of[j]

        def feed_back(i, carry):
            at = rows(i * TL, TL, 128)
            back = dot_nt(cot[at, :], ffw[there, D : D + FL, :]) * slope[j, at, :].astype(F32)
            back = back.astype(BF16)
            ugrad[at, :] = back
            sgrad[at, :] = sgrad[at, :] + dot_nt(back, ffw[there, 0:D, :])
            return carry

        lax.fori_loop(0, T // TL, feed_back, 0)
        sp[pl.ds(8 + there, 1), :] = jnp.sum(ugrad[...].astype(F32), axis=0, keepdims=True)
        gsend[j, 0:D, :] = dot_tn(second[...], ugrad[...]).astype(BF16)
        gsend[j, D : D + FL, :] = dot_tn(active[j], cot[...]).astype(BF16)
        core_start(j)

    def cotangent_wait():
        for j in range(1, N):
            there, _ = in_line(-j)
            landed(cot.at[:, rows(there * CW, CW, 128)], ct_s.at[j - 1], ct_r.at[j - 1])

    forward(0)
    plane_turn(2)
    mate_on(1)
    shards_on(3)
    plane_on(3)
    forward(1)
    mate_on(2)
    plane_turn(3)
    forward(2)
    cotangent_wait()
    backward(1)
    backward(2)
    plane_start(1)
    mate_on(3)
    forward(3)
    delta[...] = acc[...].astype(BF16)
    outd[n] = delta[:, rows(n * CW, CW, 128)]
    for j in range(1, N):
        there, to = in_line(j)
        push(delta.at[:, rows(there * CW, CW, 128)], outd.at[n], od_s.at[j - 1], od_r.at[j - 1], to)

    backward(3)
    plane_start(2)
    backward(0)
    plane_start(3)
    plane_middle(1)

    zero_row = jnp.zeros((1, D), F32)

    def norm_two_back(i, carry):
        at = rows(i * 128, 128, 128)
        unit, inverse = norm_stats(hid[at, :])
        grad = sgrad[at, :]
        scaled = grad * gain_two
        back = inverse * (
            scaled
            - jnp.mean(scaled, axis=1, keepdims=True)
            - unit * jnp.mean(scaled * unit, axis=1, keepdims=True)
        )
        top_grad = cot[at, :].astype(F32)
        whole = top_grad + back
        hgrad[at, :] = whole
        hgb[at, :] = whole.astype(BF16)
        parts = (grad * unit, grad, whole, top_grad)
        return tuple(a + jnp.sum(b, axis=0, keepdims=True) for a, b in zip(carry, parts))

    sums = lax.fori_loop(0, T // 128, norm_two_back, (zero_row,) * 4)
    sp[3:4, :] = sums[0]
    sp[4:5, :] = sums[1]
    sp[2:3, :] = sums[2]
    sp[5:6, :] = sums[3]

    plane_start(0)

    SH = R + HP
    out_grad = dot(mixg[...], hgb[...]).astype(BF16)
    for g in range(G):
        gqo[1, g * SH : g * SH + R, :] = out_grad[g * R : (g + 1) * R, :]
    qt[...] = dot_nt(wo[...], hgb[...])
    gate_grad = [jnp.zeros((1, T), F32), jnp.zeros((1, T), F32)]
    for part in range(N):
        picked_rows = [jnp.zeros((HP, T), F32), jnp.zeros((HP, T), F32)]
        for at in range(NE):
            for i in range(LE):
                lo = expert_rows(at, i, part)
                one = qt[lo : lo + HP, :]
                x = at * LE + i
                for k in range(2):
                    picked_rows[k] = picked_rows[k] + one * hot[k][x : x + 1, :]
        for k in range(2):
            span = slice(part * HP, (part + 1) * HP)
            rounded_mix = mix[k, span, :].astype(BF16).astype(F32)
            gate_grad[k] = gate_grad[k] + jnp.sum(picked_rows[k] * rounded_mix, axis=0, keepdims=True)
            mgk[k, span, :] = (picked_rows[k] * gate[k]).astype(BF16)
    middle = gate[0] * gate_grad[0] + gate[1] * gate_grad[1]
    logit_grad = sum(hot[k] * (gate[k] * (gate_grad[k] - middle)) for k in range(2))
    logit_low = logit_grad.astype(BF16)

    def attend_back(k):
        for i in range(tiles):
            at = pl.ds(i * TL, TL)
            low = prob[k, :, at]
            p = low.astype(F32)
            prob_grad = dot(vn[...], mgk[k, :, at])
            inner = jnp.sum(p * prob_grad, axis=0, keepdims=True)
            score = (p * (prob_grad - inner)).astype(BF16)
            dq[k, :, at] = (dot(kt[...], score) * scale).astype(BF16)
            key_part = dot_nt(score, qk[k, :, at])
            value_part = dot_nt(low, mgk[k, :, at])
            if k == 0 and i == 0:
                dk[...] = key_part
                dv[...] = value_part
            else:
                dk[...] = dk[...] + key_part
                dv[...] = dv[...] + value_part

    attend_back(0)
    attend_back(1)
    plane_middle(2)

    H, PC = z.reach, z.piece
    offsets = [o for o in range(-H, H + 1) if o]
    inside = T >= LONGEST

    def halo_source(o):
        if inside:
            return (spot_in_row + 1) * T - ws if o > 0 else spot_in_row * T - LONGEST - ws
        return (spot_in_row + o) * T - ws

    def halo_copy(s, o):
        to = rem(here + o + G, G)
        return pltpu.make_async_remote_copy(
            src_ref=halo_out.at[s],
            dst_ref=halo_in.at[s],
            send_sem=hl_s.at[s],
            recv_sem=hl_r.at[s],
            device_id=(d, lax.div(to, N), rem(to, N)),
            device_id_type=MESH,
        )

    for s, o in enumerate(offsets):
        valid = jnp.logical_and(spot_in_row + o >= 0, spot_in_row + o < z.per_row)

        @pl.when(valid)
        def _(s=s, o=o):
            at = rows(halo_source(o), PC, 128)
            halo_out[s, 0] = (dk[at, :] * scale).astype(BF16)
            halo_out[s, 1] = dv[at, :].astype(BF16)
            halo_copy(s, o).start()

    for part in range(N):
        for at in range(NE):
            for i in range(LE):
                lo = expert_rows(at, i, part)
                x = at * LE + i
                span = slice(part * HP, (part + 1) * HP)
                one = dq[0, span, :].astype(F32) * hot[0][x : x + 1, :]
                one = one + dq[1, span, :].astype(F32) * hot[1][x : x + 1, :]
                dqt[lo : lo + HP, :] = one.astype(BF16)
    query_w_grad = dot(dqt[...], rw[own, :]).astype(BF16)
    key_w_grad = dot_tn((dk[...] * scale).astype(BF16), rw[...]).astype(BF16)
    value_w_grad = dot_tn(dv[...].astype(BF16), rw[...]).astype(BF16)
    for g in range(G):
        shared = slice((g % N) * HP, (g % N + 1) * HP)
        gqo[0, g * SH : g * SH + R, :] = query_w_grad[g * R : (g + 1) * R, :]
        gqo[0, g * SH + R : (g + 1) * SH, :] = key_w_grad[shared, :]
        gqo[1, g * SH + R : (g + 1) * SH, :] = value_w_grad[shared, :]
    push(gqo.at[1 - c], cqo, qc_s.at[0], qc_r.at[0], mate)
    plane_middle(3)
    line_start(1)
    ones = jnp.ones((8, T), BF16)
    sp[6:7, :] = dot_nt(ones, dqt[...])[0:1, :]
    sp[7:8, :] = jnp.zeros((1, D), F32)
    sp[7:8, 0 : z.experts] = jnp.transpose(
        jnp.broadcast_to(jnp.sum(logit_grad, axis=1, keepdims=True), (z.experts, 128))
    )[0:1, :]
    acc[...] = dot_tn(dqt[...], wq[...]) + dot_tn(logit_low, r_ref[...])
    sp[16:24, :] = dot(logit_low, rw[own, :])
    sp[15:16, :] = jnp.zeros((1, D), F32)
    sp[15:16, 0:HEAD] = jnp.sum(dv[...], axis=0, keepdims=True)
    YW = D // NY
    ER = N * SH
    landed(cqo, qc_s.at[0], qc_r.at[0])
    pqo[...] = (gqo[c].astype(F32) + cqo[...].astype(F32)).astype(BF16)
    for i in range(1, NP):
        there, to = in_plane(i)
        src = pqo.at[rows(rem(there, NE) * ER, ER), rows(lax.div(there, NE) * YW, YW, 128)]
        push(src, rqo.at[i], qp_s.at[0, i - 1], qp_r.at[0, i - 1], to)
    plane_middle(0)
    line_start(2)
    line_start(3)

    dk[...] = dk[...] * scale
    for s, o in enumerate(offsets):
        back_valid = jnp.logical_and(spot_in_row - o >= 0, spot_in_row - o < z.per_row)

        @pl.when(back_valid)
        def _(s=s, o=o):
            halo_copy(s, o).wait_recv()
            at = off if (not inside or o > 0) else off + T - LONGEST
            at = rows(at, PC, 128)
            dk[at, :] = dk[at, :] + halo_in[s, 0].astype(F32)
            dv[at, :] = dv[at, :] + halo_in[s, 1].astype(F32)

    key_grad = dk[own, :]
    value_grad = dv[own, :]
    key_low, value_low = key_grad.astype(BF16), value_grad.astype(BF16)
    acc[...] = acc[...] + dot(key_low, wkv[0]) + dot(value_low, wkv[1])

    def norm_one_back(i, carry):
        at = rows(i * 128, 128, 128)
        unit, inverse = norm_stats(xw[rows(off + i * 128, 128, 128), :])
        grad = acc[at, :]
        scaled = grad * gain_one
        back = inverse * (
            scaled
            - jnp.mean(scaled, axis=1, keepdims=True)
            - unit * jnp.mean(scaled * unit, axis=1, keepdims=True)
        )
        ig_ref[at, :] = hgrad[at, :] + back
        parts = (grad * unit, grad)
        return tuple(a + jnp.sum(b, axis=0, keepdims=True) for a, b in zip(carry, parts))

    sums = lax.fori_loop(0, T // 128, norm_one_back, (zero_row,) * 2)
    ig_copy = pltpu.make_async_copy(ig_ref, ig_any, loc_sem.at[4])
    ig_copy.start()
    sp[0:1, :] = sums[0]
    sp[1:2, :] = sums[1]
    for j in range(8 + N, 15):
        sp[j : j + 1, :] = zero_row
    push(sp.at[:, other_cols], csp, qc_s.at[1], qc_r.at[1], mate)

    landed(csp, qc_s.at[1], qc_r.at[1])
    psp[...] = sp[:, mine_cols] + csp[...]
    for i in range(1, NP):
        _, to = in_plane(i)
        push(psp, rsp.at[i], qp_s.at[1, i - 1], qp_r.at[1, i - 1], to)

    line_start(0)

    whole = zsend[0].astype(F32)
    for j in range(1, N):
        there, _ = in_line(-j)
        landed(zrecv.at[there], gz_s.at[j], gz_r.at[there])
        whole = whole + zrecv[there].astype(F32)

    def fin_left(buffer, core, ys, es):
        return buffer.at[rows(core * HR + (es * NY + ys) * HS, HS), left]

    def fin_right(buffer, core, ys, es):
        return buffer.at[rows(core * HR + (ys * NE + es) * HS, HS), right]

    def fin_to_mate(i, ys, es):
        for part, piece in enumerate((fin_left, fin_right)):
            sem = 2 * NP - 2 + 2 * i + part
            src, dst = piece(fin, c, ys, es), piece(fin_any, c, ys, es)
            push(src, dst, ga_s.at[sem], ga_r.at[sem], mate)

    def fin_from_mate(i, ys, es):
        for part, piece in enumerate((fin_left, fin_right)):
            sem = 2 * NP - 2 + 2 * i + part
            landed(piece(fin_any, 1 - c, ys, es), ga_s.at[sem], ga_r.at[sem])

    fin[rows(c * HR + (e * NY + y) * HS, HS), left] = whole[:, 0:half].astype(BF16)
    fin[rows(c * HR + (y * NE + e) * HS, HS), right] = whole[:, half:].astype(BF16)
    for i in range(1, NP):
        _, to = in_plane(i)
        at = fin_left(fin, c, y, e)
        push(at, at, ga_s.at[i - 1], ga_r.at[i - 1], to)
        at = fin_right(fin, c, y, e)
        push(at, at, ga_s.at[NP - 2 + i], ga_r.at[NP - 2 + i], to)
    fin_to_mate(0, y, e)

    whole = pqo[rows(e * ER, ER), rows(y * YW, YW, 128)].astype(F32)
    for i in range(1, NP):
        landed(rqo.at[i], qp_s.at[0, i - 1], qp_r.at[0, i - 1])
        whole = whole + rqo[i].astype(F32)
    zqo[...] = whole.astype(BF16)
    for j in range(1, N):
        there, to = in_line(j)
        push(zqo.at[rows(there * SH, SH)], yqo.at[j], qz_s.at[0, j - 1], qz_r.at[0, j - 1], to)
    whole = psp[...]
    for i in range(1, NP):
        landed(rsp.at[i], qp_s.at[1, i - 1], qp_r.at[1, i - 1])
        whole = whole + rsp[i]
    zsp[...] = whole
    for j in range(1, N):
        _, to = in_line(j)
        push(zsp, ysp.at[j], qz_s.at[1, j - 1], qz_r.at[1, j - 1], to)

    cols_copy.wait()
    for j in range(1, N):
        there, _ = in_line(-j)
        landed(outd.at[there], od_s.at[j - 1], od_r.at[j - 1])
    for j in range(N):
        at = pl.ds(j * T, T)
        out_ref[at, :] = out_ref[at, :] + outd[j].astype(F32)
    out_copy = pltpu.make_async_copy(out_ref, out_any, loc_sem.at[5])
    out_copy.start()

    whole = zqo[rows(n * SH, SH), :].astype(F32)
    for j in range(1, N):
        landed(yqo.at[j], qz_s.at[0, j - 1], qz_r.at[0, j - 1])
        whole = whole + yqo[j].astype(F32)
    my_cols = rows(y * YW, YW, 128)
    fqo[c, :, my_cols] = whole.astype(BF16)
    at = fqo.at[c, :, my_cols]
    others = [(i, other) for i in range(NY) for other in range(2) if i or other]
    for k, (i, other) in enumerate(others):
        to = (2 * in_rows(i)[0] + (1 - c if other else c), e, n)
        push(at, at, qa_s.at[k], qa_r.at[k], to)
    whole = zsp[...]
    for j in range(1, N):
        landed(ysp.at[j], qz_s.at[1, j - 1], qz_r.at[1, j - 1])
        whole = whole + ysp[j]
    fsp[:, mine_cols] = whole
    at = fsp.at[:, mine_cols]
    push(at, at, qa_s.at[2 * NY - 1], qa_r.at[2 * NY - 1], mate)
    for i in range(1, NP):
        near, _ = in_plane(-i)
        ys, es = lax.div(near, NE), rem(near, NE)
        landed(fin_left(fin, c, ys, es), ga_s.at[i - 1], ga_r.at[i - 1])
        landed(fin_right(fin, c, ys, es), ga_s.at[NP - 2 + i], ga_r.at[NP - 2 + i])
        fin_to_mate(i, ys, es)
    at = rows(c * HR, HR)
    fin_copy = pltpu.make_async_copy(fin.at[at], fin_any.at[at], loc_sem.at[6])
    fin_copy.start()
    landed(fsp.at[:, other_cols], qa_s.at[2 * NY - 1], qa_r.at[2 * NY - 1])
    small_ref[...] = fsp[...]
    for k, (i, other) in enumerate(others):
        near, _ = in_rows(-i)
        at = fqo.at[1 - c if other else c, :, rows(near * YW, YW, 128)]
        landed(at, qa_s.at[k], qa_r.at[k])
    fqo_ref[...] = fqo[...]
    ig_copy.wait()
    out_copy.wait()
    fin_copy.wait()
    for i in range(NP):
        near, _ = in_plane(-i)
        fin_from_mate(i, lax.div(near, NE), rem(near, NE))

    for copy in started:
        copy.wait_send()
    for valid, copies in maybe_started:

        @pl.when(valid)
        def _(copies=copies):
            for copy in copies:
                copy.wait_send()

    for s, o in enumerate(offsets):
        valid = jnp.logical_and(spot_in_row + o >= 0, spot_in_row + o < z.per_row)

        @pl.when(valid)
        def _(s=s, o=o):
            halo_copy(s, o).wait_send()


def run(z, x, seg, chosen, vectors, q, k, v, o, r, up, down, cot):
    N, G, NP, NY, NE = z.narrow, z.group, z.plane, z.rows_y, z.expert
    T, W, D, R, HP = z.block, z.window, z.width, z.shard, z.head_part
    FL = z.ff_local
    FR = D + FL
    HR = FR // 2
    HS = HR // NP
    YW = D // NY
    SH = R + HP
    ER = N * SH
    QR = G * R
    GR = G * SH
    S = 2 * z.reach
    SMALL = z.small_rows
    vmem = pl.BlockSpec(memory_space=pltpu.VMEM)
    anywhere = pl.BlockSpec(memory_space=pltpu.HBM)
    scratch = [
        ((N * T, D // N), F32),
        ((T, D), F32),
        ((W, D), F32),
        ((W, D), BF16),
        ((QR, D), BF16),
        ((QR, D), BF16),
        ((2, HEAD, D), BF16),
        ((G, 16, 128), F32),
        ((8, 128), F32),
        ((HEAD, 128), F32),
        ((N, FR, D), BF16),
        ((T, D), BF16),
        ((8, z.row_len), F32),
        ((W, 8), F32),
        ((W, HEAD), BF16),
        ((W, HEAD), BF16),
        ((HEAD, W), BF16),
        ((HEAD, W), BF16),
        ((QR, T), F32),
        ((2, HEAD, T), BF16),
        ((2, W, T), BF16),
        ((2, HEAD, T), F32),
        ((QR, T), BF16),
        ((T, D), F32),
        ((T, D), F32),
        ((T, D), BF16),
        ((N, T, FL), BF16),
        ((N, T, FL), BF16),
        ((T, FL), BF16),
        ((T, D), F32),
        ((T, D), F32),
        ((T, D), BF16),
        ((2, HEAD, T), BF16),
        ((W, HEAD), F32),
        ((W, HEAD), F32),
        ((2, HEAD, T), BF16),
        ((QR, T), BF16),
        ((max(S, 1), 2, z.piece, HEAD), BF16),
        ((max(S, 1), 2, z.piece, HEAD), BF16),
        ((T, D), BF16),
        ((N, T, D // N), BF16),
        ((N, FR, D), BF16),
        ((N, HR, D), BF16),
        ((N, HR, D), BF16),
        ((N, NE, HR // NE, D // 2), BF16),
        ((N, NY, HR // NY, D // 2), BF16),
        ((N, HR // NE, D // 2), BF16),
        ((N, HR // NY, D // 2), BF16),
        ((N, NY, HS, D // 2), BF16),
        ((N, NE, HS, D // 2), BF16),
        ((N, HS, D), BF16),
        ((N, HS, D), BF16),
        ((FR, D), BF16),
        ((2, GR, D), BF16),
        ((GR, D), BF16),
        ((GR, D), BF16),
        ((NP, ER, YW), BF16),
        ((ER, YW), BF16),
        ((N, SH, YW), BF16),
        ((2, SH, D), BF16),
        ((SMALL, D), F32),
        ((SMALL, D // 2), F32),
        ((SMALL, D // 2), F32),
        ((NP, SMALL, D // 2), F32),
        ((SMALL, D // 2), F32),
        ((N, SMALL, D // 2), F32),
        ((SMALL, D), F32),
    ]
    pairs = [
        (N - 1,),
        (N - 1,),
        (G - 1,),
        (G - 1,),
        (G - 1,),
        (G - 1,),
        (G - 1,),
        (4, N - 1, max(NE, NY) - 1),
        (N - 1,),
        (N - 1,),
        (N - 1,),
        (max(S, 1),),
        (N,),
        (4, N, max(NE, NY) - 1),
        (N,),
        (4 * NP - 2,),
        (2,),
        (2, NP - 1),
        (2, N - 1),
        (2 * NY,),
    ]
    sems = [pltpu.SemaphoreType.DMA((7,))]
    for shape in pairs:
        sems += [pltpu.SemaphoreType.DMA(shape)] * 2
    sems += [pltpu.SemaphoreType.DMA((2, 2, N)), pltpu.SemaphoreType.DMA((2, N))]
    outs = [
        ((N * T, D // N), F32),
        ((T, D), F32),
        ((FR, D), BF16),
        ((2, SH, D), BF16),
        ((SMALL, D), F32),
    ]
    return pl.pallas_call(
        functools.partial(kernel, z),
        out_shape=[pltpu.VMEM(s, t) for s, t in outs],
        in_specs=[anywhere] + [vmem] * (7 + len(vectors)) + [anywhere] * 2 + [vmem],
        out_specs=[pl.BlockSpec(memory_space=pl.ANY)] * 3 + [vmem] * 2,
        scratch_shapes=[pltpu.VMEM(s, t) for s, t in scratch] + sems,
        compiler_params=pltpu.CompilerParams(
            collective_id=0, has_side_effects=True, vmem_limit_bytes=58 * 2**20
        ),
        name="layer",
    )(x, seg, chosen, *vectors, q, k, v, o, r, up, down, cot)


def finish_kernel(
    z,
    out_in,
    ig_in,
    fin_ref,
    fqo_ref,
    small_ref,
    out_any,
    ig_out,
    g1_ref,
    s1_ref,
    gq_ref,
    qb_ref,
    gk_ref,
    gv_ref,
    vb_ref,
    go_ref,
    ob_ref,
    rw_ref,
    rb_ref,
    g2_ref,
    s2_ref,
    gup_any,
    ub_ref,
    gdown_any,
    db_ref,
    gup,
    gdown,
    sems,
):
    e, n = lax.axis_index("expert"), lax.axis_index("narrow")
    N, T, D, R, HP, LE = z.narrow, z.block, z.width, z.shard, z.head_part, z.local_experts
    copies = []

    def put(src, dst):
        copies.append(pltpu.make_async_copy(src, dst, sems.at[len(copies)]))
        copies[-1].start()

    put(out_in, out_any)
    put(ig_in, ig_out)
    gup[...] = fin_ref[0:D, :].astype(F32)
    put(gup, gup_any)
    gdown[...] = fin_ref[D : D + z.ff_local, :].astype(F32)
    put(gdown, gdown_any)
    gq_ref[...] = fqo_ref[0, 0:R, :].astype(F32)
    go_ref[...] = fqo_ref[1, 0:R, :].astype(F32)
    gk_ref[...] = fqo_ref[0, R : R + HP, :].astype(F32)
    gv_ref[...] = fqo_ref[1, R : R + HP, :].astype(F32)
    g1_ref[...] = small_ref[0:1, :]
    s1_ref[...] = small_ref[1:2, :]
    ob_ref[...] = small_ref[2:3, :]
    g2_ref[...] = small_ref[3:4, :]
    s2_ref[...] = small_ref[4:5, :]
    db_ref[...] = small_ref[5:6, :]
    rb_ref[...] = small_ref[7:8, 0 : z.experts]
    rw_ref[...] = small_ref[16 : 16 + z.experts, :]
    upper = jnp.zeros((1, D), F32)
    for j in range(N):
        upper = jnp.where(n == j, small_ref[8 + j : 9 + j, :], upper)
    ub_ref[...] = upper
    here = e * N + n
    query = pltpu.roll(small_ref[0:8, :], lax.rem(D - here * R, D), 1)
    for i in range(LE):
        qb_ref[i : i + 1, :] = query[6:7, i * HP : (i + 1) * HP]
    value = pltpu.roll(small_ref[8:16, :], lax.rem(D - n * HP, D), 1)
    vb_ref[...] = value[7:8, 0:HP]
    for copy in copies:
        copy.wait()


def finish(z, out, ig, fin, fqo, small):
    N, T, D, R, HP = z.narrow, z.block, z.width, z.shard, z.head_part
    FL = z.ff_local
    vmem = pl.BlockSpec(memory_space=pltpu.VMEM)
    anywhere = pl.BlockSpec(memory_space=pltpu.HBM)
    shapes = [
        (N * T, D // N),
        (T, D),
        (1, D),
        (1, D),
        (R, D),
        (z.local_experts, HP),
        (HP, D),
        (HP, D),
        (1, HP),
        (R, D),
        (1, D),
        (z.experts, D),
        (1, z.experts),
        (1, D),
        (1, D),
        (D, FL),
        (1, FL),
        (FL, D),
        (1, D),
    ]
    return pl.pallas_call(
        functools.partial(finish_kernel, z),
        out_shape=[jax.ShapeDtypeStruct(s, F32) for s in shapes],
        in_specs=[pl.BlockSpec(memory_space=pl.ANY)] * 2 + [vmem] * 3,
        out_specs=[anywhere] * 2 + [vmem] * 13 + [anywhere, vmem, anywhere, vmem],
        scratch_shapes=[
            pltpu.VMEM((D, FL), F32),
            pltpu.VMEM((FL, D), F32),
            pltpu.SemaphoreType.DMA((4,)),
        ],
        compiler_params=pltpu.CompilerParams(vmem_limit_bytes=16 * 2**20),
        name="finish",
    )(out, ig, fin, fqo, small)


def per_device(
    inputs,
    seg_ids,
    chosen,
    gain_one,
    shift_one,
    query_w,
    query_b,
    key_w,
    value_w,
    value_b,
    out_w,
    out_b,
    router_w,
    router_b,
    gain_two,
    shift_two,
    up_w,
    up_b,
    down_w,
    down_b,
    cotangent,
):
    narrow = lax.axis_size("narrow")
    e, n = lax.axis_index("expert"), lax.axis_index("narrow")
    z = Sizes(
        lax.axis_size("dp"),
        lax.axis_size("expert"),
        narrow,
        inputs.shape[0],
        inputs.shape[1],
        seg_ids.shape[1],
        query_w.shape[0],
        up_w.shape[1],
    )
    D, R, HP = z.width, z.shard, z.head_part
    vectors = [gain_one, shift_one, out_b, gain_two, shift_two, down_b, up_b]
    vectors = [v.reshape(1, -1) for v in vectors]
    vectors += [query_b, value_b.reshape(1, -1), router_b.reshape(1, -1)]
    parts = run(
        z,
        inputs,
        seg_ids,
        jnp.transpose(chosen),
        vectors,
        jnp.transpose(query_w, (0, 2, 1)).reshape(R, D),
        jnp.transpose(key_w),
        jnp.transpose(value_w),
        out_w.reshape(R, D),
        jnp.transpose(router_w),
        up_w,
        down_w,
        cotangent,
    )
    out, ig, g1, s1, gq, qb, gk, gv, vb, go, ob, rw, rb, g2, s2, gup, ub, gdown, db = finish(
        z, *parts
    )
    return (
        out,
        ig,
        g1.reshape(-1),
        s1.reshape(-1),
        jnp.transpose(gq.reshape(z.local_experts, HP, D), (0, 2, 1)),
        qb,
        jnp.transpose(gk),
        jnp.transpose(gv),
        vb.reshape(-1),
        go.reshape(z.local_experts, HP, D),
        ob.reshape(-1),
        jnp.transpose(rw),
        rb.reshape(-1),
        g2.reshape(-1),
        s2.reshape(-1),
        gup,
        ub.reshape(-1),
        gdown,
        db.reshape(-1),
    )


def solution(mesh):
    return jax.shard_map(
        per_device,
        mesh=mesh,
        in_specs=(
            P("dp", None),
            P("dp", None),
            P("dp", None),
            P(),
            P(),
            P("expert", None, "narrow"),
            P("expert", "narrow"),
            P(None, "narrow"),
            P(None, "narrow"),
            P("narrow"),
            P("expert", "narrow", None),
            P(),
            P(),
            P(),
            P(),
            P(),
            P(None, "narrow"),
            P("narrow"),
            P("narrow", None),
            P(),
            P(("dp", "expert"), "narrow"),
        ),
        out_specs=(
            P(("dp", "expert"), "narrow"),
            P(("dp", "expert", "narrow"), None),
            P(),
            P(),
            P("expert", None, "narrow"),
            P("expert", "narrow"),
            P(None, "narrow"),
            P(None, "narrow"),
            P("narrow"),
            P("expert", "narrow", None),
            P(),
            P(),
            P(),
            P(),
            P(),
            P(None, "narrow"),
            P("narrow"),
            P("narrow", None),
            P(),
        ),
        check_vma=False,
    )
```

```python
import functools
import math

import jax
import jax.numpy as jnp
from jax import lax
from jax.experimental import pallas as pl
from jax.experimental.pallas import tpu as pltpu
from jax.sharding import PartitionSpec as P

HEAD = 64
LONGEST = 256
EPSILON = 1e-05
MASKED = -1000000000.0
GELU_A = math.sqrt(2.0 / math.pi)
GELU_B = 0.044715
F32 = jnp.float32
BF16 = jnp.bfloat16
MESH = pl.DeviceIdType.MESH
GROUP_BYTES = 2**20
GROUPS = 16


def dot(a, b):
    return lax.dot_general(a, b, (((1,), (0,)), ((), ())), preferred_element_type=F32)


def dot_nt(a, b):
    return lax.dot_general(a, b, (((1,), (1,)), ((), ())), preferred_element_type=F32)


def dot_tn(a, b):
    return lax.dot_general(a, b, (((0,), (0,)), ((), ())), preferred_element_type=F32)


def norm_stats(x):
    centred = x - jnp.mean(x, axis=1, keepdims=True)
    inverse = lax.rsqrt(jnp.mean(centred * centred, axis=1, keepdims=True) + EPSILON)
    return centred * inverse, inverse


def rem(a, b):
    return lax.rem(a, b)


class Sizes:
    def __init__(self, dp, expert, narrow, tokens, width, row_len, local_experts, ff_local):
        self.dp, self.expert, self.narrow = dp, expert, narrow
        self.tokens, self.width, self.row_len = tokens, width, row_len
        self.local_experts = local_experts
        self.experts = local_experts * expert
        self.group = expert * narrow
        self.block = tokens // self.group
        self.rows_y = dp // 2
        self.plane = self.rows_y * expert
        self.ff_local = ff_local
        self.head_part = HEAD // narrow
        self.shard = local_experts * self.head_part
        self.per_row = row_len // self.block
        spans = [
            min(row_len, (j + 1) * self.block + LONGEST) - max(0, j * self.block - LONGEST)
            for j in range(self.per_row)
        ]
        self.window = max(spans)
        self.reach = max(1, LONGEST // self.block) if self.per_row > 1 else 0
        self.piece = min(self.block, LONGEST)
        self.tile = min(256, self.block)
        self.up_rows = narrow * ff_local // width
        self.small_rows = 24


def kernel(
    z,
    x_any,
    seg_ref,
    chosen_ref,
    g1_ref,
    s1_ref,
    ob_ref,
    g2_ref,
    s2_ref,
    db_ref,
    ub_ref,
    qb_ref,
    vb_ref,
    rb_ref,
    q_ref,
    k_ref,
    v_ref,
    o_ref,
    r_ref,
    up_any,
    down_any,
    cot_ref,
    out_any,
    ig_any,
    g_ref,
    fqo_ref,
    small_ref,
    out_ref,
    ig_ref,
    xw,
    rw,
    wq,
    wo,
    wkv,
    bias,
    corner,
    vcol,
    ffw,
    cot,
    segs,
    segc,
    kn,
    vn,
    kt,
    vt,
    qt,
    qk,
    prob,
    mix,
    mixg,
    hid,
    acc,
    second,
    active,
    slope,
    ugrad,
    sgrad,
    hgrad,
    hgb,
    mgk,
    dk,
    dv,
    dq,
    dqt,
    halo_out,
    halo_in,
    delta,
    outd,
    gsend,
    ruler,
    crecv,
    psend,
    pea,
    pya,
    mea,
    mya,
    pyb,
    peb,
    zsend,
    zrecv,
    fin,
    gqo,
    cqo,
    pqo,
    rqo,
    zqo,
    yqo,
    fqo,
    sp,
    csp,
    psp,
    rsp,
    zsp,
    ysp,
    fsp,
    loc_sem,
    send_sems,
    w_r,
    wm_r,
    b_r,
    q_r,
    qm_r,
    o_r,
    om_r,
    fp_r,
    fm_r,
    ct_r,
    od_r,
    hl_s,
    hl_r,
    gc_r,
    gp_r,
    gz_r,
    ga_r,
    qc_r,
    qp_r,
    qz_r,
    qa_r,
    fz_s,
    fz_r,
):
    d, e, n = lax.axis_index("dp"), lax.axis_index("expert"), lax.axis_index("narrow")
    c, y = rem(d, 2), lax.div(d, 2)
    N, G, NP, NE, NY = z.narrow, z.group, z.plane, z.expert, z.rows_y
    T, W, D, R, HP, LE = z.block, z.window, z.width, z.shard, z.head_part, z.local_experts
    FL = z.ff_local
    half = D // 2
    here = e * N + n
    spot = y * NE + e
    mate = (d + 1 - 2 * c, e, n)

    def in_group(j):
        at = rem(here + j + G, G)
        return at, (d, lax.div(at, N), rem(at, N))

    def in_plane(j):
        at = rem(spot + j + NP, NP)
        return at, (2 * lax.div(at, NE) + c, rem(at, NE), n)

    def in_line(j):
        at = rem(n + j + N, N)
        return at, (d, e, at)

    def in_rows(j):
        at = rem(y + j + NY, NY)
        return at, (2 * at + c, e, n)

    sent = [0, 0]

    def push(src, dst, recv, device):
        size = math.prod(src.shape) * jnp.dtype(src.dtype).itemsize
        if src.shape[-1] == 128 and src.dtype == F32:
            kind = 0
        else:
            if sent[-1] + size > GROUP_BYTES:
                sent.append(0)
            kind = len(sent) - 1
        sent[kind] += size
        copy = pltpu.make_async_remote_copy(
            src_ref=src,
            dst_ref=dst,
            send_sem=send_sems.at[kind],
            recv_sem=recv,
            device_id=device,
            device_id_type=MESH,
        )
        copy.start()

    def landed(dst, recv):
        pltpu.make_async_remote_copy(
            src_ref=dst,
            dst_ref=dst,
            send_sem=recv,
            recv_sem=recv,
            device_id=mate,
            device_id_type=MESH,
        ).wait_recv()

    def rows(start, size, step=16):
        return pl.ds(pl.multiple_of(start, step), size)

    start = here * T
    row = lax.div(start, z.row_len)
    spot_in_row = rem(here, z.per_row)
    base = row * z.row_len
    ws = jnp.minimum(jnp.maximum(spot_in_row * T - LONGEST, 0), z.row_len - W)
    off = spot_in_row * T - ws
    own = rows(off, T, 128)

    x_copy = pltpu.make_async_copy(x_any.at[rows(base + ws, W, 128)], xw, loc_sem.at[0])
    x_copy.start()
    up_copy = pltpu.make_async_copy(up_any, ffw.at[n, pl.ds(0, D)], loc_sem.at[1])
    up_copy.start()
    down_copy = pltpu.make_async_copy(down_any, ffw.at[n, pl.ds(D, FL)], loc_sem.at[2])
    down_copy.start()
    cols_copy = pltpu.make_async_copy(
        x_any.at[rows(e * N * T, N * T, 128), rows(n * (D // N), D // N, 128)], out_ref, loc_sem.at[3]
    )
    cols_copy.start()
    wq[rows(here * R, R)] = q_ref[...]
    wo[rows(here * R, R)] = o_ref[...]
    wkv[0, rows(n * HP, HP)] = k_ref[...]
    wkv[1, rows(n * HP, HP)] = v_ref[...]
    bias[here] = jnp.zeros((16, 128), F32)
    for i in range(FL // 128):
        bias[here, i : i + 1, :] = ub_ref[0:1, i * 128 : (i + 1) * 128]
    bias[here, 8 : 8 + LE, 0:HP] = qb_ref[...]
    bias[here, 7:8, 0:HP] = vb_ref[...]

    barrier = pltpu.get_barrier_semaphore()
    pl.semaphore_signal(barrier, inc=1, device_id=mate, device_id_type=MESH)
    for j in range(1, NP):
        pl.semaphore_signal(barrier, inc=1, device_id=in_plane(j)[1], device_id_type=MESH)
    for j in range(1, G):
        pl.semaphore_signal(barrier, inc=1, device_id=in_group(j)[1], device_id_type=MESH)
    for j in range(1, NY):
        to = (2 * in_rows(j)[0] + 1 - c, e, n)
        pl.semaphore_signal(barrier, inc=1, device_id=to, device_id_type=MESH)
    pl.semaphore_wait(barrier, NP + G + NY - 2)

    mine_cols = rows(c * half, half, 128)
    other_cols = rows((1 - c) * half, half, 128)

    def in_expert(i):
        at = rem(e + i + NE, NE)
        return at, (d, at, n)

    def shard_at(i, j):
        return rem(e - i + NE, NE) * N + rem(n - j + N, N)

    def spread_start(part, recv):
        for j in range(1, N):
            at = part(here)
            push(at, at, recv.at[j - 1], in_line(j)[1])
        for i in range(1, NE):
            at = part(here)
            push(at, at, recv.at[i * N - 1], in_expert(i)[1])

    def spread_on(part, recv, to_mate):
        for j in range(1, N):
            at = part(shard_at(0, j))
            landed(at, recv.at[j - 1])
            for i in range(1, NE):
                push(at, at, recv.at[i * N + j - 1], in_expert(i)[1])
            if to_mate is not None:
                push(at, at, to_mate.at[j - 1], mate)

    def spread_end(part, recv, to_mate):
        for i in range(1, NE):
            for j in range(N):
                at = part(shard_at(i, j))
                landed(at, recv.at[i * N + j - 1])
                if to_mate is not None:
                    push(at, at, to_mate.at[i * N + j - 1], mate)

    def spread_wait(part, to_mate):
        for i in range(NE):
            for j in range(N):
                if i or j:
                    landed(part(shard_at(i, j)), to_mate.at[i * N + j - 1])

    def bias_part(g):
        return bias.at[g]

    def q_part(g):
        return wq.at[rows(g * R, R), mine_cols]

    def q_other(g):
        return wq.at[rows(g * R, R), other_cols]

    def o_part(g):
        return wo.at[rows(g * R, R), mine_cols]

    def o_other(g):
        return wo.at[rows(g * R, R), other_cols]

    for j in range(1, N):
        at = wkv.at[c, rows(n * HP, HP)]
        push(at, at, w_r.at[j - 1], in_line(j)[1])
    spread_start(q_part, q_r)
    spread_start(bias_part, b_r)
    up_copy.wait()
    down_copy.wait()
    FR = D + FL

    left, right = pl.ds(0, half), pl.ds(half, half)
    HR = FR // 2
    HS = HR // NP
    HA, HB = HR // NE, HR // NY
    def left_slice(of, ys, es):
        return ffw.at[of, rows(c * HR + (es * NY + ys) * HS, HS), left]

    def right_slice(of, ys, es):
        return ffw.at[of, rows(c * HR + (ys * NE + es) * HS, HS), right]

    def left_half(of, es):
        return ffw.at[of, rows(c * HR + es * HA, HA), left]

    def right_half(of, ys):
        return ffw.at[of, rows(c * HR + ys * HB, HB), right]

    def by_distance(at):
        return sorted((o for o in range(N) if o != at), key=lambda o: (abs(o - at), o if 2 * at >= N else -o))

    def pick(choices):
        value = choices[0]
        for at in range(1, N):
            value = jnp.where(n == at, choices[at], value)
        return value

    shard_of = [n] + [pick([by_distance(at)[k] for at in range(N)]) for k in range(N - 1)]
    maybe_started = []

    def line_push(of, step, valid):
        of = jnp.clip(of, 0, N - 1)
        to = (d, e, jnp.clip(n + step, 0, N - 1))
        way = (step + 1) // 2
        copies = [
            pltpu.make_async_remote_copy(
                src_ref=at,
                dst_ref=at,
                send_sem=fz_s.at[part, way, of],
                recv_sem=fz_r.at[part, of],
                device_id=to,
                device_id_type=MESH,
            )
            for part, at in enumerate((left_slice(of, y, e), right_slice(of, y, e)))
        ]

        @pl.when(valid)
        def _():
            for copy in copies:
                copy.start()

        maybe_started.append((valid, copies))

    def line_landed(of, valid):
        of = jnp.clip(of, 0, N - 1)

        @pl.when(valid)
        def _():
            landed(left_slice(of, y, e), fz_r.at[0, of])
            landed(right_slice(of, y, e), fz_r.at[1, of])

    def shards_start():
        line_push(n, 1, n + 1 < N)
        line_push(n, -1, n > 0)

    def shards_on(hop):
        line_landed(n - hop, n >= hop)
        line_push(n - hop, 1, jnp.logical_and(n >= hop, n + 1 < N))
        line_landed(n + hop, n + hop < N)
        line_push(n + hop, -1, jnp.logical_and(n + hop < N, n > 0))

    def plane_on(j):
        there = shard_of[j]
        at = left_slice(there, y, e)
        for i in range(1, NY):
            push(at, at, fp_r.at[0, j - 1, i - 1], in_rows(i)[1])
        at = right_slice(there, y, e)
        for i in range(1, NE):
            push(at, at, fp_r.at[1, j - 1, i - 1], in_expert(i)[1])

    def plane_turn(j):
        there = shard_of[j]
        for i in range(1, NY):
            near, _ = in_rows(-i)
            landed(left_slice(there, near, e), fp_r.at[0, j - 1, i - 1])
        at = left_half(there, e)
        for i in range(1, NE):
            push(at, at, fp_r.at[2, j - 1, i - 1], in_expert(i)[1])
        for i in range(1, NE):
            near, _ = in_expert(-i)
            landed(right_slice(there, y, near), fp_r.at[1, j - 1, i - 1])
        at = right_half(there, y)
        for i in range(1, NY):
            push(at, at, fp_r.at[3, j - 1, i - 1], in_rows(i)[1])

    def mate_on(j):
        there = shard_of[j]
        for i in range(1, NE):
            near, _ = in_expert(-i)
            landed(left_half(there, near), fp_r.at[2, j - 1, i - 1])
        for i in range(1, NY):
            near, _ = in_rows(-i)
            landed(right_half(there, near), fp_r.at[3, j - 1, i - 1])
        at = ffw.at[there, rows(c * HR, HR)]
        push(at, at, fm_r.at[j - 1], mate)

    x_copy.wait()
    gain_one, shift_one = g1_ref[...], s1_ref[...]

    def norm_one(i, carry):
        at = rows(i * 128, 128, 128)
        unit, _ = norm_stats(xw[at, :])
        rw[at, :] = (unit * gain_one + shift_one).astype(BF16)
        return carry

    lax.fori_loop(0, W // 128, norm_one, 0)

    seg_all = seg_ref[...].astype(F32)
    row_id = lax.broadcasted_iota(jnp.int32, seg_all.shape, 0)
    seg_here = jnp.sum(jnp.where(row_id == row, seg_all, 0.0), axis=0, keepdims=True)
    segs[...] = jnp.broadcast_to(seg_here, segs.shape)
    segc[...] = jnp.transpose(segs[:, rows(ws, W, 128)])
    seg_own = segs[0:1, rows(spot_in_row * T, T, 128)]
    corner[...] = jnp.zeros_like(corner)
    corner[:, 0 : z.experts] = jnp.broadcast_to(rb_ref[...], (8, z.experts))
    router_col = jnp.transpose(corner[...])[0 : z.experts, 0:1]
    logits = dot_nt(r_ref[...], rw[own, :]) + router_col
    expert_id = lax.broadcasted_iota(jnp.int32, (z.experts, T), 0)
    hot, picked = [], []
    for k in range(2):
        chosen = chosen_ref[k : k + 1, rows(start, T, 128)]
        hot.append((expert_id == chosen).astype(F32))
        picked.append(jnp.sum(logits * hot[k], axis=0, keepdims=True))
    top = jnp.maximum(picked[0], picked[1])
    raised = [jnp.exp(p - top) for p in picked]
    total = raised[0] + raised[1]
    gate = [r / total for r in raised]

    for j in range(1, N):
        there, _ = in_line(-j)
        at = wkv.at[c, rows(there * HP, HP)]
        landed(at, w_r.at[j - 1])
        push(at, at, wm_r.at[j - 1], mate)
    spread_on(q_part, q_r, qm_r)
    spread_on(bias_part, b_r, None)
    shards_start()
    spread_start(o_part, o_r)

    for j in range(1, N):
        there, _ = in_line(-j)
        landed(wkv.at[1 - c, rows(there * HP, HP)], wm_r.at[j - 1])
    kn[...] = dot_nt(rw[...], wkv[0]).astype(BF16)
    kt[...] = dot_nt(wkv[0], rw[...]).astype(BF16)
    spread_end(q_part, q_r, qm_r)
    spread_end(bias_part, b_r, None)
    columns = [jnp.transpose(bias[g, 0:16, :]) for g in range(G)]
    for part in range(N):
        vcol[part * HP : (part + 1) * HP, :] = jnp.broadcast_to(columns[part][0:HP, 7:8], (HP, 128))
    value_row = jnp.transpose(vcol[...])[0:1, :]
    vn[...] = (dot_nt(rw[...], wkv[1]) + value_row).astype(BF16)
    vt[...] = (dot_nt(wkv[1], rw[...]) + vcol[:, 0:1]).astype(BF16)

    spread_wait(q_other, qm_r)
    qt[...] = dot_nt(wq[...], rw[own, :])

    def expert_rows(at, i, part):
        return ((at * N + part) * LE + i) * HP

    for part in range(N):
        chosen_rows = [jnp.zeros((HP, T), F32), jnp.zeros((HP, T), F32)]
        for at in range(NE):
            g = at * N + part
            for i in range(LE):
                lo = expert_rows(at, i, part)
                one = qt[lo : lo + HP, :] + columns[g][0:HP, 8 + i : 9 + i]
                for k in range(2):
                    chosen_rows[k] = chosen_rows[k] + one * hot[k][at * LE + i : at * LE + i + 1, :]
        for k in range(2):
            qk[k, part * HP : (part + 1) * HP, :] = chosen_rows[k].astype(BF16)

    scale = 1.0 / math.sqrt(HEAD)
    TL = z.tile
    tiles = T // TL
    seg_tiles = [seg_own[:, i * TL : (i + 1) * TL] for i in range(tiles)]

    def attend(k):
        for i in range(tiles):
            at = pl.ds(i * TL, TL)
            scores = dot(kn[...], qk[k, :, at]) * scale
            scores = jnp.where(segc[:, 0:1] == seg_tiles[i], scores, MASKED)
            high = jnp.max(scores, axis=0, keepdims=True)
            raised_scores = jnp.exp(scores - high)
            low = (raised_scores * (1.0 / jnp.sum(raised_scores, axis=0, keepdims=True))).astype(BF16)
            prob[k, :, at] = low
            mix[k, :, at] = dot(vt[...], low)

    attend(0)
    attend(1)
    shards_on(1)
    plane_on(1)
    spread_on(o_part, o_r, om_r)
    plane_turn(1)
    shards_on(2)
    plane_on(2)
    CW = D // N
    cot[:, rows(n * CW, CW, 128)] = cot_ref[rows(n * T, T, 128), :]
    for j in range(1, N):
        there, to = in_line(j)
        push(
            cot_ref.at[rows(there * T, T, 128)],
            cot.at[:, rows(n * CW, CW, 128)],
            ct_r.at[j - 1],
            to,
        )
    spread_end(o_part, o_r, om_r)

    for part in range(N):
        for at in range(NE):
            for i in range(LE):
                lo = expert_rows(at, i, part)
                x = at * LE + i
                gated = jnp.zeros((HP, T), F32)
                for k in range(2):
                    rounded_mix = mix[k, part * HP : (part + 1) * HP, :].astype(BF16).astype(F32)
                    gated = gated + rounded_mix * (hot[k][x : x + 1, :] * gate[k])
                mixg[lo : lo + HP, :] = gated.astype(BF16)
    spread_wait(o_other, om_r)
    out_b, down_b = ob_ref[...], db_ref[...]
    gain_two, shift_two = g2_ref[...], s2_ref[...]
    attention = dot_tn(mixg[...], wo[...]) + out_b
    acc[...] = attention + down_b
    hid[...] = xw[own, :] + attention

    def norm_two(i, carry):
        at = rows(i * 128, 128, 128)
        unit, _ = norm_stats(hid[at, :])
        second[at, :] = (unit * gain_two + shift_two).astype(BF16)
        return carry

    lax.fori_loop(0, T // 128, norm_two, 0)
    sgrad[...] = jnp.zeros_like(sgrad)

    def core_start(j):
        push(
            gsend.at[j, rows((1 - c) * HR, HR)], crecv.at[j], gc_r.at[j], mate
        )

    def plane_start(j):
        landed(crecv.at[j], gc_r.at[j])
        psend[j] = (
            gsend[j, rows(c * HR, HR), :].astype(F32) + crecv[j].astype(F32)
        ).astype(BF16)
        for i in range(1, NE):
            there, to = in_expert(i)
            src = psend.at[j, rows(there * HA, HA), left]
            push(src, pea.at[j, i], gp_r.at[0, j, i - 1], to)
        for i in range(1, NY):
            there, to = in_rows(i)
            src = psend.at[j, rows(there * HB, HB), right]
            push(src, pya.at[j, i], gp_r.at[1, j, i - 1], to)

    def plane_middle(j):
        whole = psend[j, rows(e * HA, HA), left].astype(F32)
        for i in range(1, NE):
            landed(pea.at[j, i], gp_r.at[0, j, i - 1])
            whole = whole + pea[j, i].astype(F32)
        mea[j] = whole.astype(BF16)
        for i in range(1, NY):
            there, to = in_rows(i)
            src = mea.at[j, rows(there * HS, HS)]
            push(src, pyb.at[j, i], gp_r.at[2, j, i - 1], to)
        whole = psend[j, rows(y * HB, HB), right].astype(F32)
        for i in range(1, NY):
            landed(pya.at[j, i], gp_r.at[1, j, i - 1])
            whole = whole + pya[j, i].astype(F32)
        mya[j] = whole.astype(BF16)
        for i in range(1, NE):
            there, to = in_expert(i)
            src = mya.at[j, rows(there * HS, HS)]
            push(src, peb.at[j, i], gp_r.at[3, j, i - 1], to)

    def line_start(j):
        whole = mea[j, rows(y * HS, HS), :].astype(F32)
        for i in range(1, NY):
            landed(pyb.at[j, i], gp_r.at[2, j, i - 1])
            whole = whole + pyb[j, i].astype(F32)
        zsend[j, :, left] = whole.astype(BF16)
        whole = mya[j, rows(e * HS, HS), :].astype(F32)
        for i in range(1, NE):
            landed(peb.at[j, i], gp_r.at[3, j, i - 1])
            whole = whole + peb[j, i].astype(F32)
        zsend[j, :, right] = whole.astype(BF16)
        if j:
            push(zsend.at[j], zrecv.at[n], gz_r.at[n], (d, e, shard_of[j]))

    def forward(j):
        there = shard_of[j]
        if j:
            landed(ffw.at[there, rows((1 - c) * HR, HR)], fm_r.at[j - 1])
        up_b = jnp.concatenate(
            [bias[e * N + there, i : i + 1, :] for i in range(FL // 128)], axis=1
        )

        def feed(i, carry):
            at = rows(i * TL, TL, 128)
            upper = dot(second[at, :], ffw[there, 0:D, :]) + up_b
            square = upper * upper
            t = jnp.tanh(upper * (GELU_A + (GELU_A * GELU_B) * square))
            one = 0.5 + 0.5 * t
            low = (upper * one).astype(BF16)
            active[j, at, :] = low
            slope[j, at, :] = (
                one + (0.5 * upper) * (1.0 - t * t) * (GELU_A + (3.0 * GELU_A * GELU_B) * square)
            ).astype(BF16)
            acc[at, :] = acc[at, :] + dot(low, ffw[there, D : D + FL, :])
            return carry

        lax.fori_loop(0, T // TL, feed, 0)

    def backward(j):
        there = shard_of[j]

        def feed_back(i, carry):
            at = rows(i * TL, TL, 128)
            back = dot_nt(cot[at, :], ffw[there, D : D + FL, :]) * slope[j, at, :].astype(F32)
            back = back.astype(BF16)
            ugrad[at, :] = back
            sgrad[at, :] = sgrad[at, :] + dot_nt(back, ffw[there, 0:D, :])
            return carry

        lax.fori_loop(0, T // TL, feed_back, 0)
        sp[pl.ds(8 + there, 1), :] = jnp.sum(ugrad[...].astype(F32), axis=0, keepdims=True)
        gsend[j, 0:D, :] = dot_tn(second[...], ugrad[...]).astype(BF16)
        gsend[j, D : D + FL, :] = dot_tn(active[j], cot[...]).astype(BF16)
        core_start(j)

    def cotangent_wait():
        for j in range(1, N):
            there, _ = in_line(-j)
            landed(cot.at[:, rows(there * CW, CW, 128)], ct_r.at[j - 1])

    forward(0)
    plane_turn(2)
    mate_on(1)
    shards_on(3)
    plane_on(3)
    forward(1)
    mate_on(2)
    plane_turn(3)
    forward(2)
    cotangent_wait()
    backward(1)
    backward(2)
    plane_start(1)
    mate_on(3)
    forward(3)
    delta[...] = acc[...].astype(BF16)
    outd[n] = delta[:, rows(n * CW, CW, 128)]
    for j in range(1, N):
        there, to = in_line(j)
        push(delta.at[:, rows(there * CW, CW, 128)], outd.at[n], od_r.at[j - 1], to)

    backward(3)
    plane_start(2)
    backward(0)
    plane_start(3)
    plane_middle(1)

    zero_row = jnp.zeros((1, D), F32)

    def norm_two_back(i, carry):
        at = rows(i * 128, 128, 128)
        unit, inverse = norm_stats(hid[at, :])
        grad = sgrad[at, :]
        scaled = grad * gain_two
        back = inverse * (
            scaled
            - jnp.mean(scaled, axis=1, keepdims=True)
            - unit * jnp.mean(scaled * unit, axis=1, keepdims=True)
        )
        top_grad = cot[at, :].astype(F32)
        whole = top_grad + back
        hgrad[at, :] = whole
        hgb[at, :] = whole.astype(BF16)
        parts = (grad * unit, grad, whole, top_grad)
        return tuple(a + jnp.sum(b, axis=0, keepdims=True) for a, b in zip(carry, parts))

    sums = lax.fori_loop(0, T // 128, norm_two_back, (zero_row,) * 4)
    sp[3:4, :] = sums[0]
    sp[4:5, :] = sums[1]
    sp[2:3, :] = sums[2]
    sp[5:6, :] = sums[3]

    plane_start(0)

    SH = R + HP
    out_grad = dot(mixg[...], hgb[...]).astype(BF16)
    for g in range(G):
        gqo[1, g * SH : g * SH + R, :] = out_grad[g * R : (g + 1) * R, :]
    qt[...] = dot_nt(wo[...], hgb[...])
    gate_grad = [jnp.zeros((1, T), F32), jnp.zeros((1, T), F32)]
    for part in range(N):
        picked_rows = [jnp.zeros((HP, T), F32), jnp.zeros((HP, T), F32)]
        for at in range(NE):
            for i in range(LE):
                lo = expert_rows(at, i, part)
                one = qt[lo : lo + HP, :]
                x = at * LE + i
                for k in range(2):
                    picked_rows[k] = picked_rows[k] + one * hot[k][x : x + 1, :]
        for k in range(2):
            span = slice(part * HP, (part + 1) * HP)
            rounded_mix = mix[k, span, :].astype(BF16).astype(F32)
            gate_grad[k] = gate_grad[k] + jnp.sum(picked_rows[k] * rounded_mix, axis=0, keepdims=True)
            mgk[k, span, :] = (picked_rows[k] * gate[k]).astype(BF16)
    middle = gate[0] * gate_grad[0] + gate[1] * gate_grad[1]
    logit_grad = sum(hot[k] * (gate[k] * (gate_grad[k] - middle)) for k in range(2))
    logit_low = logit_grad.astype(BF16)

    def attend_back(k):
        for i in range(tiles):
            at = pl.ds(i * TL, TL)
            low = prob[k, :, at]
            p = low.astype(F32)
            prob_grad = dot(vn[...], mgk[k, :, at])
            inner = jnp.sum(p * prob_grad, axis=0, keepdims=True)
            score = (p * (prob_grad - inner)).astype(BF16)
            dq[k, :, at] = (dot(kt[...], score) * scale).astype(BF16)
            key_part = dot_nt(score, qk[k, :, at])
            value_part = dot_nt(low, mgk[k, :, at])
            if k == 0 and i == 0:
                dk[...] = key_part
                dv[...] = value_part
            else:
                dk[...] = dk[...] + key_part
                dv[...] = dv[...] + value_part

    attend_back(0)
    attend_back(1)
    plane_middle(2)

    H, PC = z.reach, z.piece
    offsets = [o for o in range(-H, H + 1) if o]
    inside = T >= LONGEST

    def halo_source(o):
        if inside:
            return (spot_in_row + 1) * T - ws if o > 0 else spot_in_row * T - LONGEST - ws
        return (spot_in_row + o) * T - ws

    def halo_copy(s, o):
        to = rem(here + o + G, G)
        return pltpu.make_async_remote_copy(
            src_ref=halo_out.at[s],
            dst_ref=halo_in.at[s],
            send_sem=hl_s.at[s],
            recv_sem=hl_r.at[s],
            device_id=(d, lax.div(to, N), rem(to, N)),
            device_id_type=MESH,
        )

    for s, o in enumerate(offsets):
        valid = jnp.logical_and(spot_in_row + o >= 0, spot_in_row + o < z.per_row)

        @pl.when(valid)
        def _(s=s, o=o):
            at = rows(halo_source(o), PC, 128)
            halo_out[s, 0] = (dk[at, :] * scale).astype(BF16)
            halo_out[s, 1] = dv[at, :].astype(BF16)
            halo_copy(s, o).start()

    for part in range(N):
        for at in range(NE):
            for i in range(LE):
                lo = expert_rows(at, i, part)
                x = at * LE + i
                span = slice(part * HP, (part + 1) * HP)
                one = dq[0, span, :].astype(F32) * hot[0][x : x + 1, :]
                one = one + dq[1, span, :].astype(F32) * hot[1][x : x + 1, :]
                dqt[lo : lo + HP, :] = one.astype(BF16)
    query_w_grad = dot(dqt[...], rw[own, :]).astype(BF16)
    key_w_grad = dot_tn((dk[...] * scale).astype(BF16), rw[...]).astype(BF16)
    value_w_grad = dot_tn(dv[...].astype(BF16), rw[...]).astype(BF16)
    for g in range(G):
        shared = slice((g % N) * HP, (g % N + 1) * HP)
        gqo[0, g * SH : g * SH + R, :] = query_w_grad[g * R : (g + 1) * R, :]
        gqo[0, g * SH + R : (g + 1) * SH, :] = key_w_grad[shared, :]
        gqo[1, g * SH + R : (g + 1) * SH, :] = value_w_grad[shared, :]
    push(gqo.at[1 - c], cqo, qc_r.at[0], mate)
    plane_middle(3)
    line_start(1)
    ones = jnp.ones((8, T), BF16)
    sp[6:7, :] = dot_nt(ones, dqt[...])[0:1, :]
    sp[7:8, :] = jnp.zeros((1, D), F32)
    sp[7:8, 0 : z.experts] = jnp.transpose(
        jnp.broadcast_to(jnp.sum(logit_grad, axis=1, keepdims=True), (z.experts, 128))
    )[0:1, :]
    acc[...] = dot_tn(dqt[...], wq[...]) + dot_tn(logit_low, r_ref[...])
    sp[16:24, :] = dot(logit_low, rw[own, :])
    sp[15:16, :] = jnp.zeros((1, D), F32)
    sp[15:16, 0:HEAD] = jnp.sum(dv[...], axis=0, keepdims=True)
    YW = D // NY
    ER = N * SH
    landed(cqo, qc_r.at[0])
    pqo[...] = (gqo[c].astype(F32) + cqo[...].astype(F32)).astype(BF16)
    for i in range(1, NP):
        there, to = in_plane(i)
        src = pqo.at[rows(rem(there, NE) * ER, ER), rows(lax.div(there, NE) * YW, YW, 128)]
        push(src, rqo.at[i], qp_r.at[0, i - 1], to)
    plane_middle(0)
    line_start(2)
    line_start(3)

    dk[...] = dk[...] * scale
    for s, o in enumerate(offsets):
        back_valid = jnp.logical_and(spot_in_row - o >= 0, spot_in_row - o < z.per_row)

        @pl.when(back_valid)
        def _(s=s, o=o):
            halo_copy(s, o).wait_recv()
            at = off if (not inside or o > 0) else off + T - LONGEST
            at = rows(at, PC, 128)
            dk[at, :] = dk[at, :] + halo_in[s, 0].astype(F32)
            dv[at, :] = dv[at, :] + halo_in[s, 1].astype(F32)

    key_grad = dk[own, :]
    value_grad = dv[own, :]
    key_low, value_low = key_grad.astype(BF16), value_grad.astype(BF16)
    acc[...] = acc[...] + dot(key_low, wkv[0]) + dot(value_low, wkv[1])

    def norm_one_back(i, carry):
        at = rows(i * 128, 128, 128)
        unit, inverse = norm_stats(xw[rows(off + i * 128, 128, 128), :])
        grad = acc[at, :]
        scaled = grad * gain_one
        back = inverse * (
            scaled
            - jnp.mean(scaled, axis=1, keepdims=True)
            - unit * jnp.mean(scaled * unit, axis=1, keepdims=True)
        )
        ig_ref[at, :] = hgrad[at, :] + back
        parts = (grad * unit, grad)
        return tuple(a + jnp.sum(b, axis=0, keepdims=True) for a, b in zip(carry, parts))

    sums = lax.fori_loop(0, T // 128, norm_one_back, (zero_row,) * 2)
    ig_copy = pltpu.make_async_copy(ig_ref, ig_any, loc_sem.at[4])
    ig_copy.start()
    sp[0:1, :] = sums[0]
    sp[1:2, :] = sums[1]
    for j in range(8 + N, 15):
        sp[j : j + 1, :] = zero_row
    push(sp.at[:, other_cols], csp, qc_r.at[1], mate)

    landed(csp, qc_r.at[1])
    psp[...] = sp[:, mine_cols] + csp[...]
    for i in range(1, NP):
        _, to = in_plane(i)
        push(psp, rsp.at[i], qp_r.at[1, i - 1], to)

    line_start(0)

    whole = zsend[0].astype(F32)
    for j in range(1, N):
        there, _ = in_line(-j)
        landed(zrecv.at[there], gz_r.at[there])
        whole = whole + zrecv[there].astype(F32)

    def fin_left(buffer, core, ys, es):
        return buffer.at[rows(core * HR + (es * NY + ys) * HS, HS), left]

    def fin_right(buffer, core, ys, es):
        return buffer.at[rows(core * HR + (ys * NE + es) * HS, HS), right]

    def fin_to_mate(i, ys, es):
        for part, piece in enumerate((fin_left, fin_right)):
            sem = 2 * NP - 2 + 2 * i + part
            at = piece(fin, c, ys, es)
            push(at, at, ga_r.at[sem], mate)

    def fin_from_mate(i, ys, es):
        for part, piece in enumerate((fin_left, fin_right)):
            sem = 2 * NP - 2 + 2 * i + part
            landed(piece(fin, 1 - c, ys, es), ga_r.at[sem])

    fin[rows(c * HR + (e * NY + y) * HS, HS), left] = whole[:, 0:half].astype(BF16)
    fin[rows(c * HR + (y * NE + e) * HS, HS), right] = whole[:, half:].astype(BF16)
    for i in range(1, NP):
        _, to = in_plane(i)
        at = fin_left(fin, c, y, e)
        push(at, at, ga_r.at[i - 1], to)
        at = fin_right(fin, c, y, e)
        push(at, at, ga_r.at[NP - 2 + i], to)
    fin_to_mate(0, y, e)

    whole = pqo[rows(e * ER, ER), rows(y * YW, YW, 128)].astype(F32)
    for i in range(1, NP):
        landed(rqo.at[i], qp_r.at[0, i - 1])
        whole = whole + rqo[i].astype(F32)
    zqo[...] = whole.astype(BF16)
    for j in range(1, N):
        there, to = in_line(j)
        push(zqo.at[rows(there * SH, SH)], yqo.at[j], qz_r.at[0, j - 1], to)
    whole = psp[...]
    for i in range(1, NP):
        landed(rsp.at[i], qp_r.at[1, i - 1])
        whole = whole + rsp[i]
    zsp[...] = whole
    for j in range(1, N):
        _, to = in_line(j)
        push(zsp, ysp.at[j], qz_r.at[1, j - 1], to)

    cols_copy.wait()
    for j in range(1, N):
        there, _ = in_line(-j)
        landed(outd.at[there], od_r.at[j - 1])
    for j in range(N):
        at = pl.ds(j * T, T)
        out_ref[at, :] = out_ref[at, :] + outd[j].astype(F32)
    out_copy = pltpu.make_async_copy(out_ref, out_any, loc_sem.at[5])
    out_copy.start()

    whole = zqo[rows(n * SH, SH), :].astype(F32)
    for j in range(1, N):
        landed(yqo.at[j], qz_r.at[0, j - 1])
        whole = whole + yqo[j].astype(F32)
    my_cols = rows(y * YW, YW, 128)
    fqo[c, :, my_cols] = whole.astype(BF16)
    at = fqo.at[c, :, my_cols]
    others = [(i, other) for i in range(NY) for other in range(2) if i or other]
    for k, (i, other) in enumerate(others):
        to = (2 * in_rows(i)[0] + (1 - c if other else c), e, n)
        push(at, at, qa_r.at[k], to)
    whole = zsp[...]
    for j in range(1, N):
        landed(ysp.at[j], qz_r.at[1, j - 1])
        whole = whole + ysp[j]
    fsp[:, mine_cols] = whole
    at = fsp.at[:, mine_cols]
    push(at, at, qa_r.at[2 * NY - 1], mate)
    for i in range(1, NP):
        near, _ = in_plane(-i)
        ys, es = lax.div(near, NE), rem(near, NE)
        landed(fin_left(fin, c, ys, es), ga_r.at[i - 1])
        landed(fin_right(fin, c, ys, es), ga_r.at[NP - 2 + i])
        fin_to_mate(i, ys, es)
    at = rows(c * HR, HR)
    g_ref[at, :] = fin[at, :].astype(F32)
    landed(fsp.at[:, other_cols], qa_r.at[2 * NY - 1])
    small_ref[...] = fsp[...]
    for k, (i, other) in enumerate(others):
        near, _ = in_rows(-i)
        at = fqo.at[1 - c if other else c, :, rows(near * YW, YW, 128)]
        landed(at, qa_r.at[k])
    fqo_ref[...] = fqo[...]
    ig_copy.wait()
    out_copy.wait()
    for i in range(NP):
        near, _ = in_plane(-i)
        fin_from_mate(i, lax.div(near, NE), rem(near, NE))
    at = rows((1 - c) * HR, HR)
    g_ref[at, :] = fin[at, :].astype(F32)

    for kind, size in enumerate(sent):
        at = ruler.at[pl.ds(0, size // 256)]
        if kind == 0:
            at = bias.at[pl.ds(0, size // (16 * 128 * 4))]
        pltpu.make_async_remote_copy(
            src_ref=at,
            dst_ref=at,
            send_sem=send_sems.at[kind],
            recv_sem=send_sems.at[kind],
            device_id=mate,
            device_id_type=MESH,
        ).wait_send()
    for valid, copies in maybe_started:

        @pl.when(valid)
        def _(copies=copies):
            for copy in copies:
                copy.wait_send()

    for s, o in enumerate(offsets):
        valid = jnp.logical_and(spot_in_row + o >= 0, spot_in_row + o < z.per_row)

        @pl.when(valid)
        def _(s=s, o=o):
            halo_copy(s, o).wait_send()


def run(z, x, seg, chosen, vectors, q, k, v, o, r, up, down, cot):
    N, G, NP, NY, NE = z.narrow, z.group, z.plane, z.rows_y, z.expert
    T, W, D, R, HP = z.block, z.window, z.width, z.shard, z.head_part
    FL = z.ff_local
    FR = D + FL
    HR = FR // 2
    HS = HR // NP
    YW = D // NY
    SH = R + HP
    ER = N * SH
    QR = G * R
    GR = G * SH
    S = 2 * z.reach
    SMALL = z.small_rows
    vmem = pl.BlockSpec(memory_space=pltpu.VMEM)
    anywhere = pl.BlockSpec(memory_space=pltpu.HBM)
    scratch = [
        ((N * T, D // N), F32),
        ((T, D), F32),
        ((W, D), F32),
        ((W, D), BF16),
        ((QR, D), BF16),
        ((QR, D), BF16),
        ((2, HEAD, D), BF16),
        ((G, 16, 128), F32),
        ((8, 128), F32),
        ((HEAD, 128), F32),
        ((N, FR, D), BF16),
        ((T, D), BF16),
        ((8, z.row_len), F32),
        ((W, 8), F32),
        ((W, HEAD), BF16),
        ((W, HEAD), BF16),
        ((HEAD, W), BF16),
        ((HEAD, W), BF16),
        ((QR, T), F32),
        ((2, HEAD, T), BF16),
        ((2, W, T), BF16),
        ((2, HEAD, T), F32),
        ((QR, T), BF16),
        ((T, D), F32),
        ((T, D), F32),
        ((T, D), BF16),
        ((N, T, FL), BF16),
        ((N, T, FL), BF16),
        ((T, FL), BF16),
        ((T, D), F32),
        ((T, D), F32),
        ((T, D), BF16),
        ((2, HEAD, T), BF16),
        ((W, HEAD), F32),
        ((W, HEAD), F32),
        ((2, HEAD, T), BF16),
        ((QR, T), BF16),
        ((max(S, 1), 2, z.piece, HEAD), BF16),
        ((max(S, 1), 2, z.piece, HEAD), BF16),
        ((T, D), BF16),
        ((N, T, D // N), BF16),
        ((N, FR, D), BF16),
        ((GROUP_BYTES // 256, 128), BF16),
        ((N, HR, D), BF16),
        ((N, HR, D), BF16),
        ((N, NE, HR // NE, D // 2), BF16),
        ((N, NY, HR // NY, D // 2), BF16),
        ((N, HR // NE, D // 2), BF16),
        ((N, HR // NY, D // 2), BF16),
        ((N, NY, HS, D // 2), BF16),
        ((N, NE, HS, D // 2), BF16),
        ((N, HS, D), BF16),
        ((N, HS, D), BF16),
        ((FR, D), BF16),
        ((2, GR, D), BF16),
        ((GR, D), BF16),
        ((GR, D), BF16),
        ((NP, ER, YW), BF16),
        ((ER, YW), BF16),
        ((N, SH, YW), BF16),
        ((2, SH, D), BF16),
        ((SMALL, D), F32),
        ((SMALL, D // 2), F32),
        ((SMALL, D // 2), F32),
        ((NP, SMALL, D // 2), F32),
        ((SMALL, D // 2), F32),
        ((N, SMALL, D // 2), F32),
        ((SMALL, D), F32),
    ]
    pairs = [
        (N - 1,),
        (N - 1,),
        (G - 1,),
        (G - 1,),
        (G - 1,),
        (G - 1,),
        (G - 1,),
        (4, N - 1, max(NE, NY) - 1),
        (N - 1,),
        (N - 1,),
        (N - 1,),
        (max(S, 1),),
        (N,),
        (4, N, max(NE, NY) - 1),
        (N,),
        (4 * NP - 2,),
        (2,),
        (2, NP - 1),
        (2, N - 1),
        (2 * NY,),
    ]
    HALO = 11
    sems = [pltpu.SemaphoreType.DMA((6,)), pltpu.SemaphoreType.DMA((GROUPS,))]
    for at, shape in enumerate(pairs):
        sems += [pltpu.SemaphoreType.DMA(shape)] * (2 if at == HALO else 1)
    sems += [pltpu.SemaphoreType.DMA((2, 2, N)), pltpu.SemaphoreType.DMA((2, N))]
    outs = [
        ((N * T, D // N), F32),
        ((T, D), F32),
        ((FR, D), F32),
        ((2, SH, D), BF16),
        ((SMALL, D), F32),
    ]
    return pl.pallas_call(
        functools.partial(kernel, z),
        out_shape=[pltpu.VMEM(s, t) for s, t in outs],
        in_specs=[anywhere] + [vmem] * (7 + len(vectors)) + [anywhere] * 2 + [vmem],
        out_specs=[pl.BlockSpec(memory_space=pl.ANY)] * 2 + [vmem] * 3,
        scratch_shapes=[pltpu.VMEM(s, t) for s, t in scratch] + sems,
        compiler_params=pltpu.CompilerParams(
            collective_id=0, has_side_effects=True, vmem_limit_bytes=58 * 2**20
        ),
        name="layer",
    )(x, seg, chosen, *vectors, q, k, v, o, r, up, down, cot)


def finish_kernel(
    z,
    out_in,
    ig_in,
    g_in,
    fqo_ref,
    small_ref,
    out_any,
    ig_out,
    g1_ref,
    s1_ref,
    gq_ref,
    qb_ref,
    gk_ref,
    gv_ref,
    vb_ref,
    go_ref,
    ob_ref,
    rw_ref,
    rb_ref,
    g2_ref,
    s2_ref,
    gup_any,
    ub_ref,
    gdown_any,
    db_ref,
    sems,
):
    e, n = lax.axis_index("expert"), lax.axis_index("narrow")
    N, T, D, R, HP, LE = z.narrow, z.block, z.width, z.shard, z.head_part, z.local_experts
    copies = []

    def put(src, dst):
        copies.append(pltpu.make_async_copy(src, dst, sems.at[len(copies)]))
        copies[-1].start()

    put(out_in, out_any)
    put(ig_in, ig_out)
    put(g_in.at[pl.ds(0, D)], gup_any)
    put(g_in.at[pl.ds(D, z.ff_local)], gdown_any)
    gq_ref[...] = fqo_ref[0, 0:R, :].astype(F32)
    go_ref[...] = fqo_ref[1, 0:R, :].astype(F32)
    gk_ref[...] = fqo_ref[0, R : R + HP, :].astype(F32)
    gv_ref[...] = fqo_ref[1, R : R + HP, :].astype(F32)
    g1_ref[...] = small_ref[0:1, :]
    s1_ref[...] = small_ref[1:2, :]
    ob_ref[...] = small_ref[2:3, :]
    g2_ref[...] = small_ref[3:4, :]
    s2_ref[...] = small_ref[4:5, :]
    db_ref[...] = small_ref[5:6, :]
    rb_ref[...] = small_ref[7:8, 0 : z.experts]
    rw_ref[...] = small_ref[16 : 16 + z.experts, :]
    upper = jnp.zeros((1, D), F32)
    for j in range(N):
        upper = jnp.where(n == j, small_ref[8 + j : 9 + j, :], upper)
    ub_ref[...] = upper
    here = e * N + n
    query = pltpu.roll(small_ref[0:8, :], lax.rem(D - here * R, D), 1)
    for i in range(LE):
        qb_ref[i : i + 1, :] = query[6:7, i * HP : (i + 1) * HP]
    value = pltpu.roll(small_ref[8:16, :], lax.rem(D - n * HP, D), 1)
    vb_ref[...] = value[7:8, 0:HP]
    for copy in copies:
        copy.wait()


def finish(z, out, ig, fin, fqo, small):
    N, T, D, R, HP = z.narrow, z.block, z.width, z.shard, z.head_part
    FL = z.ff_local
    vmem = pl.BlockSpec(memory_space=pltpu.VMEM)
    anywhere = pl.BlockSpec(memory_space=pltpu.HBM)
    shapes = [
        (N * T, D // N),
        (T, D),
        (1, D),
        (1, D),
        (R, D),
        (z.local_experts, HP),
        (HP, D),
        (HP, D),
        (1, HP),
        (R, D),
        (1, D),
        (z.experts, D),
        (1, z.experts),
        (1, D),
        (1, D),
        (D, FL),
        (1, FL),
        (FL, D),
        (1, D),
    ]
    return pl.pallas_call(
        functools.partial(finish_kernel, z),
        out_shape=[jax.ShapeDtypeStruct(s, F32) for s in shapes],
        in_specs=[pl.BlockSpec(memory_space=pl.ANY)] * 3 + [vmem] * 2,
        out_specs=[anywhere] * 2 + [vmem] * 13 + [anywhere, vmem, anywhere, vmem],
        scratch_shapes=[
            pltpu.SemaphoreType.DMA((4,)),
        ],
        compiler_params=pltpu.CompilerParams(vmem_limit_bytes=16 * 2**20),
        name="finish",
    )(out, ig, fin, fqo, small)


def per_device(
    inputs,
    seg_ids,
    chosen,
    gain_one,
    shift_one,
    query_w,
    query_b,
    key_w,
    value_w,
    value_b,
    out_w,
    out_b,
    router_w,
    router_b,
    gain_two,
    shift_two,
    up_w,
    up_b,
    down_w,
    down_b,
    cotangent,
):
    narrow = lax.axis_size("narrow")
    e, n = lax.axis_index("expert"), lax.axis_index("narrow")
    z = Sizes(
        lax.axis_size("dp"),
        lax.axis_size("expert"),
        narrow,
        inputs.shape[0],
        inputs.shape[1],
        seg_ids.shape[1],
        query_w.shape[0],
        up_w.shape[1],
    )
    D, R, HP = z.width, z.shard, z.head_part
    vectors = [gain_one, shift_one, out_b, gain_two, shift_two, down_b, up_b]
    vectors = [v.reshape(1, -1) for v in vectors]
    vectors += [query_b, value_b.reshape(1, -1), router_b.reshape(1, -1)]
    parts = run(
        z,
        inputs,
        seg_ids,
        jnp.transpose(chosen),
        vectors,
        jnp.transpose(query_w, (0, 2, 1)).reshape(R, D),
        jnp.transpose(key_w),
        jnp.transpose(value_w),
        out_w.reshape(R, D),
        jnp.transpose(router_w),
        up_w,
        down_w,
        cotangent,
    )
    out, ig, g1, s1, gq, qb, gk, gv, vb, go, ob, rw, rb, g2, s2, gup, ub, gdown, db = finish(
        z, *parts
    )
    return (
        out,
        ig,
        g1.reshape(-1),
        s1.reshape(-1),
        jnp.transpose(gq.reshape(z.local_experts, HP, D), (0, 2, 1)),
        qb,
        jnp.transpose(gk),
        jnp.transpose(gv),
        vb.reshape(-1),
        go.reshape(z.local_experts, HP, D),
        ob.reshape(-1),
        jnp.transpose(rw),
        rb.reshape(-1),
        g2.reshape(-1),
        s2.reshape(-1),
        gup,
        ub.reshape(-1),
        gdown,
        db.reshape(-1),
    )


def solution(mesh):
    return jax.shard_map(
        per_device,
        mesh=mesh,
        in_specs=(
            P("dp", None),
            P("dp", None),
            P("dp", None),
            P(),
            P(),
            P("expert", None, "narrow"),
            P("expert", "narrow"),
            P(None, "narrow"),
            P(None, "narrow"),
            P("narrow"),
            P("expert", "narrow", None),
            P(),
            P(),
            P(),
            P(),
            P(),
            P(None, "narrow"),
            P("narrow"),
            P("narrow", None),
            P(),
            P(("dp", "expert"), "narrow"),
        ),
        out_specs=(
            P(("dp", "expert"), "narrow"),
            P(("dp", "expert", "narrow"), None),
            P(),
            P(),
            P("expert", None, "narrow"),
            P("expert", "narrow"),
            P(None, "narrow"),
            P(None, "narrow"),
            P("narrow"),
            P("expert", "narrow", None),
            P(),
            P(),
            P(),
            P(),
            P(),
            P(None, "narrow"),
            P("narrow"),
            P("narrow", None),
            P(),
        ),
        check_vma=False,
    )
```

```python
import functools
import math

import jax
import jax.numpy as jnp
from jax import lax
from jax.experimental import pallas as pl
from jax.experimental.pallas import tpu as pltpu
from jax.sharding import PartitionSpec as P

HEAD = 64
LONGEST = 256
EPSILON = 1e-05
MASKED = -1000000000.0
GELU_A = math.sqrt(2.0 / math.pi)
GELU_B = 0.044715
F32 = jnp.float32
BF16 = jnp.bfloat16
MESH = pl.DeviceIdType.MESH
GROUP_BYTES = 2**21
GROUPS = 8


def dot(a, b):
    return lax.dot_general(a, b, (((1,), (0,)), ((), ())), preferred_element_type=F32)


def dot_nt(a, b):
    return lax.dot_general(a, b, (((1,), (1,)), ((), ())), preferred_element_type=F32)


def dot_tn(a, b):
    return lax.dot_general(a, b, (((0,), (0,)), ((), ())), preferred_element_type=F32)


def norm_stats(x):
    centred = x - jnp.mean(x, axis=1, keepdims=True)
    inverse = lax.rsqrt(jnp.mean(centred * centred, axis=1, keepdims=True) + EPSILON)
    return centred * inverse, inverse


def rem(a, b):
    return lax.rem(a, b)


class Sizes:
    def __init__(self, dp, expert, narrow, tokens, width, row_len, local_experts, ff_local):
        self.dp, self.expert, self.narrow = dp, expert, narrow
        self.tokens, self.width, self.row_len = tokens, width, row_len
        self.local_experts = local_experts
        self.experts = local_experts * expert
        self.group = expert * narrow
        self.block = tokens // self.group
        self.rows_y = dp // 2
        self.plane = self.rows_y * expert
        self.ff_local = ff_local
        self.head_part = HEAD // narrow
        self.shard = local_experts * self.head_part
        self.per_row = row_len // self.block
        spans = [
            min(row_len, (j + 1) * self.block + LONGEST) - max(0, j * self.block - LONGEST)
            for j in range(self.per_row)
        ]
        self.window = max(spans)
        self.reach = max(1, LONGEST // self.block) if self.per_row > 1 else 0
        self.piece = min(self.block, LONGEST)
        self.tile = min(256, self.block)
        self.up_rows = narrow * ff_local // width
        self.small_rows = 24


def kernel(
    z,
    x_any,
    seg_ref,
    chosen_ref,
    g1_ref,
    s1_ref,
    ob_ref,
    g2_ref,
    s2_ref,
    db_ref,
    ub_ref,
    qb_ref,
    vb_ref,
    rb_ref,
    q_ref,
    k_ref,
    v_ref,
    o_ref,
    r_ref,
    up_any,
    down_any,
    cot_ref,
    out_any,
    ig_any,
    g_ref,
    fqo_ref,
    small_ref,
    out_ref,
    ig_ref,
    xw,
    rw,
    wq,
    wo,
    wkv,
    bias,
    corner,
    vcol,
    ffw,
    cot,
    segs,
    segc,
    kn,
    vn,
    kt,
    vt,
    qt,
    qk,
    prob,
    mix,
    mixg,
    hid,
    acc,
    second,
    active,
    slope,
    ugrad,
    sgrad,
    hgrad,
    hgb,
    mgk,
    dk,
    dv,
    dq,
    dqt,
    halo_out,
    halo_in,
    delta,
    outd,
    gsend,
    ruler,
    crecv,
    psend,
    pea,
    pya,
    mea,
    mya,
    pyb,
    peb,
    zsend,
    zrecv,
    fin,
    gqo,
    cqo,
    pqo,
    rqo,
    zqo,
    yqo,
    fqo,
    sp,
    csp,
    psp,
    rsp,
    zsp,
    ysp,
    fsp,
    loc_sem,
    send_sems,
    w_r,
    wm_r,
    b_r,
    q_r,
    qm_r,
    o_r,
    om_r,
    fp_r,
    fm_r,
    ct_r,
    od_r,
    hl_s,
    hl_r,
    gc_r,
    gp_r,
    gz_r,
    ga_r,
    qc_r,
    qp_r,
    qz_r,
    qa_r,
    fz_s,
    fz_r,
):
    d, e, n = lax.axis_index("dp"), lax.axis_index("expert"), lax.axis_index("narrow")
    c, y = rem(d, 2), lax.div(d, 2)
    N, G, NP, NE, NY = z.narrow, z.group, z.plane, z.expert, z.rows_y
    T, W, D, R, HP, LE = z.block, z.window, z.width, z.shard, z.head_part, z.local_experts
    FL = z.ff_local
    half = D // 2
    here = e * N + n
    spot = y * NE + e
    mate = (d + 1 - 2 * c, e, n)

    def in_group(j):
        at = rem(here + j + G, G)
        return at, (d, lax.div(at, N), rem(at, N))

    def in_plane(j):
        at = rem(spot + j + NP, NP)
        return at, (2 * lax.div(at, NE) + c, rem(at, NE), n)

    def in_line(j):
        at = rem(n + j + N, N)
        return at, (d, e, at)

    def in_rows(j):
        at = rem(y + j + NY, NY)
        return at, (2 * at + c, e, n)

    sent = [0, 0]
    noted = {}

    def either(name, valid, block):
        again = name in noted
        kinds = noted.setdefault(name, [])
        turn = iter(list(kinds)) if again else None

        @pl.when(valid)
        def _():
            mode.append((kinds, turn))
            block()
            mode.pop()

    mode = []

    def push(src, dst, recv, device):
        size = math.prod(src.shape) * jnp.dtype(src.dtype).itemsize
        if mode and mode[-1][1] is not None:
            kind = next(mode[-1][1])
        else:
            kind = 0
            if not (src.shape[-1] == 128 and src.dtype == F32):
                if sent[-1] + size > GROUP_BYTES:
                    sent.append(0)
                kind = len(sent) - 1
            sent[kind] += size
            if mode:
                mode[-1][0].append(kind)
        copy = pltpu.make_async_remote_copy(
            src_ref=src,
            dst_ref=dst,
            send_sem=send_sems.at[kind],
            recv_sem=recv,
            device_id=device,
            device_id_type=MESH,
        )
        copy.start()

    def landed(dst, recv):
        pltpu.make_async_remote_copy(
            src_ref=dst,
            dst_ref=dst,
            send_sem=recv,
            recv_sem=recv,
            device_id=mate,
            device_id_type=MESH,
        ).wait_recv()

    def landed_all(count, of, recv):
        size = count * math.prod(of.shape) * jnp.dtype(of.dtype).itemsize
        landed(ruler.at[pl.ds(0, size // 256)], recv)

    def rows(start, size, step=16):
        return pl.ds(pl.multiple_of(start, step), size)

    start = here * T
    row = lax.div(start, z.row_len)
    spot_in_row = rem(here, z.per_row)
    base = row * z.row_len
    ws = jnp.minimum(jnp.maximum(spot_in_row * T - LONGEST, 0), z.row_len - W)
    off = spot_in_row * T - ws
    own = rows(off, T, 128)

    x_copy = pltpu.make_async_copy(x_any.at[rows(base + ws, W, 128)], xw, loc_sem.at[0])
    x_copy.start()
    up_copy = pltpu.make_async_copy(up_any, ffw.at[n, pl.ds(0, D)], loc_sem.at[1])
    up_copy.start()
    down_copy = pltpu.make_async_copy(down_any, ffw.at[n, pl.ds(D, FL)], loc_sem.at[2])
    down_copy.start()
    cols_copy = pltpu.make_async_copy(
        x_any.at[rows(e * N * T, N * T, 128), rows(n * (D // N), D // N, 128)], out_ref, loc_sem.at[3]
    )
    cols_copy.start()
    wq[rows(here * R, R)] = q_ref[...]
    wo[rows(here * R, R)] = o_ref[...]
    wkv[0, rows(n * HP, HP)] = k_ref[...]
    wkv[1, rows(n * HP, HP)] = v_ref[...]
    bias[here] = jnp.zeros((16, 128), F32)
    for i in range(FL // 128):
        bias[here, i : i + 1, :] = ub_ref[0:1, i * 128 : (i + 1) * 128]
    bias[here, 8 : 8 + LE, 0:HP] = qb_ref[...]
    bias[here, 7:8, 0:HP] = vb_ref[...]

    barrier = pltpu.get_barrier_semaphore()
    pl.semaphore_signal(barrier, inc=1, device_id=mate, device_id_type=MESH)
    for j in range(1, NP):
        pl.semaphore_signal(barrier, inc=1, device_id=in_plane(j)[1], device_id_type=MESH)
    for j in range(1, G):
        pl.semaphore_signal(barrier, inc=1, device_id=in_group(j)[1], device_id_type=MESH)
    for j in range(1, NY):
        to = (2 * in_rows(j)[0] + 1 - c, e, n)
        pl.semaphore_signal(barrier, inc=1, device_id=to, device_id_type=MESH)
    pl.semaphore_wait(barrier, NP + G + NY - 2)

    mine_cols = rows(c * half, half, 128)
    other_cols = rows((1 - c) * half, half, 128)

    def in_expert(i):
        at = rem(e + i + NE, NE)
        return at, (d, at, n)

    def shard_at(i, j):
        return rem(e - i + NE, NE) * N + rem(n - j + N, N)

    def spread_start(part, recv):
        for j in range(1, N):
            at = part(here)
            push(at, at, recv.at[j - 1], in_line(j)[1])
        for i in range(1, NE):
            at = part(here)
            push(at, at, recv.at[i * N - 1], in_expert(i)[1])

    def spread_on(part, recv, to_mate):
        for j in range(1, N):
            at = part(shard_at(0, j))
            landed(at, recv.at[j - 1])
            for i in range(1, NE):
                push(at, at, recv.at[i * N + j - 1], in_expert(i)[1])
            if to_mate is not None:
                push(at, at, to_mate.at[0], mate)

    def spread_end(part, recv, to_mate):
        for i in range(1, NE):
            for j in range(N):
                at = part(shard_at(i, j))
                landed(at, recv.at[i * N + j - 1])
                if to_mate is not None:
                    push(at, at, to_mate.at[0], mate)

    def spread_wait(part, to_mate):
        landed_all(G - 1, part(0), to_mate.at[0])

    def bias_part(g):
        return bias.at[g]

    def q_part(g):
        return wq.at[rows(g * R, R), mine_cols]

    def q_other(g):
        return wq.at[rows(g * R, R), other_cols]

    def o_part(g):
        return wo.at[rows(g * R, R), mine_cols]

    def o_other(g):
        return wo.at[rows(g * R, R), other_cols]

    for j in range(1, N):
        at = wkv.at[c, rows(n * HP, HP)]
        push(at, at, w_r.at[j - 1], in_line(j)[1])
    spread_start(q_part, q_r)
    spread_start(bias_part, b_r)
    up_copy.wait()
    down_copy.wait()
    FR = D + FL

    left, right = pl.ds(0, half), pl.ds(half, half)
    HR = FR // 2
    HS = HR // NP
    HA, HB = HR // NE, HR // NY
    def left_slice(of, ys, es):
        return ffw.at[of, rows(c * HR + (es * NY + ys) * HS, HS), left]

    def right_slice(of, ys, es):
        return ffw.at[of, rows(c * HR + (ys * NE + es) * HS, HS), right]

    def left_half(of, es):
        return ffw.at[of, rows(c * HR + es * HA, HA), left]

    def right_half(of, ys):
        return ffw.at[of, rows(c * HR + ys * HB, HB), right]

    def by_distance(at):
        return sorted((o for o in range(N) if o != at), key=lambda o: (abs(o - at), o if 2 * at >= N else -o))

    def pick(choices):
        value = choices[0]
        for at in range(1, N):
            value = jnp.where(n == at, choices[at], value)
        return value

    shard_of = [n] + [pick([by_distance(at)[k] for at in range(N)]) for k in range(N - 1)]
    maybe_started = []

    def line_push(of, step, valid):
        of = jnp.clip(of, 0, N - 1)
        to = (d, e, jnp.clip(n + step, 0, N - 1))
        way = (step + 1) // 2
        copies = [
            pltpu.make_async_remote_copy(
                src_ref=at,
                dst_ref=at,
                send_sem=fz_s.at[part, way, of],
                recv_sem=fz_r.at[part, of],
                device_id=to,
                device_id_type=MESH,
            )
            for part, at in enumerate((left_slice(of, y, e), right_slice(of, y, e)))
        ]

        @pl.when(valid)
        def _():
            for copy in copies:
                copy.start()

        maybe_started.append((valid, copies))

    def line_landed(of, valid):
        of = jnp.clip(of, 0, N - 1)

        @pl.when(valid)
        def _():
            landed(left_slice(of, y, e), fz_r.at[0, of])
            landed(right_slice(of, y, e), fz_r.at[1, of])

    def shards_start():
        line_push(n, 1, n + 1 < N)
        line_push(n, -1, n > 0)

    def shards_on(hop):
        line_landed(n - hop, n >= hop)
        line_push(n - hop, 1, jnp.logical_and(n >= hop, n + 1 < N))
        line_landed(n + hop, n + hop < N)
        line_push(n + hop, -1, jnp.logical_and(n + hop < N, n > 0))

    def plane_on(j):
        there = shard_of[j]
        at = left_slice(there, y, e)
        for i in range(1, NY):
            push(at, at, fp_r.at[0, j - 1, i - 1], in_rows(i)[1])
        at = right_slice(there, y, e)
        for i in range(1, NE):
            push(at, at, fp_r.at[1, j - 1, i - 1], in_expert(i)[1])

    def plane_turn(j):
        there = shard_of[j]
        for i in range(1, NY):
            near, _ = in_rows(-i)
            landed(left_slice(there, near, e), fp_r.at[0, j - 1, i - 1])
        at = left_half(there, e)
        for i in range(1, NE):
            push(at, at, fp_r.at[2, j - 1, i - 1], in_expert(i)[1])
        for i in range(1, NE):
            near, _ = in_expert(-i)
            landed(right_slice(there, y, near), fp_r.at[1, j - 1, i - 1])
        at = right_half(there, y)
        for i in range(1, NY):
            push(at, at, fp_r.at[3, j - 1, i - 1], in_rows(i)[1])

    def mate_on(j):
        there = shard_of[j]
        for i in range(1, NE):
            near, _ = in_expert(-i)
            landed(left_half(there, near), fp_r.at[2, j - 1, i - 1])
        for i in range(1, NY):
            near, _ = in_rows(-i)
            landed(right_half(there, near), fp_r.at[3, j - 1, i - 1])
        at = ffw.at[there, rows(c * HR, HR)]
        push(at, at, fm_r.at[j - 1], mate)

    x_copy.wait()
    gain_one, shift_one = g1_ref[...], s1_ref[...]

    def norm_one(i, carry):
        at = rows(i * 128, 128, 128)
        unit, _ = norm_stats(xw[at, :])
        rw[at, :] = (unit * gain_one + shift_one).astype(BF16)
        return carry

    lax.fori_loop(0, W // 128, norm_one, 0)

    seg_all = seg_ref[...].astype(F32)
    row_id = lax.broadcasted_iota(jnp.int32, seg_all.shape, 0)
    seg_here = jnp.sum(jnp.where(row_id == row, seg_all, 0.0), axis=0, keepdims=True)
    segs[...] = jnp.broadcast_to(seg_here, segs.shape)
    segc[...] = jnp.transpose(segs[:, rows(ws, W, 128)])
    seg_own = segs[0:1, rows(spot_in_row * T, T, 128)]
    corner[...] = jnp.zeros_like(corner)
    corner[:, 0 : z.experts] = jnp.broadcast_to(rb_ref[...], (8, z.experts))
    router_col = jnp.transpose(corner[...])[0 : z.experts, 0:1]
    logits = dot_nt(r_ref[...], rw[own, :]) + router_col
    expert_id = lax.broadcasted_iota(jnp.int32, (z.experts, T), 0)
    hot, picked = [], []
    for k in range(2):
        chosen = chosen_ref[k : k + 1, rows(start, T, 128)]
        hot.append((expert_id == chosen).astype(F32))
        picked.append(jnp.sum(logits * hot[k], axis=0, keepdims=True))
    top = jnp.maximum(picked[0], picked[1])
    raised = [jnp.exp(p - top) for p in picked]
    total = raised[0] + raised[1]
    gate = [r / total for r in raised]

    for j in range(1, N):
        there, _ = in_line(-j)
        at = wkv.at[c, rows(there * HP, HP)]
        landed(at, w_r.at[j - 1])
        push(at, at, wm_r.at[0], mate)
    spread_on(q_part, q_r, qm_r)
    spread_on(bias_part, b_r, None)
    shards_start()
    spread_start(o_part, o_r)

    landed_all(N - 1, wkv.at[0, pl.ds(0, HP)], wm_r.at[0])
    kn[...] = dot_nt(rw[...], wkv[0]).astype(BF16)
    kt[...] = dot_nt(wkv[0], rw[...]).astype(BF16)
    spread_end(q_part, q_r, qm_r)
    spread_end(bias_part, b_r, None)
    columns = [jnp.transpose(bias[g, 0:16, :]) for g in range(G)]
    for part in range(N):
        vcol[part * HP : (part + 1) * HP, :] = jnp.broadcast_to(columns[part][0:HP, 7:8], (HP, 128))
    value_row = jnp.transpose(vcol[...])[0:1, :]
    vn[...] = (dot_nt(rw[...], wkv[1]) + value_row).astype(BF16)
    vt[...] = (dot_nt(wkv[1], rw[...]) + vcol[:, 0:1]).astype(BF16)

    spread_wait(q_other, qm_r)
    qt[...] = dot_nt(wq[...], rw[own, :])

    def expert_rows(at, i, part):
        return ((at * N + part) * LE + i) * HP

    for part in range(N):
        chosen_rows = [jnp.zeros((HP, T), F32), jnp.zeros((HP, T), F32)]
        for at in range(NE):
            g = at * N + part
            for i in range(LE):
                lo = expert_rows(at, i, part)
                one = qt[lo : lo + HP, :] + columns[g][0:HP, 8 + i : 9 + i]
                for k in range(2):
                    chosen_rows[k] = chosen_rows[k] + one * hot[k][at * LE + i : at * LE + i + 1, :]
        for k in range(2):
            qk[k, part * HP : (part + 1) * HP, :] = chosen_rows[k].astype(BF16)

    scale = 1.0 / math.sqrt(HEAD)
    TL = z.tile
    tiles = T // TL
    seg_tiles = [seg_own[:, i * TL : (i + 1) * TL] for i in range(tiles)]

    def attend(k):
        for i in range(tiles):
            at = pl.ds(i * TL, TL)
            scores = dot(kn[...], qk[k, :, at]) * scale
            scores = jnp.where(segc[:, 0:1] == seg_tiles[i], scores, MASKED)
            high = jnp.max(scores, axis=0, keepdims=True)
            raised_scores = jnp.exp(scores - high)
            low = (raised_scores * (1.0 / jnp.sum(raised_scores, axis=0, keepdims=True))).astype(BF16)
            prob[k, :, at] = low
            mix[k, :, at] = dot(vt[...], low)

    attend(0)
    attend(1)
    shards_on(1)
    plane_on(1)
    spread_on(o_part, o_r, om_r)
    plane_turn(1)
    shards_on(2)
    plane_on(2)
    CW = D // N
    cot[:, rows(n * CW, CW, 128)] = cot_ref[rows(n * T, T, 128), :]
    for j in range(1, N):
        there, to = in_line(j)
        push(
            cot_ref.at[rows(there * T, T, 128)],
            cot.at[:, rows(n * CW, CW, 128)],
            ct_r.at[0],
            to,
        )
    outer = jnp.logical_or(n >= 3, n + 3 < N)
    inner = jnp.logical_not(outer)
    either("on", inner, lambda: plane_on(3))
    spread_end(o_part, o_r, om_r)

    for part in range(N):
        for at in range(NE):
            for i in range(LE):
                lo = expert_rows(at, i, part)
                x = at * LE + i
                gated = jnp.zeros((HP, T), F32)
                for k in range(2):
                    rounded_mix = mix[k, part * HP : (part + 1) * HP, :].astype(BF16).astype(F32)
                    gated = gated + rounded_mix * (hot[k][x : x + 1, :] * gate[k])
                mixg[lo : lo + HP, :] = gated.astype(BF16)
    spread_wait(o_other, om_r)
    out_b, down_b = ob_ref[...], db_ref[...]
    gain_two, shift_two = g2_ref[...], s2_ref[...]
    attention = dot_tn(mixg[...], wo[...]) + out_b
    acc[...] = attention + down_b
    hid[...] = xw[own, :] + attention

    def norm_two(i, carry):
        at = rows(i * 128, 128, 128)
        unit, _ = norm_stats(hid[at, :])
        second[at, :] = (unit * gain_two + shift_two).astype(BF16)
        return carry

    lax.fori_loop(0, T // 128, norm_two, 0)
    sgrad[...] = jnp.zeros_like(sgrad)

    def core_start(j):
        push(
            gsend.at[j, rows((1 - c) * HR, HR)], crecv.at[j], gc_r.at[j], mate
        )

    def plane_start(j):
        landed(crecv.at[j], gc_r.at[j])
        psend[j] = (
            gsend[j, rows(c * HR, HR), :].astype(F32) + crecv[j].astype(F32)
        ).astype(BF16)
        for i in range(1, NE):
            there, to = in_expert(i)
            src = psend.at[j, rows(there * HA, HA), left]
            push(src, pea.at[j, i], gp_r.at[0, j, i - 1], to)
        for i in range(1, NY):
            there, to = in_rows(i)
            src = psend.at[j, rows(there * HB, HB), right]
            push(src, pya.at[j, i], gp_r.at[1, j, i - 1], to)

    def plane_middle(j):
        whole = psend[j, rows(e * HA, HA), left].astype(F32)
        for i in range(1, NE):
            landed(pea.at[j, i], gp_r.at[0, j, i - 1])
            whole = whole + pea[j, i].astype(F32)
        mea[j] = whole.astype(BF16)
        for i in range(1, NY):
            there, to = in_rows(i)
            src = mea.at[j, rows(there * HS, HS)]
            push(src, pyb.at[j, i], gp_r.at[2, j, i - 1], to)
        whole = psend[j, rows(y * HB, HB), right].astype(F32)
        for i in range(1, NY):
            landed(pya.at[j, i], gp_r.at[1, j, i - 1])
            whole = whole + pya[j, i].astype(F32)
        mya[j] = whole.astype(BF16)
        for i in range(1, NE):
            there, to = in_expert(i)
            src = mya.at[j, rows(there * HS, HS)]
            push(src, peb.at[j, i], gp_r.at[3, j, i - 1], to)

    def line_start(j):
        whole = mea[j, rows(y * HS, HS), :].astype(F32)
        for i in range(1, NY):
            landed(pyb.at[j, i], gp_r.at[2, j, i - 1])
            whole = whole + pyb[j, i].astype(F32)
        zsend[j, :, left] = whole.astype(BF16)
        whole = mya[j, rows(e * HS, HS), :].astype(F32)
        for i in range(1, NE):
            landed(peb.at[j, i], gp_r.at[3, j, i - 1])
            whole = whole + peb[j, i].astype(F32)
        zsend[j, :, right] = whole.astype(BF16)
        if j:
            push(zsend.at[j], zrecv.at[n], gz_r.at[n], (d, e, shard_of[j]))

    def forward(j):
        there = shard_of[j]
        if j:
            landed(ffw.at[there, rows((1 - c) * HR, HR)], fm_r.at[j - 1])
        up_b = jnp.concatenate(
            [bias[e * N + there, i : i + 1, :] for i in range(FL // 128)], axis=1
        )

        def feed(i, carry):
            at = rows(i * TL, TL, 128)
            upper = dot(second[at, :], ffw[there, 0:D, :]) + up_b
            square = upper * upper
            t = jnp.tanh(upper * (GELU_A + (GELU_A * GELU_B) * square))
            one = 0.5 + 0.5 * t
            low = (upper * one).astype(BF16)
            active[j, at, :] = low
            slope[j, at, :] = (
                one + (0.5 * upper) * (1.0 - t * t) * (GELU_A + (3.0 * GELU_A * GELU_B) * square)
            ).astype(BF16)
            acc[at, :] = acc[at, :] + dot(low, ffw[there, D : D + FL, :])
            return carry

        lax.fori_loop(0, T // TL, feed, 0)

    def backward(j):
        there = shard_of[j]

        def feed_back(i, carry):
            at = rows(i * TL, TL, 128)
            back = dot_nt(cot[at, :], ffw[there, D : D + FL, :]) * slope[j, at, :].astype(F32)
            back = back.astype(BF16)
            ugrad[at, :] = back
            sgrad[at, :] = sgrad[at, :] + dot_nt(back, ffw[there, 0:D, :])
            return carry

        lax.fori_loop(0, T // TL, feed_back, 0)
        sp[pl.ds(8 + there, 1), :] = jnp.sum(ugrad[...].astype(F32), axis=0, keepdims=True)
        gsend[j, 0:D, :] = dot_tn(second[...], ugrad[...]).astype(BF16)
        gsend[j, D : D + FL, :] = dot_tn(active[j], cot[...]).astype(BF16)
        core_start(j)

    def cotangent_wait():
        landed_all(N - 1, cot.at[:, pl.ds(0, CW)], ct_r.at[0])

    def last_forward():
        forward(3)
        delta[...] = acc[...].astype(BF16)
        outd[n] = delta[:, rows(n * CW, CW, 128)]
        for j in range(1, N):
            there, to = in_line(j)
            push(delta.at[:, rows(there * CW, CW, 128)], outd.at[n], od_r.at[0], to)

    forward(0)
    plane_turn(2)
    mate_on(1)
    either("turn", inner, lambda: plane_turn(3))
    forward(1)
    shards_on(3)
    either("on", outer, lambda: plane_on(3))
    mate_on(2)
    either("turn", outer, lambda: plane_turn(3))
    either("mate", inner, lambda: mate_on(3))
    cotangent_wait()
    backward(1)
    either("mate", outer, lambda: mate_on(3))
    forward(2)
    plane_start(1)
    backward(2)
    last_forward()
    plane_start(2)
    backward(3)
    backward(0)
    plane_start(3)
    plane_middle(1)

    zero_row = jnp.zeros((1, D), F32)

    def norm_two_back(i, carry):
        at = rows(i * 128, 128, 128)
        unit, inverse = norm_stats(hid[at, :])
        grad = sgrad[at, :]
        scaled = grad * gain_two
        back = inverse * (
            scaled
            - jnp.mean(scaled, axis=1, keepdims=True)
            - unit * jnp.mean(scaled * unit, axis=1, keepdims=True)
        )
        top_grad = cot[at, :].astype(F32)
        whole = top_grad + back
        hgrad[at, :] = whole
        hgb[at, :] = whole.astype(BF16)
        parts = (grad * unit, grad, whole, top_grad)
        return tuple(a + jnp.sum(b, axis=0, keepdims=True) for a, b in zip(carry, parts))

    sums = lax.fori_loop(0, T // 128, norm_two_back, (zero_row,) * 4)
    sp[3:4, :] = sums[0]
    sp[4:5, :] = sums[1]
    sp[2:3, :] = sums[2]
    sp[5:6, :] = sums[3]

    plane_start(0)

    SH = R + HP
    out_grad = dot(mixg[...], hgb[...]).astype(BF16)
    for g in range(G):
        gqo[1, g * SH : g * SH + R, :] = out_grad[g * R : (g + 1) * R, :]
    qt[...] = dot_nt(wo[...], hgb[...])
    gate_grad = [jnp.zeros((1, T), F32), jnp.zeros((1, T), F32)]
    for part in range(N):
        picked_rows = [jnp.zeros((HP, T), F32), jnp.zeros((HP, T), F32)]
        for at in range(NE):
            for i in range(LE):
                lo = expert_rows(at, i, part)
                one = qt[lo : lo + HP, :]
                x = at * LE + i
                for k in range(2):
                    picked_rows[k] = picked_rows[k] + one * hot[k][x : x + 1, :]
        for k in range(2):
            span = slice(part * HP, (part + 1) * HP)
            rounded_mix = mix[k, span, :].astype(BF16).astype(F32)
            gate_grad[k] = gate_grad[k] + jnp.sum(picked_rows[k] * rounded_mix, axis=0, keepdims=True)
            mgk[k, span, :] = (picked_rows[k] * gate[k]).astype(BF16)
    middle = gate[0] * gate_grad[0] + gate[1] * gate_grad[1]
    logit_grad = sum(hot[k] * (gate[k] * (gate_grad[k] - middle)) for k in range(2))
    logit_low = logit_grad.astype(BF16)

    def attend_back(k):
        for i in range(tiles):
            at = pl.ds(i * TL, TL)
            low = prob[k, :, at]
            p = low.astype(F32)
            prob_grad = dot(vn[...], mgk[k, :, at])
            inner = jnp.sum(p * prob_grad, axis=0, keepdims=True)
            score = (p * (prob_grad - inner)).astype(BF16)
            dq[k, :, at] = (dot(kt[...], score) * scale).astype(BF16)
            key_part = dot_nt(score, qk[k, :, at])
            value_part = dot_nt(low, mgk[k, :, at])
            if k == 0 and i == 0:
                dk[...] = key_part
                dv[...] = value_part
            else:
                dk[...] = dk[...] + key_part
                dv[...] = dv[...] + value_part

    attend_back(0)
    attend_back(1)
    plane_middle(2)

    H, PC = z.reach, z.piece
    offsets = [o for o in range(-H, H + 1) if o]
    inside = T >= LONGEST

    def halo_source(o):
        if inside:
            return (spot_in_row + 1) * T - ws if o > 0 else spot_in_row * T - LONGEST - ws
        return (spot_in_row + o) * T - ws

    def halo_copy(s, o):
        to = rem(here + o + G, G)
        return pltpu.make_async_remote_copy(
            src_ref=halo_out.at[s],
            dst_ref=halo_in.at[s],
            send_sem=hl_s.at[s],
            recv_sem=hl_r.at[s],
            device_id=(d, lax.div(to, N), rem(to, N)),
            device_id_type=MESH,
        )

    for s, o in enumerate(offsets):
        valid = jnp.logical_and(spot_in_row + o >= 0, spot_in_row + o < z.per_row)

        @pl.when(valid)
        def _(s=s, o=o):
            at = rows(halo_source(o), PC, 128)
            halo_out[s, 0] = (dk[at, :] * scale).astype(BF16)
            halo_out[s, 1] = dv[at, :].astype(BF16)
            halo_copy(s, o).start()

    for part in range(N):
        for at in range(NE):
            for i in range(LE):
                lo = expert_rows(at, i, part)
                x = at * LE + i
                span = slice(part * HP, (part + 1) * HP)
                one = dq[0, span, :].astype(F32) * hot[0][x : x + 1, :]
                one = one + dq[1, span, :].astype(F32) * hot[1][x : x + 1, :]
                dqt[lo : lo + HP, :] = one.astype(BF16)
    query_w_grad = dot(dqt[...], rw[own, :]).astype(BF16)
    key_w_grad = dot_tn((dk[...] * scale).astype(BF16), rw[...]).astype(BF16)
    value_w_grad = dot_tn(dv[...].astype(BF16), rw[...]).astype(BF16)
    for g in range(G):
        shared = slice((g % N) * HP, (g % N + 1) * HP)
        gqo[0, g * SH : g * SH + R, :] = query_w_grad[g * R : (g + 1) * R, :]
        gqo[0, g * SH + R : (g + 1) * SH, :] = key_w_grad[shared, :]
        gqo[1, g * SH + R : (g + 1) * SH, :] = value_w_grad[shared, :]
    push(gqo.at[1 - c], cqo, qc_r.at[0], mate)
    plane_middle(3)
    line_start(1)
    ones = jnp.ones((8, T), BF16)
    sp[6:7, :] = dot_nt(ones, dqt[...])[0:1, :]
    sp[7:8, :] = jnp.zeros((1, D), F32)
    sp[7:8, 0 : z.experts] = jnp.transpose(
        jnp.broadcast_to(jnp.sum(logit_grad, axis=1, keepdims=True), (z.experts, 128))
    )[0:1, :]
    acc[...] = dot_tn(dqt[...], wq[...]) + dot_tn(logit_low, r_ref[...])
    sp[16:24, :] = dot(logit_low, rw[own, :])
    sp[15:16, :] = jnp.zeros((1, D), F32)
    sp[15:16, 0:HEAD] = jnp.sum(dv[...], axis=0, keepdims=True)
    YW = D // NY
    ER = N * SH
    landed(cqo, qc_r.at[0])
    plane_middle(0)
    pqo[...] = (gqo[c].astype(F32) + cqo[...].astype(F32)).astype(BF16)
    for i in range(1, NP):
        there, to = in_plane(i)
        src = pqo.at[rows(rem(there, NE) * ER, ER), rows(lax.div(there, NE) * YW, YW, 128)]
        push(src, rqo.at[i], qp_r.at[0], to)
    line_start(2)
    line_start(3)

    dk[...] = dk[...] * scale
    for s, o in enumerate(offsets):
        back_valid = jnp.logical_and(spot_in_row - o >= 0, spot_in_row - o < z.per_row)

        @pl.when(back_valid)
        def _(s=s, o=o):
            halo_copy(s, o).wait_recv()
            at = off if (not inside or o > 0) else off + T - LONGEST
            at = rows(at, PC, 128)
            dk[at, :] = dk[at, :] + halo_in[s, 0].astype(F32)
            dv[at, :] = dv[at, :] + halo_in[s, 1].astype(F32)

    key_grad = dk[own, :]
    value_grad = dv[own, :]
    key_low, value_low = key_grad.astype(BF16), value_grad.astype(BF16)
    acc[...] = acc[...] + dot(key_low, wkv[0]) + dot(value_low, wkv[1])

    def norm_one_back(i, carry):
        at = rows(i * 128, 128, 128)
        unit, inverse = norm_stats(xw[rows(off + i * 128, 128, 128), :])
        grad = acc[at, :]
        scaled = grad * gain_one
        back = inverse * (
            scaled
            - jnp.mean(scaled, axis=1, keepdims=True)
            - unit * jnp.mean(scaled * unit, axis=1, keepdims=True)
        )
        ig_ref[at, :] = hgrad[at, :] + back
        parts = (grad * unit, grad)
        return tuple(a + jnp.sum(b, axis=0, keepdims=True) for a, b in zip(carry, parts))

    sums = lax.fori_loop(0, T // 128, norm_one_back, (zero_row,) * 2)
    ig_copy = pltpu.make_async_copy(ig_ref, ig_any, loc_sem.at[4])
    ig_copy.start()
    sp[0:1, :] = sums[0]
    sp[1:2, :] = sums[1]
    for j in range(8 + N, 15):
        sp[j : j + 1, :] = zero_row
    push(sp.at[:, other_cols], csp, qc_r.at[1], mate)

    landed(csp, qc_r.at[1])
    psp[...] = sp[:, mine_cols] + csp[...]
    for i in range(1, NP):
        _, to = in_plane(i)
        push(psp, rsp.at[i], qp_r.at[1], to)

    line_start(0)

    whole = zsend[0].astype(F32)
    for j in range(1, N):
        there, _ = in_line(-j)
        landed(zrecv.at[there], gz_r.at[there])
        whole = whole + zrecv[there].astype(F32)

    def fin_left(buffer, core, ys, es):
        return buffer.at[rows(core * HR + (es * NY + ys) * HS, HS), left]

    def fin_right(buffer, core, ys, es):
        return buffer.at[rows(core * HR + (ys * NE + es) * HS, HS), right]

    def fin_to_mate(ys, es):
        for piece in (fin_left, fin_right):
            at = piece(fin, c, ys, es)
            push(at, at, ga_r.at[2 * NP - 2], mate)

    fin[rows(c * HR + (e * NY + y) * HS, HS), left] = whole[:, 0:half].astype(BF16)
    fin[rows(c * HR + (y * NE + e) * HS, HS), right] = whole[:, half:].astype(BF16)
    for i in range(1, NP):
        _, to = in_plane(i)
        at = fin_left(fin, c, y, e)
        push(at, at, ga_r.at[i - 1], to)
        at = fin_right(fin, c, y, e)
        push(at, at, ga_r.at[NP - 2 + i], to)
    fin_to_mate(y, e)

    whole = pqo[rows(e * ER, ER), rows(y * YW, YW, 128)].astype(F32)
    landed_all(NP - 1, rqo.at[0], qp_r.at[0])
    for i in range(1, NP):
        whole = whole + rqo[i].astype(F32)
    zqo[...] = whole.astype(BF16)
    for j in range(1, N):
        there, to = in_line(j)
        push(zqo.at[rows(there * SH, SH)], yqo.at[j], qz_r.at[0], to)
    whole = psp[...]
    landed_all(NP - 1, rsp.at[0], qp_r.at[1])
    for i in range(1, NP):
        whole = whole + rsp[i]
    zsp[...] = whole
    for j in range(1, N):
        _, to = in_line(j)
        push(zsp, ysp.at[j], qz_r.at[1], to)

    cols_copy.wait()
    landed_all(N - 1, outd.at[0], od_r.at[0])
    for j in range(N):
        at = pl.ds(j * T, T)
        out_ref[at, :] = out_ref[at, :] + outd[j].astype(F32)
    out_copy = pltpu.make_async_copy(out_ref, out_any, loc_sem.at[5])
    out_copy.start()

    whole = zqo[rows(n * SH, SH), :].astype(F32)
    landed_all(N - 1, yqo.at[0], qz_r.at[0])
    for j in range(1, N):
        whole = whole + yqo[j].astype(F32)
    my_cols = rows(y * YW, YW, 128)
    fqo[c, :, my_cols] = whole.astype(BF16)
    at = fqo.at[c, :, my_cols]
    others = [(i, other) for i in range(NY) for other in range(2) if i or other]
    for i, other in others:
        to = (2 * in_rows(i)[0] + (1 - c if other else c), e, n)
        push(at, at, qa_r.at[0], to)
    whole = zsp[...]
    landed_all(N - 1, ysp.at[0], qz_r.at[1])
    for j in range(1, N):
        whole = whole + ysp[j]
    fsp[:, mine_cols] = whole
    at = fsp.at[:, mine_cols]
    push(at, at, qa_r.at[1], mate)
    for i in range(1, NP):
        near, _ = in_plane(-i)
        ys, es = lax.div(near, NE), rem(near, NE)
        landed(fin_left(fin, c, ys, es), ga_r.at[i - 1])
        landed(fin_right(fin, c, ys, es), ga_r.at[NP - 2 + i])
        fin_to_mate(ys, es)
    at = rows(c * HR, HR)
    g_ref[at, :] = fin[at, :].astype(F32)
    landed(fsp.at[:, other_cols], qa_r.at[1])
    small_ref[...] = fsp[...]
    landed_all(len(others), fqo.at[0, :, pl.ds(0, YW)], qa_r.at[0])
    fqo_ref[...] = fqo[...]
    ig_copy.wait()
    out_copy.wait()
    landed(fin.at[rows((1 - c) * HR, HR)], ga_r.at[2 * NP - 2])
    at = rows((1 - c) * HR, HR)
    g_ref[at, :] = fin[at, :].astype(F32)

    for kind, size in enumerate(sent):
        at = ruler.at[pl.ds(0, size // 256)]
        if kind == 0:
            at = bias.at[pl.ds(0, size // (16 * 128 * 4))]
        pltpu.make_async_remote_copy(
            src_ref=at,
            dst_ref=at,
            send_sem=send_sems.at[kind],
            recv_sem=send_sems.at[kind],
            device_id=mate,
            device_id_type=MESH,
        ).wait_send()
    for valid, copies in maybe_started:

        @pl.when(valid)
        def _(copies=copies):
            for copy in copies:
                copy.wait_send()

    for s, o in enumerate(offsets):
        valid = jnp.logical_and(spot_in_row + o >= 0, spot_in_row + o < z.per_row)

        @pl.when(valid)
        def _(s=s, o=o):
            halo_copy(s, o).wait_send()


def run(z, x, seg, chosen, vectors, q, k, v, o, r, up, down, cot):
    N, G, NP, NY, NE = z.narrow, z.group, z.plane, z.rows_y, z.expert
    T, W, D, R, HP = z.block, z.window, z.width, z.shard, z.head_part
    FL = z.ff_local
    FR = D + FL
    HR = FR // 2
    HS = HR // NP
    YW = D // NY
    SH = R + HP
    ER = N * SH
    QR = G * R
    GR = G * SH
    S = 2 * z.reach
    SMALL = z.small_rows
    vmem = pl.BlockSpec(memory_space=pltpu.VMEM)
    anywhere = pl.BlockSpec(memory_space=pltpu.HBM)
    scratch = [
        ((N * T, D // N), F32),
        ((T, D), F32),
        ((W, D), F32),
        ((W, D), BF16),
        ((QR, D), BF16),
        ((QR, D), BF16),
        ((2, HEAD, D), BF16),
        ((G, 16, 128), F32),
        ((8, 128), F32),
        ((HEAD, 128), F32),
        ((N, FR, D), BF16),
        ((T, D), BF16),
        ((8, z.row_len), F32),
        ((W, 8), F32),
        ((W, HEAD), BF16),
        ((W, HEAD), BF16),
        ((HEAD, W), BF16),
        ((HEAD, W), BF16),
        ((QR, T), F32),
        ((2, HEAD, T), BF16),
        ((2, W, T), BF16),
        ((2, HEAD, T), F32),
        ((QR, T), BF16),
        ((T, D), F32),
        ((T, D), F32),
        ((T, D), BF16),
        ((N, T, FL), BF16),
        ((N, T, FL), BF16),
        ((T, FL), BF16),
        ((T, D), F32),
        ((T, D), F32),
        ((T, D), BF16),
        ((2, HEAD, T), BF16),
        ((W, HEAD), F32),
        ((W, HEAD), F32),
        ((2, HEAD, T), BF16),
        ((QR, T), BF16),
        ((max(S, 1), 2, z.piece, HEAD), BF16),
        ((max(S, 1), 2, z.piece, HEAD), BF16),
        ((T, D), BF16),
        ((N, T, D // N), BF16),
        ((N, FR, D), BF16),
        ((GROUP_BYTES // 256, 128), BF16),
        ((N, HR, D), BF16),
        ((N, HR, D), BF16),
        ((N, NE, HR // NE, D // 2), BF16),
        ((N, NY, HR // NY, D // 2), BF16),
        ((N, HR // NE, D // 2), BF16),
        ((N, HR // NY, D // 2), BF16),
        ((N, NY, HS, D // 2), BF16),
        ((N, NE, HS, D // 2), BF16),
        ((N, HS, D), BF16),
        ((N, HS, D), BF16),
        ((FR, D), BF16),
        ((2, GR, D), BF16),
        ((GR, D), BF16),
        ((GR, D), BF16),
        ((NP, ER, YW), BF16),
        ((ER, YW), BF16),
        ((N, SH, YW), BF16),
        ((2, SH, D), BF16),
        ((SMALL, D), F32),
        ((SMALL, D // 2), F32),
        ((SMALL, D // 2), F32),
        ((NP, SMALL, D // 2), F32),
        ((SMALL, D // 2), F32),
        ((N, SMALL, D // 2), F32),
        ((SMALL, D), F32),
    ]
    pairs = [
        (N - 1,),
        (1,),
        (G - 1,),
        (G - 1,),
        (1,),
        (G - 1,),
        (1,),
        (4, N - 1, max(NE, NY) - 1),
        (N - 1,),
        (1,),
        (1,),
        (max(S, 1),),
        (N,),
        (4, N, max(NE, NY) - 1),
        (N,),
        (2 * NP - 1,),
        (2,),
        (2,),
        (2,),
        (2,),
    ]
    HALO = 11
    sems = [pltpu.SemaphoreType.DMA((6,)), pltpu.SemaphoreType.DMA((GROUPS,))]
    for at, shape in enumerate(pairs):
        sems += [pltpu.SemaphoreType.DMA(shape)] * (2 if at == HALO else 1)
    sems += [pltpu.SemaphoreType.DMA((2, 2, N)), pltpu.SemaphoreType.DMA((2, N))]
    outs = [
        ((N * T, D // N), F32),
        ((T, D), F32),
        ((FR, D), F32),
        ((2, SH, D), BF16),
        ((SMALL, D), F32),
    ]
    return pl.pallas_call(
        functools.partial(kernel, z),
        out_shape=[pltpu.VMEM(s, t) for s, t in outs],
        in_specs=[anywhere] + [vmem] * (7 + len(vectors)) + [anywhere] * 2 + [vmem],
        out_specs=[pl.BlockSpec(memory_space=pl.ANY)] * 2 + [vmem] * 3,
        scratch_shapes=[pltpu.VMEM(s, t) for s, t in scratch] + sems,
        compiler_params=pltpu.CompilerParams(
            collective_id=0, has_side_effects=True, vmem_limit_bytes=58 * 2**20
        ),
        name="layer",
    )(x, seg, chosen, *vectors, q, k, v, o, r, up, down, cot)


def finish_kernel(
    z,
    out_in,
    ig_in,
    g_in,
    fqo_ref,
    small_ref,
    out_any,
    ig_out,
    g1_ref,
    s1_ref,
    gq_ref,
    qb_ref,
    gk_ref,
    gv_ref,
    vb_ref,
    go_ref,
    ob_ref,
    rw_ref,
    rb_ref,
    g2_ref,
    s2_ref,
    gup_any,
    ub_ref,
    gdown_any,
    db_ref,
    sems,
):
    e, n = lax.axis_index("expert"), lax.axis_index("narrow")
    N, T, D, R, HP, LE = z.narrow, z.block, z.width, z.shard, z.head_part, z.local_experts
    copies = []

    def put(src, dst):
        copies.append(pltpu.make_async_copy(src, dst, sems.at[len(copies)]))
        copies[-1].start()

    put(out_in, out_any)
    put(ig_in, ig_out)
    put(g_in.at[pl.ds(0, D)], gup_any)
    put(g_in.at[pl.ds(D, z.ff_local)], gdown_any)
    gq_ref[...] = fqo_ref[0, 0:R, :].astype(F32)
    go_ref[...] = fqo_ref[1, 0:R, :].astype(F32)
    gk_ref[...] = fqo_ref[0, R : R + HP, :].astype(F32)
    gv_ref[...] = fqo_ref[1, R : R + HP, :].astype(F32)
    g1_ref[...] = small_ref[0:1, :]
    s1_ref[...] = small_ref[1:2, :]
    ob_ref[...] = small_ref[2:3, :]
    g2_ref[...] = small_ref[3:4, :]
    s2_ref[...] = small_ref[4:5, :]
    db_ref[...] = small_ref[5:6, :]
    rb_ref[...] = small_ref[7:8, 0 : z.experts]
    rw_ref[...] = small_ref[16 : 16 + z.experts, :]
    upper = jnp.zeros((1, D), F32)
    for j in range(N):
        upper = jnp.where(n == j, small_ref[8 + j : 9 + j, :], upper)
    ub_ref[...] = upper
    here = e * N + n
    query = pltpu.roll(small_ref[0:8, :], lax.rem(D - here * R, D), 1)
    for i in range(LE):
        qb_ref[i : i + 1, :] = query[6:7, i * HP : (i + 1) * HP]
    value = pltpu.roll(small_ref[8:16, :], lax.rem(D - n * HP, D), 1)
    vb_ref[...] = value[7:8, 0:HP]
    for copy in copies:
        copy.wait()


def finish(z, out, ig, fin, fqo, small):
    N, T, D, R, HP = z.narrow, z.block, z.width, z.shard, z.head_part
    FL = z.ff_local
    vmem = pl.BlockSpec(memory_space=pltpu.VMEM)
    anywhere = pl.BlockSpec(memory_space=pltpu.HBM)
    shapes = [
        (N * T, D // N),
        (T, D),
        (1, D),
        (1, D),
        (R, D),
        (z.local_experts, HP),
        (HP, D),
        (HP, D),
        (1, HP),
        (R, D),
        (1, D),
        (z.experts, D),
        (1, z.experts),
        (1, D),
        (1, D),
        (D, FL),
        (1, FL),
        (FL, D),
        (1, D),
    ]
    return pl.pallas_call(
        functools.partial(finish_kernel, z),
        out_shape=[jax.ShapeDtypeStruct(s, F32) for s in shapes],
        in_specs=[pl.BlockSpec(memory_space=pl.ANY)] * 3 + [vmem] * 2,
        out_specs=[anywhere] * 2 + [vmem] * 13 + [anywhere, vmem, anywhere, vmem],
        scratch_shapes=[
            pltpu.SemaphoreType.DMA((4,)),
        ],
        compiler_params=pltpu.CompilerParams(vmem_limit_bytes=16 * 2**20),
        name="finish",
    )(out, ig, fin, fqo, small)


def per_device(
    inputs,
    seg_ids,
    chosen,
    gain_one,
    shift_one,
    query_w,
    query_b,
    key_w,
    value_w,
    value_b,
    out_w,
    out_b,
    router_w,
    router_b,
    gain_two,
    shift_two,
    up_w,
    up_b,
    down_w,
    down_b,
    cotangent,
):
    narrow = lax.axis_size("narrow")
    e, n = lax.axis_index("expert"), lax.axis_index("narrow")
    z = Sizes(
        lax.axis_size("dp"),
        lax.axis_size("expert"),
        narrow,
        inputs.shape[0],
        inputs.shape[1],
        seg_ids.shape[1],
        query_w.shape[0],
        up_w.shape[1],
    )
    D, R, HP = z.width, z.shard, z.head_part
    vectors = [gain_one, shift_one, out_b, gain_two, shift_two, down_b, up_b]
    vectors = [v.reshape(1, -1) for v in vectors]
    vectors += [query_b, value_b.reshape(1, -1), router_b.reshape(1, -1)]
    parts = run(
        z,
        inputs,
        seg_ids,
        jnp.transpose(chosen),
        vectors,
        jnp.transpose(query_w, (0, 2, 1)).reshape(R, D),
        jnp.transpose(key_w),
        jnp.transpose(value_w),
        out_w.reshape(R, D),
        jnp.transpose(router_w),
        up_w,
        down_w,
        cotangent,
    )
    out, ig, g1, s1, gq, qb, gk, gv, vb, go, ob, rw, rb, g2, s2, gup, ub, gdown, db = finish(
        z, *parts
    )
    return (
        out,
        ig,
        g1.reshape(-1),
        s1.reshape(-1),
        jnp.transpose(gq.reshape(z.local_experts, HP, D), (0, 2, 1)),
        qb,
        jnp.transpose(gk),
        jnp.transpose(gv),
        vb.reshape(-1),
        go.reshape(z.local_experts, HP, D),
        ob.reshape(-1),
        jnp.transpose(rw),
        rb.reshape(-1),
        g2.reshape(-1),
        s2.reshape(-1),
        gup,
        ub.reshape(-1),
        gdown,
        db.reshape(-1),
    )


def solution(mesh):
    return jax.shard_map(
        per_device,
        mesh=mesh,
        in_specs=(
            P("dp", None),
            P("dp", None),
            P("dp", None),
            P(),
            P(),
            P("expert", None, "narrow"),
            P("expert", "narrow"),
            P(None, "narrow"),
            P(None, "narrow"),
            P("narrow"),
            P("expert", "narrow", None),
            P(),
            P(),
            P(),
            P(),
            P(),
            P(None, "narrow"),
            P("narrow"),
            P("narrow", None),
            P(),
            P(("dp", "expert"), "narrow"),
        ),
        out_specs=(
            P(("dp", "expert"), "narrow"),
            P(("dp", "expert", "narrow"), None),
            P(),
            P(),
            P("expert", None, "narrow"),
            P("expert", "narrow"),
            P(None, "narrow"),
            P(None, "narrow"),
            P("narrow"),
            P("expert", "narrow", None),
            P(),
            P(),
            P(),
            P(),
            P(),
            P(None, "narrow"),
            P("narrow"),
            P("narrow", None),
            P(),
        ),
        check_vma=False,
    )
```

```python
import functools
import math

import jax
import jax.numpy as jnp
from jax import lax
from jax.experimental import pallas as pl
from jax.experimental.pallas import tpu as pltpu
from jax.sharding import PartitionSpec as P

HEAD = 64
LONGEST = 256
EPSILON = 1e-05
MASKED = -1000000000.0
GELU_A = math.sqrt(2.0 / math.pi)
GELU_B = 0.044715
F32 = jnp.float32
BF16 = jnp.bfloat16
MESH = pl.DeviceIdType.MESH
GROUP_BYTES = 2**21
GROUPS = 8


def dot(a, b):
    return lax.dot_general(a, b, (((1,), (0,)), ((), ())), preferred_element_type=F32)


def dot_nt(a, b):
    return lax.dot_general(a, b, (((1,), (1,)), ((), ())), preferred_element_type=F32)


def dot_tn(a, b):
    return lax.dot_general(a, b, (((0,), (0,)), ((), ())), preferred_element_type=F32)


def norm_stats(x):
    centred = x - jnp.mean(x, axis=1, keepdims=True)
    inverse = lax.rsqrt(jnp.mean(centred * centred, axis=1, keepdims=True) + EPSILON)
    return centred * inverse, inverse


def rem(a, b):
    return lax.rem(a, b)


class Sizes:
    def __init__(self, dp, expert, narrow, tokens, width, row_len, local_experts, ff_local):
        self.dp, self.expert, self.narrow = dp, expert, narrow
        self.tokens, self.width, self.row_len = tokens, width, row_len
        self.local_experts = local_experts
        self.experts = local_experts * expert
        self.group = expert * narrow
        self.block = tokens // self.group
        self.rows_y = dp // 2
        self.plane = self.rows_y * expert
        self.ff_local = ff_local
        self.head_part = HEAD // narrow
        self.shard = local_experts * self.head_part
        self.per_row = row_len // self.block
        spans = [
            min(row_len, (j + 1) * self.block + LONGEST) - max(0, j * self.block - LONGEST)
            for j in range(self.per_row)
        ]
        self.window = max(spans)
        self.reach = max(1, LONGEST // self.block) if self.per_row > 1 else 0
        self.piece = min(self.block, LONGEST)
        self.tile = min(256, self.block)
        self.up_rows = narrow * ff_local // width
        self.small_rows = 24


def kernel(
    z,
    x_any,
    seg_ref,
    chosen_ref,
    g1_ref,
    s1_ref,
    ob_ref,
    g2_ref,
    s2_ref,
    db_ref,
    ub_ref,
    qb_ref,
    vb_ref,
    rb_ref,
    q_ref,
    k_ref,
    v_ref,
    o_ref,
    r_ref,
    up_any,
    down_any,
    cot_ref,
    out_any,
    ig_any,
    g_ref,
    fqo_ref,
    small_ref,
    out_ref,
    ig_ref,
    xw,
    rw,
    wq,
    wo,
    wkv,
    bias,
    corner,
    vcol,
    ffw,
    cot,
    segs,
    segc,
    kn,
    vn,
    kt,
    vt,
    qt,
    qk,
    prob,
    mix,
    mixg,
    hid,
    acc,
    second,
    active,
    slope,
    ugrad,
    sgrad,
    hgrad,
    hgb,
    mgk,
    dk,
    dv,
    dq,
    dqt,
    halo_out,
    halo_in,
    delta,
    outd,
    gsend,
    ruler,
    crecv,
    psend,
    pea,
    pya,
    mea,
    mya,
    pyb,
    peb,
    zsend,
    zrecv,
    fin,
    gqo,
    cqo,
    pqo,
    rqo,
    zqo,
    yqo,
    fqo,
    sp,
    csp,
    psp,
    rsp,
    zsp,
    ysp,
    fsp,
    loc_sem,
    send_sems,
    w_r,
    wm_r,
    b_r,
    q_r,
    qm_r,
    o_r,
    om_r,
    fp_r,
    fm_r,
    ct_r,
    od_r,
    hl_s,
    hl_r,
    gc_r,
    gp_r,
    gz_r,
    ga_r,
    qc_r,
    qp_r,
    qz_r,
    qa_r,
    fz_s,
    fz_r,
):
    d, e, n = lax.axis_index("dp"), lax.axis_index("expert"), lax.axis_index("narrow")
    c, y = rem(d, 2), lax.div(d, 2)
    N, G, NP, NE, NY = z.narrow, z.group, z.plane, z.expert, z.rows_y
    T, W, D, R, HP, LE = z.block, z.window, z.width, z.shard, z.head_part, z.local_experts
    FL = z.ff_local
    half = D // 2
    here = e * N + n
    spot = y * NE + e
    mate = (d + 1 - 2 * c, e, n)

    def in_group(j):
        at = rem(here + j + G, G)
        return at, (d, lax.div(at, N), rem(at, N))

    def in_plane(j):
        at = rem(spot + j + NP, NP)
        return at, (2 * lax.div(at, NE) + c, rem(at, NE), n)

    def in_line(j):
        at = rem(n + j + N, N)
        return at, (d, e, at)

    def in_rows(j):
        at = rem(y + j + NY, NY)
        return at, (2 * at + c, e, n)

    sent = [0, 0]
    noted = {}

    def either(name, valid, block):
        again = name in noted
        kinds = noted.setdefault(name, [])
        turn = iter(list(kinds)) if again else None

        @pl.when(valid)
        def _():
            mode.append((kinds, turn))
            block()
            mode.pop()

    mode = []

    def push(src, dst, recv, device):
        size = math.prod(src.shape) * jnp.dtype(src.dtype).itemsize
        if mode and mode[-1][1] is not None:
            kind = next(mode[-1][1])
        else:
            kind = 0
            if not (src.shape[-1] == 128 and src.dtype == F32):
                if sent[-1] + size > GROUP_BYTES:
                    sent.append(0)
                kind = len(sent) - 1
            sent[kind] += size
            if mode:
                mode[-1][0].append(kind)
        copy = pltpu.make_async_remote_copy(
            src_ref=src,
            dst_ref=dst,
            send_sem=send_sems.at[kind],
            recv_sem=recv,
            device_id=device,
            device_id_type=MESH,
        )
        copy.start()

    def landed(dst, recv):
        pltpu.make_async_remote_copy(
            src_ref=dst,
            dst_ref=dst,
            send_sem=recv,
            recv_sem=recv,
            device_id=mate,
            device_id_type=MESH,
        ).wait_recv()

    def landed_all(count, of, recv):
        size = count * math.prod(of.shape) * jnp.dtype(of.dtype).itemsize
        landed(ruler.at[pl.ds(0, size // 256)], recv)

    def rows(start, size, step=16):
        return pl.ds(pl.multiple_of(start, step), size)

    start = here * T
    row = lax.div(start, z.row_len)
    spot_in_row = rem(here, z.per_row)
    base = row * z.row_len
    ws = jnp.minimum(jnp.maximum(spot_in_row * T - LONGEST, 0), z.row_len - W)
    off = spot_in_row * T - ws
    own = rows(off, T, 128)

    x_copy = pltpu.make_async_copy(x_any.at[rows(base + ws, W, 128)], xw, loc_sem.at[0])
    x_copy.start()
    up_copy = pltpu.make_async_copy(up_any, ffw.at[n, pl.ds(0, D)], loc_sem.at[1])
    up_copy.start()
    down_copy = pltpu.make_async_copy(down_any, ffw.at[n, pl.ds(D, FL)], loc_sem.at[2])
    down_copy.start()
    cols_copy = pltpu.make_async_copy(
        x_any.at[rows(e * N * T, N * T, 128), rows(n * (D // N), D // N, 128)], out_ref, loc_sem.at[3]
    )
    cols_copy.start()
    wq[rows(here * R, R)] = q_ref[...]
    wo[rows(here * R, R)] = o_ref[...]
    wkv[0, rows(n * HP, HP)] = k_ref[...]
    wkv[1, rows(n * HP, HP)] = v_ref[...]
    bias[here] = jnp.zeros((16, 128), F32)
    for i in range(FL // 128):
        bias[here, i : i + 1, :] = ub_ref[0:1, i * 128 : (i + 1) * 128]
    bias[here, 8 : 8 + LE, 0:HP] = qb_ref[...]
    bias[here, 7:8, 0:HP] = vb_ref[...]

    barrier = pltpu.get_barrier_semaphore()
    pl.semaphore_signal(barrier, inc=1, device_id=mate, device_id_type=MESH)
    for j in range(1, NP):
        pl.semaphore_signal(barrier, inc=1, device_id=in_plane(j)[1], device_id_type=MESH)
    for j in range(1, G):
        pl.semaphore_signal(barrier, inc=1, device_id=in_group(j)[1], device_id_type=MESH)
    for j in range(1, NY):
        to = (2 * in_rows(j)[0] + 1 - c, e, n)
        pl.semaphore_signal(barrier, inc=1, device_id=to, device_id_type=MESH)
    pl.semaphore_wait(barrier, NP + G + NY - 2)

    mine_cols = rows(c * half, half, 128)
    other_cols = rows((1 - c) * half, half, 128)

    def in_expert(i):
        at = rem(e + i + NE, NE)
        return at, (d, at, n)

    def shard_at(i, j):
        return rem(e - i + NE, NE) * N + rem(n - j + N, N)

    def spread_start(part, recv):
        for j in range(1, N):
            at = part(here)
            push(at, at, recv.at[j - 1], in_line(j)[1])
        for i in range(1, NE):
            at = part(here)
            push(at, at, recv.at[i * N - 1], in_expert(i)[1])

    def spread_on(part, recv, to_mate):
        for j in range(1, N):
            at = part(shard_at(0, j))
            landed(at, recv.at[j - 1])
            for i in range(1, NE):
                push(at, at, recv.at[i * N + j - 1], in_expert(i)[1])
            if to_mate is not None:
                push(at, at, to_mate.at[0], mate)

    def spread_end(part, recv, to_mate):
        for i in range(1, NE):
            for j in range(N):
                at = part(shard_at(i, j))
                landed(at, recv.at[i * N + j - 1])
                if to_mate is not None:
                    push(at, at, to_mate.at[0], mate)

    def spread_wait(part, to_mate):
        landed_all(G - 1, part(0), to_mate.at[0])

    def bias_part(g):
        return bias.at[g]

    def q_part(g):
        return wq.at[rows(g * R, R), mine_cols]

    def q_other(g):
        return wq.at[rows(g * R, R), other_cols]

    def o_part(g):
        return wo.at[rows(g * R, R), mine_cols]

    def o_other(g):
        return wo.at[rows(g * R, R), other_cols]

    for j in range(1, N):
        at = wkv.at[c, rows(n * HP, HP)]
        push(at, at, w_r.at[j - 1], in_line(j)[1])
    spread_start(q_part, q_r)
    spread_start(bias_part, b_r)
    up_copy.wait()
    down_copy.wait()
    FR = D + FL

    left, right = pl.ds(0, half), pl.ds(half, half)
    HR = FR // 2
    HS = HR // NP
    HA, HB = HR // NE, HR // NY
    def left_slice(of, ys, es):
        return ffw.at[of, rows(c * HR + (es * NY + ys) * HS, HS), left]

    def right_slice(of, ys, es):
        return ffw.at[of, rows(c * HR + (ys * NE + es) * HS, HS), right]

    def left_half(of, es):
        return ffw.at[of, rows(c * HR + es * HA, HA), left]

    def right_half(of, ys):
        return ffw.at[of, rows(c * HR + ys * HB, HB), right]

    def by_distance(at):
        return sorted((o for o in range(N) if o != at), key=lambda o: (abs(o - at), o if 2 * at >= N else -o))

    def pick(choices):
        value = choices[0]
        for at in range(1, N):
            value = jnp.where(n == at, choices[at], value)
        return value

    shard_of = [n] + [pick([by_distance(at)[k] for at in range(N)]) for k in range(N - 1)]
    maybe_started = []

    def line_push(of, step, valid):
        of = jnp.clip(of, 0, N - 1)
        to = (d, e, jnp.clip(n + step, 0, N - 1))
        way = (step + 1) // 2
        copies = [
            pltpu.make_async_remote_copy(
                src_ref=at,
                dst_ref=at,
                send_sem=fz_s.at[part, way, of],
                recv_sem=fz_r.at[part, of],
                device_id=to,
                device_id_type=MESH,
            )
            for part, at in enumerate((left_slice(of, y, e), right_slice(of, y, e)))
        ]

        @pl.when(valid)
        def _():
            for copy in copies:
                copy.start()

        maybe_started.append((valid, copies))

    def line_landed(of, valid):
        of = jnp.clip(of, 0, N - 1)

        @pl.when(valid)
        def _():
            landed(left_slice(of, y, e), fz_r.at[0, of])
            landed(right_slice(of, y, e), fz_r.at[1, of])

    def shards_start():
        line_push(n, 1, n + 1 < N)
        line_push(n, -1, n > 0)

    def shards_on(hop):
        line_landed(n - hop, n >= hop)
        line_push(n - hop, 1, jnp.logical_and(n >= hop, n + 1 < N))
        line_landed(n + hop, n + hop < N)
        line_push(n + hop, -1, jnp.logical_and(n + hop < N, n > 0))

    def plane_on(j):
        there = shard_of[j]
        at = left_slice(there, y, e)
        for i in range(1, NY):
            push(at, at, fp_r.at[0, j - 1, i - 1], in_rows(i)[1])
        at = right_slice(there, y, e)
        for i in range(1, NE):
            push(at, at, fp_r.at[1, j - 1, i - 1], in_expert(i)[1])

    def plane_turn(j):
        there = shard_of[j]
        for i in range(1, NY):
            near, _ = in_rows(-i)
            landed(left_slice(there, near, e), fp_r.at[0, j - 1, i - 1])
        at = left_half(there, e)
        for i in range(1, NE):
            push(at, at, fp_r.at[2, j - 1, i - 1], in_expert(i)[1])
        for i in range(1, NE):
            near, _ = in_expert(-i)
            landed(right_slice(there, y, near), fp_r.at[1, j - 1, i - 1])
        at = right_half(there, y)
        for i in range(1, NY):
            push(at, at, fp_r.at[3, j - 1, i - 1], in_rows(i)[1])

    def mate_on(j):
        there = shard_of[j]
        for i in range(1, NE):
            near, _ = in_expert(-i)
            landed(left_half(there, near), fp_r.at[2, j - 1, i - 1])
        for i in range(1, NY):
            near, _ = in_rows(-i)
            landed(right_half(there, near), fp_r.at[3, j - 1, i - 1])
        at = ffw.at[there, rows(c * HR, HR)]
        push(at, at, fm_r.at[j - 1], mate)

    x_copy.wait()
    gain_one, shift_one = g1_ref[...], s1_ref[...]

    def norm_one(i, carry):
        at = rows(i * 128, 128, 128)
        unit, _ = norm_stats(xw[at, :])
        rw[at, :] = (unit * gain_one + shift_one).astype(BF16)
        return carry

    lax.fori_loop(0, W // 128, norm_one, 0)

    seg_all = seg_ref[...].astype(F32)
    row_id = lax.broadcasted_iota(jnp.int32, seg_all.shape, 0)
    seg_here = jnp.sum(jnp.where(row_id == row, seg_all, 0.0), axis=0, keepdims=True)
    segs[...] = jnp.broadcast_to(seg_here, segs.shape)
    segc[...] = jnp.transpose(segs[:, rows(ws, W, 128)])
    seg_own = segs[0:1, rows(spot_in_row * T, T, 128)]
    corner[...] = jnp.zeros_like(corner)
    corner[:, 0 : z.experts] = jnp.broadcast_to(rb_ref[...], (8, z.experts))
    router_col = jnp.transpose(corner[...])[0 : z.experts, 0:1]
    logits = dot_nt(r_ref[...], rw[own, :]) + router_col
    expert_id = lax.broadcasted_iota(jnp.int32, (z.experts, T), 0)
    hot, picked = [], []
    for k in range(2):
        chosen = chosen_ref[k : k + 1, rows(start, T, 128)]
        hot.append((expert_id == chosen).astype(F32))
        picked.append(jnp.sum(logits * hot[k], axis=0, keepdims=True))
    top = jnp.maximum(picked[0], picked[1])
    raised = [jnp.exp(p - top) for p in picked]
    total = raised[0] + raised[1]
    gate = [r / total for r in raised]

    for j in range(1, N):
        there, _ = in_line(-j)
        at = wkv.at[c, rows(there * HP, HP)]
        landed(at, w_r.at[j - 1])
        push(at, at, wm_r.at[0], mate)
    spread_on(q_part, q_r, qm_r)
    spread_on(bias_part, b_r, None)
    shards_start()
    spread_start(o_part, o_r)

    landed_all(N - 1, wkv.at[0, pl.ds(0, HP)], wm_r.at[0])
    kn[...] = dot_nt(rw[...], wkv[0]).astype(BF16)
    kt[...] = dot_nt(wkv[0], rw[...]).astype(BF16)
    spread_end(q_part, q_r, qm_r)
    spread_end(bias_part, b_r, None)
    columns = [jnp.transpose(bias[g, 0:16, :]) for g in range(G)]
    for part in range(N):
        vcol[part * HP : (part + 1) * HP, :] = jnp.broadcast_to(columns[part][0:HP, 7:8], (HP, 128))
    value_row = jnp.transpose(vcol[...])[0:1, :]
    vn[...] = (dot_nt(rw[...], wkv[1]) + value_row).astype(BF16)
    vt[...] = (dot_nt(wkv[1], rw[...]) + vcol[:, 0:1]).astype(BF16)

    spread_wait(q_other, qm_r)
    qt[...] = dot_nt(wq[...], rw[own, :])

    def expert_rows(at, i, part):
        return ((at * N + part) * LE + i) * HP

    for part in range(N):
        chosen_rows = [jnp.zeros((HP, T), F32), jnp.zeros((HP, T), F32)]
        for at in range(NE):
            g = at * N + part
            for i in range(LE):
                lo = expert_rows(at, i, part)
                one = qt[lo : lo + HP, :] + columns[g][0:HP, 8 + i : 9 + i]
                for k in range(2):
                    chosen_rows[k] = chosen_rows[k] + one * hot[k][at * LE + i : at * LE + i + 1, :]
        for k in range(2):
            qk[k, part * HP : (part + 1) * HP, :] = chosen_rows[k].astype(BF16)

    scale = 1.0 / math.sqrt(HEAD)
    TL = z.tile
    tiles = T // TL
    seg_tiles = [seg_own[:, i * TL : (i + 1) * TL] for i in range(tiles)]

    def attend(k):
        for i in range(tiles):
            at = pl.ds(i * TL, TL)
            scores = dot(kn[...], qk[k, :, at]) * scale
            scores = jnp.where(segc[:, 0:1] == seg_tiles[i], scores, MASKED)
            high = jnp.max(scores, axis=0, keepdims=True)
            raised_scores = jnp.exp(scores - high)
            low = (raised_scores * (1.0 / jnp.sum(raised_scores, axis=0, keepdims=True))).astype(BF16)
            prob[k, :, at] = low
            mix[k, :, at] = dot(vt[...], low)

    attend(0)
    attend(1)
    shards_on(1)
    plane_on(1)
    spread_on(o_part, o_r, om_r)
    plane_turn(1)
    shards_on(2)
    plane_on(2)
    CW = D // N
    cot[:, rows(n * CW, CW, 128)] = cot_ref[rows(n * T, T, 128), :]
    for j in range(1, N):
        there, to = in_line(j)
        push(
            cot_ref.at[rows(there * T, T, 128)],
            cot.at[:, rows(n * CW, CW, 128)],
            ct_r.at[0],
            to,
        )
    outer = jnp.logical_or(n >= 3, n + 3 < N)
    inner = jnp.logical_not(outer)
    either("on", inner, lambda: plane_on(3))
    spread_end(o_part, o_r, om_r)

    for part in range(N):
        for at in range(NE):
            for i in range(LE):
                lo = expert_rows(at, i, part)
                x = at * LE + i
                gated = jnp.zeros((HP, T), F32)
                for k in range(2):
                    rounded_mix = mix[k, part * HP : (part + 1) * HP, :].astype(BF16).astype(F32)
                    gated = gated + rounded_mix * (hot[k][x : x + 1, :] * gate[k])
                mixg[lo : lo + HP, :] = gated.astype(BF16)
    spread_wait(o_other, om_r)
    out_b, down_b = ob_ref[...], db_ref[...]
    gain_two, shift_two = g2_ref[...], s2_ref[...]
    attention = dot_tn(mixg[...], wo[...]) + out_b
    acc[...] = attention + down_b
    hid[...] = xw[own, :] + attention

    def norm_two(i, carry):
        at = rows(i * 128, 128, 128)
        unit, _ = norm_stats(hid[at, :])
        second[at, :] = (unit * gain_two + shift_two).astype(BF16)
        return carry

    lax.fori_loop(0, T // 128, norm_two, 0)
    sgrad[...] = jnp.zeros_like(sgrad)

    def core_start(j):
        push(
            gsend.at[j, rows((1 - c) * HR, HR)], crecv.at[j], gc_r.at[j], mate
        )

    def plane_start(j):
        landed(crecv.at[j], gc_r.at[j])
        psend[j] = (
            gsend[j, rows(c * HR, HR), :].astype(F32) + crecv[j].astype(F32)
        ).astype(BF16)
        for i in range(1, NE):
            there, to = in_expert(i)
            src = psend.at[j, rows(there * HA, HA), left]
            push(src, pea.at[j, i], gp_r.at[0, j, i - 1], to)
        for i in range(1, NY):
            there, to = in_rows(i)
            src = psend.at[j, rows(there * HB, HB), right]
            push(src, pya.at[j, i], gp_r.at[1, j, i - 1], to)

    def plane_middle(j):
        whole = psend[j, rows(e * HA, HA), left].astype(F32)
        for i in range(1, NE):
            landed(pea.at[j, i], gp_r.at[0, j, i - 1])
            whole = whole + pea[j, i].astype(F32)
        mea[j] = whole.astype(BF16)
        for i in range(1, NY):
            there, to = in_rows(i)
            src = mea.at[j, rows(there * HS, HS)]
            push(src, pyb.at[j, i], gp_r.at[2, j, i - 1], to)
        whole = psend[j, rows(y * HB, HB), right].astype(F32)
        for i in range(1, NY):
            landed(pya.at[j, i], gp_r.at[1, j, i - 1])
            whole = whole + pya[j, i].astype(F32)
        mya[j] = whole.astype(BF16)
        for i in range(1, NE):
            there, to = in_expert(i)
            src = mya.at[j, rows(there * HS, HS)]
            push(src, peb.at[j, i], gp_r.at[3, j, i - 1], to)

    def line_start(j):
        whole = mea[j, rows(y * HS, HS), :].astype(F32)
        for i in range(1, NY):
            landed(pyb.at[j, i], gp_r.at[2, j, i - 1])
            whole = whole + pyb[j, i].astype(F32)
        zsend[j, :, left] = whole.astype(BF16)
        whole = mya[j, rows(e * HS, HS), :].astype(F32)
        for i in range(1, NE):
            landed(peb.at[j, i], gp_r.at[3, j, i - 1])
            whole = whole + peb[j, i].astype(F32)
        zsend[j, :, right] = whole.astype(BF16)
        if j:
            push(zsend.at[j], zrecv.at[n], gz_r.at[n], (d, e, shard_of[j]))

    def forward(j):
        there = shard_of[j]
        if j:
            landed(ffw.at[there, rows((1 - c) * HR, HR)], fm_r.at[j - 1])
        up_b = jnp.concatenate(
            [bias[e * N + there, i : i + 1, :] for i in range(FL // 128)], axis=1
        )

        def feed(i, carry):
            at = rows(i * TL, TL, 128)
            upper = dot(second[at, :], ffw[there, 0:D, :]) + up_b
            square = upper * upper
            t = jnp.tanh(upper * (GELU_A + (GELU_A * GELU_B) * square))
            one = 0.5 + 0.5 * t
            low = (upper * one).astype(BF16)
            active[j, at, :] = low
            slope[j, at, :] = (
                one + (0.5 * upper) * (1.0 - t * t) * (GELU_A + (3.0 * GELU_A * GELU_B) * square)
            ).astype(BF16)
            acc[at, :] = acc[at, :] + dot(low, ffw[there, D : D + FL, :])
            return carry

        lax.fori_loop(0, T // TL, feed, 0)

    def backward(j):
        there = shard_of[j]

        def feed_back(i, carry):
            at = rows(i * TL, TL, 128)
            back = dot_nt(cot[at, :], ffw[there, D : D + FL, :]) * slope[j, at, :].astype(F32)
            back = back.astype(BF16)
            ugrad[at, :] = back
            sgrad[at, :] = sgrad[at, :] + dot_nt(back, ffw[there, 0:D, :])
            return carry

        lax.fori_loop(0, T // TL, feed_back, 0)
        sp[pl.ds(8 + there, 1), :] = jnp.sum(ugrad[...].astype(F32), axis=0, keepdims=True)
        gsend[j, 0:D, :] = dot_tn(second[...], ugrad[...]).astype(BF16)
        gsend[j, D : D + FL, :] = dot_tn(active[j], cot[...]).astype(BF16)
        core_start(j)

    def cotangent_wait():
        landed_all(N - 1, cot.at[:, pl.ds(0, CW)], ct_r.at[0])

    def last_forward():
        forward(3)
        delta[...] = acc[...].astype(BF16)
        outd[n] = delta[:, rows(n * CW, CW, 128)]
        for j in range(1, N):
            there, to = in_line(j)
            push(delta.at[:, rows(there * CW, CW, 128)], outd.at[n], od_r.at[0], to)

    forward(0)
    plane_turn(2)
    mate_on(1)
    either("turn", inner, lambda: plane_turn(3))
    forward(1)
    shards_on(3)
    either("on", outer, lambda: plane_on(3))
    mate_on(2)
    either("turn", outer, lambda: plane_turn(3))
    either("mate", inner, lambda: mate_on(3))
    cotangent_wait()
    backward(1)
    either("mate", outer, lambda: mate_on(3))
    forward(2)
    plane_start(1)
    backward(2)
    last_forward()
    plane_start(2)
    backward(3)
    plane_middle(1)
    backward(0)
    plane_start(3)

    zero_row = jnp.zeros((1, D), F32)

    def norm_two_back(i, carry):
        at = rows(i * 128, 128, 128)
        unit, inverse = norm_stats(hid[at, :])
        grad = sgrad[at, :]
        scaled = grad * gain_two
        back = inverse * (
            scaled
            - jnp.mean(scaled, axis=1, keepdims=True)
            - unit * jnp.mean(scaled * unit, axis=1, keepdims=True)
        )
        top_grad = cot[at, :].astype(F32)
        whole = top_grad + back
        hgrad[at, :] = whole
        hgb[at, :] = whole.astype(BF16)
        parts = (grad * unit, grad, whole, top_grad)
        return tuple(a + jnp.sum(b, axis=0, keepdims=True) for a, b in zip(carry, parts))

    sums = lax.fori_loop(0, T // 128, norm_two_back, (zero_row,) * 4)
    sp[3:4, :] = sums[0]
    sp[4:5, :] = sums[1]
    sp[2:3, :] = sums[2]
    sp[5:6, :] = sums[3]

    plane_start(0)

    SH = R + HP
    out_grad = dot(mixg[...], hgb[...]).astype(BF16)
    for g in range(G):
        gqo[1, g * SH : g * SH + R, :] = out_grad[g * R : (g + 1) * R, :]
    qt[...] = dot_nt(wo[...], hgb[...])
    gate_grad = [jnp.zeros((1, T), F32), jnp.zeros((1, T), F32)]
    for part in range(N):
        picked_rows = [jnp.zeros((HP, T), F32), jnp.zeros((HP, T), F32)]
        for at in range(NE):
            for i in range(LE):
                lo = expert_rows(at, i, part)
                one = qt[lo : lo + HP, :]
                x = at * LE + i
                for k in range(2):
                    picked_rows[k] = picked_rows[k] + one * hot[k][x : x + 1, :]
        for k in range(2):
            span = slice(part * HP, (part + 1) * HP)
            rounded_mix = mix[k, span, :].astype(BF16).astype(F32)
            gate_grad[k] = gate_grad[k] + jnp.sum(picked_rows[k] * rounded_mix, axis=0, keepdims=True)
            mgk[k, span, :] = (picked_rows[k] * gate[k]).astype(BF16)
    middle = gate[0] * gate_grad[0] + gate[1] * gate_grad[1]
    logit_grad = sum(hot[k] * (gate[k] * (gate_grad[k] - middle)) for k in range(2))
    logit_low = logit_grad.astype(BF16)

    def attend_back(k):
        for i in range(tiles):
            at = pl.ds(i * TL, TL)
            low = prob[k, :, at]
            p = low.astype(F32)
            prob_grad = dot(vn[...], mgk[k, :, at])
            inner = jnp.sum(p * prob_grad, axis=0, keepdims=True)
            score = (p * (prob_grad - inner)).astype(BF16)
            dq[k, :, at] = (dot(kt[...], score) * scale).astype(BF16)
            key_part = dot_nt(score, qk[k, :, at])
            value_part = dot_nt(low, mgk[k, :, at])
            if k == 0 and i == 0:
                dk[...] = key_part
                dv[...] = value_part
            else:
                dk[...] = dk[...] + key_part
                dv[...] = dv[...] + value_part

    attend_back(0)
    plane_middle(2)
    line_start(1)
    attend_back(1)

    H, PC = z.reach, z.piece
    offsets = [o for o in range(-H, H + 1) if o]
    inside = T >= LONGEST

    def halo_source(o):
        if inside:
            return (spot_in_row + 1) * T - ws if o > 0 else spot_in_row * T - LONGEST - ws
        return (spot_in_row + o) * T - ws

    def halo_copy(s, o):
        to = rem(here + o + G, G)
        return pltpu.make_async_remote_copy(
            src_ref=halo_out.at[s],
            dst_ref=halo_in.at[s],
            send_sem=hl_s.at[s],
            recv_sem=hl_r.at[s],
            device_id=(d, lax.div(to, N), rem(to, N)),
            device_id_type=MESH,
        )

    for s, o in enumerate(offsets):
        valid = jnp.logical_and(spot_in_row + o >= 0, spot_in_row + o < z.per_row)

        @pl.when(valid)
        def _(s=s, o=o):
            at = rows(halo_source(o), PC, 128)
            halo_out[s, 0] = (dk[at, :] * scale).astype(BF16)
            halo_out[s, 1] = dv[at, :].astype(BF16)
            halo_copy(s, o).start()

    for part in range(N):
        for at in range(NE):
            for i in range(LE):
                lo = expert_rows(at, i, part)
                x = at * LE + i
                span = slice(part * HP, (part + 1) * HP)
                one = dq[0, span, :].astype(F32) * hot[0][x : x + 1, :]
                one = one + dq[1, span, :].astype(F32) * hot[1][x : x + 1, :]
                dqt[lo : lo + HP, :] = one.astype(BF16)
    query_w_grad = dot(dqt[...], rw[own, :]).astype(BF16)
    key_w_grad = dot_tn((dk[...] * scale).astype(BF16), rw[...]).astype(BF16)
    value_w_grad = dot_tn(dv[...].astype(BF16), rw[...]).astype(BF16)
    for g in range(G):
        shared = slice((g % N) * HP, (g % N + 1) * HP)
        gqo[0, g * SH : g * SH + R, :] = query_w_grad[g * R : (g + 1) * R, :]
        gqo[0, g * SH + R : (g + 1) * SH, :] = key_w_grad[shared, :]
        gqo[1, g * SH + R : (g + 1) * SH, :] = value_w_grad[shared, :]
    push(gqo.at[1 - c], cqo, qc_r.at[0], mate)
    plane_middle(3)
    ones = jnp.ones((8, T), BF16)
    sp[6:7, :] = dot_nt(ones, dqt[...])[0:1, :]
    sp[7:8, :] = jnp.zeros((1, D), F32)
    sp[7:8, 0 : z.experts] = jnp.transpose(
        jnp.broadcast_to(jnp.sum(logit_grad, axis=1, keepdims=True), (z.experts, 128))
    )[0:1, :]
    acc[...] = dot_tn(dqt[...], wq[...]) + dot_tn(logit_low, r_ref[...])
    sp[16:24, :] = dot(logit_low, rw[own, :])
    sp[15:16, :] = jnp.zeros((1, D), F32)
    sp[15:16, 0:HEAD] = jnp.sum(dv[...], axis=0, keepdims=True)
    YW = D // NY
    ER = N * SH
    landed(cqo, qc_r.at[0])
    plane_middle(0)
    pqo[...] = (gqo[c].astype(F32) + cqo[...].astype(F32)).astype(BF16)
    for i in range(1, NP):
        there, to = in_plane(i)
        src = pqo.at[rows(rem(there, NE) * ER, ER), rows(lax.div(there, NE) * YW, YW, 128)]
        push(src, rqo.at[i], qp_r.at[0], to)
    line_start(2)
    line_start(3)

    dk[...] = dk[...] * scale
    for s, o in enumerate(offsets):
        back_valid = jnp.logical_and(spot_in_row - o >= 0, spot_in_row - o < z.per_row)

        @pl.when(back_valid)
        def _(s=s, o=o):
            halo_copy(s, o).wait_recv()
            at = off if (not inside or o > 0) else off + T - LONGEST
            at = rows(at, PC, 128)
            dk[at, :] = dk[at, :] + halo_in[s, 0].astype(F32)
            dv[at, :] = dv[at, :] + halo_in[s, 1].astype(F32)

    key_grad = dk[own, :]
    value_grad = dv[own, :]
    key_low, value_low = key_grad.astype(BF16), value_grad.astype(BF16)
    acc[...] = acc[...] + dot(key_low, wkv[0]) + dot(value_low, wkv[1])

    def norm_one_back(i, carry):
        at = rows(i * 128, 128, 128)
        unit, inverse = norm_stats(xw[rows(off + i * 128, 128, 128), :])
        grad = acc[at, :]
        scaled = grad * gain_one
        back = inverse * (
            scaled
            - jnp.mean(scaled, axis=1, keepdims=True)
            - unit * jnp.mean(scaled * unit, axis=1, keepdims=True)
        )
        ig_ref[at, :] = hgrad[at, :] + back
        parts = (grad * unit, grad)
        return tuple(a + jnp.sum(b, axis=0, keepdims=True) for a, b in zip(carry, parts))

    sums = lax.fori_loop(0, T // 128, norm_one_back, (zero_row,) * 2)
    ig_copy = pltpu.make_async_copy(ig_ref, ig_any, loc_sem.at[4])
    ig_copy.start()
    sp[0:1, :] = sums[0]
    sp[1:2, :] = sums[1]
    for j in range(8 + N, 15):
        sp[j : j + 1, :] = zero_row
    push(sp.at[:, other_cols], csp, qc_r.at[1], mate)

    landed(csp, qc_r.at[1])
    psp[...] = sp[:, mine_cols] + csp[...]
    for i in range(1, NP):
        _, to = in_plane(i)
        push(psp, rsp.at[i], qp_r.at[1], to)

    line_start(0)

    whole = zsend[0].astype(F32)
    for j in range(1, N):
        there, _ = in_line(-j)
        landed(zrecv.at[there], gz_r.at[there])
        whole = whole + zrecv[there].astype(F32)

    def fin_left(buffer, core, ys, es):
        return buffer.at[rows(core * HR + (es * NY + ys) * HS, HS), left]

    def fin_right(buffer, core, ys, es):
        return buffer.at[rows(core * HR + (ys * NE + es) * HS, HS), right]

    def fin_to_mate(ys, es):
        for piece in (fin_left, fin_right):
            at = piece(fin, c, ys, es)
            push(at, at, ga_r.at[2 * NP - 2], mate)

    fin[rows(c * HR + (e * NY + y) * HS, HS), left] = whole[:, 0:half].astype(BF16)
    fin[rows(c * HR + (y * NE + e) * HS, HS), right] = whole[:, half:].astype(BF16)
    for i in range(1, NP):
        _, to = in_plane(i)
        at = fin_left(fin, c, y, e)
        push(at, at, ga_r.at[i - 1], to)
        at = fin_right(fin, c, y, e)
        push(at, at, ga_r.at[NP - 2 + i], to)
    fin_to_mate(y, e)

    whole = pqo[rows(e * ER, ER), rows(y * YW, YW, 128)].astype(F32)
    landed_all(NP - 1, rqo.at[0], qp_r.at[0])
    for i in range(1, NP):
        whole = whole + rqo[i].astype(F32)
    zqo[...] = whole.astype(BF16)
    for j in range(1, N):
        there, to = in_line(j)
        push(zqo.at[rows(there * SH, SH)], yqo.at[j], qz_r.at[0], to)
    whole = psp[...]
    landed_all(NP - 1, rsp.at[0], qp_r.at[1])
    for i in range(1, NP):
        whole = whole + rsp[i]
    zsp[...] = whole
    for j in range(1, N):
        _, to = in_line(j)
        push(zsp, ysp.at[j], qz_r.at[1], to)

    cols_copy.wait()
    landed_all(N - 1, outd.at[0], od_r.at[0])
    for j in range(N):
        at = pl.ds(j * T, T)
        out_ref[at, :] = out_ref[at, :] + outd[j].astype(F32)
    out_copy = pltpu.make_async_copy(out_ref, out_any, loc_sem.at[5])
    out_copy.start()

    whole = zqo[rows(n * SH, SH), :].astype(F32)
    landed_all(N - 1, yqo.at[0], qz_r.at[0])
    for j in range(1, N):
        whole = whole + yqo[j].astype(F32)
    my_cols = rows(y * YW, YW, 128)
    fqo[c, :, my_cols] = whole.astype(BF16)
    at = fqo.at[c, :, my_cols]
    others = [(i, other) for i in range(NY) for other in range(2) if i or other]
    for i, other in others:
        to = (2 * in_rows(i)[0] + (1 - c if other else c), e, n)
        push(at, at, qa_r.at[0], to)
    whole = zsp[...]
    landed_all(N - 1, ysp.at[0], qz_r.at[1])
    for j in range(1, N):
        whole = whole + ysp[j]
    fsp[:, mine_cols] = whole
    at = fsp.at[:, mine_cols]
    push(at, at, qa_r.at[1], mate)
    for i in range(1, NP):
        near, _ = in_plane(-i)
        ys, es = lax.div(near, NE), rem(near, NE)
        landed(fin_left(fin, c, ys, es), ga_r.at[i - 1])
        landed(fin_right(fin, c, ys, es), ga_r.at[NP - 2 + i])
        fin_to_mate(ys, es)
    at = rows(c * HR, HR)
    g_ref[at, :] = fin[at, :].astype(F32)
    landed(fsp.at[:, other_cols], qa_r.at[1])
    small_ref[...] = fsp[...]
    landed_all(len(others), fqo.at[0, :, pl.ds(0, YW)], qa_r.at[0])
    fqo_ref[...] = fqo[...]
    ig_copy.wait()
    out_copy.wait()
    landed(fin.at[rows((1 - c) * HR, HR)], ga_r.at[2 * NP - 2])
    at = rows((1 - c) * HR, HR)
    g_ref[at, :] = fin[at, :].astype(F32)

    for kind, size in enumerate(sent):
        at = ruler.at[pl.ds(0, size // 256)]
        if kind == 0:
            at = bias.at[pl.ds(0, size // (16 * 128 * 4))]
        pltpu.make_async_remote_copy(
            src_ref=at,
            dst_ref=at,
            send_sem=send_sems.at[kind],
            recv_sem=send_sems.at[kind],
            device_id=mate,
            device_id_type=MESH,
        ).wait_send()
    for valid, copies in maybe_started:

        @pl.when(valid)
        def _(copies=copies):
            for copy in copies:
                copy.wait_send()

    for s, o in enumerate(offsets):
        valid = jnp.logical_and(spot_in_row + o >= 0, spot_in_row + o < z.per_row)

        @pl.when(valid)
        def _(s=s, o=o):
            halo_copy(s, o).wait_send()


def run(z, x, seg, chosen, vectors, q, k, v, o, r, up, down, cot):
    N, G, NP, NY, NE = z.narrow, z.group, z.plane, z.rows_y, z.expert
    T, W, D, R, HP = z.block, z.window, z.width, z.shard, z.head_part
    FL = z.ff_local
    FR = D + FL
    HR = FR // 2
    HS = HR // NP
    YW = D // NY
    SH = R + HP
    ER = N * SH
    QR = G * R
    GR = G * SH
    S = 2 * z.reach
    SMALL = z.small_rows
    vmem = pl.BlockSpec(memory_space=pltpu.VMEM)
    anywhere = pl.BlockSpec(memory_space=pltpu.HBM)
    scratch = [
        ((N * T, D // N), F32),
        ((T, D), F32),
        ((W, D), F32),
        ((W, D), BF16),
        ((QR, D), BF16),
        ((QR, D), BF16),
        ((2, HEAD, D), BF16),
        ((G, 16, 128), F32),
        ((8, 128), F32),
        ((HEAD, 128), F32),
        ((N, FR, D), BF16),
        ((T, D), BF16),
        ((8, z.row_len), F32),
        ((W, 8), F32),
        ((W, HEAD), BF16),
        ((W, HEAD), BF16),
        ((HEAD, W), BF16),
        ((HEAD, W), BF16),
        ((QR, T), F32),
        ((2, HEAD, T), BF16),
        ((2, W, T), BF16),
        ((2, HEAD, T), F32),
        ((QR, T), BF16),
        ((T, D), F32),
        ((T, D), F32),
        ((T, D), BF16),
        ((N, T, FL), BF16),
        ((N, T, FL), BF16),
        ((T, FL), BF16),
        ((T, D), F32),
        ((T, D), F32),
        ((T, D), BF16),
        ((2, HEAD, T), BF16),
        ((W, HEAD), F32),
        ((W, HEAD), F32),
        ((2, HEAD, T), BF16),
        ((QR, T), BF16),
        ((max(S, 1), 2, z.piece, HEAD), BF16),
        ((max(S, 1), 2, z.piece, HEAD), BF16),
        ((T, D), BF16),
        ((N, T, D // N), BF16),
        ((N, FR, D), BF16),
        ((GROUP_BYTES // 256, 128), BF16),
        ((N, HR, D), BF16),
        ((N, HR, D), BF16),
        ((N, NE, HR // NE, D // 2), BF16),
        ((N, NY, HR // NY, D // 2), BF16),
        ((N, HR // NE, D // 2), BF16),
        ((N, HR // NY, D // 2), BF16),
        ((N, NY, HS, D // 2), BF16),
        ((N, NE, HS, D // 2), BF16),
        ((N, HS, D), BF16),
        ((N, HS, D), BF16),
        ((FR, D), BF16),
        ((2, GR, D), BF16),
        ((GR, D), BF16),
        ((GR, D), BF16),
        ((NP, ER, YW), BF16),
        ((ER, YW), BF16),
        ((N, SH, YW), BF16),
        ((2, SH, D), BF16),
        ((SMALL, D), F32),
        ((SMALL, D // 2), F32),
        ((SMALL, D // 2), F32),
        ((NP, SMALL, D // 2), F32),
        ((SMALL, D // 2), F32),
        ((N, SMALL, D // 2), F32),
        ((SMALL, D), F32),
    ]
    pairs = [
        (N - 1,),
        (1,),
        (G - 1,),
        (G - 1,),
        (1,),
        (G - 1,),
        (1,),
        (4, N - 1, max(NE, NY) - 1),
        (N - 1,),
        (1,),
        (1,),
        (max(S, 1),),
        (N,),
        (4, N, max(NE, NY) - 1),
        (N,),
        (2 * NP - 1,),
        (2,),
        (2,),
        (2,),
        (2,),
    ]
    HALO = 11
    sems = [pltpu.SemaphoreType.DMA((6,)), pltpu.SemaphoreType.DMA((GROUPS,))]
    for at, shape in enumerate(pairs):
        sems += [pltpu.SemaphoreType.DMA(shape)] * (2 if at == HALO else 1)
    sems += [pltpu.SemaphoreType.DMA((2, 2, N)), pltpu.SemaphoreType.DMA((2, N))]
    outs = [
        ((N * T, D // N), F32),
        ((T, D), F32),
        ((FR, D), F32),
        ((2, SH, D), BF16),
        ((SMALL, D), F32),
    ]
    return pl.pallas_call(
        functools.partial(kernel, z),
        out_shape=[pltpu.VMEM(s, t) for s, t in outs],
        in_specs=[anywhere] + [vmem] * (7 + len(vectors)) + [anywhere] * 2 + [vmem],
        out_specs=[pl.BlockSpec(memory_space=pl.ANY)] * 2 + [vmem] * 3,
        scratch_shapes=[pltpu.VMEM(s, t) for s, t in scratch] + sems,
        compiler_params=pltpu.CompilerParams(
            collective_id=0, has_side_effects=True, vmem_limit_bytes=58 * 2**20
        ),
        name="layer",
    )(x, seg, chosen, *vectors, q, k, v, o, r, up, down, cot)


def finish_kernel(
    z,
    out_in,
    ig_in,
    g_in,
    fqo_ref,
    small_ref,
    out_any,
    ig_out,
    g1_ref,
    s1_ref,
    gq_ref,
    qb_ref,
    gk_ref,
    gv_ref,
    vb_ref,
    go_ref,
    ob_ref,
    rw_ref,
    rb_ref,
    g2_ref,
    s2_ref,
    gup_any,
    ub_ref,
    gdown_any,
    db_ref,
    sems,
):
    e, n = lax.axis_index("expert"), lax.axis_index("narrow")
    N, T, D, R, HP, LE = z.narrow, z.block, z.width, z.shard, z.head_part, z.local_experts
    copies = []

    def put(src, dst):
        copies.append(pltpu.make_async_copy(src, dst, sems.at[len(copies)]))
        copies[-1].start()

    put(out_in, out_any)
    put(ig_in, ig_out)
    put(g_in.at[pl.ds(0, D)], gup_any)
    put(g_in.at[pl.ds(D, z.ff_local)], gdown_any)
    gq_ref[...] = fqo_ref[0, 0:R, :].astype(F32)
    go_ref[...] = fqo_ref[1, 0:R, :].astype(F32)
    gk_ref[...] = fqo_ref[0, R : R + HP, :].astype(F32)
    gv_ref[...] = fqo_ref[1, R : R + HP, :].astype(F32)
    g1_ref[...] = small_ref[0:1, :]
    s1_ref[...] = small_ref[1:2, :]
    ob_ref[...] = small_ref[2:3, :]
    g2_ref[...] = small_ref[3:4, :]
    s2_ref[...] = small_ref[4:5, :]
    db_ref[...] = small_ref[5:6, :]
    rb_ref[...] = small_ref[7:8, 0 : z.experts]
    rw_ref[...] = small_ref[16 : 16 + z.experts, :]
    upper = jnp.zeros((1, D), F32)
    for j in range(N):
        upper = jnp.where(n == j, small_ref[8 + j : 9 + j, :], upper)
    ub_ref[...] = upper
    here = e * N + n
    query = pltpu.roll(small_ref[0:8, :], lax.rem(D - here * R, D), 1)
    for i in range(LE):
        qb_ref[i : i + 1, :] = query[6:7, i * HP : (i + 1) * HP]
    value = pltpu.roll(small_ref[8:16, :], lax.rem(D - n * HP, D), 1)
    vb_ref[...] = value[7:8, 0:HP]
    for copy in copies:
        copy.wait()


def finish(z, out, ig, fin, fqo, small):
    N, T, D, R, HP = z.narrow, z.block, z.width, z.shard, z.head_part
    FL = z.ff_local
    vmem = pl.BlockSpec(memory_space=pltpu.VMEM)
    anywhere = pl.BlockSpec(memory_space=pltpu.HBM)
    shapes = [
        (N * T, D // N),
        (T, D),
        (1, D),
        (1, D),
        (R, D),
        (z.local_experts, HP),
        (HP, D),
        (HP, D),
        (1, HP),
        (R, D),
        (1, D),
        (z.experts, D),
        (1, z.experts),
        (1, D),
        (1, D),
        (D, FL),
        (1, FL),
        (FL, D),
        (1, D),
    ]
    return pl.pallas_call(
        functools.partial(finish_kernel, z),
        out_shape=[jax.ShapeDtypeStruct(s, F32) for s in shapes],
        in_specs=[pl.BlockSpec(memory_space=pl.ANY)] * 3 + [vmem] * 2,
        out_specs=[anywhere] * 2 + [vmem] * 13 + [anywhere, vmem, anywhere, vmem],
        scratch_shapes=[
            pltpu.SemaphoreType.DMA((4,)),
        ],
        compiler_params=pltpu.CompilerParams(vmem_limit_bytes=16 * 2**20),
        name="finish",
    )(out, ig, fin, fqo, small)


def per_device(
    inputs,
    seg_ids,
    chosen,
    gain_one,
    shift_one,
    query_w,
    query_b,
    key_w,
    value_w,
    value_b,
    out_w,
    out_b,
    router_w,
    router_b,
    gain_two,
    shift_two,
    up_w,
    up_b,
    down_w,
    down_b,
    cotangent,
):
    narrow = lax.axis_size("narrow")
    e, n = lax.axis_index("expert"), lax.axis_index("narrow")
    z = Sizes(
        lax.axis_size("dp"),
        lax.axis_size("expert"),
        narrow,
        inputs.shape[0],
        inputs.shape[1],
        seg_ids.shape[1],
        query_w.shape[0],
        up_w.shape[1],
    )
    D, R, HP = z.width, z.shard, z.head_part
    vectors = [gain_one, shift_one, out_b, gain_two, shift_two, down_b, up_b]
    vectors = [v.reshape(1, -1) for v in vectors]
    vectors += [query_b, value_b.reshape(1, -1), router_b.reshape(1, -1)]
    parts = run(
        z,
        inputs,
        seg_ids,
        jnp.transpose(chosen),
        vectors,
        jnp.transpose(query_w, (0, 2, 1)).reshape(R, D),
        jnp.transpose(key_w),
        jnp.transpose(value_w),
        out_w.reshape(R, D),
        jnp.transpose(router_w),
        up_w,
        down_w,
        cotangent,
    )
    out, ig, g1, s1, gq, qb, gk, gv, vb, go, ob, rw, rb, g2, s2, gup, ub, gdown, db = finish(
        z, *parts
    )
    return (
        out,
        ig,
        g1.reshape(-1),
        s1.reshape(-1),
        jnp.transpose(gq.reshape(z.local_experts, HP, D), (0, 2, 1)),
        qb,
        jnp.transpose(gk),
        jnp.transpose(gv),
        vb.reshape(-1),
        go.reshape(z.local_experts, HP, D),
        ob.reshape(-1),
        jnp.transpose(rw),
        rb.reshape(-1),
        g2.reshape(-1),
        s2.reshape(-1),
        gup,
        ub.reshape(-1),
        gdown,
        db.reshape(-1),
    )


def solution(mesh):
    return jax.shard_map(
        per_device,
        mesh=mesh,
        in_specs=(
            P("dp", None),
            P("dp", None),
            P("dp", None),
            P(),
            P(),
            P("expert", None, "narrow"),
            P("expert", "narrow"),
            P(None, "narrow"),
            P(None, "narrow"),
            P("narrow"),
            P("expert", "narrow", None),
            P(),
            P(),
            P(),
            P(),
            P(),
            P(None, "narrow"),
            P("narrow"),
            P("narrow", None),
            P(),
            P(("dp", "expert"), "narrow"),
        ),
        out_specs=(
            P(("dp", "expert"), "narrow"),
            P(("dp", "expert", "narrow"), None),
            P(),
            P(),
            P("expert", None, "narrow"),
            P("expert", "narrow"),
            P(None, "narrow"),
            P(None, "narrow"),
            P("narrow"),
            P("expert", "narrow", None),
            P(),
            P(),
            P(),
            P(),
            P(),
            P(None, "narrow"),
            P("narrow"),
            P("narrow", None),
            P(),
        ),
        check_vma=False,
    )
```

```python
import functools
import math

import jax
import jax.numpy as jnp
from jax import lax
from jax.experimental import pallas as pl
from jax.experimental.pallas import tpu as pltpu
from jax.sharding import PartitionSpec as P

HEAD = 64
LONGEST = 256
EPSILON = 1e-05
MASKED = -1000000000.0
GELU_A = math.sqrt(2.0 / math.pi)
GELU_B = 0.044715
F32 = jnp.float32
BF16 = jnp.bfloat16
MESH = pl.DeviceIdType.MESH
GROUP_BYTES = 2**21
GROUPS = 8


def dot(a, b):
    return lax.dot_general(a, b, (((1,), (0,)), ((), ())), preferred_element_type=F32)


def dot_nt(a, b):
    return lax.dot_general(a, b, (((1,), (1,)), ((), ())), preferred_element_type=F32)


def dot_tn(a, b):
    return lax.dot_general(a, b, (((0,), (0,)), ((), ())), preferred_element_type=F32)


def norm_stats(x):
    centred = x - jnp.mean(x, axis=1, keepdims=True)
    inverse = lax.rsqrt(jnp.mean(centred * centred, axis=1, keepdims=True) + EPSILON)
    return centred * inverse, inverse


def rem(a, b):
    return lax.rem(a, b)


class Sizes:
    def __init__(self, dp, expert, narrow, tokens, width, row_len, local_experts, ff_local):
        self.dp, self.expert, self.narrow = dp, expert, narrow
        self.tokens, self.width, self.row_len = tokens, width, row_len
        self.local_experts = local_experts
        self.experts = local_experts * expert
        self.group = expert * narrow
        self.block = tokens // self.group
        self.rows_y = dp // 2
        self.plane = self.rows_y * expert
        self.ff_local = ff_local
        self.head_part = HEAD // narrow
        self.shard = local_experts * self.head_part
        self.per_row = row_len // self.block
        spans = [
            min(row_len, (j + 1) * self.block + LONGEST) - max(0, j * self.block - LONGEST)
            for j in range(self.per_row)
        ]
        self.window = max(spans)
        self.reach = max(1, LONGEST // self.block) if self.per_row > 1 else 0
        self.piece = min(self.block, LONGEST)
        self.tile = min(256, self.block)
        self.up_rows = narrow * ff_local // width
        self.small_rows = 24


def kernel(
    z,
    x_any,
    seg_ref,
    chosen_ref,
    g1_ref,
    s1_ref,
    ob_ref,
    g2_ref,
    s2_ref,
    db_ref,
    ub_ref,
    qb_ref,
    vb_ref,
    rb_ref,
    q_ref,
    k_ref,
    v_ref,
    o_ref,
    r_ref,
    up_any,
    down_any,
    cot_ref,
    out_any,
    ig_any,
    g_ref,
    fqo_ref,
    small_ref,
    out_ref,
    ig_ref,
    xw,
    rw,
    wq,
    wo,
    wkv,
    bias,
    corner,
    vcol,
    ffw,
    cot,
    segs,
    segc,
    kn,
    vn,
    kt,
    vt,
    qt,
    qk,
    prob,
    mix,
    mixg,
    hid,
    acc,
    second,
    active,
    slope,
    ugrad,
    sgrad,
    hgrad,
    hgb,
    mgk,
    dk,
    dv,
    dq,
    dqt,
    halo_out,
    halo_in,
    delta,
    outd,
    gsend,
    ruler,
    crecv,
    psend,
    pea,
    pya,
    mea,
    mya,
    pyb,
    peb,
    zsend,
    zrecv,
    fin,
    gqo,
    cqo,
    pqo,
    rqo,
    zqo,
    yqo,
    fqo,
    sp,
    csp,
    psp,
    rsp,
    zsp,
    ysp,
    fsp,
    loc_sem,
    send_sems,
    w_r,
    wm_r,
    b_r,
    q_r,
    qm_r,
    o_r,
    om_r,
    fp_r,
    fm_r,
    ct_r,
    od_r,
    hl_s,
    hl_r,
    gc_r,
    gp_r,
    gz_r,
    ga_r,
    qc_r,
    qp_r,
    qz_r,
    qa_r,
    fz_s,
    fz_r,
):
    d, e, n = lax.axis_index("dp"), lax.axis_index("expert"), lax.axis_index("narrow")
    c, y = rem(d, 2), lax.div(d, 2)
    N, G, NP, NE, NY = z.narrow, z.group, z.plane, z.expert, z.rows_y
    T, W, D, R, HP, LE = z.block, z.window, z.width, z.shard, z.head_part, z.local_experts
    FL = z.ff_local
    half = D // 2
    here = e * N + n
    spot = y * NE + e
    mate = (d + 1 - 2 * c, e, n)

    def in_group(j):
        at = rem(here + j + G, G)
        return at, (d, lax.div(at, N), rem(at, N))

    def in_plane(j):
        at = rem(spot + j + NP, NP)
        return at, (2 * lax.div(at, NE) + c, rem(at, NE), n)

    def in_line(j):
        at = rem(n + j + N, N)
        return at, (d, e, at)

    def in_rows(j):
        at = rem(y + j + NY, NY)
        return at, (2 * at + c, e, n)

    sent = [0, 0]
    noted = {}

    def either(name, valid, block):
        again = name in noted
        kinds = noted.setdefault(name, [])
        turn = iter(list(kinds)) if again else None

        @pl.when(valid)
        def _():
            mode.append((kinds, turn))
            block()
            mode.pop()

    mode = []

    def push(src, dst, recv, device):
        size = math.prod(src.shape) * jnp.dtype(src.dtype).itemsize
        if mode and mode[-1][1] is not None:
            kind = next(mode[-1][1])
        else:
            kind = 0
            if not (src.shape[-1] == 128 and src.dtype == F32):
                if sent[-1] + size > GROUP_BYTES:
                    sent.append(0)
                kind = len(sent) - 1
            sent[kind] += size
            if mode:
                mode[-1][0].append(kind)
        copy = pltpu.make_async_remote_copy(
            src_ref=src,
            dst_ref=dst,
            send_sem=send_sems.at[kind],
            recv_sem=recv,
            device_id=device,
            device_id_type=MESH,
        )
        copy.start()

    def landed(dst, recv):
        pltpu.make_async_remote_copy(
            src_ref=dst,
            dst_ref=dst,
            send_sem=recv,
            recv_sem=recv,
            device_id=mate,
            device_id_type=MESH,
        ).wait_recv()

    def landed_all(count, of, recv):
        size = count * math.prod(of.shape) * jnp.dtype(of.dtype).itemsize
        landed(ruler.at[pl.ds(0, size // 256)], recv)

    def rows(start, size, step=16):
        return pl.ds(pl.multiple_of(start, step), size)

    start = here * T
    row = lax.div(start, z.row_len)
    spot_in_row = rem(here, z.per_row)
    base = row * z.row_len
    ws = jnp.minimum(jnp.maximum(spot_in_row * T - LONGEST, 0), z.row_len - W)
    off = spot_in_row * T - ws
    own = rows(off, T, 128)

    x_copy = pltpu.make_async_copy(x_any.at[rows(base + ws, W, 128)], xw, loc_sem.at[0])
    x_copy.start()
    up_copy = pltpu.make_async_copy(up_any, ffw.at[n, pl.ds(0, D)], loc_sem.at[1])
    up_copy.start()
    down_copy = pltpu.make_async_copy(down_any, ffw.at[n, pl.ds(D, FL)], loc_sem.at[2])
    down_copy.start()
    cols_copy = pltpu.make_async_copy(
        x_any.at[rows(e * N * T, N * T, 128), rows(n * (D // N), D // N, 128)], out_ref, loc_sem.at[3]
    )
    cols_copy.start()
    wq[rows(here * R, R)] = q_ref[...]
    wo[rows(here * R, R)] = o_ref[...]
    wkv[0, rows(n * HP, HP)] = k_ref[...]
    wkv[1, rows(n * HP, HP)] = v_ref[...]
    bias[here] = jnp.zeros((16, 128), F32)
    for i in range(FL // 128):
        bias[here, i : i + 1, :] = ub_ref[0:1, i * 128 : (i + 1) * 128]
    bias[here, 8 : 8 + LE, 0:HP] = qb_ref[...]
    bias[here, 7:8, 0:HP] = vb_ref[...]

    barrier = pltpu.get_barrier_semaphore()
    pl.semaphore_signal(barrier, inc=1, device_id=mate, device_id_type=MESH)
    for j in range(1, NP):
        pl.semaphore_signal(barrier, inc=1, device_id=in_plane(j)[1], device_id_type=MESH)
    for j in range(1, G):
        pl.semaphore_signal(barrier, inc=1, device_id=in_group(j)[1], device_id_type=MESH)
    for j in range(1, NY):
        to = (2 * in_rows(j)[0] + 1 - c, e, n)
        pl.semaphore_signal(barrier, inc=1, device_id=to, device_id_type=MESH)
    pl.semaphore_wait(barrier, NP + G + NY - 2)

    mine_cols = rows(c * half, half, 128)
    other_cols = rows((1 - c) * half, half, 128)

    def in_expert(i):
        at = rem(e + i + NE, NE)
        return at, (d, at, n)

    def shard_at(i, j):
        return rem(e - i + NE, NE) * N + rem(n - j + N, N)

    def spread_start(part, recv):
        for j in range(1, N):
            at = part(here)
            push(at, at, recv.at[j - 1], in_line(j)[1])
        for i in range(1, NE):
            at = part(here)
            push(at, at, recv.at[i * N - 1], in_expert(i)[1])

    def spread_on(part, recv, to_mate):
        for j in range(1, N):
            at = part(shard_at(0, j))
            landed(at, recv.at[j - 1])
            for i in range(1, NE):
                push(at, at, recv.at[i * N + j - 1], in_expert(i)[1])
            if to_mate is not None:
                push(at, at, to_mate.at[0], mate)

    def spread_end(part, recv, to_mate):
        for i in range(1, NE):
            for j in range(N):
                at = part(shard_at(i, j))
                landed(at, recv.at[i * N + j - 1])
                if to_mate is not None:
                    push(at, at, to_mate.at[0], mate)

    def spread_wait(part, to_mate):
        landed_all(G - 1, part(0), to_mate.at[0])

    def bias_part(g):
        return bias.at[g]

    def q_part(g):
        return wq.at[rows(g * R, R), mine_cols]

    def q_other(g):
        return wq.at[rows(g * R, R), other_cols]

    def o_part(g):
        return wo.at[rows(g * R, R), mine_cols]

    def o_other(g):
        return wo.at[rows(g * R, R), other_cols]

    for j in range(1, N):
        at = wkv.at[c, rows(n * HP, HP)]
        push(at, at, w_r.at[j - 1], in_line(j)[1])
    spread_start(q_part, q_r)
    spread_start(bias_part, b_r)
    up_copy.wait()
    down_copy.wait()
    FR = D + FL

    left, right = pl.ds(0, half), pl.ds(half, half)
    HR = FR // 2
    HS = HR // NP
    HA, HB = HR // NE, HR // NY
    def left_slice(of, ys, es):
        return ffw.at[of, rows(c * HR + (es * NY + ys) * HS, HS), left]

    def right_slice(of, ys, es):
        return ffw.at[of, rows(c * HR + (ys * NE + es) * HS, HS), right]

    def left_half(of, es):
        return ffw.at[of, rows(c * HR + es * HA, HA), left]

    def right_half(of, ys):
        return ffw.at[of, rows(c * HR + ys * HB, HB), right]

    def by_distance(at):
        return sorted((o for o in range(N) if o != at), key=lambda o: (abs(o - at), o if 2 * at >= N else -o))

    def pick(choices):
        value = choices[0]
        for at in range(1, N):
            value = jnp.where(n == at, choices[at], value)
        return value

    shard_of = [n] + [pick([by_distance(at)[k] for at in range(N)]) for k in range(N - 1)]
    maybe_started = []

    def line_push(of, step, valid):
        of = jnp.clip(of, 0, N - 1)
        to = (d, e, jnp.clip(n + step, 0, N - 1))
        way = (step + 1) // 2
        copies = [
            pltpu.make_async_remote_copy(
                src_ref=at,
                dst_ref=at,
                send_sem=fz_s.at[part, way, of],
                recv_sem=fz_r.at[part, of],
                device_id=to,
                device_id_type=MESH,
            )
            for part, at in enumerate((left_slice(of, y, e), right_slice(of, y, e)))
        ]

        @pl.when(valid)
        def _():
            for copy in copies:
                copy.start()

        maybe_started.append((valid, copies))

    def line_landed(of, valid):
        of = jnp.clip(of, 0, N - 1)

        @pl.when(valid)
        def _():
            landed(left_slice(of, y, e), fz_r.at[0, of])
            landed(right_slice(of, y, e), fz_r.at[1, of])

    def shards_start():
        line_push(n, 1, n + 1 < N)
        line_push(n, -1, n > 0)

    def shards_on(hop):
        line_landed(n - hop, n >= hop)
        line_push(n - hop, 1, jnp.logical_and(n >= hop, n + 1 < N))
        line_landed(n + hop, n + hop < N)
        line_push(n + hop, -1, jnp.logical_and(n + hop < N, n > 0))

    def plane_on(j):
        there = shard_of[j]
        at = left_slice(there, y, e)
        for i in range(1, NY):
            push(at, at, fp_r.at[0, j - 1, i - 1], in_rows(i)[1])
        at = right_slice(there, y, e)
        for i in range(1, NE):
            push(at, at, fp_r.at[1, j - 1, i - 1], in_expert(i)[1])

    def plane_turn(j):
        there = shard_of[j]
        for i in range(1, NY):
            near, _ = in_rows(-i)
            landed(left_slice(there, near, e), fp_r.at[0, j - 1, i - 1])
        at = left_half(there, e)
        for i in range(1, NE):
            push(at, at, fp_r.at[2, j - 1, i - 1], in_expert(i)[1])
        for i in range(1, NE):
            near, _ = in_expert(-i)
            landed(right_slice(there, y, near), fp_r.at[1, j - 1, i - 1])
        at = right_half(there, y)
        for i in range(1, NY):
            push(at, at, fp_r.at[3, j - 1, i - 1], in_rows(i)[1])

    def mate_on(j):
        there = shard_of[j]
        for i in range(1, NE):
            near, _ = in_expert(-i)
            landed(left_half(there, near), fp_r.at[2, j - 1, i - 1])
        for i in range(1, NY):
            near, _ = in_rows(-i)
            landed(right_half(there, near), fp_r.at[3, j - 1, i - 1])
        at = ffw.at[there, rows(c * HR, HR)]
        push(at, at, fm_r.at[j - 1], mate)

    x_copy.wait()
    gain_one, shift_one = g1_ref[...], s1_ref[...]

    def norm_one(i, carry):
        at = rows(i * 128, 128, 128)
        unit, _ = norm_stats(xw[at, :])
        rw[at, :] = (unit * gain_one + shift_one).astype(BF16)
        return carry

    lax.fori_loop(0, W // 128, norm_one, 0)

    seg_all = seg_ref[...].astype(F32)
    row_id = lax.broadcasted_iota(jnp.int32, seg_all.shape, 0)
    seg_here = jnp.sum(jnp.where(row_id == row, seg_all, 0.0), axis=0, keepdims=True)
    segs[...] = jnp.broadcast_to(seg_here, segs.shape)
    segc[...] = jnp.transpose(segs[:, rows(ws, W, 128)])
    seg_own = segs[0:1, rows(spot_in_row * T, T, 128)]
    corner[...] = jnp.zeros_like(corner)
    corner[:, 0 : z.experts] = jnp.broadcast_to(rb_ref[...], (8, z.experts))
    router_col = jnp.transpose(corner[...])[0 : z.experts, 0:1]
    logits = dot_nt(r_ref[...], rw[own, :]) + router_col
    expert_id = lax.broadcasted_iota(jnp.int32, (z.experts, T), 0)
    hot, picked = [], []
    for k in range(2):
        chosen = chosen_ref[k : k + 1, rows(start, T, 128)]
        hot.append((expert_id == chosen).astype(F32))
        picked.append(jnp.sum(logits * hot[k], axis=0, keepdims=True))
    top = jnp.maximum(picked[0], picked[1])
    raised = [jnp.exp(p - top) for p in picked]
    total = raised[0] + raised[1]
    gate = [r / total for r in raised]

    for j in range(1, N):
        there, _ = in_line(-j)
        at = wkv.at[c, rows(there * HP, HP)]
        landed(at, w_r.at[j - 1])
        push(at, at, wm_r.at[0], mate)
    spread_on(q_part, q_r, qm_r)
    spread_on(bias_part, b_r, None)
    shards_start()
    spread_start(o_part, o_r)

    landed_all(N - 1, wkv.at[0, pl.ds(0, HP)], wm_r.at[0])
    kn[...] = dot_nt(rw[...], wkv[0]).astype(BF16)
    kt[...] = dot_nt(wkv[0], rw[...]).astype(BF16)
    spread_end(q_part, q_r, qm_r)
    spread_end(bias_part, b_r, None)
    columns = [jnp.transpose(bias[g, 0:16, :]) for g in range(G)]
    for part in range(N):
        vcol[part * HP : (part + 1) * HP, :] = jnp.broadcast_to(columns[part][0:HP, 7:8], (HP, 128))
    value_row = jnp.transpose(vcol[...])[0:1, :]
    vn[...] = (dot_nt(rw[...], wkv[1]) + value_row).astype(BF16)
    vt[...] = (dot_nt(wkv[1], rw[...]) + vcol[:, 0:1]).astype(BF16)

    spread_wait(q_other, qm_r)
    qt[...] = dot_nt(wq[...], rw[own, :])

    def expert_rows(at, i, part):
        return ((at * N + part) * LE + i) * HP

    for part in range(N):
        chosen_rows = [jnp.zeros((HP, T), F32), jnp.zeros((HP, T), F32)]
        for at in range(NE):
            g = at * N + part
            for i in range(LE):
                lo = expert_rows(at, i, part)
                one = qt[lo : lo + HP, :] + columns[g][0:HP, 8 + i : 9 + i]
                for k in range(2):
                    chosen_rows[k] = chosen_rows[k] + one * hot[k][at * LE + i : at * LE + i + 1, :]
        for k in range(2):
            qk[k, part * HP : (part + 1) * HP, :] = chosen_rows[k].astype(BF16)

    scale = 1.0 / math.sqrt(HEAD)
    TL = z.tile
    tiles = T // TL
    seg_tiles = [seg_own[:, i * TL : (i + 1) * TL] for i in range(tiles)]

    def attend(k):
        for i in range(tiles):
            at = pl.ds(i * TL, TL)
            scores = dot(kn[...], qk[k, :, at]) * scale
            scores = jnp.where(segc[:, 0:1] == seg_tiles[i], scores, MASKED)
            high = jnp.max(scores, axis=0, keepdims=True)
            raised_scores = jnp.exp(scores - high)
            low = (raised_scores * (1.0 / jnp.sum(raised_scores, axis=0, keepdims=True))).astype(BF16)
            prob[k, :, at] = low
            mix[k, :, at] = dot(vt[...], low)

    attend(0)
    attend(1)
    shards_on(1)
    plane_on(1)
    spread_on(o_part, o_r, om_r)
    plane_turn(1)
    shards_on(2)
    plane_on(2)
    CW = D // N
    cot[:, rows(n * CW, CW, 128)] = cot_ref[rows(n * T, T, 128), :]
    for j in range(1, N):
        there, to = in_line(j)
        push(
            cot_ref.at[rows(there * T, T, 128)],
            cot.at[:, rows(n * CW, CW, 128)],
            ct_r.at[0],
            to,
        )
    outer = jnp.logical_or(n >= 3, n + 3 < N)
    inner = jnp.logical_not(outer)
    either("on", inner, lambda: plane_on(3))
    spread_end(o_part, o_r, om_r)

    for part in range(N):
        for at in range(NE):
            for i in range(LE):
                lo = expert_rows(at, i, part)
                x = at * LE + i
                gated = jnp.zeros((HP, T), F32)
                for k in range(2):
                    rounded_mix = mix[k, part * HP : (part + 1) * HP, :].astype(BF16).astype(F32)
                    gated = gated + rounded_mix * (hot[k][x : x + 1, :] * gate[k])
                mixg[lo : lo + HP, :] = gated.astype(BF16)
    spread_wait(o_other, om_r)
    out_b, down_b = ob_ref[...], db_ref[...]
    gain_two, shift_two = g2_ref[...], s2_ref[...]
    attention = dot_tn(mixg[...], wo[...]) + out_b
    acc[...] = attention + down_b
    hid[...] = xw[own, :] + attention

    def norm_two(i, carry):
        at = rows(i * 128, 128, 128)
        unit, _ = norm_stats(hid[at, :])
        second[at, :] = (unit * gain_two + shift_two).astype(BF16)
        return carry

    lax.fori_loop(0, T // 128, norm_two, 0)
    sgrad[...] = jnp.zeros_like(sgrad)

    def core_start(j):
        push(
            gsend.at[j, rows((1 - c) * HR, HR)], crecv.at[j], gc_r.at[j], mate
        )

    def plane_start(j):
        landed(crecv.at[j], gc_r.at[j])
        psend[j] = (
            gsend[j, rows(c * HR, HR), :].astype(F32) + crecv[j].astype(F32)
        ).astype(BF16)
        for i in range(1, NE):
            there, to = in_expert(i)
            src = psend.at[j, rows(there * HA, HA), left]
            push(src, pea.at[j, i], gp_r.at[0, j, i - 1], to)
        for i in range(1, NY):
            there, to = in_rows(i)
            src = psend.at[j, rows(there * HB, HB), right]
            push(src, pya.at[j, i], gp_r.at[1, j, i - 1], to)

    def plane_middle(j):
        whole = psend[j, rows(e * HA, HA), left].astype(F32)
        for i in range(1, NE):
            landed(pea.at[j, i], gp_r.at[0, j, i - 1])
            whole = whole + pea[j, i].astype(F32)
        mea[j] = whole.astype(BF16)
        for i in range(1, NY):
            there, to = in_rows(i)
            src = mea.at[j, rows(there * HS, HS)]
            push(src, pyb.at[j, i], gp_r.at[2, j, i - 1], to)
        whole = psend[j, rows(y * HB, HB), right].astype(F32)
        for i in range(1, NY):
            landed(pya.at[j, i], gp_r.at[1, j, i - 1])
            whole = whole + pya[j, i].astype(F32)
        mya[j] = whole.astype(BF16)
        for i in range(1, NE):
            there, to = in_expert(i)
            src = mya.at[j, rows(there * HS, HS)]
            push(src, peb.at[j, i], gp_r.at[3, j, i - 1], to)

    def line_start(j):
        whole = mea[j, rows(y * HS, HS), :].astype(F32)
        for i in range(1, NY):
            landed(pyb.at[j, i], gp_r.at[2, j, i - 1])
            whole = whole + pyb[j, i].astype(F32)
        zsend[j, :, left] = whole.astype(BF16)
        whole = mya[j, rows(e * HS, HS), :].astype(F32)
        for i in range(1, NE):
            landed(peb.at[j, i], gp_r.at[3, j, i - 1])
            whole = whole + peb[j, i].astype(F32)
        zsend[j, :, right] = whole.astype(BF16)
        if j:
            push(zsend.at[j], zrecv.at[n], gz_r.at[n], (d, e, shard_of[j]))

    def forward(j):
        there = shard_of[j]
        if j:
            landed(ffw.at[there, rows((1 - c) * HR, HR)], fm_r.at[j - 1])
        up_b = jnp.concatenate(
            [bias[e * N + there, i : i + 1, :] for i in range(FL // 128)], axis=1
        )

        def feed(i, carry):
            at = rows(i * TL, TL, 128)
            upper = dot(second[at, :], ffw[there, 0:D, :]) + up_b
            square = upper * upper
            t = jnp.tanh(upper * (GELU_A + (GELU_A * GELU_B) * square))
            one = 0.5 + 0.5 * t
            low = (upper * one).astype(BF16)
            active[j, at, :] = low
            slope[j, at, :] = (
                one + (0.5 * upper) * (1.0 - t * t) * (GELU_A + (3.0 * GELU_A * GELU_B) * square)
            ).astype(BF16)
            acc[at, :] = acc[at, :] + dot(low, ffw[there, D : D + FL, :])
            return carry

        lax.fori_loop(0, T // TL, feed, 0)

    def backward(j):
        there = shard_of[j]

        def feed_back(i, carry):
            at = rows(i * TL, TL, 128)
            back = dot_nt(cot[at, :], ffw[there, D : D + FL, :]) * slope[j, at, :].astype(F32)
            back = back.astype(BF16)
            ugrad[at, :] = back
            sgrad[at, :] = sgrad[at, :] + dot_nt(back, ffw[there, 0:D, :])
            return carry

        lax.fori_loop(0, T // TL, feed_back, 0)
        sp[pl.ds(8 + there, 1), :] = jnp.sum(ugrad[...].astype(F32), axis=0, keepdims=True)
        gsend[j, 0:D, :] = dot_tn(second[...], ugrad[...]).astype(BF16)
        gsend[j, D : D + FL, :] = dot_tn(active[j], cot[...]).astype(BF16)
        core_start(j)

    def cotangent_wait():
        landed_all(N - 1, cot.at[:, pl.ds(0, CW)], ct_r.at[0])

    def last_forward():
        forward(3)
        delta[...] = acc[...].astype(BF16)
        outd[n] = delta[:, rows(n * CW, CW, 128)]
        for j in range(1, N):
            there, to = in_line(j)
            push(delta.at[:, rows(there * CW, CW, 128)], outd.at[n], od_r.at[0], to)

    forward(0)
    plane_turn(2)
    mate_on(1)
    either("turn", inner, lambda: plane_turn(3))
    forward(1)
    shards_on(3)
    either("on", outer, lambda: plane_on(3))
    mate_on(2)
    either("turn", outer, lambda: plane_turn(3))
    either("mate", inner, lambda: mate_on(3))
    cotangent_wait()
    backward(1)
    either("mate", outer, lambda: mate_on(3))
    forward(2)
    plane_start(1)
    backward(2)
    last_forward()
    plane_start(2)
    backward(3)
    plane_middle(1)
    backward(0)
    plane_start(3)

    zero_row = jnp.zeros((1, D), F32)

    def norm_two_back(i, carry):
        at = rows(i * 128, 128, 128)
        unit, inverse = norm_stats(hid[at, :])
        grad = sgrad[at, :]
        scaled = grad * gain_two
        back = inverse * (
            scaled
            - jnp.mean(scaled, axis=1, keepdims=True)
            - unit * jnp.mean(scaled * unit, axis=1, keepdims=True)
        )
        top_grad = cot[at, :].astype(F32)
        whole = top_grad + back
        hgrad[at, :] = whole
        hgb[at, :] = whole.astype(BF16)
        parts = (grad * unit, grad, whole, top_grad)
        return tuple(a + jnp.sum(b, axis=0, keepdims=True) for a, b in zip(carry, parts))

    sums = lax.fori_loop(0, T // 128, norm_two_back, (zero_row,) * 4)
    sp[3:4, :] = sums[0]
    sp[4:5, :] = sums[1]
    sp[2:3, :] = sums[2]
    sp[5:6, :] = sums[3]

    plane_start(0)

    SH = R + HP
    out_grad = dot(mixg[...], hgb[...]).astype(BF16)
    for g in range(G):
        gqo[1, g * SH : g * SH + R, :] = out_grad[g * R : (g + 1) * R, :]
    qt[...] = dot_nt(wo[...], hgb[...])
    gate_grad = [jnp.zeros((1, T), F32), jnp.zeros((1, T), F32)]
    for part in range(N):
        picked_rows = [jnp.zeros((HP, T), F32), jnp.zeros((HP, T), F32)]
        for at in range(NE):
            for i in range(LE):
                lo = expert_rows(at, i, part)
                one = qt[lo : lo + HP, :]
                x = at * LE + i
                for k in range(2):
                    picked_rows[k] = picked_rows[k] + one * hot[k][x : x + 1, :]
        for k in range(2):
            span = slice(part * HP, (part + 1) * HP)
            rounded_mix = mix[k, span, :].astype(BF16).astype(F32)
            gate_grad[k] = gate_grad[k] + jnp.sum(picked_rows[k] * rounded_mix, axis=0, keepdims=True)
            mgk[k, span, :] = (picked_rows[k] * gate[k]).astype(BF16)
    middle = gate[0] * gate_grad[0] + gate[1] * gate_grad[1]
    logit_grad = sum(hot[k] * (gate[k] * (gate_grad[k] - middle)) for k in range(2))
    logit_low = logit_grad.astype(BF16)

    def attend_back(k):
        for i in range(tiles):
            at = pl.ds(i * TL, TL)
            low = prob[k, :, at]
            p = low.astype(F32)
            prob_grad = dot(vn[...], mgk[k, :, at])
            inner = jnp.sum(p * prob_grad, axis=0, keepdims=True)
            score = (p * (prob_grad - inner)).astype(BF16)
            dq[k, :, at] = (dot(kt[...], score) * scale).astype(BF16)
            key_part = dot_nt(score, qk[k, :, at])
            value_part = dot_nt(low, mgk[k, :, at])
            if k == 0 and i == 0:
                dk[...] = key_part
                dv[...] = value_part
            else:
                dk[...] = dk[...] + key_part
                dv[...] = dv[...] + value_part

    attend_back(0)
    plane_middle(2)
    line_start(1)
    attend_back(1)
    plane_middle(3)

    H, PC = z.reach, z.piece
    offsets = [o for o in range(-H, H + 1) if o]
    inside = T >= LONGEST

    def halo_source(o):
        if inside:
            return (spot_in_row + 1) * T - ws if o > 0 else spot_in_row * T - LONGEST - ws
        return (spot_in_row + o) * T - ws

    def halo_copy(s, o):
        to = rem(here + o + G, G)
        return pltpu.make_async_remote_copy(
            src_ref=halo_out.at[s],
            dst_ref=halo_in.at[s],
            send_sem=hl_s.at[s],
            recv_sem=hl_r.at[s],
            device_id=(d, lax.div(to, N), rem(to, N)),
            device_id_type=MESH,
        )

    for s, o in enumerate(offsets):
        valid = jnp.logical_and(spot_in_row + o >= 0, spot_in_row + o < z.per_row)

        @pl.when(valid)
        def _(s=s, o=o):
            at = rows(halo_source(o), PC, 128)
            halo_out[s, 0] = (dk[at, :] * scale).astype(BF16)
            halo_out[s, 1] = dv[at, :].astype(BF16)
            halo_copy(s, o).start()

    for part in range(N):
        for at in range(NE):
            for i in range(LE):
                lo = expert_rows(at, i, part)
                x = at * LE + i
                span = slice(part * HP, (part + 1) * HP)
                one = dq[0, span, :].astype(F32) * hot[0][x : x + 1, :]
                one = one + dq[1, span, :].astype(F32) * hot[1][x : x + 1, :]
                dqt[lo : lo + HP, :] = one.astype(BF16)
    query_w_grad = dot(dqt[...], rw[own, :]).astype(BF16)
    key_w_grad = dot_tn((dk[...] * scale).astype(BF16), rw[...]).astype(BF16)
    value_w_grad = dot_tn(dv[...].astype(BF16), rw[...]).astype(BF16)
    for g in range(G):
        shared = slice((g % N) * HP, (g % N + 1) * HP)
        gqo[0, g * SH : g * SH + R, :] = query_w_grad[g * R : (g + 1) * R, :]
        gqo[0, g * SH + R : (g + 1) * SH, :] = key_w_grad[shared, :]
        gqo[1, g * SH + R : (g + 1) * SH, :] = value_w_grad[shared, :]
    push(gqo.at[1 - c], cqo, qc_r.at[0], mate)
    ones = jnp.ones((8, T), BF16)
    sp[6:7, :] = dot_nt(ones, dqt[...])[0:1, :]
    sp[7:8, :] = jnp.zeros((1, D), F32)
    sp[7:8, 0 : z.experts] = jnp.transpose(
        jnp.broadcast_to(jnp.sum(logit_grad, axis=1, keepdims=True), (z.experts, 128))
    )[0:1, :]
    acc[...] = dot_tn(dqt[...], wq[...]) + dot_tn(logit_low, r_ref[...])
    sp[16:24, :] = dot(logit_low, rw[own, :])
    sp[15:16, :] = jnp.zeros((1, D), F32)
    sp[15:16, 0:HEAD] = jnp.sum(dv[...], axis=0, keepdims=True)
    YW = D // NY
    ER = N * SH
    landed(cqo, qc_r.at[0])
    plane_middle(0)
    pqo[...] = (gqo[c].astype(F32) + cqo[...].astype(F32)).astype(BF16)
    for i in range(1, NP):
        there, to = in_plane(i)
        src = pqo.at[rows(rem(there, NE) * ER, ER), rows(lax.div(there, NE) * YW, YW, 128)]
        push(src, rqo.at[i], qp_r.at[0], to)
    line_start(2)
    line_start(3)

    dk[...] = dk[...] * scale
    for s, o in enumerate(offsets):
        back_valid = jnp.logical_and(spot_in_row - o >= 0, spot_in_row - o < z.per_row)

        @pl.when(back_valid)
        def _(s=s, o=o):
            halo_copy(s, o).wait_recv()
            at = off if (not inside or o > 0) else off + T - LONGEST
            at = rows(at, PC, 128)
            dk[at, :] = dk[at, :] + halo_in[s, 0].astype(F32)
            dv[at, :] = dv[at, :] + halo_in[s, 1].astype(F32)

    key_grad = dk[own, :]
    value_grad = dv[own, :]
    key_low, value_low = key_grad.astype(BF16), value_grad.astype(BF16)
    acc[...] = acc[...] + dot(key_low, wkv[0]) + dot(value_low, wkv[1])

    def norm_one_back(i, carry):
        at = rows(i * 128, 128, 128)
        unit, inverse = norm_stats(xw[rows(off + i * 128, 128, 128), :])
        grad = acc[at, :]
        scaled = grad * gain_one
        back = inverse * (
            scaled
            - jnp.mean(scaled, axis=1, keepdims=True)
            - unit * jnp.mean(scaled * unit, axis=1, keepdims=True)
        )
        ig_ref[at, :] = hgrad[at, :] + back
        parts = (grad * unit, grad)
        return tuple(a + jnp.sum(b, axis=0, keepdims=True) for a, b in zip(carry, parts))

    sums = lax.fori_loop(0, T // 128, norm_one_back, (zero_row,) * 2)
    ig_copy = pltpu.make_async_copy(ig_ref, ig_any, loc_sem.at[4])
    ig_copy.start()
    sp[0:1, :] = sums[0]
    sp[1:2, :] = sums[1]
    for j in range(8 + N, 15):
        sp[j : j + 1, :] = zero_row
    push(sp.at[:, other_cols], csp, qc_r.at[1], mate)

    landed(csp, qc_r.at[1])
    psp[...] = sp[:, mine_cols] + csp[...]
    for i in range(1, NP):
        _, to = in_plane(i)
        push(psp, rsp.at[i], qp_r.at[1], to)

    line_start(0)

    whole = zsend[0].astype(F32)
    for j in range(1, N):
        there, _ = in_line(-j)
        landed(zrecv.at[there], gz_r.at[there])
        whole = whole + zrecv[there].astype(F32)

    def fin_left(buffer, core, ys, es):
        return buffer.at[rows(core * HR + (es * NY + ys) * HS, HS), left]

    def fin_right(buffer, core, ys, es):
        return buffer.at[rows(core * HR + (ys * NE + es) * HS, HS), right]

    def fin_to_mate(ys, es):
        for piece in (fin_left, fin_right):
            at = piece(fin, c, ys, es)
            push(at, at, ga_r.at[2 * NP - 2], mate)

    fin[rows(c * HR + (e * NY + y) * HS, HS), left] = whole[:, 0:half].astype(BF16)
    fin[rows(c * HR + (y * NE + e) * HS, HS), right] = whole[:, half:].astype(BF16)
    for i in range(1, NP):
        _, to = in_plane(i)
        at = fin_left(fin, c, y, e)
        push(at, at, ga_r.at[i - 1], to)
        at = fin_right(fin, c, y, e)
        push(at, at, ga_r.at[NP - 2 + i], to)
    fin_to_mate(y, e)

    whole = pqo[rows(e * ER, ER), rows(y * YW, YW, 128)].astype(F32)
    landed_all(NP - 1, rqo.at[0], qp_r.at[0])
    for i in range(1, NP):
        whole = whole + rqo[i].astype(F32)
    zqo[...] = whole.astype(BF16)
    for j in range(1, N):
        there, to = in_line(j)
        push(zqo.at[rows(there * SH, SH)], yqo.at[j], qz_r.at[0], to)
    whole = psp[...]
    landed_all(NP - 1, rsp.at[0], qp_r.at[1])
    for i in range(1, NP):
        whole = whole + rsp[i]
    zsp[...] = whole
    for j in range(1, N):
        _, to = in_line(j)
        push(zsp, ysp.at[j], qz_r.at[1], to)

    cols_copy.wait()
    landed_all(N - 1, outd.at[0], od_r.at[0])
    for j in range(N):
        at = pl.ds(j * T, T)
        out_ref[at, :] = out_ref[at, :] + outd[j].astype(F32)
    out_copy = pltpu.make_async_copy(out_ref, out_any, loc_sem.at[5])
    out_copy.start()

    whole = zqo[rows(n * SH, SH), :].astype(F32)
    landed_all(N - 1, yqo.at[0], qz_r.at[0])
    for j in range(1, N):
        whole = whole + yqo[j].astype(F32)
    my_cols = rows(y * YW, YW, 128)
    fqo[c, :, my_cols] = whole.astype(BF16)
    at = fqo.at[c, :, my_cols]
    others = [(i, other) for i in range(NY) for other in range(2) if i or other]
    for i, other in others:
        to = (2 * in_rows(i)[0] + (1 - c if other else c), e, n)
        push(at, at, qa_r.at[0], to)
    whole = zsp[...]
    landed_all(N - 1, ysp.at[0], qz_r.at[1])
    for j in range(1, N):
        whole = whole + ysp[j]
    fsp[:, mine_cols] = whole
    at = fsp.at[:, mine_cols]
    push(at, at, qa_r.at[1], mate)
    for i in range(1, NP):
        near, _ = in_plane(-i)
        ys, es = lax.div(near, NE), rem(near, NE)
        landed(fin_left(fin, c, ys, es), ga_r.at[i - 1])
        landed(fin_right(fin, c, ys, es), ga_r.at[NP - 2 + i])
        fin_to_mate(ys, es)
    at = rows(c * HR, HR)
    g_ref[at, :] = fin[at, :].astype(F32)
    landed(fsp.at[:, other_cols], qa_r.at[1])
    small_ref[...] = fsp[...]
    landed_all(len(others), fqo.at[0, :, pl.ds(0, YW)], qa_r.at[0])
    fqo_ref[...] = fqo[...]
    ig_copy.wait()
    out_copy.wait()
    landed(fin.at[rows((1 - c) * HR, HR)], ga_r.at[2 * NP - 2])
    at = rows((1 - c) * HR, HR)
    g_ref[at, :] = fin[at, :].astype(F32)

    for kind, size in enumerate(sent):
        at = ruler.at[pl.ds(0, size // 256)]
        if kind == 0:
            at = bias.at[pl.ds(0, size // (16 * 128 * 4))]
        pltpu.make_async_remote_copy(
            src_ref=at,
            dst_ref=at,
            send_sem=send_sems.at[kind],
            recv_sem=send_sems.at[kind],
            device_id=mate,
            device_id_type=MESH,
        ).wait_send()
    for valid, copies in maybe_started:

        @pl.when(valid)
        def _(copies=copies):
            for copy in copies:
                copy.wait_send()

    for s, o in enumerate(offsets):
        valid = jnp.logical_and(spot_in_row + o >= 0, spot_in_row + o < z.per_row)

        @pl.when(valid)
        def _(s=s, o=o):
            halo_copy(s, o).wait_send()


def run(z, x, seg, chosen, vectors, q, k, v, o, r, up, down, cot):
    N, G, NP, NY, NE = z.narrow, z.group, z.plane, z.rows_y, z.expert
    T, W, D, R, HP = z.block, z.window, z.width, z.shard, z.head_part
    FL = z.ff_local
    FR = D + FL
    HR = FR // 2
    HS = HR // NP
    YW = D // NY
    SH = R + HP
    ER = N * SH
    QR = G * R
    GR = G * SH
    S = 2 * z.reach
    SMALL = z.small_rows
    vmem = pl.BlockSpec(memory_space=pltpu.VMEM)
    anywhere = pl.BlockSpec(memory_space=pltpu.HBM)
    scratch = [
        ((N * T, D // N), F32),
        ((T, D), F32),
        ((W, D), F32),
        ((W, D), BF16),
        ((QR, D), BF16),
        ((QR, D), BF16),
        ((2, HEAD, D), BF16),
        ((G, 16, 128), F32),
        ((8, 128), F32),
        ((HEAD, 128), F32),
        ((N, FR, D), BF16),
        ((T, D), BF16),
        ((8, z.row_len), F32),
        ((W, 8), F32),
        ((W, HEAD), BF16),
        ((W, HEAD), BF16),
        ((HEAD, W), BF16),
        ((HEAD, W), BF16),
        ((QR, T), F32),
        ((2, HEAD, T), BF16),
        ((2, W, T), BF16),
        ((2, HEAD, T), F32),
        ((QR, T), BF16),
        ((T, D), F32),
        ((T, D), F32),
        ((T, D), BF16),
        ((N, T, FL), BF16),
        ((N, T, FL), BF16),
        ((T, FL), BF16),
        ((T, D), F32),
        ((T, D), F32),
        ((T, D), BF16),
        ((2, HEAD, T), BF16),
        ((W, HEAD), F32),
        ((W, HEAD), F32),
        ((2, HEAD, T), BF16),
        ((QR, T), BF16),
        ((max(S, 1), 2, z.piece, HEAD), BF16),
        ((max(S, 1), 2, z.piece, HEAD), BF16),
        ((T, D), BF16),
        ((N, T, D // N), BF16),
        ((N, FR, D), BF16),
        ((GROUP_BYTES // 256, 128), BF16),
        ((N, HR, D), BF16),
        ((N, HR, D), BF16),
        ((N, NE, HR // NE, D // 2), BF16),
        ((N, NY, HR // NY, D // 2), BF16),
        ((N, HR // NE, D // 2), BF16),
        ((N, HR // NY, D // 2), BF16),
        ((N, NY, HS, D // 2), BF16),
        ((N, NE, HS, D // 2), BF16),
        ((N, HS, D), BF16),
        ((N, HS, D), BF16),
        ((FR, D), BF16),
        ((2, GR, D), BF16),
        ((GR, D), BF16),
        ((GR, D), BF16),
        ((NP, ER, YW), BF16),
        ((ER, YW), BF16),
        ((N, SH, YW), BF16),
        ((2, SH, D), BF16),
        ((SMALL, D), F32),
        ((SMALL, D // 2), F32),
        ((SMALL, D // 2), F32),
        ((NP, SMALL, D // 2), F32),
        ((SMALL, D // 2), F32),
        ((N, SMALL, D // 2), F32),
        ((SMALL, D), F32),
    ]
    pairs = [
        (N - 1,),
        (1,),
        (G - 1,),
        (G - 1,),
        (1,),
        (G - 1,),
        (1,),
        (4, N - 1, max(NE, NY) - 1),
        (N - 1,),
        (1,),
        (1,),
        (max(S, 1),),
        (N,),
        (4, N, max(NE, NY) - 1),
        (N,),
        (2 * NP - 1,),
        (2,),
        (2,),
        (2,),
        (2,),
    ]
    HALO = 11
    sems = [pltpu.SemaphoreType.DMA((6,)), pltpu.SemaphoreType.DMA((GROUPS,))]
    for at, shape in enumerate(pairs):
        sems += [pltpu.SemaphoreType.DMA(shape)] * (2 if at == HALO else 1)
    sems += [pltpu.SemaphoreType.DMA((2, 2, N)), pltpu.SemaphoreType.DMA((2, N))]
    outs = [
        ((N * T, D // N), F32),
        ((T, D), F32),
        ((FR, D), F32),
        ((2, SH, D), BF16),
        ((SMALL, D), F32),
    ]
    return pl.pallas_call(
        functools.partial(kernel, z),
        out_shape=[pltpu.VMEM(s, t) for s, t in outs],
        in_specs=[anywhere] + [vmem] * (7 + len(vectors)) + [anywhere] * 2 + [vmem],
        out_specs=[pl.BlockSpec(memory_space=pl.ANY)] * 2 + [vmem] * 3,
        scratch_shapes=[pltpu.VMEM(s, t) for s, t in scratch] + sems,
        compiler_params=pltpu.CompilerParams(
            collective_id=0, has_side_effects=True, vmem_limit_bytes=58 * 2**20
        ),
        name="layer",
    )(x, seg, chosen, *vectors, q, k, v, o, r, up, down, cot)


def finish_kernel(
    z,
    out_in,
    ig_in,
    g_in,
    fqo_ref,
    small_ref,
    out_any,
    ig_out,
    g1_ref,
    s1_ref,
    gq_ref,
    qb_ref,
    gk_ref,
    gv_ref,
    vb_ref,
    go_ref,
    ob_ref,
    rw_ref,
    rb_ref,
    g2_ref,
    s2_ref,
    gup_any,
    ub_ref,
    gdown_any,
    db_ref,
    sems,
):
    e, n = lax.axis_index("expert"), lax.axis_index("narrow")
    N, T, D, R, HP, LE = z.narrow, z.block, z.width, z.shard, z.head_part, z.local_experts
    copies = []

    def put(src, dst):
        copies.append(pltpu.make_async_copy(src, dst, sems.at[len(copies)]))
        copies[-1].start()

    put(out_in, out_any)
    put(ig_in, ig_out)
    put(g_in.at[pl.ds(0, D)], gup_any)
    put(g_in.at[pl.ds(D, z.ff_local)], gdown_any)
    gq_ref[...] = fqo_ref[0, 0:R, :].astype(F32)
    go_ref[...] = fqo_ref[1, 0:R, :].astype(F32)
    gk_ref[...] = fqo_ref[0, R : R + HP, :].astype(F32)
    gv_ref[...] = fqo_ref[1, R : R + HP, :].astype(F32)
    g1_ref[...] = small_ref[0:1, :]
    s1_ref[...] = small_ref[1:2, :]
    ob_ref[...] = small_ref[2:3, :]
    g2_ref[...] = small_ref[3:4, :]
    s2_ref[...] = small_ref[4:5, :]
    db_ref[...] = small_ref[5:6, :]
    rb_ref[...] = small_ref[7:8, 0 : z.experts]
    rw_ref[...] = small_ref[16 : 16 + z.experts, :]
    upper = jnp.zeros((1, D), F32)
    for j in range(N):
        upper = jnp.where(n == j, small_ref[8 + j : 9 + j, :], upper)
    ub_ref[...] = upper
    here = e * N + n
    query = pltpu.roll(small_ref[0:8, :], lax.rem(D - here * R, D), 1)
    for i in range(LE):
        qb_ref[i : i + 1, :] = query[6:7, i * HP : (i + 1) * HP]
    value = pltpu.roll(small_ref[8:16, :], lax.rem(D - n * HP, D), 1)
    vb_ref[...] = value[7:8, 0:HP]
    for copy in copies:
        copy.wait()


def finish(z, out, ig, fin, fqo, small):
    N, T, D, R, HP = z.narrow, z.block, z.width, z.shard, z.head_part
    FL = z.ff_local
    vmem = pl.BlockSpec(memory_space=pltpu.VMEM)
    anywhere = pl.BlockSpec(memory_space=pltpu.HBM)
    shapes = [
        (N * T, D // N),
        (T, D),
        (1, D),
        (1, D),
        (R, D),
        (z.local_experts, HP),
        (HP, D),
        (HP, D),
        (1, HP),
        (R, D),
        (1, D),
        (z.experts, D),
        (1, z.experts),
        (1, D),
        (1, D),
        (D, FL),
        (1, FL),
        (FL, D),
        (1, D),
    ]
    return pl.pallas_call(
        functools.partial(finish_kernel, z),
        out_shape=[jax.ShapeDtypeStruct(s, F32) for s in shapes],
        in_specs=[pl.BlockSpec(memory_space=pl.ANY)] * 3 + [vmem] * 2,
        out_specs=[anywhere] * 2 + [vmem] * 13 + [anywhere, vmem, anywhere, vmem],
        scratch_shapes=[
            pltpu.SemaphoreType.DMA((4,)),
        ],
        compiler_params=pltpu.CompilerParams(vmem_limit_bytes=16 * 2**20),
        name="finish",
    )(out, ig, fin, fqo, small)


def per_device(
    inputs,
    seg_ids,
    chosen,
    gain_one,
    shift_one,
    query_w,
    query_b,
    key_w,
    value_w,
    value_b,
    out_w,
    out_b,
    router_w,
    router_b,
    gain_two,
    shift_two,
    up_w,
    up_b,
    down_w,
    down_b,
    cotangent,
):
    narrow = lax.axis_size("narrow")
    e, n = lax.axis_index("expert"), lax.axis_index("narrow")
    z = Sizes(
        lax.axis_size("dp"),
        lax.axis_size("expert"),
        narrow,
        inputs.shape[0],
        inputs.shape[1],
        seg_ids.shape[1],
        query_w.shape[0],
        up_w.shape[1],
    )
    D, R, HP = z.width, z.shard, z.head_part
    vectors = [gain_one, shift_one, out_b, gain_two, shift_two, down_b, up_b]
    vectors = [v.reshape(1, -1) for v in vectors]
    vectors += [query_b, value_b.reshape(1, -1), router_b.reshape(1, -1)]
    parts = run(
        z,
        inputs,
        seg_ids,
        jnp.transpose(chosen),
        vectors,
        jnp.transpose(query_w, (0, 2, 1)).reshape(R, D),
        jnp.transpose(key_w),
        jnp.transpose(value_w),
        out_w.reshape(R, D),
        jnp.transpose(router_w),
        up_w,
        down_w,
        cotangent,
    )
    out, ig, g1, s1, gq, qb, gk, gv, vb, go, ob, rw, rb, g2, s2, gup, ub, gdown, db = finish(
        z, *parts
    )
    return (
        out,
        ig,
        g1.reshape(-1),
        s1.reshape(-1),
        jnp.transpose(gq.reshape(z.local_experts, HP, D), (0, 2, 1)),
        qb,
        jnp.transpose(gk),
        jnp.transpose(gv),
        vb.reshape(-1),
        go.reshape(z.local_experts, HP, D),
        ob.reshape(-1),
        jnp.transpose(rw),
        rb.reshape(-1),
        g2.reshape(-1),
        s2.reshape(-1),
        gup,
        ub.reshape(-1),
        gdown,
        db.reshape(-1),
    )


def solution(mesh):
    return jax.shard_map(
        per_device,
        mesh=mesh,
        in_specs=(
            P("dp", None),
            P("dp", None),
            P("dp", None),
            P(),
            P(),
            P("expert", None, "narrow"),
            P("expert", "narrow"),
            P(None, "narrow"),
            P(None, "narrow"),
            P("narrow"),
            P("expert", "narrow", None),
            P(),
            P(),
            P(),
            P(),
            P(),
            P(None, "narrow"),
            P("narrow"),
            P("narrow", None),
            P(),
            P(("dp", "expert"), "narrow"),
        ),
        out_specs=(
            P(("dp", "expert"), "narrow"),
            P(("dp", "expert", "narrow"), None),
            P(),
            P(),
            P("expert", None, "narrow"),
            P("expert", "narrow"),
            P(None, "narrow"),
            P(None, "narrow"),
            P("narrow"),
            P("expert", "narrow", None),
            P(),
            P(),
            P(),
            P(),
            P(),
            P(None, "narrow"),
            P("narrow"),
            P("narrow", None),
            P(),
        ),
        check_vma=False,
    )
```
